32 devices in a mesh: tx: 4 (over z), ty: 8 (over y, x, core).
Axes of the slice: x: 2, y: 2, z: 4, core: 2. Of those that a mesh axis runs over, the one named last changes fastest.
Arguments:
- points: bfloat16 [32, 1024, 256], P(('tx', 'ty')), may hold values from -6 to 6
- counts: int32 [32], P(('tx', 'ty')), may hold values from 512 to 1024, as said below
- owner: int32 [32, 1024], P(('tx', 'ty')), may hold values from 0 to 31, as said below
- zorder: int32 [32, 2048], P(('tx', 'ty')), may hold values from 0 to 2047, as said below
- border: int32 [32, 4, 64], P(('tx', 'ty')), may hold values from 0 to 1023, as said below
- near: int32 [32, 16, 1024], P(('tx', 'ty')), may hold values from 0 to 1279, as said below
- w_near: bfloat16 [256, 256], replicated, may hold values from -0.375 to 0.375
- gain_one: float32 [256], replicated, may hold values from 0.1 to 1.9
- conv_w: bfloat16 [3, 8, 32, 32], replicated, may hold values from -0.625 to 0.625
- gain_two: float32 [256], replicated, may hold values from 0.1 to 1.9
- w_up: bfloat16 [256, 1024], replicated, may hold values from -0.375 to 0.375
- w_down: bfloat16 [1024, 256], replicated, may hold values from -0.1875 to 0.1875
- grad_out: bfloat16 [32, 1024, 256], P(('tx', 'ty')), may hold values from -6 to 6
Outputs:
- out_rows: bfloat16 [32, 1024, 256], P(('tx', 'ty'))
- grad_points: bfloat16 [32, 1024, 256], P(('tx', 'ty'))
- grad_w_near: float32 [256, 256], replicated
- grad_gain_one: float32 [256], replicated
- grad_conv: float32 [3, 8, 32, 32], replicated
- grad_gain_two: float32 [256], replicated
- grad_w_up: float32 [256, 1024], replicated
- grad_w_down: float32 [1024, 256], replicated
The draws below stay inside these ranges and needn't reach their ends.
Inputs may be any that keep to these rules, and one draw needn't show every extreme that they name: `counts`: every tile has at least half of its slots live, and some tile has all of them live. Only live rows count. Among the live rows of one tile at most 64 name the same owner. One particular owner receives exactly 64 live rows from every tile; every other owner receives at most 64 live rows from each tile, so its receive buffer may be partly empty. `zorder`: each owner's entry is a permutation of its 2048 receive slots whose first entries name exactly the filled slots. `border`: each list names distinct live rows of its tile; lists toward a side outside the grid are never read. `near`: indices below 1024 name live rows of the tile; the others name halo rows of blocks whose neighbour tile exists.
All inputs are finite; a program needn't handle non-finite values.
Results may differ from the reference program's by a relative error of at most 0.015.
Values may be sent and summed in bfloat16 or wider, within the bound.
No kernel may reach another device: no remote copies, remote signals or barrier semaphores. Data moves between devices by JAX's collectives and lax.ppermute only.
A program may use at most 64 MiB of HBM per device.

```python
import math
import jax
import jax.numpy as jnp
from jax import lax

C = 256
FFN = 1024
GROUPS = 8
PATCH = 1024
K_NEAR = 16
TILE_ROWS = 1024
GW = 32
BORDER = 64
RECV = 2048
TILE_COLS = 4
TILE_LINES = 8
TILES = 32
ALL_ROWS = 32768


def ranked_by(score):
    order = jnp.argsort(score, stable=True).astype(jnp.int32)
    return jnp.zeros(score.shape, jnp.int32).at[order].set(jnp.arange(score.shape[0], dtype=jnp.int32))


def tile_counts(key):
    count_key = jax.random.fold_in(key, 101)
    full_key = jax.random.fold_in(key, 102)
    counts = jax.random.randint(count_key, (TILES,), TILE_ROWS // 2, TILE_ROWS + 1).astype(jnp.int32)
    fullest = jax.random.randint(full_key, (), 0, TILES)
    return counts.at[fullest].set(TILE_ROWS)


def layout_tables(key):
    capacity = RECV // TILES
    counts = tile_counts(key)
    star = jax.random.randint(jax.random.fold_in(key, 103), (), 0, TILES).astype(jnp.int32)
    route_key = jax.random.fold_in(key, 104)
    order_key = jax.random.fold_in(key, 105)
    index = jnp.arange(TILE_ROWS, dtype=jnp.int32)

    def tile_owner(tile_key, count):
        first_key, second_key = jax.random.split(tile_key)
        mixing = jax.random.permutation(first_key, TILE_ROWS).astype(jnp.int32)
        rank = ranked_by(jnp.where(index < count, mixing, TILE_ROWS + mixing))
        others = jax.random.permutation(second_key, TILES - 1).astype(jnp.int32)
        others = others + (others >= star).astype(jnp.int32)
        spread = jnp.take(others, jnp.maximum(rank - capacity, 0) % (TILES - 1))
        return jnp.where(rank < capacity, star, spread).astype(jnp.int32)
    owner = jax.vmap(tile_owner)(jax.random.split(route_key, TILES), counts)
    live = (index[None, :] < counts[:, None]).astype(jnp.int32)
    source = jnp.broadcast_to(jnp.arange(TILES, dtype=jnp.int32)[:, None], owner.shape)
    pair_load = jnp.zeros((TILES, TILES), jnp.int32).at[source, owner].add(live)
    filled = jnp.arange(capacity, dtype=jnp.int32)[None, None, :] < jnp.transpose(pair_load)[:, :, None]
    filled = filled.reshape(TILES, RECV)

    def receiver_order(recv_key, mask):
        mixing = jax.random.permutation(recv_key, RECV).astype(jnp.int32)
        return jnp.argsort(jnp.where(mask, mixing, RECV + mixing), stable=True).astype(jnp.int32)
    zorder = jax.vmap(receiver_order)(jax.random.split(order_key, TILES), filled)
    return (owner, zorder)


def draw_counts(key, part):
    return tile_counts(key)


def draw_owner(key, part):
    return layout_tables(key)[0]


def draw_zorder(key, part):
    return layout_tables(key)[1]


def draw_border(key, part):
    counts = tile_counts(key)
    index = jnp.arange(TILE_ROWS, dtype=jnp.int32)
    list_ids = jnp.arange(4, dtype=jnp.int32)

    def tile_lists(tile_key, count):

        def one_list(list_key, list_id):
            mixing = jax.random.permutation(list_key, TILE_ROWS).astype(jnp.int32)
            mixing = jnp.where((index == count - 1) & (list_id == 0), -1, mixing).astype(jnp.int32)
            order = jnp.argsort(jnp.where(index < count, mixing, TILE_ROWS + mixing), stable=True).astype(jnp.int32)
            return order[:BORDER]
        return jax.vmap(one_list)(jax.random.split(tile_key, 4), list_ids)
    return jax.vmap(tile_lists)(jax.random.split(jax.random.fold_in(key, 201), TILES), counts)


def draw_near(key, part):
    counts = tile_counts(key)
    tile_ids = jnp.arange(TILES, dtype=jnp.int32)
    column = tile_ids // TILE_LINES
    line = tile_ids % TILE_LINES
    present = jnp.stack([column + 1 < TILE_COLS, column > 0, line + 1 < TILE_LINES, line > 0], axis=1)
    slot_index = jnp.arange(K_NEAR, dtype=jnp.int32)[:, None]

    def tile_near(tile_key, count, exists):
        first_key, second_key, third_key, fourth_key = jax.random.split(tile_key, 4)
        inside = jax.random.randint(first_key, (K_NEAR, TILE_ROWS), 0, count).astype(jnp.int32)
        direction = jax.random.randint(second_key, (K_NEAR, TILE_ROWS), 0, 4).astype(jnp.int32)
        offset = jax.random.randint(third_key, (K_NEAR, TILE_ROWS), 0, BORDER).astype(jnp.int32)
        edge_point = jax.random.randint(fourth_key, (1, TILE_ROWS), 0, 4) == 0
        usable = jnp.take(exists, direction) & edge_point & (slot_index < K_NEAR // 2)
        return jnp.where(usable, TILE_ROWS + direction * BORDER + offset, inside).astype(jnp.int32)
    return jax.vmap(tile_near)(jax.random.split(jax.random.fold_in(key, 301), TILES), counts, present)


def shard_levels(stream_key, dims, shards, low, high):
    def one(axis_at, parts):
        steps = jax.random.uniform(jax.random.fold_in(jax.random.fold_in(stream_key, 6), axis_at), (parts,), jnp.float32, low / len(shards), high / len(shards))
        return jnp.repeat(jnp.exp(steps), dims[axis_at] // parts).reshape((-1,) + (1,) * (len(dims) - axis_at - 1))

    level = one(*shards[0])
    for cut in shards[1:]:
        level = level * one(*cut)
    return level


def bell_draw(stream_key, shape, scale, limit, cuts=(), held_as=jnp.bfloat16):
    values = jax.random.normal(stream_key, shape, jnp.float32) * scale
    if len(cuts) > 0:
        values = shard_levels(stream_key, shape, cuts, -0.22, 0.18) * values
    return jnp.clip(values, min=-limit, max=limit).astype(held_as)


def setup_inputs(seed: int = 0) -> dict:
    streams_of = jax.random.split(jax.random.key(seed), 14)
    return {
        "points": bell_draw(streams_of[0], (TILES, TILE_ROWS, C), 1.0, 6.0, ((0, 32),)),
        "counts": draw_counts(jax.random.fold_in(streams_of[13], 71), 0),
        "owner": draw_owner(jax.random.fold_in(streams_of[13], 71), 0),
        "zorder": draw_zorder(jax.random.fold_in(streams_of[13], 71), 0),
        "border": draw_border(jax.random.fold_in(streams_of[13], 71), 0),
        "near": draw_near(jax.random.fold_in(streams_of[13], 71), 0),
        "w_near": bell_draw(streams_of[6], (C, C), C ** -0.5, 0.375),
        "gain_one": jnp.clip(1.0 + 0.18 * jax.random.normal(streams_of[7], (C,), jnp.float32), 0.1, 1.9),
        "conv_w": bell_draw(streams_of[8], (3, GROUPS, GW, GW), (3 * GW) ** -0.5, 0.625),
        "gain_two": jnp.clip(1.0 + 0.18 * jax.random.normal(streams_of[9], (C,), jnp.float32), 0.1, 1.9),
        "w_up": bell_draw(streams_of[10], (C, FFN), C ** -0.5, 0.375),
        "w_down": bell_draw(streams_of[11], (FFN, C), FFN ** -0.5, 0.1875),
        "grad_out": bell_draw(streams_of[12], (TILES, TILE_ROWS, C), 1.0, 6.0, ((0, 32),)),
    }


eps_norm = 1e-06
gelu_coef = 0.7978845608028654
cubic_coef = 0.044715

def gelu_tanh(value):
    inner = gelu_coef * (value + cubic_coef * value * value * value)
    return 0.5 * value * (1.0 + jnp.tanh(inner))

def gelu_slope(value):
    inner = gelu_coef * (value + cubic_coef * value * value * value)
    tangent = jnp.tanh(inner)
    return 0.5 * (1.0 + tangent) + 0.5 * value * (1.0 - tangent * tangent) * gelu_coef * (1.0 + 3.0 * cubic_coef * value * value)

def inverse_rms(value):
    return lax.rsqrt(lax.optimization_barrier(jnp.mean(value * value, axis=-1, keepdims=True)) + eps_norm)

def tile_forward(points_tile, halo_rows, near_tile, w_near):
    extended = jnp.concatenate([points_tile, halo_rows], axis=0)
    count_near = near_tile.shape[0]

    def add_neighbour(index, total):
        return total + jnp.take(extended, near_tile[index], axis=0).astype(jnp.float32)
    total = lax.fori_loop(0, count_near, add_neighbour, jnp.zeros(points_tile.shape, jnp.float32))
    average = (total * (1.0 / count_near)).astype(jnp.bfloat16)
    linear_part = jnp.dot(average, w_near, preferred_element_type=jnp.float32)
    lifted = (points_tile.astype(jnp.float32) + gelu_tanh(linear_part)).astype(jnp.bfloat16)
    return (average, linear_part, lifted)

def tile_backward(lifted_grad, average, linear_part, near_tile, w_near, ext_count):
    count_near = near_tile.shape[0]
    tile_rows = lifted_grad.shape[0]
    act_grad = (lifted_grad.astype(jnp.float32) * gelu_slope(linear_part)).astype(jnp.bfloat16)
    near_grad = lax.dot_general(average, act_grad, (((0,), (0,)), ((), ())), preferred_element_type=jnp.float32)
    spread = lax.dot_general(act_grad, w_near, (((1,), (1,)), ((), ())), preferred_element_type=jnp.float32) * (1.0 / count_near)

    def scatter_neighbour(index, total):
        return total.at[near_tile[index]].add(spread)
    ext_grad = lax.fori_loop(0, count_near, scatter_neighbour, jnp.zeros((ext_count, spread.shape[1]), jnp.float32))
    row_grad = lifted_grad.astype(jnp.float32) + ext_grad[:tile_rows]
    halo_grad = ext_grad[tile_rows:].astype(jnp.bfloat16)
    return (near_grad, row_grad, halo_grad)

def route_ranks(owner_tile, count, tiles):
    tile_rows = owner_tile.shape[0]
    index = jnp.arange(tile_rows, dtype=jnp.int32)
    live = index < count
    score = jnp.where(live, owner_tile * tile_rows + index, tiles * tile_rows + index).astype(jnp.int32)
    order = jnp.argsort(score, stable=True).astype(jnp.int32)
    members = (owner_tile[:, None] == jnp.arange(tiles, dtype=jnp.int32)[None, :]) & live[:, None]
    per_owner = lax.optimization_barrier(jnp.sum(members.astype(jnp.int32), axis=0)).astype(jnp.int32)
    starts = (jnp.cumsum(per_owner) - per_owner).astype(jnp.int32)
    sorted_owner = jnp.take(owner_tile, order)
    ranked = (index - jnp.take(starts, sorted_owner)).astype(jnp.int32)
    rank = jnp.zeros((tile_rows,), jnp.int32).at[order].set(ranked)
    return (rank, live)

def shift_down(rows):
    return jnp.concatenate([jnp.zeros_like(rows[:1]), rows[:-1]], axis=0)

def shift_up(rows):
    return jnp.concatenate([rows[1:], jnp.zeros_like(rows[:1])], axis=0)

def grouped_apply(rows, conv_tap):
    length, width = rows.shape
    split = rows.astype(jnp.float32).reshape(length, conv_tap.shape[0], conv_tap.shape[1])
    return jnp.einsum('pga,gab->pgb', split, conv_tap.astype(jnp.float32)).reshape(length, width)

def grouped_back(rows, conv_tap):
    length, width = rows.shape
    split = rows.astype(jnp.float32).reshape(length, conv_tap.shape[0], conv_tap.shape[1])
    return jnp.einsum('pgb,gab->pga', split, conv_tap.astype(jnp.float32)).reshape(length, width)

def grouped_weight(inputs, outputs, groups, inner):
    length = inputs.shape[0]
    left = inputs.astype(jnp.float32).reshape(length, groups, inner)
    right = outputs.astype(jnp.float32).reshape(length, groups, inner)
    return jnp.einsum('pga,pgb->gab', left, right)

def patch_pass(serial, out_grad, gain_one, conv_w, gain_two, w_up, w_down):
    groups, inner = (conv_w.shape[1], conv_w.shape[2])
    serial_f = serial.astype(jnp.float32)
    scale_one = inverse_rms(serial_f)
    normed = (serial_f * scale_one * gain_one).astype(jnp.bfloat16)
    taps = (shift_down(normed), normed, shift_up(normed))
    mixed = grouped_apply(taps[0], conv_w[0]) + grouped_apply(taps[1], conv_w[1]) + grouped_apply(taps[2], conv_w[2])
    state = serial_f + mixed
    scale_two = inverse_rms(state)
    second = (state * scale_two * gain_two).astype(jnp.bfloat16)
    hidden_pre = jnp.dot(second, w_up, preferred_element_type=jnp.float32)
    hidden = gelu_tanh(hidden_pre).astype(jnp.bfloat16)
    result = (state + jnp.dot(hidden, w_down, preferred_element_type=jnp.float32)).astype(jnp.bfloat16)
    down_grad = lax.dot_general(hidden, out_grad, (((0,), (0,)), ((), ())), preferred_element_type=jnp.float32)
    hidden_grad = lax.dot_general(out_grad, w_down, (((1,), (1,)), ((), ())), preferred_element_type=jnp.float32).astype(jnp.bfloat16)
    pre_grad = (hidden_grad.astype(jnp.float32) * gelu_slope(hidden_pre)).astype(jnp.bfloat16)
    up_grad = lax.dot_general(second, pre_grad, (((0,), (0,)), ((), ())), preferred_element_type=jnp.float32)
    second_grad = lax.dot_general(pre_grad, w_up, (((1,), (1,)), ((), ())), preferred_element_type=jnp.float32).astype(jnp.bfloat16)
    unit_two = state * scale_two
    weighted_two = second_grad.astype(jnp.float32) * gain_two
    gain_two_grad = lax.optimization_barrier(jnp.sum(second_grad.astype(jnp.float32) * unit_two, axis=0))
    state_grad = out_grad.astype(jnp.float32) + scale_two * (weighted_two - unit_two * lax.optimization_barrier(jnp.mean(weighted_two * unit_two, axis=-1, keepdims=True)))
    mixed_grad = state_grad.astype(jnp.bfloat16)
    conv_grad = jnp.stack([grouped_weight(taps[0], mixed_grad, groups, inner), grouped_weight(taps[1], mixed_grad, groups, inner), grouped_weight(taps[2], mixed_grad, groups, inner)], axis=0)
    normed_grad = (shift_up(grouped_back(mixed_grad, conv_w[0])) + grouped_back(mixed_grad, conv_w[1]) + shift_down(grouped_back(mixed_grad, conv_w[2]))).astype(jnp.bfloat16)
    unit_one = serial_f * scale_one
    weighted_one = normed_grad.astype(jnp.float32) * gain_one
    gain_one_grad = lax.optimization_barrier(jnp.sum(normed_grad.astype(jnp.float32) * unit_one, axis=0))
    serial_grad = (state_grad + scale_one * (weighted_one - unit_one * lax.optimization_barrier(jnp.mean(weighted_one * unit_one, axis=-1, keepdims=True)))).astype(jnp.bfloat16)
    return (result, serial_grad, (gain_one_grad, conv_grad, gain_two_grad, up_grad, down_grad))

def gather_halo(sent):
    border_rows, width = (sent.shape[2], sent.shape[3])
    grid = sent.reshape(TILE_COLS, TILE_LINES, 4, border_rows, width)
    zeros_col = jnp.zeros((1, TILE_LINES, border_rows, width), sent.dtype)
    zeros_line = jnp.zeros((TILE_COLS, 1, border_rows, width), sent.dtype)
    from_next_col = jnp.concatenate([grid[1:, :, 0], zeros_col], axis=0)
    from_prev_col = jnp.concatenate([zeros_col, grid[:-1, :, 1]], axis=0)
    from_next_line = jnp.concatenate([grid[:, 1:, 2], zeros_line], axis=1)
    from_prev_line = jnp.concatenate([zeros_line, grid[:, :-1, 3]], axis=1)
    stacked = jnp.stack([from_next_col, from_prev_col, from_next_line, from_prev_line], axis=2)
    return stacked.reshape(TILE_COLS * TILE_LINES, 4 * border_rows, width)

def return_halo(halo_grads, border_rows):
    width = halo_grads.shape[2]
    grid = halo_grads.reshape(TILE_COLS, TILE_LINES, 4, border_rows, width)
    zeros_col = jnp.zeros((1, TILE_LINES, border_rows, width), halo_grads.dtype)
    zeros_line = jnp.zeros((TILE_COLS, 1, border_rows, width), halo_grads.dtype)
    back_zero = jnp.concatenate([zeros_col, grid[:-1, :, 0]], axis=0)
    back_one = jnp.concatenate([grid[1:, :, 1], zeros_col], axis=0)
    back_two = jnp.concatenate([zeros_line, grid[:, :-1, 2]], axis=1)
    back_three = jnp.concatenate([grid[:, 1:, 3], zeros_line], axis=1)
    stacked = jnp.stack([back_zero, back_one, back_two, back_three], axis=2)
    return stacked.reshape(TILE_COLS * TILE_LINES, 4, border_rows, width)

def reference(points, counts, owner, zorder, border, near, w_near, gain_one, conv_w, gain_two, w_up, w_down, grad_out):
    tiles = TILES
    tile_rows = TILE_ROWS
    width = points.shape[2]
    capacity = RECV // tiles
    border_rows = border.shape[2]
    sent = jax.vmap(lambda rows, lists: jnp.take(rows, lists.reshape(-1), axis=0).reshape(4, border_rows, width))(points, border)
    halo = gather_halo(sent)
    lifted = lax.map(lambda item: tile_forward(item[0], item[1], item[2], w_near)[2], (points, halo, near))
    rank, live = jax.vmap(lambda owned, count: route_ranks(owned, count, tiles))(owner, counts)
    source = jnp.arange(tiles, dtype=jnp.int32)[:, None]
    target = jnp.where(live, owner * RECV + source * capacity + rank, tiles * RECV).astype(jnp.int32)
    row_ids = jnp.arange(tiles * tile_rows, dtype=jnp.int32)
    buffer_ids = jnp.full((tiles * RECV,), tiles * tile_rows, jnp.int32).at[target.reshape(-1)].set(row_ids, mode='drop')
    serial_ids = jnp.take_along_axis(buffer_ids.reshape(tiles, RECV), zorder, axis=1).reshape(-1)
    serial = jnp.take(lifted.reshape(-1, width), serial_ids, axis=0, mode='fill', fill_value=0)
    serial_out_grad = jnp.take(grad_out.reshape(-1, width), serial_ids, axis=0, mode='fill', fill_value=0)
    zero_sums = (jnp.zeros((width,), jnp.float32), jnp.zeros(conv_w.shape, jnp.float32), jnp.zeros((width,), jnp.float32), jnp.zeros(w_up.shape, jnp.float32), jnp.zeros(w_down.shape, jnp.float32))

    def patch_step(carry, block):
        result, serial_grad, grads = patch_pass(block[0], block[1], gain_one, conv_w, gain_two, w_up, w_down)
        return (jax.tree.map(lambda left, right: left + right, carry, grads), (result, serial_grad))
    sums, (results, serial_grads) = lax.scan(patch_step, zero_sums, (serial.reshape(-1, PATCH, width), serial_out_grad.reshape(-1, PATCH, width)))
    out_flat = jnp.zeros((tiles * tile_rows, width), jnp.bfloat16).at[serial_ids].set(results.reshape(-1, width), mode='drop')
    lifted_grad = jnp.zeros((tiles * tile_rows, width), jnp.bfloat16).at[serial_ids].set(serial_grads.reshape(-1, width), mode='drop')

    def tile_step(carry, item):
        average, linear_part, unused = tile_forward(item[0], item[1], item[2], w_near)
        near_grad, row_grad, halo_grad = tile_backward(item[3], average, linear_part, item[2], w_near, tile_rows + 4 * border_rows)
        return (carry + near_grad, (row_grad, halo_grad))
    near_sum, (row_grads, halo_grads) = lax.scan(tile_step, jnp.zeros(w_near.shape, jnp.float32), (points, halo, near, lifted_grad.reshape(points.shape)))
    returned = return_halo(halo_grads, border_rows)

    def add_returned(row_grad, lists, back):
        return row_grad.at[lists.reshape(-1)].add(back.reshape(-1, width).astype(jnp.float32))
    row_grads = jax.vmap(add_returned)(row_grads, border, returned)
    scale = 1.0 / math.sqrt(ALL_ROWS)
    return (out_flat.reshape(points.shape), row_grads.astype(jnp.bfloat16), near_sum * scale, sums[0] * scale, sums[1] * scale, sums[2] * scale, sums[3] * scale, sums[4] * scale)
```

```python
import functools
import math

import jax
import jax.numpy as jnp
from jax import lax
from jax.experimental import pallas as pl
from jax.experimental.pallas import tpu as pltpu
from jax.sharding import PartitionSpec as P

PATCH = 1024
CHUNK = 256
LANES = 128
PAD = 8

eps_norm = 1e-06
gelu_coef = 0.7978845608028654
cubic_coef = 0.044715

bf16 = jnp.bfloat16
f32 = jnp.float32
NN = (((1,), (0,)), ((), ()))
NT = (((1,), (1,)), ((), ()))
TN = (((0,), (0,)), ((), ()))


def dot(left, right, dims=NN):
    return lax.dot_general(left, right, dims, preferred_element_type=f32)


def iota(shape, axis):
    return lax.broadcasted_iota(jnp.int32, shape, axis)


def marks(mask):
    return jnp.where(mask, 1.0, 0.0).astype(bf16)


def gelu_parts(value):
    square = value * value
    tangent = jnp.tanh(value * (gelu_coef + (gelu_coef * cubic_coef) * square))
    return square, tangent


def gelu_tanh(value):
    _, tangent = gelu_parts(value)
    half = 0.5 * value
    return half + half * tangent


def slope_of(value, square, tangent):
    inner_slope = gelu_coef + (3.0 * gelu_coef * cubic_coef) * square
    return 0.5 * (1.0 + tangent) + (0.5 * value) * (1.0 - tangent * tangent) * inner_slope


def inverse_rms(value):
    return lax.rsqrt(jnp.mean(value * value, axis=-1, keepdims=True) + eps_norm)


def column_of(row, count):
    return jnp.transpose(jnp.broadcast_to(row, (LANES, count)))


def pick_rows(column, depth):
    count = column.shape[0]
    lane = iota((count, LANES), 1)
    return jnp.concatenate(
        [marks(column == lane + base) for base in range(0, depth, LANES)], axis=1
    )


def mark_slots(row, start, count):
    return marks(iota((count, row.shape[1]), 0) + start == row)


def chunks(total):
    return lax.div(total, CHUNK)


def route_kernel(counts_ref, owner_ref, lists_ref, points_ref, slots_ref, sent_ref, *, tiles, capacity):
    rows = owner_ref.shape[1]
    live = iota((1, rows), 1) < counts_ref[0]
    owned = jnp.where(live, owner_ref[...], tiles)
    members = owned == iota((tiles, rows), 0)
    earlier = marks(iota((rows, rows), 0) < iota((rows, rows), 1))
    before = dot(marks(members), earlier)
    rank = jnp.sum(jnp.where(members, before, 0.0), axis=0, keepdims=True)
    slots_ref[...] = jnp.where(live, owned * capacity + rank.astype(jnp.int32), -1)
    lists = lists_ref[...]
    chosen = marks(iota((rows, lists.shape[1]), 0) == lists)
    sent_ref[...] = dot(chosen, points_ref[...], TN).astype(bf16)


def pack_kernel(slots_ref, rows_ref, packed_ref):
    slots = slots_ref[...]

    def one(at, _):
        start = pl.multiple_of(at * CHUNK, CHUNK)
        packed_ref[pl.ds(start, CHUNK), :] = dot(
            mark_slots(slots, start, CHUNK), rows_ref[...]
        ).astype(bf16)
        return 0

    lax.fori_loop(0, packed_ref.shape[0] // CHUNK, one, 0)


def unpack_kernel(slots_ref, packed_ref, rows_ref):
    for start in range(0, rows_ref.shape[0], CHUNK):
        column = column_of(slots_ref[:, start : start + CHUNK], CHUNK)
        rows_ref[pl.ds(start, CHUNK), :] = dot(
            pick_rows(column, packed_ref.shape[0]), packed_ref[...]
        ).astype(bf16)


def count_kernel(near_ref, table_ref):
    neighbours, rows = near_ref.shape
    step = 16
    zero = jnp.zeros((step, LANES), bf16)
    one = jnp.ones((step, LANES), bf16)

    def block(at, _):
        lane_block = lax.rem(at, rows // LANES)
        row_block = lax.div(at, rows // LANES)
        lane_at = pl.multiple_of(lane_block * LANES, LANES)
        row_at = pl.multiple_of(row_block * CHUNK, CHUNK)
        local = (near_ref[:, pl.ds(lane_at, LANES)] - row_at).astype(f32)
        spread = [
            jnp.broadcast_to(local[k : k + 1, :], (step, LANES)).astype(bf16)
            for k in range(neighbours)
        ]
        base = iota((step, LANES), 0).astype(f32)
        for inner in range(0, CHUNK, step):
            here = (base + float(inner)).astype(bf16)
            total = zero
            for k in range(neighbours):
                total = total + jnp.where(spread[k] == here, one, zero)
            table_ref[pl.ds(row_at + inner, step), pl.ds(lane_at, LANES)] = total
        return 0

    lax.fori_loop(0, (rows // LANES) * (table_ref.shape[0] // CHUNK), block, 0)


def lift_kernel(
    slots_ref, points_ref, halo0, halo1, halo2, halo3, table_ref, w_ref, average_ref, pre_ref, packed_ref,
    lifted_ref, *, neighbours
):
    ext = jnp.concatenate([points_ref[...], halo0[...], halo1[...], halo2[...], halo3[...]], axis=0)
    average = (dot(ext, table_ref[...], TN) * (1.0 / neighbours)).astype(bf16)
    average_ref[...] = average
    pre_act = dot(average, w_ref[...], TN)
    pre_ref[...] = pre_act
    lifted_ref[...] = (points_ref[...].astype(f32) + gelu_tanh(pre_act)).astype(bf16)
    pack_kernel(slots_ref, lifted_ref, packed_ref)


def tile_back_kernel(
    slots_ref, back_ref, table_ref, average_ref, pre_ref, w_ref, near_ref, row_ref, halo_ref,
    act_ref, spread_ref, *, neighbours
):
    rows = row_ref.shape[0]
    for start in range(0, rows, CHUNK):
        here = pl.ds(start, CHUNK)
        column = column_of(slots_ref[:, start : start + CHUNK], CHUNK)
        lifted_grad = dot(pick_rows(column, back_ref.shape[0]), back_ref[...])
        row_ref[here, :] = lifted_grad
        value = pre_ref[here, :]
        square, tangent = gelu_parts(value)
        act_grad = (lifted_grad * slope_of(value, square, tangent)).astype(bf16)
        act_ref[here, :] = act_grad
        spread_ref[here, :] = (dot(act_grad, w_ref[...], NT) * (1.0 / neighbours)).astype(bf16)
    near_ref[...] = dot(average_ref[...], act_ref[...]).astype(near_ref.dtype)
    for start in range(0, rows, CHUNK):
        here = pl.ds(start, CHUNK)
        row_ref[here, :] = row_ref[here, :] + dot(table_ref[here, :], spread_ref[...])
    halo_ref[...] = dot(table_ref[rows:, :], spread_ref[...]).astype(bf16)


def finish_kernel(lists_ref, row_ref, back0, back1, back2, back3, out_ref):
    lists = lists_ref[...]
    came = jnp.concatenate([back0[...], back1[...], back2[...], back3[...]], axis=0)
    chosen = marks(iota((row_ref.shape[0], lists.shape[1]), 0) == lists)
    out_ref[...] = (row_ref[...] + dot(chosen, came)).astype(bf16)


def full_taps(conv_ref, groups, inner):
    width = groups * inner
    rows = conv_ref.shape[0]
    repeat = marks(lax.rem(iota((inner, width), 1), inner) == iota((inner, width), 0))
    wide = dot(conv_ref[...], repeat)
    row_group = lax.div(lax.rem(iota((rows, width), 0), width), inner)
    same = row_group == lax.div(iota((rows, width), 1), inner)
    return jnp.where(same, wide, 0.0).astype(bf16)


def padded_zeros(ref):
    edge = jnp.zeros((PAD, ref.shape[1]), f32)
    ref[0:PAD, :] = edge
    ref[PAD + PATCH :, :] = edge


def write_back(zorder_ref, rows_ref, out_ref):
    zorder = zorder_ref[...]

    def one(at, _):
        start = pl.multiple_of(at * CHUNK, CHUNK)
        out_ref[pl.ds(start, CHUNK), :] = dot(
            mark_slots(zorder, start, CHUNK), rows_ref[...]
        ).astype(bf16)
        return 0

    lax.fori_loop(0, out_ref.shape[0] // CHUNK, one, 0)


def forward_kernel(
    zorder_ref, lifted_ref, grad_ref, conv_ref, gain_one_ref, gain_two_ref, up_ref, down_ref,
    serial_ref, out_grad_ref, state_ref, back_ref,
    taps_ref, normed_ref, before_ref, here_ref, after_ref, result_ref, *, groups, inner
):
    slots, width = lifted_ref.shape
    taps_ref[...] = full_taps(conv_ref, groups, inner)
    padded_zeros(before_ref)
    padded_zeros(after_ref)

    def patch(at, _):
        origin = pl.multiple_of(at * PATCH, PATCH)
        for start in range(0, PATCH, CHUNK):
            column = column_of(zorder_ref[:, pl.ds(origin + start, CHUNK)], CHUNK)
            chosen = pick_rows(column, slots)
            serial = dot(chosen, lifted_ref[...])
            serial_ref[pl.ds(origin + start, CHUNK), :] = serial.astype(bf16)
            out_grad_ref[pl.ds(origin + start, CHUNK), :] = dot(chosen, grad_ref[...]).astype(bf16)
            normed = (serial * inverse_rms(serial) * gain_one_ref[...]).astype(bf16)
            before_ref[pl.ds(PAD + start, CHUNK), :] = dot(normed, taps_ref[0:width, :])
            here_ref[pl.ds(start, CHUNK), :] = dot(normed, taps_ref[width : 2 * width, :])
            after_ref[pl.ds(PAD + start, CHUNK), :] = dot(normed, taps_ref[2 * width :, :])
        for start in range(0, PATCH, CHUNK):
            place = pl.ds(origin + start, CHUNK)
            mixed = (
                before_ref[pl.ds(PAD + start - 1, CHUNK), :]
                + here_ref[pl.ds(start, CHUNK), :]
                + after_ref[pl.ds(PAD + start + 1, CHUNK), :]
            )
            state = serial_ref[place, :].astype(f32) + mixed
            state_ref[place, :] = state
            second = (state * inverse_rms(state) * gain_two_ref[...]).astype(bf16)
            hidden = gelu_tanh(dot(second, up_ref[...])).astype(bf16)
            result_ref[place, :] = (state + dot(hidden, down_ref[...])).astype(bf16)
        return 0

    lax.fori_loop(0, slots // PATCH, patch, 0)
    write_back(zorder_ref, result_ref, back_ref)


def backward_kernel(
    zorder_ref, serial_ref, out_grad_ref, state_ref, conv_ref, gain_one_ref, gain_two_ref, up_ref, down_ref,
    back_ref, weights_ref,
    taps_ref, second_ref, hidden_ref, pre_grad_ref, state_grad_ref, mixed_ref, before_ref, here_ref,
    after_ref, normed_ref, serial_grad_ref, conv_sum_ref, gains_ref, *, groups, inner
):
    slots, width = serial_ref.shape
    hidden_width = up_ref.shape[1]
    taps_ref[...] = full_taps(conv_ref, groups, inner)
    padded_zeros(before_ref)
    padded_zeros(after_ref)
    padded_zeros(mixed_ref)
    conv_sum_ref[...] = jnp.zeros_like(conv_sum_ref)
    gains_ref[...] = jnp.zeros_like(gains_ref)

    def patch(at, _):
        origin = pl.multiple_of(at * PATCH, PATCH)
        for start in range(0, PATCH, CHUNK):
            place = pl.ds(origin + start, CHUNK)
            state = state_ref[place, :]
            scale_two = inverse_rms(state)
            unit_two = state * scale_two
            second = (unit_two * gain_two_ref[...]).astype(bf16)
            second_ref[place, :] = second
            value = dot(second, up_ref[...])
            square, tangent = gelu_parts(value)
            half = 0.5 * value
            hidden_ref[place, :] = (half + half * tangent).astype(bf16)
            out_grad = out_grad_ref[place, :]
            hidden_grad = dot(out_grad, down_ref[...], NT).astype(bf16).astype(f32)
            pre_grad = (hidden_grad * slope_of(value, square, tangent)).astype(bf16)
            pre_grad_ref[place, :] = pre_grad
            second_grad = dot(pre_grad, up_ref[...], NT).astype(bf16).astype(f32)
            weighted = second_grad * gain_two_ref[...]
            gains_ref[1:2, :] += jnp.sum(second_grad * unit_two, axis=0, keepdims=True)
            middle = jnp.mean(weighted * unit_two, axis=-1, keepdims=True)
            state_grad = out_grad.astype(f32) + scale_two * (weighted - unit_two * middle)
            state_grad_ref[pl.ds(start, CHUNK), :] = state_grad
            mixed_grad = state_grad.astype(bf16)
            mixed_ref[pl.ds(PAD + start, CHUNK), :] = mixed_grad.astype(f32)
            before_ref[pl.ds(PAD + start, CHUNK), :] = dot(mixed_grad, taps_ref[0:width, :], NT)
            here_ref[pl.ds(start, CHUNK), :] = dot(mixed_grad, taps_ref[width : 2 * width, :], NT)
            after_ref[pl.ds(PAD + start, CHUNK), :] = dot(mixed_grad, taps_ref[2 * width :, :], NT)
        for start in range(0, PATCH, CHUNK):
            place = pl.ds(origin + start, CHUNK)
            serial = serial_ref[place, :].astype(f32)
            scale_one = inverse_rms(serial)
            unit_one = serial * scale_one
            normed_ref[pl.ds(start, CHUNK), :] = (unit_one * gain_one_ref[...]).astype(bf16)
            normed_grad = (
                before_ref[pl.ds(PAD + start + 1, CHUNK), :]
                + here_ref[pl.ds(start, CHUNK), :]
                + after_ref[pl.ds(PAD + start - 1, CHUNK), :]
            ).astype(bf16).astype(f32)
            gains_ref[0:1, :] += jnp.sum(normed_grad * unit_one, axis=0, keepdims=True)
            weighted = normed_grad * gain_one_ref[...]
            middle = jnp.mean(weighted * unit_one, axis=-1, keepdims=True)
            serial_grad_ref[place, :] = (
                state_grad_ref[pl.ds(start, CHUNK), :] + scale_one * (weighted - unit_one * middle)
            ).astype(bf16)
        for tap in range(3):
            moved = mixed_ref[pl.ds(PAD + 1 - tap, PATCH), :].astype(bf16)
            conv_sum_ref[tap] += dot(normed_ref[...], moved, TN)
        return 0

    lax.fori_loop(0, slots // PATCH, patch, 0)
    write_back(zorder_ref, serial_grad_ref, back_ref)
    for start in range(0, hidden_width, width):
        weights_ref[start : start + width, :] = dot(
            hidden_ref[:, start : start + width], out_grad_ref[...], TN
        ).astype(weights_ref.dtype)
        weights_ref[hidden_width + start : hidden_width + start + width, :] = dot(
            second_ref[...], pre_grad_ref[:, start : start + width], TN
        ).astype(weights_ref.dtype)
    same = lax.div(iota((width, width), 0), inner) == lax.div(iota((width, width), 1), inner)
    for tap in range(3):
        kept = jnp.where(same, conv_sum_ref[tap], 0.0).reshape(groups, inner, width)
        at = 2 * hidden_width + tap * inner
        weights_ref[at : at + inner, :] = jnp.sum(kept, axis=0).astype(weights_ref.dtype)
    at = 2 * hidden_width + 3 * inner
    weights_ref[at:, :] = gains_ref[...].astype(weights_ref.dtype)


def call(kernel, outs, args, scratch=(), smem=0, flops=0, limit=32, **static):
    moved = sum(math.prod(a.shape) * a.dtype.itemsize for a in (*args, *outs))
    specs = [pl.BlockSpec(memory_space=pltpu.SMEM)] * smem
    specs += [pl.BlockSpec(memory_space=pltpu.VMEM)] * (len(args) - smem)
    return pl.pallas_call(
        functools.partial(kernel, **static) if static else kernel,
        out_shape=tuple(outs),
        in_specs=specs,
        out_specs=tuple(pl.BlockSpec(memory_space=pltpu.VMEM) for _ in outs),
        scratch_shapes=list(scratch),
        compiler_params=pltpu.CompilerParams(vmem_limit_bytes=limit * 1024 * 1024),
        cost_estimate=pl.CostEstimate(flops=int(flops), bytes_accessed=moved, transcendentals=0),
    )(*args)


def shaped(*shape, dtype=bf16):
    return jax.ShapeDtypeStruct(shape, dtype)


def shifted(value, axis, steps):
    count = lax.axis_size(axis)
    initial, last = (max(0, -steps), min(count, count - steps))
    return lax.ppermute(value, axis, [(source, source + steps) for source in range(initial, last)])


def exchange(rows, tiles):
    return lax.all_to_all(rows, ("tx", "ty"), split_axis=0, concat_axis=0, tiled=True)


def body(
    points,
    counts,
    owner,
    zorder,
    border,
    near,
    w_near,
    gain_one,
    conv_w,
    gain_two,
    w_up,
    w_down,
    grad_out,
):
    points_tile = points[0]
    tile_rows, width = points_tile.shape
    border_rows = border.shape[2]
    edge = 4 * border_rows
    ext = tile_rows + edge
    lists = border.reshape(1, edge)
    near_tile = near[0]
    neighbours = near_tile.shape[0]
    tiles = lax.axis_size("tx") * lax.axis_size("ty")
    slots_count = zorder.shape[1]
    capacity = slots_count // tiles
    taps, groups, inner = conv_w.shape[:3]
    conv_rows = conv_w.reshape(taps * groups * inner, inner)
    gain_one_row = gain_one.reshape(1, width)
    gain_two_row = gain_two.reshape(1, width)
    hidden = w_up.shape[1]

    slots, sent = call(
        route_kernel,
        [shaped(1, tile_rows, dtype=jnp.int32), shaped(edge, width)],
        [counts, owner, lists, points_tile],
        smem=1,
        flops=4e9,
        tiles=tiles,
        capacity=capacity,
    )
    halos = [
        shifted(sent[0:border_rows], "tx", -1),
        shifted(sent[border_rows : 2 * border_rows], "tx", 1),
        shifted(sent[2 * border_rows : 3 * border_rows], "ty", -1),
        shifted(sent[3 * border_rows :], "ty", 1),
    ]
    (packed_grad,) = call(
        pack_kernel, [shaped(slots_count, width)], [slots, grad_out[0]], flops=4e9
    )
    came_grad = exchange(packed_grad, tiles)
    (table,) = call(count_kernel, [shaped(ext, tile_rows)], [near_tile], flops=8e9)
    average, pre_act, packed_lifted = call(
        lift_kernel,
        [
            shaped(width, tile_rows),
            shaped(tile_rows, width, dtype=f32),
            shaped(slots_count, width),
        ],
        [slots, points_tile, *halos, table, w_near],
        scratch=[pltpu.VMEM((tile_rows, width), bf16)],
        flops=4e9,
        neighbours=neighbours,
    )
    came_lifted = exchange(packed_lifted, tiles)
    patch_scratch = [
        pltpu.VMEM((PATCH + 2 * PAD, width), f32),
        pltpu.VMEM((PATCH, width), f32),
        pltpu.VMEM((PATCH + 2 * PAD, width), f32),
    ]
    serial, serial_out_grad, state, back_result = call(
        forward_kernel,
        [
            shaped(slots_count, width),
            shaped(slots_count, width),
            shaped(slots_count, width, dtype=f32),
            shaped(slots_count, width),
        ],
        [zorder, came_lifted, came_grad, conv_rows, gain_one_row, gain_two_row, w_up, w_down],
        scratch=[
            pltpu.VMEM((taps * width, width), bf16),
            pltpu.VMEM((PATCH, width), bf16),
            *patch_scratch,
            pltpu.VMEM((slots_count, width), bf16),
        ],
        flops=10e9,
        limit=48,
        groups=groups,
        inner=inner,
    )
    came_result = exchange(back_result, tiles)
    sums_rows = 2 * hidden + taps * inner + 16
    back_grad, sums = call(
        backward_kernel,
        [shaped(slots_count, width), shaped(sums_rows, width)],
        [
            zorder,
            serial,
            serial_out_grad,
            state,
            conv_rows,
            gain_one_row,
            gain_two_row,
            w_up,
            w_down,
        ],
        scratch=[
            pltpu.VMEM((taps * width, width), bf16),
            pltpu.VMEM((slots_count, width), bf16),
            pltpu.VMEM((slots_count, hidden), bf16),
            pltpu.VMEM((slots_count, hidden), bf16),
            pltpu.VMEM((PATCH, width), f32),
            pltpu.VMEM((PATCH + 2 * PAD, width), f32),
            *patch_scratch,
            pltpu.VMEM((PATCH, width), bf16),
            pltpu.VMEM((slots_count, width), bf16),
            pltpu.VMEM((taps, width, width), f32),
            pltpu.VMEM((16, width), f32),
        ],
        flops=15e9,
        limit=48,
        groups=groups,
        inner=inner,
    )
    came_back = exchange(back_grad, tiles)
    totals = lax.psum(sums, ("tx", "ty"))
    (out_rows,) = call(
        unpack_kernel, [shaped(tile_rows, width)], [slots, came_result], flops=4e9
    )
    near_grad, row_grad, halo_grad = call(
        tile_back_kernel,
        [
            shaped(width, width),
            shaped(tile_rows, width, dtype=f32),
            shaped(edge, width),
        ],
        [slots, came_back, table, average, pre_act, w_near],
        scratch=[pltpu.VMEM((tile_rows, width), bf16), pltpu.VMEM((tile_rows, width), bf16)],
        flops=6e9,
        neighbours=neighbours,
    )
    returned = [
        shifted(halo_grad[0:border_rows], "tx", 1),
        shifted(halo_grad[border_rows : 2 * border_rows], "tx", -1),
        shifted(halo_grad[2 * border_rows : 3 * border_rows], "ty", 1),
        shifted(halo_grad[3 * border_rows :], "ty", -1),
    ]
    near_sum = lax.psum(near_grad, ("tx", "ty"))
    (grad_points,) = call(
        finish_kernel, [shaped(tile_rows, width)], [lists, row_grad, *returned], flops=1e9
    )
    scale = 1.0 / math.sqrt(tiles * tile_rows)
    scaled = totals.astype(f32) * scale
    down_sum = scaled[0:hidden]
    up_sum = jnp.concatenate(
        [scaled[hidden + at : hidden + at + width] for at in range(0, hidden, width)], axis=1
    )
    conv_sum = scaled[2 * hidden : 2 * hidden + taps * inner].reshape(taps, inner, groups, inner)
    gains = scaled[2 * hidden + taps * inner :]
    return (
        out_rows[None],
        grad_points[None],
        near_sum.astype(f32) * scale,
        gains[0],
        conv_sum.transpose(0, 2, 1, 3),
        gains[1],
        up_sum,
        down_sum,
    )


def solution(mesh):
    placed = (
        P(("tx", "ty"), None, None),
        P(("tx", "ty")),
        P(("tx", "ty"), None),
        P(("tx", "ty"), None),
        P(("tx", "ty"), None, None),
        P(("tx", "ty"), None, None),
        P(),
        P(),
        P(),
        P(),
        P(),
        P(),
        P(("tx", "ty"), None, None),
    )
    return jax.shard_map(
        body,
        mesh=mesh,
        in_specs=placed,
        out_specs=(
            P(("tx", "ty"), None, None),
            P(("tx", "ty"), None, None),
            P(),
            P(),
            P(),
            P(),
            P(),
            P(),
        ),
        check_vma=False,
    )
```

```python
import functools
import math

import jax
import jax.numpy as jnp
from jax import lax
from jax.experimental import pallas as pl
from jax.experimental.pallas import tpu as pltpu
from jax.sharding import PartitionSpec as P

PATCH = 1024
CHUNK = 256
WIDE = 512
BLOCK = 64
LANES = 128
PAD = 8

eps_norm = 1e-06
gelu_coef = 0.7978845608028654
cubic_coef = 0.044715

bf16 = jnp.bfloat16
f32 = jnp.float32
NN = (((1,), (0,)), ((), ()))
NT = (((1,), (1,)), ((), ()))
TN = (((0,), (0,)), ((), ()))


def dot(left, right, dims=NN):
    return lax.dot_general(left, right, dims, preferred_element_type=f32)


def iota(shape, axis):
    return lax.broadcasted_iota(jnp.int32, shape, axis)


def marks(mask):
    return jnp.where(mask, 1.0, 0.0).astype(bf16)


def gelu_parts(value):
    square = value * value
    tangent = jnp.tanh(value * (gelu_coef + (gelu_coef * cubic_coef) * square))
    return square, tangent


def gelu_tanh(value):
    _, tangent = gelu_parts(value)
    half = 0.5 * value
    return half + half * tangent


def slope_of(value, square, tangent):
    inner_slope = gelu_coef + (3.0 * gelu_coef * cubic_coef) * square
    return 0.5 * (1.0 + tangent) + (0.5 * value) * (1.0 - tangent * tangent) * inner_slope


def inverse_rms(value):
    return lax.rsqrt(jnp.mean(value * value, axis=-1, keepdims=True) + eps_norm)


def column_of(row, count):
    return jnp.transpose(jnp.broadcast_to(row, (LANES, count)))


def pick_rows(column, depth):
    count = column.shape[0]
    lane = iota((count, LANES), 1)
    return jnp.concatenate(
        [marks(column == lane + base) for base in range(0, depth, LANES)], axis=1
    )


def mark_slots(row, start, count):
    return marks(iota((count, row.shape[1]), 0) + start == row)


def route_kernel(counts_ref, owner_ref, lists_ref, points_ref, slots_ref, sent_ref, *, tiles, capacity):
    rows = owner_ref.shape[1]
    live = iota((1, rows), 1) < counts_ref[0]
    owned = jnp.where(live, owner_ref[...], tiles)
    members = owned == iota((tiles, rows), 0)
    earlier = marks(iota((rows, rows), 0) < iota((rows, rows), 1))
    before = dot(marks(members), earlier)
    rank = jnp.sum(jnp.where(members, before, 0.0), axis=0, keepdims=True)
    slots_ref[...] = jnp.where(live, owned * capacity + rank.astype(jnp.int32), -1)
    lists = lists_ref[...]
    chosen = marks(iota((rows, lists.shape[1]), 0) == lists)
    sent_ref[...] = dot(chosen, points_ref[...], TN).astype(bf16)


def pack_kernel(slots_ref, rows_ref, packed_ref):
    slots = slots_ref[...]
    for start in range(0, packed_ref.shape[0], WIDE):
        packed_ref[pl.ds(start, WIDE), :] = dot(
            mark_slots(slots, start, WIDE), rows_ref[...]
        ).astype(bf16)


def unpack_kernel(slots_ref, packed_ref, rows_ref):
    for start in range(0, rows_ref.shape[0], CHUNK):
        column = column_of(slots_ref[:, start : start + CHUNK], CHUNK)
        rows_ref[pl.ds(start, CHUNK), :] = dot(
            pick_rows(column, packed_ref.shape[0]), packed_ref[...]
        ).astype(bf16)


def count_kernel(near_ref, table_ref):
    neighbours, rows = near_ref.shape
    step = 16
    zero = jnp.zeros((step, LANES), bf16)
    one = jnp.ones((step, LANES), bf16)

    def block(at, _):
        lane_block = lax.rem(at, rows // LANES)
        row_block = lax.div(at, rows // LANES)
        lane_at = pl.multiple_of(lane_block * LANES, LANES)
        row_at = pl.multiple_of(row_block * CHUNK, CHUNK)
        local = (near_ref[:, pl.ds(lane_at, LANES)] - row_at).astype(f32)
        spread = [
            jnp.broadcast_to(local[k : k + 1, :], (step, LANES)).astype(bf16)
            for k in range(neighbours)
        ]
        base = iota((step, LANES), 0).astype(f32)
        for inner in range(0, CHUNK, step):
            here = (base + float(inner)).astype(bf16)
            total = zero
            for k in range(neighbours):
                total = total + jnp.where(spread[k] == here, one, zero)
            table_ref[pl.ds(row_at + inner, step), pl.ds(lane_at, LANES)] = total
        return 0

    lax.fori_loop(0, (rows // LANES) * (table_ref.shape[0] // CHUNK), block, 0)


def lift_kernel(
    slots_ref, points_ref, halo0, halo1, halo2, halo3, table_ref, w_ref, average_ref, pre_ref, packed_ref,
    lifted_ref, *, neighbours
):
    ext = jnp.concatenate([points_ref[...], halo0[...], halo1[...], halo2[...], halo3[...]], axis=0)
    average = (dot(ext, table_ref[...], TN) * (1.0 / neighbours)).astype(bf16)
    average_ref[...] = average
    pre_act = dot(average, w_ref[...], TN)
    pre_ref[...] = pre_act
    lifted_ref[...] = (points_ref[...].astype(f32) + gelu_tanh(pre_act)).astype(bf16)
    pack_kernel(slots_ref, lifted_ref, packed_ref)


def act_kernel(slots_ref, back_ref, average_ref, pre_ref, lifted_ref, act_ref, near_ref):
    for start in range(0, lifted_ref.shape[0], CHUNK):
        here = pl.ds(start, CHUNK)
        column = column_of(slots_ref[:, start : start + CHUNK], CHUNK)
        lifted_grad = dot(pick_rows(column, back_ref.shape[0]), back_ref[...])
        lifted_ref[here, :] = lifted_grad.astype(bf16)
        value = pre_ref[here, :]
        square, tangent = gelu_parts(value)
        act_ref[here, :] = (lifted_grad * slope_of(value, square, tangent)).astype(bf16)
    near_ref[...] = dot(average_ref[...], act_ref[...]).astype(near_ref.dtype)


def spread_rows_kernel(
    lifted_ref, act_ref, table_ref, w_ref, row_ref, halo_ref, spread_ref, *, neighbours
):
    rows = row_ref.shape[0]
    spread_ref[...] = (dot(act_ref[...], w_ref[...], NT) * (1.0 / neighbours)).astype(bf16)
    halo_ref[...] = dot(table_ref[rows:, :], spread_ref[...]).astype(bf16)
    for start in range(0, rows, WIDE):
        here = pl.ds(start, WIDE)
        row_ref[here, :] = lifted_ref[here, :].astype(f32) + dot(table_ref[here, :], spread_ref[...])


def finish_kernel(lists_ref, row_ref, back0, back1, back2, back3, out_ref):
    lists = lists_ref[...]
    came = jnp.concatenate([back0[...], back1[...], back2[...], back3[...]], axis=0)
    chosen = marks(iota((row_ref.shape[0], lists.shape[1]), 0) == lists)
    out_ref[...] = (row_ref[...] + dot(chosen, came)).astype(bf16)


def full_taps(conv_ref, groups, inner):
    width = groups * inner
    rows = conv_ref.shape[0]
    repeat = marks(lax.rem(iota((inner, width), 1), inner) == iota((inner, width), 0))
    wide = dot(conv_ref[...], repeat)
    row_group = lax.div(lax.rem(iota((rows, width), 0), width), inner)
    same = row_group == lax.div(iota((rows, width), 1), inner)
    return jnp.where(same, wide, 0.0).astype(bf16)


def padded_zeros(ref):
    edge = jnp.zeros((PAD, ref.shape[1]), f32)
    ref[0:PAD, :] = edge
    ref[PAD + PATCH :, :] = edge


def write_back(zorder_ref, rows_ref, out_ref):
    pack_kernel(zorder_ref, rows_ref, out_ref)


def order_kernel(zorder_ref, slots_ref, rows_ref):
    for start in range(0, rows_ref.shape[0], WIDE):
        column = column_of(zorder_ref[:, start : start + WIDE], WIDE)
        rows_ref[pl.ds(start, WIDE), :] = dot(
            pick_rows(column, slots_ref.shape[0]), slots_ref[...]
        ).astype(bf16)


def forward_kernel(
    zorder_ref, lifted_ref, conv_ref, gain_one_ref, gain_two_ref, up_ref, down_ref,
    serial_ref, state_ref, back_ref,
    taps_ref, normed_ref, before_ref, here_ref, after_ref, second_ref, hidden_ref, result_ref,
    *, groups, inner
):
    slots, width = lifted_ref.shape
    hidden_width = up_ref.shape[1]
    taps_ref[...] = full_taps(conv_ref, groups, inner)
    padded_zeros(before_ref)
    padded_zeros(after_ref)

    def patch(at, _):
        origin = pl.multiple_of(at * PATCH, PATCH)
        for start in range(0, PATCH, WIDE):
            column = column_of(zorder_ref[:, pl.ds(origin + start, WIDE)], WIDE)
            wide = dot(pick_rows(column, slots), lifted_ref[...])
            for row in range(0, WIDE, BLOCK):
                serial = wide[row : row + BLOCK]
                serial_ref[pl.ds(origin + start + row, BLOCK), :] = serial.astype(bf16)
                normed = serial * inverse_rms(serial) * gain_one_ref[...]
                normed_ref[pl.ds(start + row, BLOCK), :] = normed.astype(bf16)
        before_ref[pl.ds(PAD, PATCH), :] = dot(normed_ref[...], taps_ref[0:width, :])
        here_ref[...] = dot(normed_ref[...], taps_ref[width : 2 * width, :])
        after_ref[pl.ds(PAD, PATCH), :] = dot(normed_ref[...], taps_ref[2 * width :, :])
        for row in range(0, PATCH, BLOCK):
            place = pl.ds(origin + row, BLOCK)
            state = serial_ref[place, :].astype(f32) + (
                before_ref[pl.ds(PAD + row - 1, BLOCK), :]
                + here_ref[pl.ds(row, BLOCK), :]
                + after_ref[pl.ds(PAD + row + 1, BLOCK), :]
            )
            state_ref[place, :] = state
            second = state * inverse_rms(state) * gain_two_ref[...]
            second_ref[pl.ds(row, BLOCK), :] = second.astype(bf16)
        for start in range(0, PATCH, CHUNK):
            value = dot(second_ref[pl.ds(start, CHUNK), :], up_ref[...])
            for row in range(0, CHUNK, 16):
                for col in range(0, hidden_width, 2 * LANES):
                    hidden_ref[pl.ds(start + row, 16), pl.ds(col, 2 * LANES)] = gelu_tanh(
                        value[row : row + 16, col : col + 2 * LANES]
                    ).astype(bf16)
        for start in range(0, PATCH, WIDE):
            place = pl.ds(origin + start, WIDE)
            result_ref[place, :] = (
                state_ref[place, :] + dot(hidden_ref[pl.ds(start, WIDE), :], down_ref[...])
            ).astype(bf16)
        return 0

    lax.fori_loop(0, slots // PATCH, patch, 0)
    write_back(zorder_ref, result_ref, back_ref)


def hold_kernel(zorder_ref, rows_ref, _, back_ref):
    write_back(zorder_ref, rows_ref, back_ref)


def backward_kernel(
    serial_ref, out_grad_ref, state_ref, conv_ref, gain_one_ref, gain_two_ref, up_ref, down_ref,
    serial_grad_ref, weights_ref,
    taps_ref, second_ref, hidden_ref, pre_grad_ref, state_grad_ref, mixed_ref, before_ref, here_ref,
    after_ref, normed_ref, conv_sum_ref, gains_ref, *, groups, inner
):
    slots, width = serial_ref.shape
    hidden_width = up_ref.shape[1]
    taps_ref[...] = full_taps(conv_ref, groups, inner)
    padded_zeros(before_ref)
    padded_zeros(after_ref)
    padded_zeros(mixed_ref)
    conv_sum_ref[...] = jnp.zeros_like(conv_sum_ref)
    gains_ref[...] = jnp.zeros_like(gains_ref)

    def patch(at, _):
        origin = pl.multiple_of(at * PATCH, PATCH)
        for start in range(0, PATCH, CHUNK):
            place = pl.ds(origin + start, CHUNK)
            state = state_ref[place, :]
            scale_two = inverse_rms(state)
            unit_two = state * scale_two
            second = (unit_two * gain_two_ref[...]).astype(bf16)
            second_ref[place, :] = second
            value = dot(second, up_ref[...])
            square, tangent = gelu_parts(value)
            half = 0.5 * value
            hidden_ref[place, :] = (half + half * tangent).astype(bf16)
            out_grad = out_grad_ref[place, :]
            hidden_grad = dot(out_grad, down_ref[...], NT).astype(bf16).astype(f32)
            pre_grad = (hidden_grad * slope_of(value, square, tangent)).astype(bf16)
            pre_grad_ref[place, :] = pre_grad
            second_grad = dot(pre_grad, up_ref[...], NT).astype(bf16).astype(f32)
            weighted = second_grad * gain_two_ref[...]
            gains_ref[1:2, :] += jnp.sum(second_grad * unit_two, axis=0, keepdims=True)
            middle = jnp.mean(weighted * unit_two, axis=-1, keepdims=True)
            state_grad = out_grad.astype(f32) + scale_two * (weighted - unit_two * middle)
            state_grad_ref[pl.ds(start, CHUNK), :] = state_grad
            mixed_grad = state_grad.astype(bf16)
            mixed_ref[pl.ds(PAD + start, CHUNK), :] = mixed_grad.astype(f32)
            before_ref[pl.ds(PAD + start, CHUNK), :] = dot(mixed_grad, taps_ref[0:width, :], NT)
            here_ref[pl.ds(start, CHUNK), :] = dot(mixed_grad, taps_ref[width : 2 * width, :], NT)
            after_ref[pl.ds(PAD + start, CHUNK), :] = dot(mixed_grad, taps_ref[2 * width :, :], NT)
        for start in range(0, PATCH, CHUNK):
            place = pl.ds(origin + start, CHUNK)
            serial = serial_ref[place, :].astype(f32)
            scale_one = inverse_rms(serial)
            unit_one = serial * scale_one
            normed_ref[pl.ds(start, CHUNK), :] = (unit_one * gain_one_ref[...]).astype(bf16)
            normed_grad = (
                before_ref[pl.ds(PAD + start + 1, CHUNK), :]
                + here_ref[pl.ds(start, CHUNK), :]
                + after_ref[pl.ds(PAD + start - 1, CHUNK), :]
            ).astype(bf16).astype(f32)
            gains_ref[0:1, :] += jnp.sum(normed_grad * unit_one, axis=0, keepdims=True)
            weighted = normed_grad * gain_one_ref[...]
            middle = jnp.mean(weighted * unit_one, axis=-1, keepdims=True)
            serial_grad_ref[place, :] = (
                state_grad_ref[pl.ds(start, CHUNK), :] + scale_one * (weighted - unit_one * middle)
            ).astype(bf16)
        for tap in range(3):
            moved = mixed_ref[pl.ds(PAD + 1 - tap, PATCH), :].astype(bf16)
            conv_sum_ref[tap] += dot(normed_ref[...], moved, TN)
        return 0

    lax.fori_loop(0, slots // PATCH, patch, 0)
    for start in range(0, hidden_width, width):
        weights_ref[start : start + width, :] = dot(
            hidden_ref[:, start : start + width], out_grad_ref[...], TN
        ).astype(weights_ref.dtype)
        weights_ref[hidden_width + start : hidden_width + start + width, :] = dot(
            second_ref[...], pre_grad_ref[:, start : start + width], TN
        ).astype(weights_ref.dtype)
    same = lax.div(iota((width, width), 0), inner) == lax.div(iota((width, width), 1), inner)
    for tap in range(3):
        kept = jnp.where(same, conv_sum_ref[tap], 0.0).reshape(groups, inner, width)
        at = 2 * hidden_width + tap * inner
        weights_ref[at : at + inner, :] = jnp.sum(kept, axis=0).astype(weights_ref.dtype)
    at = 2 * hidden_width + 3 * inner
    weights_ref[at : at + 16, :] = gains_ref[...].astype(weights_ref.dtype)
    at = at + 16
    weights_ref[at:, :] = jnp.zeros((weights_ref.shape[0] - at, width), weights_ref.dtype)


def spread_kernel(sums_ref, up_ref, down_ref, conv_ref, gain_one_ref, gain_two_ref, *, scale):
    width, hidden_width = up_ref.shape
    taps, groups, inner = conv_ref.shape[:3]
    down_ref[...] = sums_ref[0:hidden_width, :].astype(f32) * scale
    for start in range(0, hidden_width, width):
        up_ref[:, start : start + width] = (
            sums_ref[hidden_width + start : hidden_width + start + width, :].astype(f32) * scale
        )
    for tap in range(taps):
        at = 2 * hidden_width + tap * inner
        rows = sums_ref[at : at + inner, :].astype(f32) * scale
        for group in range(groups):
            conv_ref[tap, group] = rows[:, group * inner : (group + 1) * inner]
    at = 2 * hidden_width + taps * inner
    gains = sums_ref[at : at + 16, :].astype(f32) * scale
    gain_one_ref[...] = gains[0:1, :]
    gain_two_ref[...] = gains[1:2, :]


def call(kernel, outs, args, scratch=(), smem=0, flops=0, limit=16, held=0, **static):
    moved = sum(math.prod(a.shape) * a.dtype.itemsize for a in (*args, *outs))
    specs = [pl.BlockSpec(memory_space=pltpu.SMEM)] * smem
    specs += [pl.BlockSpec(memory_space=pltpu.VMEM)] * (len(args) - smem - held)
    specs += [pl.BlockSpec(memory_space=pl.ANY)] * held
    return pl.pallas_call(
        functools.partial(kernel, **static) if static else kernel,
        out_shape=tuple(outs),
        in_specs=specs,
        out_specs=tuple(pl.BlockSpec(memory_space=pltpu.VMEM) for _ in outs),
        scratch_shapes=list(scratch),
        compiler_params=pltpu.CompilerParams(vmem_limit_bytes=limit * 1024 * 1024),
        cost_estimate=pl.CostEstimate(flops=int(flops), bytes_accessed=moved, transcendentals=0),
    )(*args)


def shaped(*shape, dtype=bf16):
    return jax.ShapeDtypeStruct(shape, dtype)


def shifted(value, axis, steps):
    count = lax.axis_size(axis)
    initial, last = (max(0, -steps), min(count, count - steps))
    return lax.ppermute(value, axis, [(source, source + steps) for source in range(initial, last)])


def exchange(rows, tiles):
    return lax.all_to_all(rows, ("tx", "ty"), split_axis=0, concat_axis=0, tiled=True)


def body(
    points,
    counts,
    owner,
    zorder,
    border,
    near,
    w_near,
    gain_one,
    conv_w,
    gain_two,
    w_up,
    w_down,
    grad_out,
):
    points_tile = points[0]
    tile_rows, width = points_tile.shape
    border_rows = border.shape[2]
    edge = 4 * border_rows
    ext = tile_rows + edge
    lists = border.reshape(1, edge)
    near_tile = near[0]
    neighbours = near_tile.shape[0]
    tiles = lax.axis_size("tx") * lax.axis_size("ty")
    slots_count = zorder.shape[1]
    capacity = slots_count // tiles
    taps, groups, inner = conv_w.shape[:3]
    conv_rows = conv_w.reshape(taps * groups * inner, inner)
    gain_one_row = gain_one.reshape(1, width)
    gain_two_row = gain_two.reshape(1, width)
    hidden = w_up.shape[1]

    slots, sent = call(
        route_kernel,
        [shaped(1, tile_rows, dtype=jnp.int32), shaped(edge, width)],
        [counts, owner, lists, points_tile],
        smem=1,
        flops=4e9,
        tiles=tiles,
        capacity=capacity,
    )
    halos = [
        shifted(sent[0:border_rows], "tx", -1),
        shifted(sent[border_rows : 2 * border_rows], "tx", 1),
        shifted(sent[2 * border_rows : 3 * border_rows], "ty", -1),
        shifted(sent[3 * border_rows :], "ty", 1),
    ]
    (packed_grad,) = call(
        pack_kernel, [shaped(slots_count, width)], [slots, grad_out[0]], flops=4e9
    )
    came_grad = exchange(packed_grad, tiles)
    (table,) = call(count_kernel, [shaped(ext, tile_rows)], [near_tile], flops=8e9)
    average, pre_act, packed_lifted = call(
        lift_kernel,
        [
            shaped(width, tile_rows),
            shaped(tile_rows, width, dtype=f32),
            shaped(slots_count, width),
        ],
        [slots, points_tile, *halos, table, w_near],
        scratch=[pltpu.VMEM((tile_rows, width), bf16)],
        flops=4e9,
        neighbours=neighbours,
    )
    came_lifted = exchange(packed_lifted, tiles)
    patch_scratch = [
        pltpu.VMEM((PATCH + 2 * PAD, width), f32),
        pltpu.VMEM((PATCH, width), f32),
        pltpu.VMEM((PATCH + 2 * PAD, width), f32),
    ]
    (serial_out_grad,) = call(
        order_kernel, [shaped(slots_count, width)], [zorder, came_grad], flops=8e9
    )
    serial, state, back_result = call(
        forward_kernel,
        [
            shaped(slots_count, width),
            shaped(slots_count, width, dtype=f32),
            shaped(slots_count, width),
        ],
        [zorder, came_lifted, conv_rows, gain_one_row, gain_two_row, w_up, w_down],
        scratch=[
            pltpu.VMEM((taps * width, width), bf16),
            pltpu.VMEM((PATCH, width), bf16),
            *patch_scratch,
            pltpu.VMEM((PATCH, width), bf16),
            pltpu.VMEM((PATCH, hidden), bf16),
            pltpu.VMEM((slots_count, width), bf16),
        ],
        flops=10e9,
        limit=32,
        groups=groups,
        inner=inner,
    )
    came_result = exchange(back_result, tiles)
    lines = lax.axis_size("ty")
    sums_rows = 2 * hidden + taps * inner + 16
    sums_rows = -(-sums_rows // (16 * lines)) * (16 * lines)
    serial_grad, sums = call(
        backward_kernel,
        [shaped(slots_count, width), shaped(sums_rows, width)],
        [
            serial,
            serial_out_grad,
            state,
            conv_rows,
            gain_one_row,
            gain_two_row,
            w_up,
            w_down,
        ],
        scratch=[
            pltpu.VMEM((taps * width, width), bf16),
            pltpu.VMEM((slots_count, width), bf16),
            pltpu.VMEM((slots_count, hidden), bf16),
            pltpu.VMEM((slots_count, hidden), bf16),
            pltpu.VMEM((PATCH, width), f32),
            pltpu.VMEM((PATCH + 2 * PAD, width), f32),
            *patch_scratch,
            pltpu.VMEM((PATCH, width), bf16),
            pltpu.VMEM((taps, width, width), f32),
            pltpu.VMEM((16, width), f32),
        ],
        flops=40e9,
        limit=40,
        groups=groups,
        inner=inner,
    )
    (back_grad,) = call(
        hold_kernel,
        [shaped(slots_count, width)],
        [zorder, serial_grad, came_result],
        held=1,
        flops=4e9,
    )
    came_back = exchange(back_grad, tiles)
    share = lax.psum_scatter(sums, "ty", scatter_dimension=0, tiled=True)
    totals = lax.all_gather(lax.psum(share, "tx"), "ty", axis=0, tiled=True)
    (out_rows,) = call(
        unpack_kernel, [shaped(tile_rows, width)], [slots, came_result], flops=4e9
    )
    lifted_grad, act_grad, near_grad = call(
        act_kernel,
        [shaped(tile_rows, width), shaped(tile_rows, width), shaped(width, width)],
        [slots, came_back, average, pre_act],
        flops=3e9,
    )
    near_parts = exchange(near_grad, tiles).reshape(tiles, width // tiles, width)
    near_share = jnp.sum(near_parts.astype(f32), axis=0)
    near_all = jnp.broadcast_to(near_share.astype(bf16), (tiles, *near_share.shape))
    near_sum = exchange(near_all.reshape(width, width), tiles)
    row_grad, halo_grad = call(
        spread_rows_kernel,
        [shaped(tile_rows, width, dtype=f32), shaped(edge, width)],
        [lifted_grad, act_grad, table, w_near],
        scratch=[pltpu.VMEM((tile_rows, width), bf16)],
        flops=3e9,
        neighbours=neighbours,
    )
    returned = [
        shifted(halo_grad[0:border_rows], "tx", 1),
        shifted(halo_grad[border_rows : 2 * border_rows], "tx", -1),
        shifted(halo_grad[2 * border_rows : 3 * border_rows], "ty", 1),
        shifted(halo_grad[3 * border_rows :], "ty", -1),
    ]
    (grad_points,) = call(
        finish_kernel, [shaped(tile_rows, width)], [lists, row_grad, *returned], flops=1e9
    )
    scale = 1.0 / math.sqrt(tiles * tile_rows)
    up_sum, down_sum, conv_sum, gain_one_sum, gain_two_sum = call(
        spread_kernel,
        [
            shaped(width, hidden, dtype=f32),
            shaped(hidden, width, dtype=f32),
            shaped(*conv_w.shape, dtype=f32),
            shaped(1, width, dtype=f32),
            shaped(1, width, dtype=f32),
        ],
        [totals],
        flops=1e6,
        scale=scale,
    )
    return (
        out_rows[None],
        grad_points[None],
        near_sum.astype(f32) * scale,
        gain_one_sum[0],
        conv_sum,
        gain_two_sum[0],
        up_sum,
        down_sum,
    )


def solution(mesh):
    placed = (
        P(("tx", "ty"), None, None),
        P(("tx", "ty")),
        P(("tx", "ty"), None),
        P(("tx", "ty"), None),
        P(("tx", "ty"), None, None),
        P(("tx", "ty"), None, None),
        P(),
        P(),
        P(),
        P(),
        P(),
        P(),
        P(("tx", "ty"), None, None),
    )
    return jax.shard_map(
        body,
        mesh=mesh,
        in_specs=placed,
        out_specs=(
            P(("tx", "ty"), None, None),
            P(("tx", "ty"), None, None),
            P(),
            P(),
            P(),
            P(),
            P(),
            P(),
        ),
        check_vma=False,
    )
```

```python
import math

import jax
import jax.numpy as jnp
from jax import lax
from jax.experimental import pallas as pl
from jax.experimental.pallas import tpu as pltpu
from jax.sharding import PartitionSpec as P

PATCH = 1024
CHUNK = 256
WIDE = 512
BLOCK = 64
LANES = 128
PAD = 8

eps_norm = 1e-06
gelu_coef = 0.7978845608028654
cubic_coef = 0.044715

bf16 = jnp.bfloat16
f32 = jnp.float32
NN = (((1,), (0,)), ((), ()))
NT = (((1,), (1,)), ((), ()))
TN = (((0,), (0,)), ((), ()))


def dot(left, right, dims=NN):
    return lax.dot_general(left, right, dims, preferred_element_type=f32)


def iota(shape, axis):
    return lax.broadcasted_iota(jnp.int32, shape, axis)


def marks(mask):
    return jnp.where(mask, 1.0, 0.0).astype(bf16)


def gelu_parts(value):
    square = value * value
    tangent = jnp.tanh(value * (gelu_coef + (gelu_coef * cubic_coef) * square))
    return square, tangent


def gelu_tanh(value):
    _, tangent = gelu_parts(value)
    half = 0.5 * value
    return half + half * tangent


def slope_of(value, square, tangent):
    inner_slope = gelu_coef + (3.0 * gelu_coef * cubic_coef) * square
    return 0.5 * (1.0 + tangent) + (0.5 * value) * (1.0 - tangent * tangent) * inner_slope


def inverse_rms(value):
    return lax.rsqrt(jnp.mean(value * value, axis=-1, keepdims=True) + eps_norm)


def column_of(row, count):
    return jnp.transpose(jnp.broadcast_to(row, (LANES, count)))


def pick_rows(column, depth):
    count = column.shape[0]
    lane = iota((count, LANES), 1)
    return jnp.concatenate(
        [marks(column == lane + base) for base in range(0, depth, LANES)], axis=1
    )


def mark_slots(row, start, count):
    return marks(iota((count, row.shape[1]), 0) + start == row)


def route_kernel(counts_ref, owner_ref, lists_ref, points_ref, slots_ref, sent_ref, *, tiles, capacity):
    rows = owner_ref.shape[1]
    live = iota((1, rows), 1) < counts_ref[0]
    owned = jnp.where(live, owner_ref[...], tiles)
    members = owned == iota((tiles, rows), 0)
    earlier = marks(iota((rows, rows), 0) < iota((rows, rows), 1))
    before = dot(marks(members), earlier)
    rank = jnp.sum(jnp.where(members, before, 0.0), axis=0, keepdims=True)
    slots_ref[...] = jnp.where(live, owned * capacity + rank.astype(jnp.int32), -1)
    lists = lists_ref[...]
    chosen = marks(iota((rows, lists.shape[1]), 0) == lists)
    sent_ref[...] = dot(chosen, points_ref[...], TN).astype(bf16)


def pack_rows(slots_ref, rows_ref, packed_out, stage_ref, sems):
    slots = slots_ref[...]
    copies = []
    for at, start in enumerate(range(0, packed_out.shape[0], WIDE)):
        place = pl.ds(start, WIDE)
        stage_ref[place, :] = dot(mark_slots(slots, start, WIDE), rows_ref[...]).astype(bf16)
        copies.append(pltpu.make_async_copy(stage_ref.at[place], packed_out.at[place], sems.at[at]))
        copies[-1].start()
    for copy in copies:
        copy.wait()


def unpack_kernel(slots_ref, packed_ref, rows_ref):
    for start in range(0, rows_ref.shape[0], CHUNK):
        column = column_of(slots_ref[:, start : start + CHUNK], CHUNK)
        rows_ref[pl.ds(start, CHUNK), :] = dot(
            pick_rows(column, packed_ref.shape[0]), packed_ref[...]
        ).astype(bf16)


def count_kernel(near_ref, kept_ref, table_ref, sems):
    neighbours, rows = near_ref.shape
    step = 16
    zero = jnp.zeros((step, LANES), bf16)
    one = jnp.ones((step, LANES), bf16)
    row_blocks = table_ref.shape[0] // CHUNK

    def copy_out(row_block):
        place = pl.ds(pl.multiple_of(row_block * CHUNK, CHUNK), CHUNK)
        return pltpu.make_async_copy(table_ref.at[place], kept_ref.at[place], sems.at[row_block])

    def rows_of(row_block, _):
        row_at = pl.multiple_of(row_block * CHUNK, CHUNK)

        def block(lane_block, _):
            lane_at = pl.multiple_of(lane_block * LANES, LANES)
            local = (near_ref[:, pl.ds(lane_at, LANES)] - row_at).astype(f32)
            spread = [
                jnp.broadcast_to(local[k : k + 1, :], (step, LANES)).astype(bf16)
                for k in range(neighbours)
            ]
            base = iota((step, LANES), 0).astype(f32)
            for inner in range(0, CHUNK, step):
                here = (base + float(inner)).astype(bf16)
                total = zero
                for k in range(neighbours):
                    total = total + jnp.where(spread[k] == here, one, zero)
                table_ref[pl.ds(row_at + inner, step), pl.ds(lane_at, LANES)] = total
            return 0

        lax.fori_loop(0, rows // LANES, block, 0)
        copy_out(row_block).start()
        return 0

    lax.fori_loop(0, row_blocks, rows_of, 0)
    for row_block in range(row_blocks):
        copy_out(row_block).wait()


def lift_kernel(
    slots_ref, points_ref, grad_ref, halo0, halo1, halo2, halo3, table_ref, w_ref,
    average_out, pre_out, packed_out,
    average_ref, pre_ref, both_ref, stage_ref, sems, pack_sems, *, neighbours
):
    width = points_ref.shape[1]
    ext = jnp.concatenate([points_ref[...], halo0[...], halo1[...], halo2[...], halo3[...]], axis=0)
    average = (dot(ext, table_ref[...], TN) * (1.0 / neighbours)).astype(bf16)
    average_ref[...] = average
    keep_average = pltpu.make_async_copy(average_ref, average_out, sems.at[0])
    keep_average.start()
    pre_ref[...] = dot(average, w_ref[...], TN)
    keep_pre = pltpu.make_async_copy(pre_ref, pre_out, sems.at[1])
    keep_pre.start()
    for row in range(0, points_ref.shape[0], BLOCK):
        here = pl.ds(row, BLOCK)
        both_ref[here, 0:width] = (
            points_ref[here, :].astype(f32) + gelu_tanh(pre_ref[here, :])
        ).astype(bf16)
    both_ref[:, width:] = grad_ref[...]
    pack_rows(slots_ref, both_ref, packed_out, stage_ref, pack_sems)
    keep_average.wait()
    keep_pre.wait()


def tile_back_kernel(
    slots_ref, back_ref, w_ref, table_in, average_in, pre_in,
    row_out, near_ref, halo_ref,
    row_ref, table_ref, average_ref, pre_ref, act_ref, spread_ref, sems, *, neighbours
):
    rows = row_ref.shape[0]
    fetch_pre = pltpu.make_async_copy(pre_in, pre_ref, sems.at[0])
    fetch_average = pltpu.make_async_copy(average_in, average_ref, sems.at[1])
    fetch_table = pltpu.make_async_copy(table_in, table_ref, sems.at[2])

    def keep_row(start):
        place = pl.ds(start, WIDE)
        return pltpu.make_async_copy(row_ref.at[place], row_out.at[place], sems.at[3 + start // WIDE])

    fetch_pre.start()
    fetch_average.start()
    fetch_table.start()
    fetch_pre.wait()
    for start in range(0, rows, CHUNK):
        column = column_of(slots_ref[:, start : start + CHUNK], CHUNK)
        wide = dot(pick_rows(column, back_ref.shape[0]), back_ref[...])
        for row in range(0, CHUNK, BLOCK):
            here = pl.ds(start + row, BLOCK)
            lifted_grad = wide[row : row + BLOCK]
            row_ref[here, :] = lifted_grad
            value = pre_ref[here, :]
            square, tangent = gelu_parts(value)
            act_ref[here, :] = (lifted_grad * slope_of(value, square, tangent)).astype(bf16)
    fetch_average.wait()
    near_ref[...] = dot(average_ref[...], act_ref[...]).astype(near_ref.dtype)
    spread_ref[...] = (dot(act_ref[...], w_ref[...], NT) * (1.0 / neighbours)).astype(bf16)
    fetch_table.wait()
    halo_ref[...] = dot(table_ref[rows:, :], spread_ref[...]).astype(bf16)
    for start in range(0, rows, WIDE):
        here = pl.ds(start, WIDE)
        row_ref[here, :] = row_ref[here, :] + dot(table_ref[here, :], spread_ref[...])
        keep_row(start).start()
    for start in range(0, rows, WIDE):
        keep_row(start).wait()


def finish_kernel(lists_ref, row_ref, back0, back1, back2, back3, out_ref):
    lists = lists_ref[...]
    came = jnp.concatenate([back0[...], back1[...], back2[...], back3[...]], axis=0)
    chosen = marks(iota((row_ref.shape[0], lists.shape[1]), 0) == lists)
    out_ref[...] = (row_ref[...] + dot(chosen, came)).astype(bf16)


def full_taps(conv_ref, groups, inner):
    width = groups * inner
    rows = conv_ref.shape[0]
    repeat = marks(lax.rem(iota((inner, width), 1), inner) == iota((inner, width), 0))
    wide = dot(conv_ref[...], repeat)
    row_group = lax.div(lax.rem(iota((rows, width), 0), width), inner)
    same = row_group == lax.div(iota((rows, width), 1), inner)
    return jnp.where(same, wide, 0.0).astype(bf16)


def padded_zeros(ref):
    edge = jnp.zeros((PAD, ref.shape[1]), f32)
    ref[0:PAD, :] = edge
    ref[PAD + PATCH :, :] = edge


def forward_kernel(
    zorder_ref, conv_ref, gain_one_ref, gain_two_ref, up_ref, down_ref, came_in,
    serial_out, state_out, back_out,
    lifted_ref, serial_ref, state_ref, taps_ref, normed_ref, before_ref, here_ref, after_ref, second_ref, hidden_ref,
    result_ref, stage_ref, sems, pack_sems, *, groups, inner
):
    slots, width = lifted_ref.shape
    fetch = pltpu.make_async_copy(came_in.at[:, pl.ds(0, width)], lifted_ref, sems.at[2, 0])
    fetch.start()
    hidden_width = up_ref.shape[1]
    taps_ref[...] = full_taps(conv_ref, groups, inner)
    padded_zeros(before_ref)
    padded_zeros(after_ref)

    def keep(at):
        place = pl.ds(pl.multiple_of(at * PATCH, PATCH), PATCH)
        return (
            pltpu.make_async_copy(serial_ref.at[place], serial_out.at[place], sems.at[0, at]),
            pltpu.make_async_copy(state_ref.at[place], state_out.at[place], sems.at[1, at]),
        )

    def patch(at, _):
        origin = pl.multiple_of(at * PATCH, PATCH)
        for start in range(0, PATCH, WIDE):
            column = column_of(zorder_ref[:, pl.ds(origin + start, WIDE)], WIDE)
            wide = dot(pick_rows(column, slots), lifted_ref[...])
            for row in range(0, WIDE, BLOCK):
                serial = wide[row : row + BLOCK]
                serial_ref[pl.ds(origin + start + row, BLOCK), :] = serial.astype(bf16)
                normed = serial * inverse_rms(serial) * gain_one_ref[...]
                normed_ref[pl.ds(start + row, BLOCK), :] = normed.astype(bf16)
        before_ref[pl.ds(PAD, PATCH), :] = dot(normed_ref[...], taps_ref[0:width, :])
        here_ref[...] = dot(normed_ref[...], taps_ref[width : 2 * width, :])
        after_ref[pl.ds(PAD, PATCH), :] = dot(normed_ref[...], taps_ref[2 * width :, :])
        for row in range(0, PATCH, BLOCK):
            place = pl.ds(origin + row, BLOCK)
            state = serial_ref[place, :].astype(f32) + (
                before_ref[pl.ds(PAD + row - 1, BLOCK), :]
                + here_ref[pl.ds(row, BLOCK), :]
                + after_ref[pl.ds(PAD + row + 1, BLOCK), :]
            )
            state_ref[place, :] = state
            second = state * inverse_rms(state) * gain_two_ref[...]
            second_ref[pl.ds(row, BLOCK), :] = second.astype(bf16)
        for copy in keep(at):
            copy.start()
        for start in range(0, PATCH, CHUNK):
            value = dot(second_ref[pl.ds(start, CHUNK), :], up_ref[...])
            for row in range(0, CHUNK, 16):
                for col in range(0, hidden_width, 2 * LANES):
                    hidden_ref[pl.ds(start + row, 16), pl.ds(col, 2 * LANES)] = gelu_tanh(
                        value[row : row + 16, col : col + 2 * LANES]
                    ).astype(bf16)
        for start in range(0, PATCH, WIDE):
            place = pl.ds(origin + start, WIDE)
            result_ref[place, :] = (
                state_ref[place, :] + dot(hidden_ref[pl.ds(start, WIDE), :], down_ref[...])
            ).astype(bf16)
        return 0

    fetch.wait()
    lax.fori_loop(0, slots // PATCH, patch, 0)
    pack_rows(zorder_ref, result_ref, back_out, stage_ref, pack_sems)
    for at in range(slots // PATCH):
        for copy in keep(at):
            copy.wait()


def backward_kernel(
    bit_ref, zorder_ref, conv_ref, gain_one_ref, gain_two_ref, up_ref, down_ref, came_in, serial_in, state_in,
    serial_grad_out, keep_ref, send_ref,
    grad_ref, serial_ref, state_ref, out_grad_ref, serial_grad_ref, weights_ref, taps_ref, second_ref, hidden_ref, pre_grad_ref, state_grad_ref, mixed_ref, before_ref, here_ref,
    after_ref, normed_ref, conv_sum_ref, gains_ref, sems, *, groups, inner
):
    slots, width = serial_ref.shape
    fetch_grad = pltpu.make_async_copy(came_in.at[:, pl.ds(width, width)], grad_ref, sems.at[1, 0])
    fetch_state = pltpu.make_async_copy(state_in, state_ref, sems.at[2, 0])
    fetch_serial = pltpu.make_async_copy(serial_in, serial_ref, sems.at[3, 0])
    fetch_grad.start()
    fetch_state.start()
    fetch_serial.start()
    hidden_width = up_ref.shape[1]
    taps_ref[...] = full_taps(conv_ref, groups, inner)
    padded_zeros(before_ref)
    padded_zeros(after_ref)
    padded_zeros(mixed_ref)
    conv_sum_ref[...] = jnp.zeros_like(conv_sum_ref)
    gains_ref[...] = jnp.zeros_like(gains_ref)

    def keep_grad(at):
        place = pl.ds(pl.multiple_of(at * PATCH, PATCH), PATCH)
        return pltpu.make_async_copy(serial_grad_ref.at[place], serial_grad_out.at[place], sems.at[0, at])

    def patch(at, _):
        origin = pl.multiple_of(at * PATCH, PATCH)
        for start in range(0, PATCH, WIDE):
            column = column_of(zorder_ref[:, pl.ds(origin + start, WIDE)], WIDE)
            out_grad_ref[pl.ds(origin + start, WIDE), :] = dot(
                pick_rows(column, slots), grad_ref[...]
            ).astype(bf16)
        for start in range(0, PATCH, CHUNK):
            place = pl.ds(origin + start, CHUNK)
            state = state_ref[place, :]
            scale_two = inverse_rms(state)
            unit_two = state * scale_two
            second = (unit_two * gain_two_ref[...]).astype(bf16)
            second_ref[place, :] = second
            value = dot(second, up_ref[...])
            square, tangent = gelu_parts(value)
            half = 0.5 * value
            hidden_ref[place, :] = (half + half * tangent).astype(bf16)
            out_grad = out_grad_ref[place, :]
            hidden_grad = dot(out_grad, down_ref[...], NT).astype(bf16).astype(f32)
            pre_grad = (hidden_grad * slope_of(value, square, tangent)).astype(bf16)
            pre_grad_ref[place, :] = pre_grad
            second_grad = dot(pre_grad, up_ref[...], NT).astype(bf16).astype(f32)
            weighted = second_grad * gain_two_ref[...]
            gains_ref[1:2, :] += jnp.sum(second_grad * unit_two, axis=0, keepdims=True)
            middle = jnp.mean(weighted * unit_two, axis=-1, keepdims=True)
            state_grad = out_grad.astype(f32) + scale_two * (weighted - unit_two * middle)
            state_grad_ref[pl.ds(start, CHUNK), :] = state_grad
            mixed_grad = state_grad.astype(bf16)
            mixed_ref[pl.ds(PAD + start, CHUNK), :] = mixed_grad.astype(f32)
            before_ref[pl.ds(PAD + start, CHUNK), :] = dot(mixed_grad, taps_ref[0:width, :], NT)
            here_ref[pl.ds(start, CHUNK), :] = dot(mixed_grad, taps_ref[width : 2 * width, :], NT)
            after_ref[pl.ds(PAD + start, CHUNK), :] = dot(mixed_grad, taps_ref[2 * width :, :], NT)
        for start in range(0, PATCH, CHUNK):
            place = pl.ds(origin + start, CHUNK)
            serial = serial_ref[place, :].astype(f32)
            scale_one = inverse_rms(serial)
            unit_one = serial * scale_one
            normed_ref[pl.ds(start, CHUNK), :] = (unit_one * gain_one_ref[...]).astype(bf16)
            normed_grad = (
                before_ref[pl.ds(PAD + start + 1, CHUNK), :]
                + here_ref[pl.ds(start, CHUNK), :]
                + after_ref[pl.ds(PAD + start - 1, CHUNK), :]
            ).astype(bf16).astype(f32)
            gains_ref[0:1, :] += jnp.sum(normed_grad * unit_one, axis=0, keepdims=True)
            weighted = normed_grad * gain_one_ref[...]
            middle = jnp.mean(weighted * unit_one, axis=-1, keepdims=True)
            serial_grad_ref[place, :] = (
                state_grad_ref[pl.ds(start, CHUNK), :] + scale_one * (weighted - unit_one * middle)
            ).astype(bf16)
        keep_grad(at).start()
        for tap in range(3):
            moved = mixed_ref[pl.ds(PAD + 1 - tap, PATCH), :].astype(bf16)
            conv_sum_ref[tap] += dot(normed_ref[...], moved, TN)
        return 0

    fetch_grad.wait()
    fetch_state.wait()
    fetch_serial.wait()
    lax.fori_loop(0, slots // PATCH, patch, 0)
    for start in range(0, hidden_width, width):
        weights_ref[start : start + width, :] = dot(
            hidden_ref[:, start : start + width], out_grad_ref[...], TN
        ).astype(weights_ref.dtype)
        weights_ref[hidden_width + start : hidden_width + start + width, :] = dot(
            second_ref[...], pre_grad_ref[:, start : start + width], TN
        ).astype(weights_ref.dtype)
    same = lax.div(iota((width, width), 0), inner) == lax.div(iota((width, width), 1), inner)
    for tap in range(3):
        kept = jnp.where(same, conv_sum_ref[tap], 0.0).reshape(groups, inner, width)
        at = 2 * hidden_width + tap * inner
        weights_ref[at : at + inner, :] = jnp.sum(kept, axis=0).astype(weights_ref.dtype)
    at = 2 * hidden_width + 3 * inner
    weights_ref[at : at + 16, :] = gains_ref[...].astype(weights_ref.dtype)
    at = at + 16
    weights_ref[at:, :] = jnp.zeros((weights_ref.shape[0] - at, width), weights_ref.dtype)
    split_rows(bit_ref[0], weights_ref, keep_ref, send_ref)
    for at in range(slots // PATCH):
        keep_grad(at).wait()


def split_rows(bit, rows_ref, keep_ref, send_ref):
    half = keep_ref.shape[0]
    keep_ref[...] = rows_ref[pl.ds(pl.multiple_of(bit * half, 16), half), :]
    send_ref[...] = rows_ref[pl.ds(pl.multiple_of((1 - bit) * half, 16), half), :]


def add_split_kernel(bit_ref, mine_ref, came_ref, keep_ref, send_ref, total_ref):
    total_ref[...] = (mine_ref[...].astype(f32) + came_ref[...].astype(f32)).astype(bf16)
    split_rows(bit_ref[0], total_ref, keep_ref, send_ref)


def add_kernel(mine_ref, came_ref, total_ref):
    total_ref[...] = (mine_ref[...].astype(f32) + came_ref[...].astype(f32)).astype(bf16)


def join_kernel(bit_ref, mine_ref, came_ref, both_ref):
    half = mine_ref.shape[0]
    bit = bit_ref[0]
    both_ref[pl.ds(pl.multiple_of(bit * half, 16), half), :] = mine_ref[...]
    both_ref[pl.ds(pl.multiple_of((1 - bit) * half, 16), half), :] = came_ref[...]


def spread_kernel(
    bit_ref, mine_ref, came_ref, up_ref, down_ref, conv_ref, gain_one_ref, gain_two_ref, sums_ref, *, scale
):
    join_kernel(bit_ref, mine_ref, came_ref, sums_ref)
    width, hidden_width = up_ref.shape
    taps, groups, inner = conv_ref.shape[:3]
    down_ref[...] = sums_ref[0:hidden_width, :].astype(f32) * scale
    for start in range(0, hidden_width, width):
        up_ref[:, start : start + width] = (
            sums_ref[hidden_width + start : hidden_width + start + width, :].astype(f32) * scale
        )
    for tap in range(taps):
        at = 2 * hidden_width + tap * inner
        rows = sums_ref[at : at + inner, :].astype(f32) * scale
        for group in range(groups):
            conv_ref[tap, group] = rows[:, group * inner : (group + 1) * inner]
    at = 2 * hidden_width + taps * inner
    gains = sums_ref[at : at + 16, :].astype(f32) * scale
    gain_one_ref[...] = gains[0:1, :]
    gain_two_ref[...] = gains[1:2, :]


def call(kernel, outs, args, scratch=(), smem=0, flops=0, limit=16, held=0, stored=0, after=(), **static):
    moved = sum(math.prod(a.shape) * a.dtype.itemsize for a in (*args, *outs))
    specs = [pl.BlockSpec(memory_space=pltpu.SMEM)] * smem
    specs += [pl.BlockSpec(memory_space=pltpu.VMEM)] * (len(args) - smem - held)
    specs += [pl.BlockSpec(memory_space=pltpu.HBM)] * held
    specs += [pl.BlockSpec(memory_space=pl.ANY)] * len(after)
    out_specs = [pl.BlockSpec(memory_space=pltpu.HBM)] * stored
    shapes = [pltpu.HBM(a.shape, a.dtype) for a in outs[:stored]] + list(outs[stored:])
    first_held = len(args) - held
    args = [*args[:first_held], *(pltpu.with_memory_space_constraint(a, pltpu.HBM) for a in args[first_held:])]
    out_specs += [pl.BlockSpec(memory_space=pltpu.VMEM)] * (len(outs) - stored)
    count = len(args)

    def run(*refs):
        kernel(*refs[:count], *refs[count + len(after) :], **static)

    return pl.pallas_call(
        run,
        out_shape=tuple(shapes),
        in_specs=specs,
        out_specs=tuple(out_specs),
        scratch_shapes=list(scratch),
        compiler_params=pltpu.CompilerParams(vmem_limit_bytes=limit * 1024 * 1024),
        cost_estimate=pl.CostEstimate(flops=int(flops), bytes_accessed=moved, transcendentals=0),
    )(*args, *after)


def shaped(*shape, dtype=bf16):
    return jax.ShapeDtypeStruct(shape, dtype)


def shifted(value, axis, steps):
    count = lax.axis_size(axis)
    initial, last = (max(0, -steps), min(count, count - steps))
    return lax.ppermute(value, axis, [(source, source + steps) for source in range(initial, last)])


def partner(value, axis, step):
    return lax.ppermute(value, axis, [(at, at ^ step) for at in range(lax.axis_size(axis))])


def bit_of(axis, step):
    return lax.rem(lax.div(lax.axis_index(axis), step), 2).astype(jnp.int32).reshape(1)


def steps_of(axis):
    return [1 << at for at in range(int(math.log2(lax.axis_size(axis))))]


def sum_over_mesh(keep, send):
    width = keep.shape[1]
    steps = steps_of("ty")
    for step, later in zip(steps, steps[1:] + [0]):
        came = partner(send, "ty", step)
        rows = keep.shape[0]
        if later:
            half = shaped(rows // 2, width)
            keep, send = call(
                add_split_kernel,
                [half, half],
                [bit_of("ty", later), keep, came],
                scratch=[pltpu.VMEM((rows, width), bf16)],
                smem=1,
                flops=1e6,
            )
        else:
            (share,) = call(add_kernel, [shaped(rows, width)], [keep, came], flops=1e6)
    for step in steps_of("tx"):
        (share,) = call(
            add_kernel, [shaped(*share.shape)], [share, partner(share, "tx", step)], flops=1e6
        )
    for step in steps[:0:-1]:
        (share,) = call(
            join_kernel,
            [shaped(2 * share.shape[0], width)],
            [bit_of("ty", step), share, partner(share, "ty", step)],
            smem=1,
            flops=1e6,
        )
    return share, partner(share, "ty", steps[0])


def exchange(rows, tiles):
    return lax.all_to_all(rows, ("tx", "ty"), split_axis=0, concat_axis=0, tiled=True)


def body(
    points,
    counts,
    owner,
    zorder,
    border,
    near,
    w_near,
    gain_one,
    conv_w,
    gain_two,
    w_up,
    w_down,
    grad_out,
):
    points_tile = points[0]
    tile_rows, width = points_tile.shape
    border_rows = border.shape[2]
    edge = 4 * border_rows
    ext = tile_rows + edge
    lists = border.reshape(1, edge)
    near_tile = near[0]
    neighbours = near_tile.shape[0]
    tiles = lax.axis_size("tx") * lax.axis_size("ty")
    slots_count = zorder.shape[1]
    capacity = slots_count // tiles
    taps, groups, inner = conv_w.shape[:3]
    conv_rows = conv_w.reshape(taps * groups * inner, inner)
    gain_one_row = gain_one.reshape(1, width)
    gain_two_row = gain_two.reshape(1, width)
    hidden = w_up.shape[1]

    slots, sent = call(
        route_kernel,
        [shaped(1, tile_rows, dtype=jnp.int32), shaped(edge, width)],
        [counts, owner, lists, points_tile],
        smem=1,
        flops=4e9,
        tiles=tiles,
        capacity=capacity,
    )
    halos = [
        shifted(sent[0:border_rows], "tx", -1),
        shifted(sent[border_rows : 2 * border_rows], "tx", 1),
        shifted(sent[2 * border_rows : 3 * border_rows], "ty", -1),
        shifted(sent[3 * border_rows :], "ty", 1),
    ]
    kept_table, table = call(
        count_kernel,
        [shaped(ext, tile_rows), shaped(ext, tile_rows)],
        [near_tile],
        scratch=[pltpu.SemaphoreType.DMA((ext // CHUNK,))],
        flops=8e9,
        stored=1,
    )
    average, pre_act, packed = call(
        lift_kernel,
        [
            shaped(width, tile_rows),
            shaped(tile_rows, width, dtype=f32),
            shaped(slots_count, 2 * width),
        ],
        [slots, points_tile, grad_out[0], *halos, table, w_near],
        scratch=[
            pltpu.VMEM((width, tile_rows), bf16),
            pltpu.VMEM((tile_rows, width), f32),
            pltpu.VMEM((tile_rows, 2 * width), bf16),
            pltpu.VMEM((slots_count, 2 * width), bf16),
            pltpu.SemaphoreType.DMA((2,)),
            pltpu.SemaphoreType.DMA((slots_count // WIDE,)),
        ],
        flops=4e9,
        stored=3,
        neighbours=neighbours,
    )
    came = exchange(packed, tiles)
    patch_scratch = [
        pltpu.VMEM((PATCH + 2 * PAD, width), f32),
        pltpu.VMEM((PATCH, width), f32),
        pltpu.VMEM((PATCH + 2 * PAD, width), f32),
    ]
    serial, state, back_result = call(
        forward_kernel,
        [
            shaped(slots_count, width),
            shaped(slots_count, width, dtype=f32),
            shaped(slots_count, width),
        ],
        [zorder, conv_rows, gain_one_row, gain_two_row, w_up, w_down, came],
        held=1,
        scratch=[
            pltpu.VMEM((slots_count, width), bf16),
            pltpu.VMEM((slots_count, width), bf16),
            pltpu.VMEM((slots_count, width), f32),
            pltpu.VMEM((taps * width, width), bf16),
            pltpu.VMEM((PATCH, width), bf16),
            *patch_scratch,
            pltpu.VMEM((PATCH, width), bf16),
            pltpu.VMEM((PATCH, hidden), bf16),
            pltpu.VMEM((slots_count, width), bf16),
            pltpu.VMEM((slots_count, width), bf16),
            pltpu.SemaphoreType.DMA((3, slots_count // PATCH)),
            pltpu.SemaphoreType.DMA((slots_count // WIDE,)),
        ],
        flops=10e9,
        limit=32,
        stored=3,
        groups=groups,
        inner=inner,
    )
    came_result = exchange(back_result, tiles)
    lines = lax.axis_size("ty")
    sums_rows = 2 * hidden + taps * inner + 16
    sums_rows = -(-sums_rows // (16 * lines)) * (16 * lines)
    serial_grad, keep, send = call(
        backward_kernel,
        [
            shaped(slots_count, width),
            shaped(sums_rows // 2, width),
            shaped(sums_rows // 2, width),
        ],
        [
            bit_of("ty", 1),
            zorder,
            conv_rows,
            gain_one_row,
            gain_two_row,
            w_up,
            w_down,
            came,
            serial,
            state,
        ],
        held=3,
        scratch=[
            pltpu.VMEM((slots_count, width), bf16),
            pltpu.VMEM((slots_count, width), bf16),
            pltpu.VMEM((slots_count, width), f32),
            pltpu.VMEM((slots_count, width), bf16),
            pltpu.VMEM((slots_count, width), bf16),
            pltpu.VMEM((sums_rows, width), bf16),
            pltpu.VMEM((taps * width, width), bf16),
            pltpu.VMEM((slots_count, width), bf16),
            pltpu.VMEM((slots_count, hidden), bf16),
            pltpu.VMEM((slots_count, hidden), bf16),
            pltpu.VMEM((PATCH, width), f32),
            pltpu.VMEM((PATCH + 2 * PAD, width), f32),
            *patch_scratch,
            pltpu.VMEM((PATCH, width), bf16),
            pltpu.VMEM((taps, width, width), f32),
            pltpu.VMEM((16, width), f32),
            pltpu.SemaphoreType.DMA((4, slots_count // PATCH)),
        ],
        stored=1,
        smem=1,
        flops=40e9,
        limit=40,
        groups=groups,
        inner=inner,
    )
    (back_grad,) = call(
        pack_rows,
        [shaped(slots_count, width)],
        [zorder, serial_grad],
        after=[came_result],
        scratch=[
            pltpu.VMEM((slots_count, width), bf16),
            pltpu.SemaphoreType.DMA((slots_count // WIDE,)),
        ],
        stored=1,
        flops=4e9,
    )
    came_back = exchange(back_grad, tiles)
    totals = sum_over_mesh(keep, send)
    (out_rows,) = call(
        unpack_kernel, [shaped(tile_rows, width)], [slots, came_result], flops=4e9
    )
    row_grad, near_grad, halo_grad = call(
        tile_back_kernel,
        [shaped(tile_rows, width, dtype=f32), shaped(width, width), shaped(edge, width)],
        [slots, came_back, w_near, kept_table, average, pre_act],
        after=[out_rows],
        scratch=[
            pltpu.VMEM((tile_rows, width), f32),
            pltpu.VMEM((ext, tile_rows), bf16),
            pltpu.VMEM((width, tile_rows), bf16),
            pltpu.VMEM((tile_rows, width), f32),
            pltpu.VMEM((tile_rows, width), bf16),
            pltpu.VMEM((tile_rows, width), bf16),
            pltpu.SemaphoreType.DMA((3 + tile_rows // WIDE,)),
        ],
        flops=6e9,
        limit=24,
        held=3,
        stored=1,
        neighbours=neighbours,
    )
    near_parts = exchange(near_grad, tiles).reshape(tiles, width // tiles, width)
    near_share = jnp.sum(near_parts.astype(f32), axis=0)
    near_all = jnp.broadcast_to(near_share.astype(bf16), (tiles, *near_share.shape))
    near_sum = exchange(near_all.reshape(width, width), tiles)
    returned = [
        shifted(halo_grad[0:border_rows], "tx", 1),
        shifted(halo_grad[border_rows : 2 * border_rows], "tx", -1),
        shifted(halo_grad[2 * border_rows : 3 * border_rows], "ty", 1),
        shifted(halo_grad[3 * border_rows :], "ty", -1),
    ]
    (grad_points,) = call(
        finish_kernel, [shaped(tile_rows, width)], [lists, row_grad, *returned], flops=1e9
    )
    scale = 1.0 / math.sqrt(tiles * tile_rows)
    up_sum, down_sum, conv_sum, gain_one_sum, gain_two_sum = call(
        spread_kernel,
        [
            shaped(width, hidden, dtype=f32),
            shaped(hidden, width, dtype=f32),
            shaped(*conv_w.shape, dtype=f32),
            shaped(1, width, dtype=f32),
            shaped(1, width, dtype=f32),
        ],
        [bit_of("ty", 1), *totals],
        scratch=[pltpu.VMEM((sums_rows, width), bf16)],
        smem=1,
        flops=1e6,
        scale=scale,
    )
    return (
        out_rows[None],
        grad_points[None],
        near_sum.astype(f32) * scale,
        gain_one_sum[0],
        conv_sum,
        gain_two_sum[0],
        up_sum,
        down_sum,
    )


def solution(mesh):
    placed = (
        P(("tx", "ty"), None, None),
        P(("tx", "ty")),
        P(("tx", "ty"), None),
        P(("tx", "ty"), None),
        P(("tx", "ty"), None, None),
        P(("tx", "ty"), None, None),
        P(),
        P(),
        P(),
        P(),
        P(),
        P(),
        P(("tx", "ty"), None, None),
    )
    return jax.shard_map(
        body,
        mesh=mesh,
        in_specs=placed,
        out_specs=(
            P(("tx", "ty"), None, None),
            P(("tx", "ty"), None, None),
            P(),
            P(),
            P(),
            P(),
            P(),
            P(),
        ),
        check_vma=False,
    )
```

```python
import math

import jax
import jax.numpy as jnp
from jax import lax
from jax.experimental import pallas as pl
from jax.experimental.pallas import tpu as pltpu
from jax.sharding import PartitionSpec as P

PATCH = 1024
CHUNK = 256
WIDE = 512
BLOCK = 64
LANES = 128
PAD = 8

eps_norm = 1e-06
gelu_coef = 0.7978845608028654
cubic_coef = 0.044715

bf16 = jnp.bfloat16
f32 = jnp.float32
NN = (((1,), (0,)), ((), ()))
NT = (((1,), (1,)), ((), ()))
TN = (((0,), (0,)), ((), ()))


def dot(left, right, dims=NN):
    return lax.dot_general(left, right, dims, preferred_element_type=f32)


def iota(shape, axis):
    return lax.broadcasted_iota(jnp.int32, shape, axis)


def marks(mask):
    return jnp.where(mask, 1.0, 0.0).astype(bf16)


def gelu_parts(value):
    square = value * value
    tangent = jnp.tanh(value * (gelu_coef + (gelu_coef * cubic_coef) * square))
    return square, tangent


def gelu_tanh(value):
    _, tangent = gelu_parts(value)
    half = 0.5 * value
    return half + half * tangent


def slope_of(value, square, tangent):
    inner_slope = gelu_coef + (3.0 * gelu_coef * cubic_coef) * square
    return 0.5 * (1.0 + tangent) + (0.5 * value) * (1.0 - tangent * tangent) * inner_slope


def inverse_rms(value):
    return lax.rsqrt(jnp.mean(value * value, axis=-1, keepdims=True) + eps_norm)


def column_of(row, count):
    return jnp.transpose(jnp.broadcast_to(row, (LANES, count)))


def pick_rows(column, depth):
    count = column.shape[0]
    lane = iota((count, LANES), 1)
    return jnp.concatenate(
        [marks(column == lane + base) for base in range(0, depth, LANES)], axis=1
    )


def mark_slots(row, start, count):
    return marks(iota((count, row.shape[1]), 0) + start == row)


def route_kernel(counts_ref, owner_ref, lists_ref, points_ref, slots_ref, sent_ref, *, tiles, capacity):
    rows = owner_ref.shape[1]
    live = iota((1, rows), 1) < counts_ref[0]
    owned = jnp.where(live, owner_ref[...], tiles)
    members = owned == iota((tiles, rows), 0)
    earlier = marks(iota((rows, rows), 0) < iota((rows, rows), 1))
    before = dot(marks(members), earlier)
    rank = jnp.sum(jnp.where(members, before, 0.0), axis=0, keepdims=True)
    slots_ref[...] = jnp.where(live, owned * capacity + rank.astype(jnp.int32), -1)
    lists = lists_ref[...]
    chosen = marks(iota((rows, lists.shape[1]), 0) == lists)
    sent_ref[...] = dot(chosen, points_ref[...], TN).astype(bf16)


def pack_rows(slots_ref, rows_ref, packed_out, stage_ref, sems):
    slots = slots_ref[...]
    copies = []
    for at, start in enumerate(range(0, packed_out.shape[0], WIDE)):
        place = pl.ds(start, WIDE)
        stage_ref[place, :] = dot(mark_slots(slots, start, WIDE), rows_ref[...]).astype(bf16)
        copies.append(pltpu.make_async_copy(stage_ref.at[place], packed_out.at[place], sems.at[at]))
        copies[-1].start()
    for copy in copies:
        copy.wait()


def unpack_kernel(slots_ref, packed_ref, rows_ref):
    for start in range(0, rows_ref.shape[0], CHUNK):
        column = column_of(slots_ref[:, start : start + CHUNK], CHUNK)
        rows_ref[pl.ds(start, CHUNK), :] = dot(
            pick_rows(column, packed_ref.shape[0]), packed_ref[...]
        ).astype(bf16)


def count_kernel(near_ref, kept_ref, table_ref, sems):
    neighbours, rows = near_ref.shape
    step = 16
    zero = jnp.zeros((step, LANES), bf16)
    one = jnp.ones((step, LANES), bf16)
    row_blocks = table_ref.shape[0] // CHUNK

    def copy_out(row_block):
        place = pl.ds(pl.multiple_of(row_block * CHUNK, CHUNK), CHUNK)
        return pltpu.make_async_copy(table_ref.at[place], kept_ref.at[place], sems.at[row_block])

    def rows_of(row_block, _):
        row_at = pl.multiple_of(row_block * CHUNK, CHUNK)

        def block(lane_block, _):
            lane_at = pl.multiple_of(lane_block * LANES, LANES)
            local = (near_ref[:, pl.ds(lane_at, LANES)] - row_at).astype(f32)
            spread = [
                jnp.broadcast_to(local[k : k + 1, :], (step, LANES)).astype(bf16)
                for k in range(neighbours)
            ]
            base = iota((step, LANES), 0).astype(f32)
            for inner in range(0, CHUNK, step):
                here = (base + float(inner)).astype(bf16)
                total = zero
                for k in range(neighbours):
                    total = total + jnp.where(spread[k] == here, one, zero)
                table_ref[pl.ds(row_at + inner, step), pl.ds(lane_at, LANES)] = total
            return 0

        lax.fori_loop(0, rows // LANES, block, 0)
        copy_out(row_block).start()
        return 0

    lax.fori_loop(0, row_blocks, rows_of, 0)
    for row_block in range(row_blocks):
        copy_out(row_block).wait()


def lift_kernel(
    slots_ref, points_ref, grad_ref, halo0, halo1, halo2, halo3, table_ref, w_ref,
    average_out, pre_out, packed_out,
    average_ref, pre_ref, both_ref, stage_ref, sems, pack_sems, *, neighbours
):
    width = points_ref.shape[1]
    ext = jnp.concatenate([points_ref[...], halo0[...], halo1[...], halo2[...], halo3[...]], axis=0)
    average = (dot(ext, table_ref[...], TN) * (1.0 / neighbours)).astype(bf16)
    average_ref[...] = average
    keep_average = pltpu.make_async_copy(average_ref, average_out, sems.at[0])
    keep_average.start()
    pre_ref[...] = dot(average, w_ref[...], TN)
    keep_pre = pltpu.make_async_copy(pre_ref, pre_out, sems.at[1])
    keep_pre.start()
    for row in range(0, points_ref.shape[0], BLOCK):
        here = pl.ds(row, BLOCK)
        both_ref[here, 0:width] = (
            points_ref[here, :].astype(f32) + gelu_tanh(pre_ref[here, :])
        ).astype(bf16)
    both_ref[:, width:] = grad_ref[...]
    pack_rows(slots_ref, both_ref, packed_out, stage_ref, pack_sems)
    keep_average.wait()
    keep_pre.wait()


def tile_back_kernel(
    slots_ref, back_ref, w_ref, table_in, average_in, pre_in,
    row_out, near_ref, halo_ref,
    row_ref, table_ref, average_ref, pre_ref, act_ref, spread_ref, sems, *, neighbours
):
    rows = row_ref.shape[0]
    fetch_pre = pltpu.make_async_copy(pre_in, pre_ref, sems.at[0])
    fetch_average = pltpu.make_async_copy(average_in, average_ref, sems.at[1])
    fetch_table = pltpu.make_async_copy(table_in, table_ref, sems.at[2])

    def keep_row(start):
        place = pl.ds(start, WIDE)
        return pltpu.make_async_copy(row_ref.at[place], row_out.at[place], sems.at[3 + start // WIDE])

    fetch_pre.start()
    fetch_average.start()
    fetch_table.start()
    fetch_pre.wait()
    for start in range(0, rows, CHUNK):
        column = column_of(slots_ref[:, start : start + CHUNK], CHUNK)
        wide = dot(pick_rows(column, back_ref.shape[0]), back_ref[...])
        for row in range(0, CHUNK, BLOCK):
            here = pl.ds(start + row, BLOCK)
            lifted_grad = wide[row : row + BLOCK]
            row_ref[here, :] = lifted_grad
            value = pre_ref[here, :]
            square, tangent = gelu_parts(value)
            act_ref[here, :] = (lifted_grad * slope_of(value, square, tangent)).astype(bf16)
    fetch_average.wait()
    near_ref[...] = dot(average_ref[...], act_ref[...]).astype(near_ref.dtype)
    spread_ref[...] = (dot(act_ref[...], w_ref[...], NT) * (1.0 / neighbours)).astype(bf16)
    fetch_table.wait()
    halo_ref[...] = dot(table_ref[rows:, :], spread_ref[...]).astype(bf16)
    for start in range(0, rows, WIDE):
        here = pl.ds(start, WIDE)
        row_ref[here, :] = row_ref[here, :] + dot(table_ref[here, :], spread_ref[...])
        keep_row(start).start()
    for start in range(0, rows, WIDE):
        keep_row(start).wait()


def finish_kernel(lists_ref, row_ref, back0, back1, back2, back3, out_ref):
    lists = lists_ref[...]
    came = jnp.concatenate([back0[...], back1[...], back2[...], back3[...]], axis=0)
    chosen = marks(iota((row_ref.shape[0], lists.shape[1]), 0) == lists)
    out_ref[...] = (row_ref[...] + dot(chosen, came)).astype(bf16)


def full_taps(conv_ref, groups, inner):
    width = groups * inner
    rows = conv_ref.shape[0]
    repeat = marks(lax.rem(iota((inner, width), 1), inner) == iota((inner, width), 0))
    wide = dot(conv_ref[...], repeat)
    row_group = lax.div(lax.rem(iota((rows, width), 0), width), inner)
    same = row_group == lax.div(iota((rows, width), 1), inner)
    return jnp.where(same, wide, 0.0).astype(bf16)


def padded_zeros(ref):
    edge = jnp.zeros((PAD, ref.shape[1]), f32)
    ref[0:PAD, :] = edge
    ref[PAD + PATCH :, :] = edge


def forward_kernel(
    zorder_ref, conv_ref, gain_one_ref, gain_two_ref, up_ref, down_ref, came_in,
    serial_out, state_out, back_out,
    lifted_ref, serial_ref, state_ref, taps_ref, normed_ref, before_ref, here_ref, after_ref, second_ref, hidden_ref,
    result_ref, stage_ref, sems, pack_sems, *, groups, inner
):
    slots, width = lifted_ref.shape
    fetch = pltpu.make_async_copy(came_in.at[:, pl.ds(0, width)], lifted_ref, sems.at[2, 0])
    fetch.start()
    hidden_width = up_ref.shape[1]
    taps_ref[...] = full_taps(conv_ref, groups, inner)
    padded_zeros(before_ref)
    padded_zeros(after_ref)

    def keep(at):
        place = pl.ds(pl.multiple_of(at * PATCH, PATCH), PATCH)
        return (
            pltpu.make_async_copy(serial_ref.at[place], serial_out.at[place], sems.at[0, at]),
            pltpu.make_async_copy(state_ref.at[place], state_out.at[place], sems.at[1, at]),
        )

    def patch(at, _):
        origin = pl.multiple_of(at * PATCH, PATCH)
        for start in range(0, PATCH, WIDE):
            column = column_of(zorder_ref[:, pl.ds(origin + start, WIDE)], WIDE)
            wide = dot(pick_rows(column, slots), lifted_ref[...])
            for row in range(0, WIDE, BLOCK):
                serial = wide[row : row + BLOCK]
                serial_ref[pl.ds(origin + start + row, BLOCK), :] = serial.astype(bf16)
                normed = serial * inverse_rms(serial) * gain_one_ref[...]
                normed_ref[pl.ds(start + row, BLOCK), :] = normed.astype(bf16)
        before_ref[pl.ds(PAD, PATCH), :] = dot(normed_ref[...], taps_ref[0:width, :])
        here_ref[...] = dot(normed_ref[...], taps_ref[width : 2 * width, :])
        after_ref[pl.ds(PAD, PATCH), :] = dot(normed_ref[...], taps_ref[2 * width :, :])
        for row in range(0, PATCH, BLOCK):
            place = pl.ds(origin + row, BLOCK)
            state = serial_ref[place, :].astype(f32) + (
                before_ref[pl.ds(PAD + row - 1, BLOCK), :]
                + here_ref[pl.ds(row, BLOCK), :]
                + after_ref[pl.ds(PAD + row + 1, BLOCK), :]
            )
            state_ref[place, :] = state
            second = state * inverse_rms(state) * gain_two_ref[...]
            second_ref[pl.ds(row, BLOCK), :] = second.astype(bf16)
        for copy in keep(at):
            copy.start()
        for start in range(0, PATCH, CHUNK):
            value = dot(second_ref[pl.ds(start, CHUNK), :], up_ref[...])
            for row in range(0, CHUNK, 16):
                for col in range(0, hidden_width, 2 * LANES):
                    hidden_ref[pl.ds(start + row, 16), pl.ds(col, 2 * LANES)] = gelu_tanh(
                        value[row : row + 16, col : col + 2 * LANES]
                    ).astype(bf16)
        for start in range(0, PATCH, WIDE):
            place = pl.ds(origin + start, WIDE)
            result_ref[place, :] = (
                state_ref[place, :] + dot(hidden_ref[pl.ds(start, WIDE), :], down_ref[...])
            ).astype(bf16)
        return 0

    fetch.wait()
    lax.fori_loop(0, slots // PATCH, patch, 0)
    pack_rows(zorder_ref, result_ref, back_out, stage_ref, pack_sems)
    for at in range(slots // PATCH):
        for copy in keep(at):
            copy.wait()


def backward_kernel(
    bit_ref, zorder_ref, conv_ref, gain_one_ref, gain_two_ref, up_ref, down_ref, came_in, serial_in, state_in,
    back_out, keep_out, send_out,
    grad_ref, serial_ref, state_ref, out_grad_ref, serial_grad_ref, stage_ref, weights_ref, taps_ref,
    second_ref, hidden_ref, pre_grad_ref, state_grad_ref, mixed_ref, mixed_half_ref, before_ref, here_ref,
    after_ref, normed_ref, conv_sum_ref, gains_ref, sems, pack_sems, *, groups, inner
):
    slots, width = serial_ref.shape
    hidden_width = up_ref.shape[1]
    fetch_grad = pltpu.make_async_copy(came_in.at[:, pl.ds(width, width)], grad_ref, sems.at[0])
    fetch_state = pltpu.make_async_copy(state_in, state_ref, sems.at[1])
    fetch_serial = pltpu.make_async_copy(serial_in, serial_ref, sems.at[2])
    fetch_grad.start()
    fetch_state.start()
    fetch_serial.start()
    taps_ref[...] = full_taps(conv_ref, groups, inner)
    padded_zeros(before_ref)
    padded_zeros(after_ref)
    padded_zeros(mixed_ref)
    conv_sum_ref[...] = jnp.zeros_like(conv_sum_ref)
    gains_ref[...] = jnp.zeros_like(gains_ref)

    def patch(at, _):
        origin = pl.multiple_of(at * PATCH, PATCH)
        for start in range(0, PATCH, WIDE):
            column = column_of(zorder_ref[:, pl.ds(origin + start, WIDE)], WIDE)
            out_grad_ref[pl.ds(origin + start, WIDE), :] = dot(
                pick_rows(column, slots), grad_ref[...]
            ).astype(bf16)
        for start in range(0, PATCH, CHUNK):
            place = pl.ds(origin + start, CHUNK)
            for row in range(start, start + CHUNK, BLOCK):
                state = state_ref[pl.ds(origin + row, BLOCK), :]
                second = state * inverse_rms(state) * gain_two_ref[...]
                second_ref[pl.ds(origin + row, BLOCK), :] = second.astype(bf16)
            value_all = dot(second_ref[place, :], up_ref[...])
            hidden_grad_all = dot(out_grad_ref[place, :], down_ref[...], NT)
            for row in range(0, CHUNK, 16):
                for col in range(0, hidden_width, 2 * LANES):
                    value = value_all[row : row + 16, col : col + 2 * LANES]
                    hidden_grad = hidden_grad_all[row : row + 16, col : col + 2 * LANES]
                    square, tangent = gelu_parts(value)
                    half = 0.5 * value
                    piece = pl.ds(origin + start + row, 16), pl.ds(col, 2 * LANES)
                    hidden_ref[piece] = (half + half * tangent).astype(bf16)
                    pre_grad_ref[piece] = (
                        hidden_grad.astype(bf16).astype(f32) * slope_of(value, square, tangent)
                    ).astype(bf16)
            second_grad_all = dot(pre_grad_ref[place, :], up_ref[...], NT)
            for row in range(0, CHUNK, BLOCK):
                here = pl.ds(origin + start + row, BLOCK)
                state = state_ref[here, :]
                scale_two = inverse_rms(state)
                unit_two = state * scale_two
                second_grad = second_grad_all[row : row + BLOCK].astype(bf16).astype(f32)
                weighted = second_grad * gain_two_ref[...]
                product = second_grad * unit_two
                gains_ref[1:2, :] += jnp.sum(product, axis=0, keepdims=True)
                middle = jnp.mean(product * gain_two_ref[...], axis=-1, keepdims=True)
                state_grad = out_grad_ref[here, :].astype(f32) + scale_two * (weighted - unit_two * middle)
                state_grad_ref[pl.ds(start + row, BLOCK), :] = state_grad
                mixed_grad = state_grad.astype(bf16)
                mixed_half_ref[pl.ds(start + row, BLOCK), :] = mixed_grad
                mixed_ref[pl.ds(PAD + start + row, BLOCK), :] = mixed_grad.astype(f32)
        before_ref[pl.ds(PAD, PATCH), :] = dot(mixed_half_ref[...], taps_ref[0:width, :], NT)
        here_ref[...] = dot(mixed_half_ref[...], taps_ref[width : 2 * width, :], NT)
        after_ref[pl.ds(PAD, PATCH), :] = dot(mixed_half_ref[...], taps_ref[2 * width :, :], NT)
        for row in range(0, PATCH, BLOCK):
            place = pl.ds(origin + row, BLOCK)
            serial = serial_ref[place, :].astype(f32)
            scale_one = inverse_rms(serial)
            unit_one = serial * scale_one
            normed_ref[pl.ds(row, BLOCK), :] = (unit_one * gain_one_ref[...]).astype(bf16)
            normed_grad = (
                before_ref[pl.ds(PAD + row + 1, BLOCK), :]
                + here_ref[pl.ds(row, BLOCK), :]
                + after_ref[pl.ds(PAD + row - 1, BLOCK), :]
            ).astype(bf16).astype(f32)
            product = normed_grad * unit_one
            gains_ref[0:1, :] += jnp.sum(product, axis=0, keepdims=True)
            middle = jnp.mean(product * gain_one_ref[...], axis=-1, keepdims=True)
            weighted = normed_grad * gain_one_ref[...]
            serial_grad_ref[place, :] = (
                state_grad_ref[pl.ds(row, BLOCK), :] + scale_one * (weighted - unit_one * middle)
            ).astype(bf16)
        for tap in range(3):
            moved = mixed_ref[pl.ds(PAD + 1 - tap, PATCH), :].astype(bf16)
            conv_sum_ref[tap] += dot(normed_ref[...], moved, TN)
        return 0

    fetch_grad.wait()
    fetch_state.wait()
    fetch_serial.wait()
    lax.fori_loop(0, slots // PATCH, patch, 0)
    for start in range(0, hidden_width, width):
        block = slice(start, start + width)
        weights_ref[start : start + width, :] = jnp.transpose(
            dot(out_grad_ref[...], hidden_ref[:, block], TN)
        ).astype(bf16)
        weights_ref[hidden_width + start : hidden_width + start + width, :] = dot(
            second_ref[...], pre_grad_ref[:, block], TN
        ).astype(bf16)
    same = lax.div(iota((width, width), 0), inner) == lax.div(iota((width, width), 1), inner)
    for tap in range(3):
        kept = jnp.where(same, conv_sum_ref[tap], 0.0).reshape(groups, inner, width)
        at = 2 * hidden_width + tap * inner
        weights_ref[at : at + inner, :] = jnp.sum(kept, axis=0).astype(bf16)
    at = 2 * hidden_width + 3 * inner
    weights_ref[at : at + 16, :] = gains_ref[...].astype(bf16)
    at = at + 16
    weights_ref[at:, :] = jnp.zeros((weights_ref.shape[0] - at, width), bf16)
    half = keep_out.shape[0]
    bit = bit_ref[0]
    hand_out = [
        pltpu.make_async_copy(
            weights_ref.at[pl.ds(pl.multiple_of(at * half, 16), half)], out, sems.at[3 + which]
        )
        for which, (at, out) in enumerate(((bit, keep_out), (1 - bit, send_out)))
    ]
    for copy in hand_out:
        copy.start()
    pack_rows(zorder_ref, serial_grad_ref, back_out, stage_ref, pack_sems)
    for copy in hand_out:
        copy.wait()


def hold_kernel(rows_in, rows_out):
    pass


def split_rows(bit, rows_ref, keep_ref, send_ref):
    half = keep_ref.shape[0]
    keep_ref[...] = rows_ref[pl.ds(pl.multiple_of(bit * half, 16), half), :]
    send_ref[...] = rows_ref[pl.ds(pl.multiple_of((1 - bit) * half, 16), half), :]


def add_split_kernel(bit_ref, mine_ref, came_ref, keep_ref, send_ref, total_ref):
    total_ref[...] = (mine_ref[...].astype(f32) + came_ref[...].astype(f32)).astype(bf16)
    split_rows(bit_ref[0], total_ref, keep_ref, send_ref)


def add_kernel(mine_ref, came_ref, total_ref):
    total_ref[...] = (mine_ref[...].astype(f32) + came_ref[...].astype(f32)).astype(bf16)


def spread_kernel(
    shares_ref, up_ref, down_ref, conv_ref, gain_one_ref, gain_two_ref, sums_ref, *, bits, scale
):
    share = shares_ref.shape[0] >> bits
    for at in range(1 << bits):
        source = sum(((at >> bit) & 1) << (bits - 1 - bit) for bit in range(bits))
        sums_ref[at * share : (at + 1) * share, :] = shares_ref[source * share : (source + 1) * share, :]
    width, hidden_width = up_ref.shape
    taps, groups, inner = conv_ref.shape[:3]
    down_ref[...] = sums_ref[0:hidden_width, :].astype(f32) * scale
    for start in range(0, hidden_width, width):
        up_ref[:, start : start + width] = (
            sums_ref[hidden_width + start : hidden_width + start + width, :].astype(f32) * scale
        )
    for tap in range(taps):
        at = 2 * hidden_width + tap * inner
        rows = sums_ref[at : at + inner, :].astype(f32) * scale
        for group in range(groups):
            conv_ref[tap, group] = rows[:, group * inner : (group + 1) * inner]
    at = 2 * hidden_width + taps * inner
    gains = sums_ref[at : at + 16, :].astype(f32) * scale
    gain_one_ref[...] = gains[0:1, :]
    gain_two_ref[...] = gains[1:2, :]


def call(kernel, outs, args, scratch=(), smem=0, flops=0, limit=16, held=0, stored=0, after=(), same=None, **static):
    moved = sum(math.prod(a.shape) * a.dtype.itemsize for a in (*args, *outs))
    specs = [pl.BlockSpec(memory_space=pltpu.SMEM)] * smem
    specs += [pl.BlockSpec(memory_space=pltpu.VMEM)] * (len(args) - smem - held)
    specs += [pl.BlockSpec(memory_space=pltpu.HBM)] * held
    specs += [pl.BlockSpec(memory_space=pl.ANY)] * len(after)
    out_specs = [pl.BlockSpec(memory_space=pltpu.HBM)] * stored
    shapes = [pltpu.HBM(a.shape, a.dtype) for a in outs[:stored]] + list(outs[stored:])
    first_held = len(args) - held
    args = [*args[:first_held], *(pltpu.with_memory_space_constraint(a, pltpu.HBM) for a in args[first_held:])]
    out_specs += [pl.BlockSpec(memory_space=pltpu.VMEM)] * (len(outs) - stored)
    count = len(args)

    def run(*refs):
        kernel(*refs[:count], *refs[count + len(after) :], **static)

    return pl.pallas_call(
        run,
        out_shape=tuple(shapes),
        in_specs=specs,
        out_specs=tuple(out_specs),
        scratch_shapes=list(scratch),
        input_output_aliases=same or {},
        compiler_params=pltpu.CompilerParams(vmem_limit_bytes=limit * 1024 * 1024),
        cost_estimate=pl.CostEstimate(flops=int(flops), bytes_accessed=moved, transcendentals=0),
    )(*args, *after)


def shaped(*shape, dtype=bf16):
    return jax.ShapeDtypeStruct(shape, dtype)


def shifted(value, axis, steps):
    count = lax.axis_size(axis)
    initial, last = (max(0, -steps), min(count, count - steps))
    return lax.ppermute(value, axis, [(source, source + steps) for source in range(initial, last)])


def partner(value, axis, step):
    return lax.ppermute(value, axis, [(at, at ^ step) for at in range(lax.axis_size(axis))])


def bit_of(axis, step):
    return lax.rem(lax.div(lax.axis_index(axis), step), 2).astype(jnp.int32).reshape(1)


def steps_of(axis):
    return [1 << at for at in range(int(math.log2(lax.axis_size(axis))))]


def sum_over_mesh(keep, send, after):
    width = keep.shape[1]
    steps = steps_of("ty")
    for step, later in zip(steps, steps[1:] + [0]):
        came = partner(send, "ty", step)
        rows = keep.shape[0]
        if later:
            half = shaped(rows // 2, width)
            keep, send = call(
                add_split_kernel,
                [half, half],
                [bit_of("ty", later), keep, came],
                scratch=[pltpu.VMEM((rows, width), bf16)],
                smem=1,
                flops=1e6,
            )
        else:
            (share,) = call(add_kernel, [shaped(rows, width)], [keep, came], flops=1e6)
    steps = steps_of("tx")
    for step in steps:
        (share,) = call(
            add_kernel,
            [shaped(*share.shape)],
            [share, partner(share, "tx", step)],
            after=after if step == steps[-1] else (),
            flops=1e6,
        )
    return lax.all_gather(share, "ty", axis=0, tiled=True)


def exchange(rows, tiles):
    return lax.all_to_all(rows, ("tx", "ty"), split_axis=0, concat_axis=0, tiled=True)


def body(
    points,
    counts,
    owner,
    zorder,
    border,
    near,
    w_near,
    gain_one,
    conv_w,
    gain_two,
    w_up,
    w_down,
    grad_out,
):
    points_tile = points[0]
    tile_rows, width = points_tile.shape
    border_rows = border.shape[2]
    edge = 4 * border_rows
    ext = tile_rows + edge
    lists = border.reshape(1, edge)
    near_tile = near[0]
    neighbours = near_tile.shape[0]
    tiles = lax.axis_size("tx") * lax.axis_size("ty")
    slots_count = zorder.shape[1]
    capacity = slots_count // tiles
    taps, groups, inner = conv_w.shape[:3]
    conv_rows = conv_w.reshape(taps * groups * inner, inner)
    gain_one_row = gain_one.reshape(1, width)
    gain_two_row = gain_two.reshape(1, width)
    hidden = w_up.shape[1]

    slots, sent = call(
        route_kernel,
        [shaped(1, tile_rows, dtype=jnp.int32), shaped(edge, width)],
        [counts, owner, lists, points_tile],
        smem=1,
        flops=4e9,
        tiles=tiles,
        capacity=capacity,
    )
    halos = [
        shifted(sent[0:border_rows], "tx", -1),
        shifted(sent[border_rows : 2 * border_rows], "tx", 1),
        shifted(sent[2 * border_rows : 3 * border_rows], "ty", -1),
        shifted(sent[3 * border_rows :], "ty", 1),
    ]
    kept_table, table = call(
        count_kernel,
        [shaped(ext, tile_rows), shaped(ext, tile_rows)],
        [near_tile],
        scratch=[pltpu.SemaphoreType.DMA((ext // CHUNK,))],
        flops=8e9,
        stored=1,
    )
    average, pre_act, packed = call(
        lift_kernel,
        [
            shaped(width, tile_rows),
            shaped(tile_rows, width, dtype=f32),
            shaped(slots_count, 2 * width),
        ],
        [slots, points_tile, grad_out[0], *halos, table, w_near],
        scratch=[
            pltpu.VMEM((width, tile_rows), bf16),
            pltpu.VMEM((tile_rows, width), f32),
            pltpu.VMEM((tile_rows, 2 * width), bf16),
            pltpu.VMEM((slots_count, 2 * width), bf16),
            pltpu.SemaphoreType.DMA((2,)),
            pltpu.SemaphoreType.DMA((slots_count // WIDE,)),
        ],
        flops=4e9,
        stored=3,
        neighbours=neighbours,
    )
    came = exchange(packed, tiles)
    patch_scratch = [
        pltpu.VMEM((PATCH + 2 * PAD, width), f32),
        pltpu.VMEM((PATCH, width), f32),
        pltpu.VMEM((PATCH + 2 * PAD, width), f32),
    ]
    serial, state, back_result = call(
        forward_kernel,
        [
            shaped(slots_count, width),
            shaped(slots_count, width, dtype=f32),
            shaped(slots_count, width),
        ],
        [zorder, conv_rows, gain_one_row, gain_two_row, w_up, w_down, came],
        held=1,
        scratch=[
            pltpu.VMEM((slots_count, width), bf16),
            pltpu.VMEM((slots_count, width), bf16),
            pltpu.VMEM((slots_count, width), f32),
            pltpu.VMEM((taps * width, width), bf16),
            pltpu.VMEM((PATCH, width), bf16),
            *patch_scratch,
            pltpu.VMEM((PATCH, width), bf16),
            pltpu.VMEM((PATCH, hidden), bf16),
            pltpu.VMEM((slots_count, width), bf16),
            pltpu.VMEM((slots_count, width), bf16),
            pltpu.SemaphoreType.DMA((3, slots_count // PATCH)),
            pltpu.SemaphoreType.DMA((slots_count // WIDE,)),
        ],
        flops=10e9,
        limit=32,
        stored=3,
        groups=groups,
        inner=inner,
    )
    came_result = exchange(back_result, tiles)
    lines = lax.axis_size("ty")
    sums_rows = 2 * hidden + taps * inner + 16
    sums_rows = -(-sums_rows // (16 * lines)) * (16 * lines)
    back_grad, keep, send = call(
        backward_kernel,
        [
            shaped(slots_count, width),
            shaped(sums_rows // 2, width),
            shaped(sums_rows // 2, width),
        ],
        [
            bit_of("ty", 1),
            zorder,
            conv_rows,
            gain_one_row,
            gain_two_row,
            w_up,
            w_down,
            came,
            serial,
            state,
        ],
        held=3,
        scratch=[
            pltpu.VMEM((slots_count, width), bf16),
            pltpu.VMEM((slots_count, width), bf16),
            pltpu.VMEM((slots_count, width), f32),
            pltpu.VMEM((slots_count, width), bf16),
            pltpu.VMEM((slots_count, width), bf16),
            pltpu.VMEM((slots_count, width), bf16),
            pltpu.VMEM((sums_rows, width), bf16),
            pltpu.VMEM((taps * width, width), bf16),
            pltpu.VMEM((slots_count, width), bf16),
            pltpu.VMEM((slots_count, hidden), bf16),
            pltpu.VMEM((slots_count, hidden), bf16),
            pltpu.VMEM((PATCH, width), f32),
            pltpu.VMEM((PATCH + 2 * PAD, width), f32),
            pltpu.VMEM((PATCH, width), bf16),
            *patch_scratch,
            pltpu.VMEM((PATCH, width), bf16),
            pltpu.VMEM((taps, width, width), f32),
            pltpu.VMEM((16, width), f32),
            pltpu.SemaphoreType.DMA((5,)),
            pltpu.SemaphoreType.DMA((slots_count // WIDE,)),
        ],
        stored=3,
        smem=1,
        flops=40e9,
        limit=44,
        groups=groups,
        inner=inner,
    )
    (back_grad,) = call(
        hold_kernel,
        [shaped(slots_count, width)],
        [back_grad],
        after=[came_result],
        held=1,
        stored=1,
        same={0: 0},
    )
    came_back = exchange(back_grad, tiles)
    (out_rows,) = call(
        unpack_kernel, [shaped(tile_rows, width)], [slots, came_result], flops=4e9
    )
    row_grad, near_grad, halo_grad = call(
        tile_back_kernel,
        [shaped(tile_rows, width, dtype=f32), shaped(width, width), shaped(edge, width)],
        [slots, came_back, w_near, kept_table, average, pre_act],
        after=[out_rows],
        scratch=[
            pltpu.VMEM((tile_rows, width), f32),
            pltpu.VMEM((ext, tile_rows), bf16),
            pltpu.VMEM((width, tile_rows), bf16),
            pltpu.VMEM((tile_rows, width), f32),
            pltpu.VMEM((tile_rows, width), bf16),
            pltpu.VMEM((tile_rows, width), bf16),
            pltpu.SemaphoreType.DMA((3 + tile_rows // WIDE,)),
        ],
        flops=6e9,
        limit=24,
        held=3,
        stored=1,
        neighbours=neighbours,
    )
    totals = sum_over_mesh(keep, send, [near_grad])
    near_parts = exchange(near_grad, tiles).reshape(tiles, width // tiles, width)
    near_share = jnp.sum(near_parts.astype(f32), axis=0)
    near_all = jnp.broadcast_to(near_share.astype(bf16), (tiles, *near_share.shape))
    near_sum = exchange(near_all.reshape(width, width), tiles)
    returned = [
        shifted(halo_grad[0:border_rows], "tx", 1),
        shifted(halo_grad[border_rows : 2 * border_rows], "tx", -1),
        shifted(halo_grad[2 * border_rows : 3 * border_rows], "ty", 1),
        shifted(halo_grad[3 * border_rows :], "ty", -1),
    ]
    (grad_points,) = call(
        finish_kernel, [shaped(tile_rows, width)], [lists, row_grad, *returned], flops=1e9
    )
    scale = 1.0 / math.sqrt(tiles * tile_rows)
    up_sum, down_sum, conv_sum, gain_one_sum, gain_two_sum = call(
        spread_kernel,
        [
            shaped(width, hidden, dtype=f32),
            shaped(hidden, width, dtype=f32),
            shaped(*conv_w.shape, dtype=f32),
            shaped(1, width, dtype=f32),
            shaped(1, width, dtype=f32),
        ],
        [totals],
        scratch=[pltpu.VMEM((sums_rows, width), bf16)],
        flops=1e6,
        bits=len(steps_of("ty")),
        scale=scale,
    )
    return (
        out_rows[None],
        grad_points[None],
        near_sum.astype(f32) * scale,
        gain_one_sum[0],
        conv_sum,
        gain_two_sum[0],
        up_sum,
        down_sum,
    )


def solution(mesh):
    placed = (
        P(("tx", "ty"), None, None),
        P(("tx", "ty")),
        P(("tx", "ty"), None),
        P(("tx", "ty"), None),
        P(("tx", "ty"), None, None),
        P(("tx", "ty"), None, None),
        P(),
        P(),
        P(),
        P(),
        P(),
        P(),
        P(("tx", "ty"), None, None),
    )
    return jax.shard_map(
        body,
        mesh=mesh,
        in_specs=placed,
        out_specs=(
            P(("tx", "ty"), None, None),
            P(("tx", "ty"), None, None),
            P(),
            P(),
            P(),
            P(),
            P(),
            P(),
        ),
        check_vma=False,
    )
```

```python
import math

import jax
import jax.numpy as jnp
from jax import lax
from jax.experimental import pallas as pl
from jax.experimental.pallas import tpu as pltpu
from jax.sharding import PartitionSpec as P

PATCH = 1024
CHUNK = 256
WIDE = 512
BLOCK = 64
LANES = 128
PAD = 8

eps_norm = 1e-06
gelu_coef = 0.7978845608028654
cubic_coef = 0.044715

bf16 = jnp.bfloat16
f32 = jnp.float32
NN = (((1,), (0,)), ((), ()))
NT = (((1,), (1,)), ((), ()))
TN = (((0,), (0,)), ((), ()))


def dot(left, right, dims=NN):
    return lax.dot_general(left, right, dims, preferred_element_type=f32)


def iota(shape, axis):
    return lax.broadcasted_iota(jnp.int32, shape, axis)


def marks(mask):
    return jnp.where(mask, 1.0, 0.0).astype(bf16)


def gelu_parts(value):
    square = value * value
    tangent = jnp.tanh(value * (gelu_coef + (gelu_coef * cubic_coef) * square))
    return square, tangent


def gelu_tanh(value):
    _, tangent = gelu_parts(value)
    half = 0.5 * value
    return half + half * tangent


def slope_of(value, square, tangent):
    inner_slope = gelu_coef + (3.0 * gelu_coef * cubic_coef) * square
    return 0.5 * (1.0 + tangent) + (0.5 * value) * (1.0 - tangent * tangent) * inner_slope


def inverse_rms(value):
    return lax.rsqrt(jnp.mean(value * value, axis=-1, keepdims=True) + eps_norm)


def column_of(row, count):
    return jnp.transpose(jnp.broadcast_to(row, (LANES, count)))


def pick_rows(column, depth):
    count = column.shape[0]
    lane = iota((count, LANES), 1)
    return jnp.concatenate(
        [marks(column == lane + base) for base in range(0, depth, LANES)], axis=1
    )


def mark_slots(row, start, count):
    return marks(iota((count, row.shape[1]), 0) + start == row)


def route_kernel(
    counts_ref, owner_in, lists_in, points_in, slots_ref, sent0, sent1, sent2, sent3,
    owner_ref, lists_ref, points_ref, sems, *, tiles, capacity
):
    fetches = [
        pltpu.make_async_copy(source, target, sems.at[at])
        for at, (source, target) in enumerate(
            ((owner_in, owner_ref), (lists_in, lists_ref), (points_in, points_ref))
        )
    ]
    for fetch in fetches:
        fetch.start()
    for fetch in fetches:
        fetch.wait()
    rows = owner_ref.shape[1]
    live = iota((1, rows), 1) < counts_ref[0]
    owned = jnp.where(live, owner_ref[...], tiles)
    members = owned == iota((tiles, rows), 0)
    earlier = marks(iota((rows, rows), 0) < iota((rows, rows), 1))
    before = dot(marks(members), earlier)
    rank = jnp.sum(jnp.where(members, before, 0.0), axis=0, keepdims=True)
    slots_ref[...] = jnp.where(live, owned * capacity + rank.astype(jnp.int32), -1)
    for direction, sent_ref in enumerate((sent0, sent1, sent2, sent3)):
        sent_ref[...] = dot(chosen_rows(lists_ref, direction, rows), points_ref[...], TN).astype(bf16)


def chosen_rows(lists_ref, direction, rows):
    listed = lists_ref[direction : direction + 1, :]
    return marks(iota((rows, listed.shape[1]), 0) == listed)


def pack_rows(slots_ref, rows_ref, packed_out, stage_ref, sems):
    slots = slots_ref[...]
    copies = []
    for at, start in enumerate(range(0, packed_out.shape[0], WIDE)):
        place = pl.ds(start, WIDE)
        stage_ref[place, :] = dot(mark_slots(slots, start, WIDE), rows_ref[...]).astype(bf16)
        copies.append(pltpu.make_async_copy(stage_ref.at[place], packed_out.at[place], sems.at[at]))
        copies[-1].start()
    for copy in copies:
        copy.wait()


def unpack_kernel(slots_ref, packed_ref, rows_ref):
    for start in range(0, rows_ref.shape[0], CHUNK):
        column = column_of(slots_ref[:, start : start + CHUNK], CHUNK)
        rows_ref[pl.ds(start, CHUNK), :] = dot(
            pick_rows(column, packed_ref.shape[0]), packed_ref[...]
        ).astype(bf16)


def count_kernel(near_ref, kept_ref, table_ref, sems):
    neighbours, rows = near_ref.shape
    step = 16
    zero = jnp.zeros((step, LANES), bf16)
    one = jnp.ones((step, LANES), bf16)
    row_blocks = table_ref.shape[0] // CHUNK

    def copy_out(row_block):
        place = pl.ds(pl.multiple_of(row_block * CHUNK, CHUNK), CHUNK)
        return pltpu.make_async_copy(table_ref.at[place], kept_ref.at[place], sems.at[row_block])

    def rows_of(row_block, _):
        row_at = pl.multiple_of(row_block * CHUNK, CHUNK)

        def block(lane_block, _):
            lane_at = pl.multiple_of(lane_block * LANES, LANES)
            local = (near_ref[:, pl.ds(lane_at, LANES)] - row_at).astype(f32)
            spread = [
                jnp.broadcast_to(local[k : k + 1, :], (step, LANES)).astype(bf16)
                for k in range(neighbours)
            ]
            base = iota((step, LANES), 0).astype(f32)
            for inner in range(0, CHUNK, step):
                here = (base + float(inner)).astype(bf16)
                total = zero
                for k in range(neighbours):
                    total = total + jnp.where(spread[k] == here, one, zero)
                table_ref[pl.ds(row_at + inner, step), pl.ds(lane_at, LANES)] = total
            return 0

        lax.fori_loop(0, rows // LANES, block, 0)
        copy_out(row_block).start()
        return 0

    lax.fori_loop(0, row_blocks, rows_of, 0)
    for row_block in range(row_blocks):
        copy_out(row_block).wait()


def lift_kernel(
    slots_ref, points_ref, grad_ref, halo0, halo1, halo2, halo3, table_ref, w_ref,
    average_out, pre_out, packed_out,
    average_ref, pre_ref, both_ref, stage_ref, sems, pack_sems, *, neighbours
):
    width = points_ref.shape[1]
    ext = jnp.concatenate([points_ref[...], halo0[...], halo1[...], halo2[...], halo3[...]], axis=0)
    average = (dot(ext, table_ref[...], TN) * (1.0 / neighbours)).astype(bf16)
    average_ref[...] = average
    keep_average = pltpu.make_async_copy(average_ref, average_out, sems.at[0])
    keep_average.start()
    pre_ref[...] = dot(average, w_ref[...], TN)
    keep_pre = pltpu.make_async_copy(pre_ref, pre_out, sems.at[1])
    keep_pre.start()
    for row in range(0, points_ref.shape[0], BLOCK):
        here = pl.ds(row, BLOCK)
        both_ref[here, 0:width] = (
            points_ref[here, :].astype(f32) + gelu_tanh(pre_ref[here, :])
        ).astype(bf16)
    both_ref[:, width:] = grad_ref[...]
    pack_rows(slots_ref, both_ref, packed_out, stage_ref, pack_sems)
    keep_average.wait()
    keep_pre.wait()


def tile_back_kernel(
    slots_ref, back_ref, w_ref, table_in, average_in, pre_in,
    row_out, near_ref, halo0, halo1, halo2, halo3,
    row_ref, table_ref, average_ref, pre_ref, act_ref, spread_ref, sems, *, neighbours
):
    rows = row_ref.shape[0]
    fetch_pre = pltpu.make_async_copy(pre_in, pre_ref, sems.at[0])
    fetch_average = pltpu.make_async_copy(average_in, average_ref, sems.at[1])
    fetch_table = pltpu.make_async_copy(table_in, table_ref, sems.at[2])

    def keep_row(start):
        place = pl.ds(start, WIDE)
        return pltpu.make_async_copy(row_ref.at[place], row_out.at[place], sems.at[3 + start // WIDE])

    fetch_pre.start()
    fetch_average.start()
    fetch_table.start()
    fetch_pre.wait()
    for start in range(0, rows, CHUNK):
        column = column_of(slots_ref[:, start : start + CHUNK], CHUNK)
        wide = dot(pick_rows(column, back_ref.shape[0]), back_ref[...])
        for row in range(0, CHUNK, BLOCK):
            here = pl.ds(start + row, BLOCK)
            lifted_grad = wide[row : row + BLOCK]
            row_ref[here, :] = lifted_grad
            value = pre_ref[here, :]
            square, tangent = gelu_parts(value)
            act_ref[here, :] = (lifted_grad * slope_of(value, square, tangent)).astype(bf16)
    fetch_average.wait()
    near_ref[...] = dot(average_ref[...], act_ref[...]).astype(near_ref.dtype)
    spread_ref[...] = (dot(act_ref[...], w_ref[...], NT) * (1.0 / neighbours)).astype(bf16)
    fetch_table.wait()
    halo = dot(table_ref[rows:, :], spread_ref[...]).astype(bf16)
    size = halo0.shape[0]
    for direction, halo_ref in enumerate((halo0, halo1, halo2, halo3)):
        halo_ref[...] = halo[direction * size : (direction + 1) * size]
    for start in range(0, rows, WIDE):
        here = pl.ds(start, WIDE)
        row_ref[here, :] = row_ref[here, :] + dot(table_ref[here, :], spread_ref[...])
        keep_row(start).start()
    for start in range(0, rows, WIDE):
        keep_row(start).wait()


def finish_kernel(lists_ref, back0, back1, back2, back3, row_in, out_ref, row_ref, sems):
    fetch = pltpu.make_async_copy(row_in, row_ref, sems.at[0])
    fetch.start()
    rows = row_ref.shape[0]
    total = sum(
        dot(chosen_rows(lists_ref, direction, rows), came[...])
        for direction, came in enumerate((back0, back1, back2, back3))
    )
    fetch.wait()
    out_ref[...] = (row_ref[...] + total).astype(bf16)


def near_sum_kernel(parts_ref, share_ref, *, share):
    rows = parts_ref.shape[0]
    same = lax.rem(iota((rows, rows), 0), share) == lax.rem(iota((rows, rows), 1), share)
    share_ref[...] = dot(marks(same), parts_ref[...]).astype(bf16)


def full_taps(conv_ref, groups, inner):
    width = groups * inner
    rows = conv_ref.shape[0]
    repeat = marks(lax.rem(iota((inner, width), 1), inner) == iota((inner, width), 0))
    wide = dot(conv_ref[...], repeat)
    row_group = lax.div(lax.rem(iota((rows, width), 0), width), inner)
    same = row_group == lax.div(iota((rows, width), 1), inner)
    return jnp.where(same, wide, 0.0).astype(bf16)


def padded_zeros(ref):
    edge = jnp.zeros((PAD, ref.shape[1]), f32)
    ref[0:PAD, :] = edge
    ref[PAD + PATCH :, :] = edge


def forward_kernel(
    zorder_ref, conv_ref, gain_one_ref, gain_two_ref, up_ref, down_ref, came_in,
    serial_out, state_out, back_out,
    lifted_ref, serial_ref, state_ref, taps_ref, normed_ref, before_ref, here_ref, after_ref, second_ref, hidden_ref,
    result_ref, stage_ref, sems, pack_sems, *, groups, inner
):
    slots, width = lifted_ref.shape
    fetch = pltpu.make_async_copy(came_in.at[:, pl.ds(0, width)], lifted_ref, sems.at[2, 0])
    fetch.start()
    hidden_width = up_ref.shape[1]
    taps_ref[...] = full_taps(conv_ref, groups, inner)
    padded_zeros(before_ref)
    padded_zeros(after_ref)

    def keep(at):
        place = pl.ds(pl.multiple_of(at * PATCH, PATCH), PATCH)
        return (
            pltpu.make_async_copy(serial_ref.at[place], serial_out.at[place], sems.at[0, at]),
            pltpu.make_async_copy(state_ref.at[place], state_out.at[place], sems.at[1, at]),
        )

    def patch(at, _):
        origin = pl.multiple_of(at * PATCH, PATCH)
        for start in range(0, PATCH, WIDE):
            column = column_of(zorder_ref[:, pl.ds(origin + start, WIDE)], WIDE)
            wide = dot(pick_rows(column, slots), lifted_ref[...])
            for row in range(0, WIDE, BLOCK):
                serial = wide[row : row + BLOCK]
                serial_ref[pl.ds(origin + start + row, BLOCK), :] = serial.astype(bf16)
                normed = serial * inverse_rms(serial) * gain_one_ref[...]
                normed_ref[pl.ds(start + row, BLOCK), :] = normed.astype(bf16)
        before_ref[pl.ds(PAD, PATCH), :] = dot(normed_ref[...], taps_ref[0:width, :])
        here_ref[...] = dot(normed_ref[...], taps_ref[width : 2 * width, :])
        after_ref[pl.ds(PAD, PATCH), :] = dot(normed_ref[...], taps_ref[2 * width :, :])
        for row in range(0, PATCH, BLOCK):
            place = pl.ds(origin + row, BLOCK)
            state = serial_ref[place, :].astype(f32) + (
                before_ref[pl.ds(PAD + row - 1, BLOCK), :]
                + here_ref[pl.ds(row, BLOCK), :]
                + after_ref[pl.ds(PAD + row + 1, BLOCK), :]
            )
            state_ref[place, :] = state
            second = state * inverse_rms(state) * gain_two_ref[...]
            second_ref[pl.ds(row, BLOCK), :] = second.astype(bf16)
        for copy in keep(at):
            copy.start()
        for start in range(0, PATCH, CHUNK):
            value = dot(second_ref[pl.ds(start, CHUNK), :], up_ref[...])
            for row in range(0, CHUNK, 16):
                for col in range(0, hidden_width, 2 * LANES):
                    hidden_ref[pl.ds(start + row, 16), pl.ds(col, 2 * LANES)] = gelu_tanh(
                        value[row : row + 16, col : col + 2 * LANES]
                    ).astype(bf16)
        for start in range(0, PATCH, WIDE):
            place = pl.ds(origin + start, WIDE)
            result_ref[place, :] = (
                state_ref[place, :] + dot(hidden_ref[pl.ds(start, WIDE), :], down_ref[...])
            ).astype(bf16)
        return 0

    fetch.wait()
    lax.fori_loop(0, slots // PATCH, patch, 0)
    pack_rows(zorder_ref, result_ref, back_out, stage_ref, pack_sems)
    for at in range(slots // PATCH):
        for copy in keep(at):
            copy.wait()


def backward_kernel(
    bit_ref, zorder_ref, conv_ref, gain_one_ref, gain_two_ref, up_ref, down_ref, came_in, serial_in, state_in,
    back_out, keep_out, send_out,
    grad_ref, serial_ref, state_ref, out_grad_ref, serial_grad_ref, stage_ref, weights_ref, taps_ref,
    second_ref, hidden_ref, pre_grad_ref, state_grad_ref, mixed_ref, mixed_half_ref, before_ref, here_ref,
    after_ref, normed_ref, conv_sum_ref, gains_ref, sems, pack_sems, *, groups, inner
):
    slots, width = serial_ref.shape
    hidden_width = up_ref.shape[1]
    fetch_grad = pltpu.make_async_copy(came_in.at[:, pl.ds(width, width)], grad_ref, sems.at[0])
    fetch_state = pltpu.make_async_copy(state_in, state_ref, sems.at[1])
    fetch_serial = pltpu.make_async_copy(serial_in, serial_ref, sems.at[2])
    fetch_grad.start()
    fetch_state.start()
    fetch_serial.start()
    taps_ref[...] = full_taps(conv_ref, groups, inner)
    padded_zeros(before_ref)
    padded_zeros(after_ref)
    padded_zeros(mixed_ref)
    conv_sum_ref[...] = jnp.zeros_like(conv_sum_ref)
    gains_ref[...] = jnp.zeros_like(gains_ref)

    def patch(at, _):
        origin = pl.multiple_of(at * PATCH, PATCH)
        for start in range(0, PATCH, WIDE):
            column = column_of(zorder_ref[:, pl.ds(origin + start, WIDE)], WIDE)
            out_grad_ref[pl.ds(origin + start, WIDE), :] = dot(
                pick_rows(column, slots), grad_ref[...]
            ).astype(bf16)
        for start in range(0, PATCH, CHUNK):
            place = pl.ds(origin + start, CHUNK)
            for row in range(start, start + CHUNK, BLOCK):
                state = state_ref[pl.ds(origin + row, BLOCK), :]
                second = state * inverse_rms(state) * gain_two_ref[...]
                second_ref[pl.ds(origin + row, BLOCK), :] = second.astype(bf16)
            value_all = dot(second_ref[place, :], up_ref[...])
            hidden_grad_all = dot(out_grad_ref[place, :], down_ref[...], NT)
            for row in range(0, CHUNK, 16):
                for col in range(0, hidden_width, 2 * LANES):
                    value = value_all[row : row + 16, col : col + 2 * LANES]
                    hidden_grad = hidden_grad_all[row : row + 16, col : col + 2 * LANES]
                    square, tangent = gelu_parts(value)
                    half = 0.5 * value
                    piece = pl.ds(origin + start + row, 16), pl.ds(col, 2 * LANES)
                    hidden_ref[piece] = (half + half * tangent).astype(bf16)
                    pre_grad_ref[piece] = (
                        hidden_grad.astype(bf16).astype(f32) * slope_of(value, square, tangent)
                    ).astype(bf16)
            second_grad_all = dot(pre_grad_ref[place, :], up_ref[...], NT)
            for row in range(0, CHUNK, BLOCK):
                here = pl.ds(origin + start + row, BLOCK)
                state = state_ref[here, :]
                scale_two = inverse_rms(state)
                unit_two = state * scale_two
                second_grad = second_grad_all[row : row + BLOCK].astype(bf16).astype(f32)
                weighted = second_grad * gain_two_ref[...]
                product = second_grad * unit_two
                gains_ref[1:2, :] += jnp.sum(product, axis=0, keepdims=True)
                middle = jnp.mean(product * gain_two_ref[...], axis=-1, keepdims=True)
                state_grad = out_grad_ref[here, :].astype(f32) + scale_two * (weighted - unit_two * middle)
                state_grad_ref[pl.ds(start + row, BLOCK), :] = state_grad
                mixed_grad = state_grad.astype(bf16)
                mixed_half_ref[pl.ds(start + row, BLOCK), :] = mixed_grad
                mixed_ref[pl.ds(PAD + start + row, BLOCK), :] = mixed_grad.astype(f32)
        before_ref[pl.ds(PAD, PATCH), :] = dot(mixed_half_ref[...], taps_ref[0:width, :], NT)
        here_ref[...] = dot(mixed_half_ref[...], taps_ref[width : 2 * width, :], NT)
        after_ref[pl.ds(PAD, PATCH), :] = dot(mixed_half_ref[...], taps_ref[2 * width :, :], NT)
        for row in range(0, PATCH, BLOCK):
            place = pl.ds(origin + row, BLOCK)
            serial = serial_ref[place, :].astype(f32)
            scale_one = inverse_rms(serial)
            unit_one = serial * scale_one
            normed_ref[pl.ds(row, BLOCK), :] = (unit_one * gain_one_ref[...]).astype(bf16)
            normed_grad = (
                before_ref[pl.ds(PAD + row + 1, BLOCK), :]
                + here_ref[pl.ds(row, BLOCK), :]
                + after_ref[pl.ds(PAD + row - 1, BLOCK), :]
            ).astype(bf16).astype(f32)
            product = normed_grad * unit_one
            gains_ref[0:1, :] += jnp.sum(product, axis=0, keepdims=True)
            middle = jnp.mean(product * gain_one_ref[...], axis=-1, keepdims=True)
            weighted = normed_grad * gain_one_ref[...]
            serial_grad_ref[place, :] = (
                state_grad_ref[pl.ds(row, BLOCK), :] + scale_one * (weighted - unit_one * middle)
            ).astype(bf16)
        for tap in range(3):
            moved = mixed_ref[pl.ds(PAD + 1 - tap, PATCH), :].astype(bf16)
            conv_sum_ref[tap] += dot(normed_ref[...], moved, TN)
        return 0

    fetch_grad.wait()
    fetch_state.wait()
    fetch_serial.wait()
    lax.fori_loop(0, slots // PATCH, patch, 0)
    for start in range(0, hidden_width, width):
        block = slice(start, start + width)
        weights_ref[start : start + width, :] = jnp.transpose(
            dot(out_grad_ref[...], hidden_ref[:, block], TN)
        ).astype(bf16)
        weights_ref[hidden_width + start : hidden_width + start + width, :] = dot(
            second_ref[...], pre_grad_ref[:, block], TN
        ).astype(bf16)
    same = lax.div(iota((width, width), 0), inner) == lax.div(iota((width, width), 1), inner)
    for tap in range(3):
        kept = jnp.where(same, conv_sum_ref[tap], 0.0).reshape(groups, inner, width)
        at = 2 * hidden_width + tap * inner
        weights_ref[at : at + inner, :] = jnp.sum(kept, axis=0).astype(bf16)
    at = 2 * hidden_width + 3 * inner
    weights_ref[at : at + 16, :] = gains_ref[...].astype(bf16)
    at = at + 16
    weights_ref[at:, :] = jnp.zeros((weights_ref.shape[0] - at, width), bf16)
    half = keep_out.shape[0]
    bit = bit_ref[0]
    hand_out = [
        pltpu.make_async_copy(
            weights_ref.at[pl.ds(pl.multiple_of(at * half, 16), half)], out, sems.at[3 + which]
        )
        for which, (at, out) in enumerate(((bit, keep_out), (1 - bit, send_out)))
    ]
    for copy in hand_out:
        copy.start()
    pack_rows(zorder_ref, serial_grad_ref, back_out, stage_ref, pack_sems)
    for copy in hand_out:
        copy.wait()


def hold_kernel(rows_in, rows_out):
    pass


def split_rows(bit, rows, scratch_ref, keep_ref, send_ref):
    scratch_ref[...] = rows.astype(bf16)
    half = keep_ref.shape[0]
    keep_ref[...] = scratch_ref[pl.ds(pl.multiple_of(bit * half, 16), half), :]
    send_ref[...] = scratch_ref[pl.ds(pl.multiple_of((1 - bit) * half, 16), half), :]


def added(mine_ref, came_ref):
    return mine_ref[...].astype(f32) + came_ref[...].astype(f32)


def first_split_kernel(
    bit0_ref, bit1_ref, mine_ref, came_ref, keep0, send0, keep1, send1, scratch0, scratch1
):
    half = scratch0.shape[0]
    total = added(mine_ref, came_ref)
    split_rows(bit0_ref[0], total[:half], scratch0, keep0, send0)
    split_rows(bit1_ref[0], total[half:], scratch1, keep1, send1)


def next_split_kernel(
    bit0_ref, bit1_ref, mine0, came0, mine1, came1, keep0, send0, keep1, send1, scratch0, scratch1
):
    split_rows(bit0_ref[0], added(mine0, came0), scratch0, keep0, send0)
    split_rows(bit1_ref[0], added(mine1, came1), scratch1, keep1, send1)


def add_join_kernel(mine0, came0, mine1, came1, share_ref):
    half = mine0.shape[0]
    share_ref[0:half, :] = added(mine0, came0).astype(bf16)
    share_ref[half:, :] = added(mine1, came1).astype(bf16)


def add_kernel(mine_ref, came_ref, total_ref):
    total_ref[...] = added(mine_ref, came_ref).astype(bf16)


def join_kernel(bit_ref, mine_ref, came_ref, both_ref):
    half = mine_ref.shape[0]
    bit = bit_ref[0]
    both_ref[pl.ds(pl.multiple_of(bit * half, 16), half), :] = mine_ref[...]
    both_ref[pl.ds(pl.multiple_of((1 - bit) * half, 16), half), :] = came_ref[...]


def spread_kernel(
    bit_ref, mine_ref, came_ref, up_ref, down_ref, conv_ref, gain_one_ref, gain_two_ref,
    joined_ref, sums_ref, *, bits, scale
):
    join_kernel(bit_ref, mine_ref, came_ref, joined_ref)
    rows = sums_ref.shape[0]
    piece = (rows >> bits) // 2
    for at in range(1 << bits):
        digits = [(at >> (bits - 1 - bit)) & 1 for bit in range(bits)]
        for part, order in enumerate((digits[1:], digits[:0:-1])):
            place = 0
            for digit in order:
                place = 2 * place + digit
            start = digits[0] * (rows // 2) + part * (rows // 4) + place * piece
            source = (2 * at + part) * piece
            sums_ref[start : start + piece, :] = joined_ref[source : source + piece, :]
    width, hidden_width = up_ref.shape
    taps, groups, inner = conv_ref.shape[:3]
    down_ref[...] = sums_ref[0:hidden_width, :].astype(f32) * scale
    for start in range(0, hidden_width, width):
        up_ref[:, start : start + width] = (
            sums_ref[hidden_width + start : hidden_width + start + width, :].astype(f32) * scale
        )
    for tap in range(taps):
        at = 2 * hidden_width + tap * inner
        rows = sums_ref[at : at + inner, :].astype(f32) * scale
        for group in range(groups):
            conv_ref[tap, group] = rows[:, group * inner : (group + 1) * inner]
    at = 2 * hidden_width + taps * inner
    gains = sums_ref[at : at + 16, :].astype(f32) * scale
    gain_one_ref[...] = gains[0:1, :]
    gain_two_ref[...] = gains[1:2, :]


def call(kernel, outs, args, scratch=(), smem=0, flops=0, limit=16, held=0, stored=0, after=(), same=None, **static):
    moved = sum(math.prod(a.shape) * a.dtype.itemsize for a in (*args, *outs))
    specs = [pl.BlockSpec(memory_space=pltpu.SMEM)] * smem
    specs += [pl.BlockSpec(memory_space=pltpu.VMEM)] * (len(args) - smem - held)
    specs += [pl.BlockSpec(memory_space=pltpu.HBM)] * held
    specs += [pl.BlockSpec(memory_space=pl.ANY)] * len(after)
    out_specs = [pl.BlockSpec(memory_space=pltpu.HBM)] * stored
    shapes = [pltpu.HBM(a.shape, a.dtype) for a in outs[:stored]] + list(outs[stored:])
    first_held = len(args) - held
    args = [*args[:first_held], *(pltpu.with_memory_space_constraint(a, pltpu.HBM) for a in args[first_held:])]
    out_specs += [pl.BlockSpec(memory_space=pltpu.VMEM)] * (len(outs) - stored)
    count = len(args)

    def run(*refs):
        kernel(*refs[:count], *refs[count + len(after) :], **static)

    return pl.pallas_call(
        run,
        out_shape=tuple(shapes),
        in_specs=specs,
        out_specs=tuple(out_specs),
        scratch_shapes=list(scratch),
        input_output_aliases=same or {},
        compiler_params=pltpu.CompilerParams(vmem_limit_bytes=limit * 1024 * 1024),
        cost_estimate=pl.CostEstimate(flops=int(flops), bytes_accessed=moved, transcendentals=0),
    )(*args, *after)


def shaped(*shape, dtype=bf16):
    return jax.ShapeDtypeStruct(shape, dtype)


def shifted(value, axis, steps):
    count = lax.axis_size(axis)
    initial, last = (max(0, -steps), min(count, count - steps))
    return lax.ppermute(value, axis, [(source, source + steps) for source in range(initial, last)])


def partner(value, axis, step):
    return lax.ppermute(value, axis, [(at, at ^ step) for at in range(lax.axis_size(axis))])


def bit_of(axis, step):
    return lax.rem(lax.div(lax.axis_index(axis), step), 2).astype(jnp.int32).reshape(1)


def steps_of(axis):
    return [1 << at for at in range(int(math.log2(lax.axis_size(axis))))]


def sum_over_mesh(keep, send, early, late, returned):
    width = keep.shape[1]
    steps = steps_of("ty")
    orders = steps[1:], steps[:0:-1]

    def halves(kernel, rows, at, args, **options):
        return call(
            kernel,
            [shaped(rows // 2, width)] * 4,
            [bit_of("ty", order[at]) for order in orders] + list(args),
            scratch=[pltpu.VMEM((rows, width), bf16)] * 2,
            smem=2,
            flops=1e6,
            **options,
        )

    came = partner(send, "ty", steps[0])
    rows = keep.shape[0] // 2
    parts = halves(first_split_kernel, rows, 0, [keep, came], after=early)
    for at in range(len(orders[0])):
        rows = rows // 2
        pairs = []
        for which, order in enumerate(orders):
            pairs += [parts[2 * which], partner(parts[2 * which + 1], "ty", order[at])]
        if at + 1 < len(orders[0]):
            parts = halves(next_split_kernel, rows, at + 1, pairs)
    (share,) = call(add_join_kernel, [shaped(2 * rows, width)], pairs, flops=1e6)
    for step in steps_of("tx"):
        (share,) = call(
            add_kernel,
            [shaped(*share.shape)],
            [share, partner(share, "tx", step)],
            after=late if step == steps_of("tx")[-1] else (),
            flops=1e6,
        )
    for at, step in enumerate(steps[:0:-1]):
        (share,) = call(
            join_kernel,
            [shaped(2 * share.shape[0], width)],
            [bit_of("ty", step), share, partner(share, "ty", step)],
            after=returned[2 * at : 2 * at + 2],
            smem=1,
            flops=1e6,
        )
    return share, partner(share, "ty", steps[0])


def exchange(rows, tiles):
    return lax.all_to_all(rows, ("tx", "ty"), split_axis=0, concat_axis=0, tiled=True)


def body(
    points,
    counts,
    owner,
    zorder,
    border,
    near,
    w_near,
    gain_one,
    conv_w,
    gain_two,
    w_up,
    w_down,
    grad_out,
):
    points_tile = points[0]
    tile_rows, width = points_tile.shape
    border_rows = border.shape[2]
    edge = 4 * border_rows
    ext = tile_rows + edge
    lists = border[0]
    near_tile = near[0]
    neighbours = near_tile.shape[0]
    tiles = lax.axis_size("tx") * lax.axis_size("ty")
    slots_count = zorder.shape[1]
    capacity = slots_count // tiles
    taps, groups, inner = conv_w.shape[:3]
    conv_rows = conv_w.reshape(taps * groups * inner, inner)
    gain_one_row = gain_one.reshape(1, width)
    gain_two_row = gain_two.reshape(1, width)
    hidden = w_up.shape[1]

    slots, *sent = call(
        route_kernel,
        [shaped(1, tile_rows, dtype=jnp.int32)] + [shaped(border_rows, width)] * 4,
        [counts, owner, lists, points_tile],
        scratch=[
            pltpu.VMEM((1, tile_rows), jnp.int32),
            pltpu.VMEM((4, border_rows), jnp.int32),
            pltpu.VMEM((tile_rows, width), bf16),
            pltpu.SemaphoreType.DMA((3,)),
        ],
        smem=1,
        held=3,
        flops=4e9,
        tiles=tiles,
        capacity=capacity,
    )
    halos = [
        shifted(sent[0], "tx", -1),
        shifted(sent[1], "tx", 1),
        shifted(sent[2], "ty", -1),
        shifted(sent[3], "ty", 1),
    ]
    kept_table, table = call(
        count_kernel,
        [shaped(ext, tile_rows), shaped(ext, tile_rows)],
        [near_tile],
        scratch=[pltpu.SemaphoreType.DMA((ext // CHUNK,))],
        flops=8e9,
        stored=1,
    )
    average, pre_act, packed = call(
        lift_kernel,
        [
            shaped(width, tile_rows),
            shaped(tile_rows, width, dtype=f32),
            shaped(slots_count, 2 * width),
        ],
        [slots, points_tile, grad_out[0], *halos, table, w_near],
        scratch=[
            pltpu.VMEM((width, tile_rows), bf16),
            pltpu.VMEM((tile_rows, width), f32),
            pltpu.VMEM((tile_rows, 2 * width), bf16),
            pltpu.VMEM((slots_count, 2 * width), bf16),
            pltpu.SemaphoreType.DMA((2,)),
            pltpu.SemaphoreType.DMA((slots_count // WIDE,)),
        ],
        flops=4e9,
        stored=3,
        neighbours=neighbours,
    )
    came = exchange(packed, tiles)
    patch_scratch = [
        pltpu.VMEM((PATCH + 2 * PAD, width), f32),
        pltpu.VMEM((PATCH, width), f32),
        pltpu.VMEM((PATCH + 2 * PAD, width), f32),
    ]
    serial, state, back_result = call(
        forward_kernel,
        [
            shaped(slots_count, width),
            shaped(slots_count, width, dtype=f32),
            shaped(slots_count, width),
        ],
        [zorder, conv_rows, gain_one_row, gain_two_row, w_up, w_down, came],
        held=1,
        scratch=[
            pltpu.VMEM((slots_count, width), bf16),
            pltpu.VMEM((slots_count, width), bf16),
            pltpu.VMEM((slots_count, width), f32),
            pltpu.VMEM((taps * width, width), bf16),
            pltpu.VMEM((PATCH, width), bf16),
            *patch_scratch,
            pltpu.VMEM((PATCH, width), bf16),
            pltpu.VMEM((PATCH, hidden), bf16),
            pltpu.VMEM((slots_count, width), bf16),
            pltpu.VMEM((slots_count, width), bf16),
            pltpu.SemaphoreType.DMA((3, slots_count // PATCH)),
            pltpu.SemaphoreType.DMA((slots_count // WIDE,)),
        ],
        flops=10e9,
        limit=32,
        stored=3,
        groups=groups,
        inner=inner,
    )
    came_result = exchange(back_result, tiles)
    lines = lax.axis_size("ty")
    sums_rows = 2 * hidden + taps * inner + 16
    sums_rows = -(-sums_rows // (32 * lines)) * (32 * lines)
    back_grad, keep, send = call(
        backward_kernel,
        [
            shaped(slots_count, width),
            shaped(sums_rows // 2, width),
            shaped(sums_rows // 2, width),
        ],
        [
            bit_of("ty", 1),
            zorder,
            conv_rows,
            gain_one_row,
            gain_two_row,
            w_up,
            w_down,
            came,
            serial,
            state,
        ],
        held=3,
        scratch=[
            pltpu.VMEM((slots_count, width), bf16),
            pltpu.VMEM((slots_count, width), bf16),
            pltpu.VMEM((slots_count, width), f32),
            pltpu.VMEM((slots_count, width), bf16),
            pltpu.VMEM((slots_count, width), bf16),
            pltpu.VMEM((slots_count, width), bf16),
            pltpu.VMEM((sums_rows, width), bf16),
            pltpu.VMEM((taps * width, width), bf16),
            pltpu.VMEM((slots_count, width), bf16),
            pltpu.VMEM((slots_count, hidden), bf16),
            pltpu.VMEM((slots_count, hidden), bf16),
            pltpu.VMEM((PATCH, width), f32),
            pltpu.VMEM((PATCH + 2 * PAD, width), f32),
            pltpu.VMEM((PATCH, width), bf16),
            *patch_scratch,
            pltpu.VMEM((PATCH, width), bf16),
            pltpu.VMEM((taps, width, width), f32),
            pltpu.VMEM((16, width), f32),
            pltpu.SemaphoreType.DMA((5,)),
            pltpu.SemaphoreType.DMA((slots_count // WIDE,)),
        ],
        stored=3,
        smem=1,
        flops=40e9,
        limit=44,
        groups=groups,
        inner=inner,
    )
    (back_grad,) = call(
        hold_kernel,
        [shaped(slots_count, width)],
        [back_grad],
        after=[came_result],
        held=1,
        stored=1,
        same={0: 0},
    )
    came_back = exchange(back_grad, tiles)
    (out_rows,) = call(
        unpack_kernel, [shaped(tile_rows, width)], [slots, came_result], flops=4e9
    )
    row_grad, near_grad, *halo_grad = call(
        tile_back_kernel,
        [shaped(tile_rows, width, dtype=f32), shaped(width, width)]
        + [shaped(border_rows, width)] * 4,
        [slots, came_back, w_near, kept_table, average, pre_act],
        after=[out_rows],
        scratch=[
            pltpu.VMEM((tile_rows, width), f32),
            pltpu.VMEM((ext, tile_rows), bf16),
            pltpu.VMEM((width, tile_rows), bf16),
            pltpu.VMEM((tile_rows, width), f32),
            pltpu.VMEM((tile_rows, width), bf16),
            pltpu.VMEM((tile_rows, width), bf16),
            pltpu.SemaphoreType.DMA((3 + tile_rows // WIDE,)),
        ],
        flops=6e9,
        limit=24,
        held=3,
        stored=1,
        neighbours=neighbours,
    )
    returned = [
        shifted(halo_grad[0], "tx", 1),
        shifted(halo_grad[1], "tx", -1),
        shifted(halo_grad[2], "ty", 1),
        shifted(halo_grad[3], "ty", -1),
    ]
    totals = sum_over_mesh(keep, send, [out_rows], [near_grad], returned)
    (near_share,) = call(
        near_sum_kernel,
        [shaped(width, width)],
        [exchange(near_grad, tiles)],
        after=returned,
        flops=1e6,
        share=width // tiles,
    )
    near_sum = exchange(near_share, tiles)
    (grad_points,) = call(
        finish_kernel,
        [shaped(tile_rows, width)],
        [lists, *returned, row_grad],
        scratch=[pltpu.VMEM((tile_rows, width), f32), pltpu.SemaphoreType.DMA((1,))],
        held=1,
        flops=1e9,
    )
    scale = 1.0 / math.sqrt(tiles * tile_rows)
    up_sum, down_sum, conv_sum, gain_one_sum, gain_two_sum = call(
        spread_kernel,
        [
            shaped(width, hidden, dtype=f32),
            shaped(hidden, width, dtype=f32),
            shaped(*conv_w.shape, dtype=f32),
            shaped(1, width, dtype=f32),
            shaped(1, width, dtype=f32),
        ],
        [bit_of("ty", 1), *totals],
        scratch=[pltpu.VMEM((sums_rows, width), bf16)] * 2,
        smem=1,
        flops=1e6,
        bits=len(steps_of("ty")),
        scale=scale,
    )
    return (
        out_rows[None],
        grad_points[None],
        near_sum.astype(f32) * scale,
        gain_one_sum[0],
        conv_sum,
        gain_two_sum[0],
        up_sum,
        down_sum,
    )


def solution(mesh):
    placed = (
        P(("tx", "ty"), None, None),
        P(("tx", "ty")),
        P(("tx", "ty"), None),
        P(("tx", "ty"), None),
        P(("tx", "ty"), None, None),
        P(("tx", "ty"), None, None),
        P(),
        P(),
        P(),
        P(),
        P(),
        P(),
        P(("tx", "ty"), None, None),
    )
    return jax.shard_map(
        body,
        mesh=mesh,
        in_specs=placed,
        out_specs=(
            P(("tx", "ty"), None, None),
            P(("tx", "ty"), None, None),
            P(),
            P(),
            P(),
            P(),
            P(),
            P(),
        ),
        check_vma=False,
    )
```

```python
import math

import jax
import jax.numpy as jnp
from jax import lax
from jax.experimental import pallas as pl
from jax.experimental.pallas import tpu as pltpu
from jax.sharding import PartitionSpec as P

PATCH = 1024
CHUNK = 256
WIDE = 512
BLOCK = 64
LANES = 128
PAD = 8

eps_norm = 1e-06
gelu_coef = 0.7978845608028654
cubic_coef = 0.044715

bf16 = jnp.bfloat16
f32 = jnp.float32
NN = (((1,), (0,)), ((), ()))
NT = (((1,), (1,)), ((), ()))
TN = (((0,), (0,)), ((), ()))


def dot(left, right, dims=NN):
    return lax.dot_general(left, right, dims, preferred_element_type=f32)


def iota(shape, axis):
    return lax.broadcasted_iota(jnp.int32, shape, axis)


def marks(mask):
    return jnp.where(mask, 1.0, 0.0).astype(bf16)


def gelu_parts(value):
    square = value * value
    tangent = jnp.tanh(value * (gelu_coef + (gelu_coef * cubic_coef) * square))
    return square, tangent


def gelu_tanh(value):
    _, tangent = gelu_parts(value)
    half = 0.5 * value
    return half + half * tangent


def slope_of(value, square, tangent):
    inner_slope = gelu_coef + (3.0 * gelu_coef * cubic_coef) * square
    return 0.5 * (1.0 + tangent) + (0.5 * value) * (1.0 - tangent * tangent) * inner_slope


def inverse_rms(value):
    return lax.rsqrt(jnp.mean(value * value, axis=-1, keepdims=True) + eps_norm)


def column_of(row, count):
    return jnp.transpose(jnp.broadcast_to(row, (LANES, count)))


def parts_of(value):
    high = lax.shift_right_arithmetic(value, 8)
    return high.astype(f32), (value - high * 256).astype(f32)


def pick_rows(column, depth):
    count = column.shape[0]
    zero = jnp.zeros((count, LANES), bf16)
    one = jnp.ones((count, LANES), bf16)
    high, low = (part.astype(bf16) for part in parts_of(column))
    lane = iota((count, LANES), 1).astype(f32)
    halves = [jnp.where(low == (lane + float(at)).astype(bf16), one, zero) for at in (0, LANES)]
    pieces = []
    for block in range(depth // 256):
        here = high == jnp.full((count, LANES), block, bf16)
        pieces += [jnp.where(here, half, zero) for half in halves]
    return jnp.concatenate(pieces, axis=1)


def mark_low(row):
    count = row.shape[1]
    high, low = parts_of(row)
    high = jnp.broadcast_to(high, (16, count)).astype(bf16)
    low = jnp.broadcast_to(low, (16, count)).astype(bf16)
    zero = jnp.zeros((16, count), bf16)
    one = jnp.ones((16, count), bf16)
    index = iota((16, count), 0).astype(f32)
    return high, jnp.concatenate(
        [jnp.where(low == (index + float(at)).astype(bf16), one, zero) for at in range(0, 256, 16)], axis=0
    )


def mark_block(high, low_ref, block):
    count = low_ref.shape[1]
    zero = jnp.zeros((16, count), bf16)
    here = high == jnp.full((16, count), block, bf16)
    return jnp.concatenate(
        [jnp.where(here, low_ref[pl.ds(at, 16), :], zero) for at in range(0, 256, 16)], axis=0
    )


def route_kernel(
    counts_ref, owner_in, lists_in, points_in, slots_ref, sent0, sent1, sent2, sent3,
    owner_ref, lists_ref, points_ref, sems, *, tiles, capacity
):
    fetches = [
        pltpu.make_async_copy(source, target, sems.at[at])
        for at, (source, target) in enumerate(
            ((owner_in, owner_ref), (lists_in, lists_ref), (points_in, points_ref))
        )
    ]
    for fetch in fetches:
        fetch.start()
    for fetch in fetches:
        fetch.wait()
    rows = owner_ref.shape[1]
    live = iota((1, rows), 1) < counts_ref[0]
    owned = jnp.where(live, owner_ref[...], tiles)
    members = owned == iota((tiles, rows), 0)
    earlier = marks(iota((rows, rows), 0) < iota((rows, rows), 1))
    before = dot(marks(members), earlier)
    rank = jnp.sum(jnp.where(members, before, 0.0), axis=0, keepdims=True)
    slots_ref[...] = jnp.where(live, owned * capacity + rank.astype(jnp.int32), -1)
    for direction, sent_ref in enumerate((sent0, sent1, sent2, sent3)):
        sent_ref[...] = dot(chosen_rows(lists_ref, direction, rows), points_ref[...], TN).astype(bf16)


def chosen_rows(lists_ref, direction, rows):
    listed = lists_ref[direction : direction + 1, :]
    return marks(iota((rows, listed.shape[1]), 0) == listed)


def pack_rows(slots_ref, rows_ref, packed_out, stage_ref, low_ref, sems):
    high, low_ref[...] = mark_low(slots_ref[...])
    copies = []
    for at, start in enumerate(range(0, packed_out.shape[0], WIDE)):
        marked = [mark_block(high, low_ref, block) for block in range(start // 256, (start + WIDE) // 256)]
        place = pl.ds(start, WIDE)
        stage_ref[place, :] = dot(jnp.concatenate(marked, axis=0), rows_ref[...]).astype(bf16)
        copies.append(pltpu.make_async_copy(stage_ref.at[place], packed_out.at[place], sems.at[at]))
        copies[-1].start()
    for copy in copies:
        copy.wait()


def unpack_kernel(slots_ref, packed_ref, rows_ref):
    for start in range(0, rows_ref.shape[0], CHUNK):
        column = column_of(slots_ref[:, start : start + CHUNK], CHUNK)
        rows_ref[pl.ds(start, CHUNK), :] = dot(
            pick_rows(column, packed_ref.shape[0]), packed_ref[...]
        ).astype(bf16)


def count_kernel(near_ref, kept_ref, table_ref, sems):
    neighbours, rows = near_ref.shape
    step = 16
    zero = jnp.zeros((step, LANES), bf16)
    one = jnp.ones((step, LANES), bf16)
    row_blocks = table_ref.shape[0] // CHUNK

    def copy_out(row_block):
        place = pl.ds(pl.multiple_of(row_block * CHUNK, CHUNK), CHUNK)
        return pltpu.make_async_copy(table_ref.at[place], kept_ref.at[place], sems.at[row_block])

    def rows_of(row_block, _):
        row_at = pl.multiple_of(row_block * CHUNK, CHUNK)

        def block(lane_block, _):
            lane_at = pl.multiple_of(lane_block * LANES, LANES)
            local = (near_ref[:, pl.ds(lane_at, LANES)] - row_at).astype(f32)
            spread = [
                jnp.broadcast_to(local[k : k + 1, :], (step, LANES)).astype(bf16)
                for k in range(neighbours)
            ]
            base = iota((step, LANES), 0).astype(f32)
            for inner in range(0, CHUNK, step):
                here = (base + float(inner)).astype(bf16)
                total = zero
                for k in range(neighbours):
                    total = total + jnp.where(spread[k] == here, one, zero)
                table_ref[pl.ds(row_at + inner, step), pl.ds(lane_at, LANES)] = total
            return 0

        lax.fori_loop(0, rows // LANES, block, 0)
        copy_out(row_block).start()
        return 0

    lax.fori_loop(0, row_blocks, rows_of, 0)
    for row_block in range(row_blocks):
        copy_out(row_block).wait()


def lift_kernel(
    slots_ref, points_ref, grad_ref, halo0, halo1, halo2, halo3, table_ref, w_ref,
    average_out, pre_out, packed_out,
    average_ref, pre_ref, both_ref, stage_ref, low_ref, sems, pack_sems, *, neighbours
):
    width = points_ref.shape[1]
    ext = jnp.concatenate([points_ref[...], halo0[...], halo1[...], halo2[...], halo3[...]], axis=0)
    average = (dot(ext, table_ref[...], TN) * (1.0 / neighbours)).astype(bf16)
    average_ref[...] = average
    keep_average = pltpu.make_async_copy(average_ref, average_out, sems.at[0])
    keep_average.start()
    pre_ref[...] = dot(average, w_ref[...], TN)
    keep_pre = pltpu.make_async_copy(pre_ref, pre_out, sems.at[1])
    keep_pre.start()
    for row in range(0, points_ref.shape[0], BLOCK):
        here = pl.ds(row, BLOCK)
        both_ref[here, 0:width] = (
            points_ref[here, :].astype(f32) + gelu_tanh(pre_ref[here, :])
        ).astype(bf16)
    both_ref[:, width:] = grad_ref[...]
    pack_rows(slots_ref, both_ref, packed_out, stage_ref, low_ref, pack_sems)
    keep_average.wait()
    keep_pre.wait()


def tile_back_kernel(
    slots_ref, back_ref, w_ref, table_in, average_in, pre_in,
    row_out, near_ref, halo0, halo1, halo2, halo3,
    row_ref, table_ref, average_ref, pre_ref, act_ref, spread_ref, sems, *, neighbours
):
    rows = row_ref.shape[0]
    fetch_pre = pltpu.make_async_copy(pre_in, pre_ref, sems.at[0])
    fetch_average = pltpu.make_async_copy(average_in, average_ref, sems.at[1])
    fetch_table = pltpu.make_async_copy(table_in, table_ref, sems.at[2])

    def keep_row(start):
        place = pl.ds(start, WIDE)
        return pltpu.make_async_copy(row_ref.at[place], row_out.at[place], sems.at[3 + start // WIDE])

    fetch_pre.start()
    fetch_average.start()
    fetch_table.start()
    fetch_pre.wait()
    for start in range(0, rows, CHUNK):
        column = column_of(slots_ref[:, start : start + CHUNK], CHUNK)
        wide = dot(pick_rows(column, back_ref.shape[0]), back_ref[...])
        for row in range(0, CHUNK, BLOCK):
            here = pl.ds(start + row, BLOCK)
            lifted_grad = wide[row : row + BLOCK]
            row_ref[here, :] = lifted_grad
            value = pre_ref[here, :]
            square, tangent = gelu_parts(value)
            act_ref[here, :] = (lifted_grad * slope_of(value, square, tangent)).astype(bf16)
    fetch_average.wait()
    near_ref[...] = dot(average_ref[...], act_ref[...]).astype(near_ref.dtype)
    spread_ref[...] = (dot(act_ref[...], w_ref[...], NT) * (1.0 / neighbours)).astype(bf16)
    fetch_table.wait()
    halo = dot(table_ref[rows:, :], spread_ref[...]).astype(bf16)
    size = halo0.shape[0]
    for direction, halo_ref in enumerate((halo0, halo1, halo2, halo3)):
        halo_ref[...] = halo[direction * size : (direction + 1) * size]
    for start in range(0, rows, WIDE):
        here = pl.ds(start, WIDE)
        row_ref[here, :] = row_ref[here, :] + dot(table_ref[here, :], spread_ref[...])
        keep_row(start).start()
    for start in range(0, rows, WIDE):
        keep_row(start).wait()


def finish_kernel(lists_ref, back0, back1, back2, back3, row_in, out_ref, row_ref, sems):
    fetch = pltpu.make_async_copy(row_in, row_ref, sems.at[0])
    fetch.start()
    rows = row_ref.shape[0]
    total = sum(
        dot(chosen_rows(lists_ref, direction, rows), came[...])
        for direction, came in enumerate((back0, back1, back2, back3))
    )
    fetch.wait()
    out_ref[...] = (row_ref[...] + total).astype(bf16)


def full_taps(conv_ref, groups, inner):
    width = groups * inner
    rows = conv_ref.shape[0]
    repeat = marks(lax.rem(iota((inner, width), 1), inner) == iota((inner, width), 0))
    wide = dot(conv_ref[...], repeat)
    row_group = lax.div(lax.rem(iota((rows, width), 0), width), inner)
    same = row_group == lax.div(iota((rows, width), 1), inner)
    return jnp.where(same, wide, 0.0).astype(bf16)


def padded_zeros(ref):
    edge = jnp.zeros((PAD, ref.shape[1]), f32)
    ref[0:PAD, :] = edge
    ref[PAD + PATCH :, :] = edge


def forward_kernel(
    zorder_ref, conv_ref, gain_one_ref, gain_two_ref, up_ref, down_ref, came_in,
    serial_out, state_out, back_out,
    lifted_ref, serial_ref, state_ref, taps_ref, normed_ref, before_ref, here_ref, after_ref, second_ref, hidden_ref,
    result_ref, stage_ref, low_ref, sems, pack_sems, *, groups, inner
):
    slots, width = lifted_ref.shape
    fetch = pltpu.make_async_copy(came_in.at[:, pl.ds(0, width)], lifted_ref, sems.at[2, 0])
    fetch.start()
    hidden_width = up_ref.shape[1]
    taps_ref[...] = full_taps(conv_ref, groups, inner)
    padded_zeros(before_ref)
    padded_zeros(after_ref)

    def keep(at):
        place = pl.ds(pl.multiple_of(at * PATCH, PATCH), PATCH)
        return (
            pltpu.make_async_copy(serial_ref.at[place], serial_out.at[place], sems.at[0, at]),
            pltpu.make_async_copy(state_ref.at[place], state_out.at[place], sems.at[1, at]),
        )

    def patch(at, _):
        origin = pl.multiple_of(at * PATCH, PATCH)
        for start in range(0, PATCH, WIDE):
            column = column_of(zorder_ref[:, pl.ds(origin + start, WIDE)], WIDE)
            wide = dot(pick_rows(column, slots), lifted_ref[...])
            for row in range(0, WIDE, BLOCK):
                serial = wide[row : row + BLOCK]
                serial_ref[pl.ds(origin + start + row, BLOCK), :] = serial.astype(bf16)
                normed = serial * inverse_rms(serial) * gain_one_ref[...]
                normed_ref[pl.ds(start + row, BLOCK), :] = normed.astype(bf16)
        before_ref[pl.ds(PAD, PATCH), :] = dot(normed_ref[...], taps_ref[0:width, :])
        here_ref[...] = dot(normed_ref[...], taps_ref[width : 2 * width, :])
        after_ref[pl.ds(PAD, PATCH), :] = dot(normed_ref[...], taps_ref[2 * width :, :])
        for row in range(0, PATCH, BLOCK):
            place = pl.ds(origin + row, BLOCK)
            state = serial_ref[place, :].astype(f32) + (
                before_ref[pl.ds(PAD + row - 1, BLOCK), :]
                + here_ref[pl.ds(row, BLOCK), :]
                + after_ref[pl.ds(PAD + row + 1, BLOCK), :]
            )
            state_ref[place, :] = state
            second = state * inverse_rms(state) * gain_two_ref[...]
            second_ref[pl.ds(row, BLOCK), :] = second.astype(bf16)
        for copy in keep(at):
            copy.start()
        for start in range(0, PATCH, CHUNK):
            value = dot(second_ref[pl.ds(start, CHUNK), :], up_ref[...])
            for row in range(0, CHUNK, 16):
                for col in range(0, hidden_width, 2 * LANES):
                    hidden_ref[pl.ds(start + row, 16), pl.ds(col, 2 * LANES)] = gelu_tanh(
                        value[row : row + 16, col : col + 2 * LANES]
                    ).astype(bf16)
        for start in range(0, PATCH, WIDE):
            place = pl.ds(origin + start, WIDE)
            result_ref[place, :] = (
                state_ref[place, :] + dot(hidden_ref[pl.ds(start, WIDE), :], down_ref[...])
            ).astype(bf16)
        return 0

    fetch.wait()
    lax.fori_loop(0, slots // PATCH, patch, 0)
    pack_rows(zorder_ref, result_ref, back_out, stage_ref, low_ref, pack_sems)
    for at in range(slots // PATCH):
        for copy in keep(at):
            copy.wait()


def backward_kernel(
    bit_ref, zorder_ref, conv_ref, gain_one_ref, gain_two_ref, up_ref, down_ref, came_in, serial_in, state_in,
    back_out, keep_out, send_out,
    grad_ref, serial_ref, state_ref, out_grad_ref, serial_grad_ref, stage_ref, weights_ref, taps_ref,
    second_ref, hidden_ref, pre_grad_ref, state_grad_ref, mixed_ref, mixed_half_ref, before_ref, here_ref,
    after_ref, normed_ref, conv_sum_ref, gains_ref, low_ref, sems, pack_sems, *, groups, inner
):
    slots, width = serial_ref.shape
    hidden_width = up_ref.shape[1]
    fetch_grad = pltpu.make_async_copy(came_in.at[:, pl.ds(width, width)], grad_ref, sems.at[0])
    fetch_state = pltpu.make_async_copy(state_in, state_ref, sems.at[1])
    fetch_serial = pltpu.make_async_copy(serial_in, serial_ref, sems.at[2])
    fetch_grad.start()
    fetch_state.start()
    fetch_serial.start()
    taps_ref[...] = full_taps(conv_ref, groups, inner)
    padded_zeros(before_ref)
    padded_zeros(after_ref)
    padded_zeros(mixed_ref)
    conv_sum_ref[...] = jnp.zeros_like(conv_sum_ref)
    gains_ref[...] = jnp.zeros_like(gains_ref)

    def patch(at, _):
        origin = pl.multiple_of(at * PATCH, PATCH)
        for start in range(0, PATCH, WIDE):
            column = column_of(zorder_ref[:, pl.ds(origin + start, WIDE)], WIDE)
            out_grad_ref[pl.ds(origin + start, WIDE), :] = dot(
                pick_rows(column, slots), grad_ref[...]
            ).astype(bf16)
        for start in range(0, PATCH, CHUNK):
            place = pl.ds(origin + start, CHUNK)
            for row in range(start, start + CHUNK, BLOCK):
                state = state_ref[pl.ds(origin + row, BLOCK), :]
                second = state * inverse_rms(state) * gain_two_ref[...]
                second_ref[pl.ds(origin + row, BLOCK), :] = second.astype(bf16)
            value_all = dot(second_ref[place, :], up_ref[...])
            hidden_grad_all = dot(out_grad_ref[place, :], down_ref[...], NT)
            for row in range(0, CHUNK, 16):
                for col in range(0, hidden_width, 2 * LANES):
                    value = value_all[row : row + 16, col : col + 2 * LANES]
                    hidden_grad = hidden_grad_all[row : row + 16, col : col + 2 * LANES]
                    square, tangent = gelu_parts(value)
                    half = 0.5 * value
                    piece = pl.ds(origin + start + row, 16), pl.ds(col, 2 * LANES)
                    hidden_ref[piece] = (half + half * tangent).astype(bf16)
                    pre_grad_ref[piece] = (
                        hidden_grad.astype(bf16).astype(f32) * slope_of(value, square, tangent)
                    ).astype(bf16)
            second_grad_all = dot(pre_grad_ref[place, :], up_ref[...], NT)
            for row in range(0, CHUNK, BLOCK):
                here = pl.ds(origin + start + row, BLOCK)
                state = state_ref[here, :]
                scale_two = inverse_rms(state)
                unit_two = state * scale_two
                second_grad = second_grad_all[row : row + BLOCK].astype(bf16).astype(f32)
                weighted = second_grad * gain_two_ref[...]
                product = second_grad * unit_two
                gains_ref[1:2, :] += jnp.sum(product, axis=0, keepdims=True)
                middle = jnp.mean(product * gain_two_ref[...], axis=-1, keepdims=True)
                state_grad = out_grad_ref[here, :].astype(f32) + scale_two * (weighted - unit_two * middle)
                state_grad_ref[pl.ds(start + row, BLOCK), :] = state_grad
                mixed_grad = state_grad.astype(bf16)
                mixed_half_ref[pl.ds(start + row, BLOCK), :] = mixed_grad
                mixed_ref[pl.ds(PAD + start + row, BLOCK), :] = mixed_grad.astype(f32)
        before_ref[pl.ds(PAD, PATCH), :] = dot(mixed_half_ref[...], taps_ref[0:width, :], NT)
        here_ref[...] = dot(mixed_half_ref[...], taps_ref[width : 2 * width, :], NT)
        after_ref[pl.ds(PAD, PATCH), :] = dot(mixed_half_ref[...], taps_ref[2 * width :, :], NT)
        for row in range(0, PATCH, BLOCK):
            place = pl.ds(origin + row, BLOCK)
            serial = serial_ref[place, :].astype(f32)
            scale_one = inverse_rms(serial)
            unit_one = serial * scale_one
            normed_ref[pl.ds(row, BLOCK), :] = (unit_one * gain_one_ref[...]).astype(bf16)
            normed_grad = (
                before_ref[pl.ds(PAD + row + 1, BLOCK), :]
                + here_ref[pl.ds(row, BLOCK), :]
                + after_ref[pl.ds(PAD + row - 1, BLOCK), :]
            ).astype(bf16).astype(f32)
            product = normed_grad * unit_one
            gains_ref[0:1, :] += jnp.sum(product, axis=0, keepdims=True)
            middle = jnp.mean(product * gain_one_ref[...], axis=-1, keepdims=True)
            weighted = normed_grad * gain_one_ref[...]
            serial_grad_ref[place, :] = (
                state_grad_ref[pl.ds(row, BLOCK), :] + scale_one * (weighted - unit_one * middle)
            ).astype(bf16)
        for tap in range(3):
            moved = mixed_ref[pl.ds(PAD + 1 - tap, PATCH), :].astype(bf16)
            conv_sum_ref[tap] += dot(normed_ref[...], moved, TN)
        return 0

    fetch_grad.wait()
    fetch_state.wait()
    fetch_serial.wait()
    lax.fori_loop(0, slots // PATCH, patch, 0)
    for start in range(0, hidden_width, width):
        block = slice(start, start + width)
        weights_ref[start : start + width, :] = jnp.transpose(
            dot(out_grad_ref[...], hidden_ref[:, block], TN)
        ).astype(bf16)
        weights_ref[hidden_width + start : hidden_width + start + width, :] = dot(
            second_ref[...], pre_grad_ref[:, block], TN
        ).astype(bf16)
    same = lax.div(iota((width, width), 0), inner) == lax.div(iota((width, width), 1), inner)
    for tap in range(3):
        kept = jnp.where(same, conv_sum_ref[tap], 0.0).reshape(groups, inner, width)
        at = 2 * hidden_width + tap * inner
        weights_ref[at : at + inner, :] = jnp.sum(kept, axis=0).astype(bf16)
    at = 2 * hidden_width + 3 * inner
    weights_ref[at : at + 16, :] = gains_ref[...].astype(bf16)
    at = at + 16
    weights_ref[at:, :] = jnp.zeros((weights_ref.shape[0] - at, width), bf16)
    half = keep_out.shape[0]
    bit = bit_ref[0]
    hand_out = [
        pltpu.make_async_copy(
            weights_ref.at[pl.ds(pl.multiple_of(at * half, 16), half)], out, sems.at[3 + which]
        )
        for which, (at, out) in enumerate(((bit, keep_out), (1 - bit, send_out)))
    ]
    for copy in hand_out:
        copy.start()
    pack_rows(zorder_ref, serial_grad_ref, back_out, stage_ref, low_ref, pack_sems)
    for copy in hand_out:
        copy.wait()


def hold_kernel(rows_in, rows_out):
    pass


def split_rows(bit, rows, scratch_ref, keep_ref, send_ref):
    scratch_ref[...] = rows.astype(bf16)
    half = keep_ref.shape[0]
    keep_ref[...] = scratch_ref[pl.ds(pl.multiple_of(bit * half, 16), half), :]
    send_ref[...] = scratch_ref[pl.ds(pl.multiple_of((1 - bit) * half, 16), half), :]


def added(mine_ref, came_ref):
    return mine_ref[...].astype(f32) + came_ref[...].astype(f32)


def first_split_kernel(
    bit0_ref, bit1_ref, mine_ref, came_ref, keep0, send0, keep1, send1, scratch0, scratch1
):
    half = scratch0.shape[0]
    total = added(mine_ref, came_ref)
    split_rows(bit0_ref[0], total[:half], scratch0, keep0, send0)
    split_rows(bit1_ref[0], total[half:], scratch1, keep1, send1)


def next_split_kernel(
    bit0_ref, bit1_ref, mine0, came0, mine1, came1, keep0, send0, keep1, send1, scratch0, scratch1
):
    split_rows(bit0_ref[0], added(mine0, came0), scratch0, keep0, send0)
    split_rows(bit1_ref[0], added(mine1, came1), scratch1, keep1, send1)


def add_join_kernel(mine0, came0, mine1, came1, near_ref, share_ref):
    half = mine0.shape[0]
    share_ref[0:half, :] = added(mine0, came0).astype(bf16)
    share_ref[half : 2 * half, :] = added(mine1, came1).astype(bf16)
    lines, rows, width = near_ref.shape
    total = near_ref[0].astype(f32)
    for line in range(1, lines):
        total = total + near_ref[line].astype(f32)
    spare = share_ref.shape[0] - 2 * half - rows
    if spare:
        total = jnp.concatenate([total, jnp.zeros((spare, width), f32)], axis=0)
    share_ref[2 * half :, :] = total.astype(bf16)


def add_kernel(mine_ref, came_ref, total_ref):
    total_ref[...] = added(mine_ref, came_ref).astype(bf16)


def join_kernel(bit_ref, mine_ref, came_ref, both_ref):
    half = mine_ref.shape[0]
    bit = bit_ref[0]
    both_ref[pl.ds(pl.multiple_of(bit * half, 16), half), :] = mine_ref[...]
    both_ref[pl.ds(pl.multiple_of((1 - bit) * half, 16), half), :] = came_ref[...]


def spread_kernel(
    bit_ref, mine_ref, came_ref, up_ref, down_ref, conv_ref, gain_one_ref, gain_two_ref, near_ref,
    joined_ref, sums_ref, *, bits, scale
):
    join_kernel(bit_ref, mine_ref, came_ref, joined_ref)
    rows = sums_ref.shape[0]
    piece = (rows >> bits) // 2
    share = joined_ref.shape[0] >> bits
    near_rows = near_ref.shape[0] >> bits
    for at in range(1 << bits):
        digits = [(at >> (bits - 1 - bit)) & 1 for bit in range(bits)]
        for part, order in enumerate((digits[1:], digits[:0:-1])):
            place = 0
            for digit in order:
                place = 2 * place + digit
            start = digits[0] * (rows // 2) + part * (rows // 4) + place * piece
            source = at * share + part * piece
            sums_ref[start : start + piece, :] = joined_ref[source : source + piece, :]
        line = sum(digit << bit for bit, digit in enumerate(digits))
        source = at * share + 2 * piece
        part = joined_ref[source : source + share - 2 * piece, :].astype(f32) * scale
        near_ref[line * near_rows : (line + 1) * near_rows, :] = part[:near_rows]
    width, hidden_width = up_ref.shape
    taps, groups, inner = conv_ref.shape[:3]
    down_ref[...] = sums_ref[0:hidden_width, :].astype(f32) * scale
    for start in range(0, hidden_width, width):
        up_ref[:, start : start + width] = (
            sums_ref[hidden_width + start : hidden_width + start + width, :].astype(f32) * scale
        )
    for tap in range(taps):
        at = 2 * hidden_width + tap * inner
        rows = sums_ref[at : at + inner, :].astype(f32) * scale
        for group in range(groups):
            conv_ref[tap, group] = rows[:, group * inner : (group + 1) * inner]
    at = 2 * hidden_width + taps * inner
    gains = sums_ref[at : at + 16, :].astype(f32) * scale
    gain_one_ref[...] = gains[0:1, :]
    gain_two_ref[...] = gains[1:2, :]


def call(kernel, outs, args, scratch=(), smem=0, flops=0, limit=16, held=0, stored=0, after=(), same=None, **static):
    moved = sum(math.prod(a.shape) * a.dtype.itemsize for a in (*args, *outs))
    specs = [pl.BlockSpec(memory_space=pltpu.SMEM)] * smem
    specs += [pl.BlockSpec(memory_space=pltpu.VMEM)] * (len(args) - smem - held)
    specs += [pl.BlockSpec(memory_space=pltpu.HBM)] * held
    specs += [pl.BlockSpec(memory_space=pltpu.HBM if a.shape[0] >= PATCH else pl.ANY) for a in after]
    after = [pltpu.with_memory_space_constraint(a, pltpu.HBM) if a.shape[0] >= PATCH else a for a in after]
    out_specs = [pl.BlockSpec(memory_space=pltpu.HBM)] * stored
    shapes = [pltpu.HBM(a.shape, a.dtype) for a in outs[:stored]] + list(outs[stored:])
    first_held = len(args) - held
    args = [*args[:first_held], *(pltpu.with_memory_space_constraint(a, pltpu.HBM) for a in args[first_held:])]
    out_specs += [pl.BlockSpec(memory_space=pltpu.VMEM)] * (len(outs) - stored)
    count = len(args)

    def run(*refs):
        kernel(*refs[:count], *refs[count + len(after) :], **static)

    return pl.pallas_call(
        run,
        out_shape=tuple(shapes),
        in_specs=specs,
        out_specs=tuple(out_specs),
        scratch_shapes=list(scratch),
        input_output_aliases=same or {},
        compiler_params=pltpu.CompilerParams(vmem_limit_bytes=limit * 1024 * 1024),
        cost_estimate=pl.CostEstimate(flops=int(flops), bytes_accessed=moved, transcendentals=0),
    )(*args, *after)


def shaped(*shape, dtype=bf16):
    return jax.ShapeDtypeStruct(shape, dtype)


def shifted(value, axis, steps):
    count = lax.axis_size(axis)
    initial, last = (max(0, -steps), min(count, count - steps))
    return lax.ppermute(value, axis, [(source, source + steps) for source in range(initial, last)])


def partner(value, axis, step):
    return lax.ppermute(value, axis, [(at, at ^ step) for at in range(lax.axis_size(axis))])


def bit_of(axis, step):
    return lax.rem(lax.div(lax.axis_index(axis), step), 2).astype(jnp.int32).reshape(1)


def steps_of(axis):
    return [1 << at for at in range(int(math.log2(lax.axis_size(axis))))]


def scatter_sums(keep, send, early):
    width = keep.shape[1]
    steps = steps_of("ty")
    orders = steps[1:], steps[:0:-1]

    def halves(kernel, rows, at, args, **options):
        return call(
            kernel,
            [shaped(rows // 2, width)] * 4,
            [bit_of("ty", order[at]) for order in orders] + list(args),
            scratch=[pltpu.VMEM((rows, width), bf16)] * 2,
            smem=2,
            flops=1e6,
            **options,
        )

    came = partner(send, "ty", steps[0])
    rows = keep.shape[0] // 2
    parts = halves(first_split_kernel, rows, 0, [keep, came], after=early)
    for at in range(len(orders[0])):
        rows = rows // 2
        pairs = []
        for which, order in enumerate(orders):
            pairs += [parts[2 * which], partner(parts[2 * which + 1], "ty", order[at])]
        if at + 1 < len(orders[0]):
            parts = halves(next_split_kernel, rows, at + 1, pairs)
    return pairs


def gather_sums(pairs, near_parts, late):
    rows, width = pairs[0].shape
    steps = steps_of("ty")
    near_rows = -(-near_parts.shape[1] // 16) * 16
    (share,) = call(
        add_join_kernel,
        [shaped(2 * rows + near_rows, width)],
        [*pairs, near_parts],
        after=late[0],
        flops=1e6,
    )
    for at, step in enumerate(steps_of("tx")):
        (share,) = call(
            add_kernel,
            [shaped(*share.shape)],
            [share, partner(share, "tx", step)],
            after=late[1 + at],
            flops=1e6,
        )
    for step in steps[:0:-1]:
        (share,) = call(
            join_kernel,
            [shaped(2 * share.shape[0], width)],
            [bit_of("ty", step), share, partner(share, "ty", step)],
            smem=1,
            flops=1e6,
        )
    return share, partner(share, "ty", steps[0])


def exchange(rows, tiles):
    return lax.all_to_all(rows, ("tx", "ty"), split_axis=0, concat_axis=0, tiled=True)


def body(
    points,
    counts,
    owner,
    zorder,
    border,
    near,
    w_near,
    gain_one,
    conv_w,
    gain_two,
    w_up,
    w_down,
    grad_out,
):
    points_tile = points[0]
    tile_rows, width = points_tile.shape
    border_rows = border.shape[2]
    edge = 4 * border_rows
    ext = tile_rows + edge
    lists = border[0]
    near_tile = near[0]
    neighbours = near_tile.shape[0]
    tiles = lax.axis_size("tx") * lax.axis_size("ty")
    slots_count = zorder.shape[1]
    capacity = slots_count // tiles
    taps, groups, inner = conv_w.shape[:3]
    conv_rows = conv_w.reshape(taps * groups * inner, inner)
    gain_one_row = gain_one.reshape(1, width)
    gain_two_row = gain_two.reshape(1, width)
    hidden = w_up.shape[1]

    slots, *sent = call(
        route_kernel,
        [shaped(1, tile_rows, dtype=jnp.int32)] + [shaped(border_rows, width)] * 4,
        [counts, owner, lists, points_tile],
        scratch=[
            pltpu.VMEM((1, tile_rows), jnp.int32),
            pltpu.VMEM((4, border_rows), jnp.int32),
            pltpu.VMEM((tile_rows, width), bf16),
            pltpu.SemaphoreType.DMA((3,)),
        ],
        smem=1,
        held=3,
        flops=4e9,
        tiles=tiles,
        capacity=capacity,
    )
    halos = [
        shifted(sent[0], "tx", -1),
        shifted(sent[1], "tx", 1),
        shifted(sent[2], "ty", -1),
        shifted(sent[3], "ty", 1),
    ]
    kept_table, table = call(
        count_kernel,
        [shaped(ext, tile_rows), shaped(ext, tile_rows)],
        [near_tile],
        scratch=[pltpu.SemaphoreType.DMA((ext // CHUNK,))],
        flops=8e9,
        stored=1,
    )
    average, pre_act, packed = call(
        lift_kernel,
        [
            shaped(width, tile_rows),
            shaped(tile_rows, width, dtype=f32),
            shaped(slots_count, 2 * width),
        ],
        [slots, points_tile, grad_out[0], *halos, table, w_near],
        scratch=[
            pltpu.VMEM((width, tile_rows), bf16),
            pltpu.VMEM((tile_rows, width), f32),
            pltpu.VMEM((tile_rows, 2 * width), bf16),
            pltpu.VMEM((slots_count, 2 * width), bf16),
            pltpu.VMEM((256, tile_rows), bf16),
            pltpu.SemaphoreType.DMA((2,)),
            pltpu.SemaphoreType.DMA((slots_count // WIDE,)),
        ],
        flops=4e9,
        stored=3,
        neighbours=neighbours,
    )
    came = exchange(packed, tiles)
    patch_scratch = [
        pltpu.VMEM((PATCH + 2 * PAD, width), f32),
        pltpu.VMEM((PATCH, width), f32),
        pltpu.VMEM((PATCH + 2 * PAD, width), f32),
    ]
    serial, state, back_result = call(
        forward_kernel,
        [
            shaped(slots_count, width),
            shaped(slots_count, width, dtype=f32),
            shaped(slots_count, width),
        ],
        [zorder, conv_rows, gain_one_row, gain_two_row, w_up, w_down, came],
        held=1,
        scratch=[
            pltpu.VMEM((slots_count, width), bf16),
            pltpu.VMEM((slots_count, width), bf16),
            pltpu.VMEM((slots_count, width), f32),
            pltpu.VMEM((taps * width, width), bf16),
            pltpu.VMEM((PATCH, width), bf16),
            *patch_scratch,
            pltpu.VMEM((PATCH, width), bf16),
            pltpu.VMEM((PATCH, hidden), bf16),
            pltpu.VMEM((slots_count, width), bf16),
            pltpu.VMEM((slots_count, width), bf16),
            pltpu.VMEM((256, slots_count), bf16),
            pltpu.SemaphoreType.DMA((3, slots_count // PATCH)),
            pltpu.SemaphoreType.DMA((slots_count // WIDE,)),
        ],
        flops=10e9,
        limit=32,
        stored=3,
        groups=groups,
        inner=inner,
    )
    came_result = exchange(back_result, tiles)
    lines = lax.axis_size("ty")
    sums_rows = 2 * hidden + taps * inner + 16
    sums_rows = -(-sums_rows // (32 * lines)) * (32 * lines)
    back_grad, keep, send = call(
        backward_kernel,
        [
            shaped(slots_count, width),
            shaped(sums_rows // 2, width),
            shaped(sums_rows // 2, width),
        ],
        [
            bit_of("ty", 1),
            zorder,
            conv_rows,
            gain_one_row,
            gain_two_row,
            w_up,
            w_down,
            came,
            serial,
            state,
        ],
        held=3,
        scratch=[
            pltpu.VMEM((slots_count, width), bf16),
            pltpu.VMEM((slots_count, width), bf16),
            pltpu.VMEM((slots_count, width), f32),
            pltpu.VMEM((slots_count, width), bf16),
            pltpu.VMEM((slots_count, width), bf16),
            pltpu.VMEM((slots_count, width), bf16),
            pltpu.VMEM((sums_rows, width), bf16),
            pltpu.VMEM((taps * width, width), bf16),
            pltpu.VMEM((slots_count, width), bf16),
            pltpu.VMEM((slots_count, hidden), bf16),
            pltpu.VMEM((slots_count, hidden), bf16),
            pltpu.VMEM((PATCH, width), f32),
            pltpu.VMEM((PATCH + 2 * PAD, width), f32),
            pltpu.VMEM((PATCH, width), bf16),
            *patch_scratch,
            pltpu.VMEM((PATCH, width), bf16),
            pltpu.VMEM((taps, width, width), f32),
            pltpu.VMEM((16, width), f32),
            pltpu.VMEM((256, slots_count), bf16),
            pltpu.SemaphoreType.DMA((5,)),
            pltpu.SemaphoreType.DMA((slots_count // WIDE,)),
        ],
        stored=3,
        smem=1,
        flops=40e9,
        limit=44,
        groups=groups,
        inner=inner,
    )
    (back_grad,) = call(
        hold_kernel,
        [shaped(slots_count, width)],
        [back_grad],
        after=[came_result.reshape(tiles, capacity, width)],
        held=1,
        stored=1,
        same={0: 0},
    )
    came_back = exchange(back_grad, tiles)
    (out_rows,) = call(
        unpack_kernel, [shaped(tile_rows, width)], [slots, came_result], flops=4e9
    )
    pairs = scatter_sums(keep, send, [out_rows])
    row_grad, near_grad, *halo_grad = call(
        tile_back_kernel,
        [shaped(tile_rows, width, dtype=f32), shaped(width, width)]
        + [shaped(border_rows, width)] * 4,
        [slots, came_back, w_near, kept_table, average, pre_act],
        after=pairs[1::2],
        scratch=[
            pltpu.VMEM((tile_rows, width), f32),
            pltpu.VMEM((ext, tile_rows), bf16),
            pltpu.VMEM((width, tile_rows), bf16),
            pltpu.VMEM((tile_rows, width), f32),
            pltpu.VMEM((tile_rows, width), bf16),
            pltpu.VMEM((tile_rows, width), bf16),
            pltpu.SemaphoreType.DMA((3 + tile_rows // WIDE,)),
        ],
        flops=6e9,
        limit=24,
        held=3,
        stored=1,
        neighbours=neighbours,
    )
    returned = [
        shifted(halo_grad[0], "tx", 1),
        shifted(halo_grad[1], "tx", -1),
        shifted(halo_grad[2], "ty", 1),
        shifted(halo_grad[3], "ty", -1),
    ]
    (grad_points,) = call(
        finish_kernel,
        [shaped(tile_rows, width)],
        [lists, *returned, row_grad],
        scratch=[pltpu.VMEM((tile_rows, width), f32), pltpu.SemaphoreType.DMA((1,))],
        held=1,
        flops=1e9,
    )
    near_parts = lax.all_to_all(
        near_grad.reshape(lines, width // lines, width), "ty", split_axis=0, concat_axis=0, tiled=True
    )
    totals = gather_sums(pairs, near_parts, [returned[:2], returned[2:], [grad_points]])
    scale = 1.0 / math.sqrt(tiles * tile_rows)
    up_sum, down_sum, conv_sum, gain_one_sum, gain_two_sum, near_sum = call(
        spread_kernel,
        [
            shaped(width, hidden, dtype=f32),
            shaped(hidden, width, dtype=f32),
            shaped(*conv_w.shape, dtype=f32),
            shaped(1, width, dtype=f32),
            shaped(1, width, dtype=f32),
            shaped(width, width, dtype=f32),
        ],
        [bit_of("ty", 1), *totals],
        scratch=[
            pltpu.VMEM((2 * totals[0].shape[0], width), bf16),
            pltpu.VMEM((sums_rows, width), bf16),
        ],
        smem=1,
        flops=1e6,
        bits=len(steps_of("ty")),
        scale=scale,
    )
    return (
        out_rows[None],
        grad_points[None],
        near_sum,
        gain_one_sum[0],
        conv_sum,
        gain_two_sum[0],
        up_sum,
        down_sum,
    )


def solution(mesh):
    placed = (
        P(("tx", "ty"), None, None),
        P(("tx", "ty")),
        P(("tx", "ty"), None),
        P(("tx", "ty"), None),
        P(("tx", "ty"), None, None),
        P(("tx", "ty"), None, None),
        P(),
        P(),
        P(),
        P(),
        P(),
        P(),
        P(("tx", "ty"), None, None),
    )
    return jax.shard_map(
        body,
        mesh=mesh,
        in_specs=placed,
        out_specs=(
            P(("tx", "ty"), None, None),
            P(("tx", "ty"), None, None),
            P(),
            P(),
            P(),
            P(),
            P(),
            P(),
        ),
        check_vma=False,
    )
```

```python
import math

import jax
import jax.numpy as jnp
from jax import lax
from jax.experimental import pallas as pl
from jax.experimental.pallas import tpu as pltpu
from jax.sharding import PartitionSpec as P

PATCH = 1024
CHUNK = 256
WIDE = 512
BLOCK = 64
LANES = 128
PAD = 8

eps_norm = 1e-06
gelu_coef = 0.7978845608028654
cubic_coef = 0.044715

bf16 = jnp.bfloat16
f32 = jnp.float32
NN = (((1,), (0,)), ((), ()))
NT = (((1,), (1,)), ((), ()))
TN = (((0,), (0,)), ((), ()))


def dot(left, right, dims=NN):
    return lax.dot_general(left, right, dims, preferred_element_type=f32)


def iota(shape, axis):
    return lax.broadcasted_iota(jnp.int32, shape, axis)


def marks(mask):
    return jnp.where(mask, 1.0, 0.0).astype(bf16)


def gelu_parts(value):
    square = value * value
    tangent = jnp.tanh(value * (gelu_coef + (gelu_coef * cubic_coef) * square))
    return square, tangent


def gelu_tanh(value):
    _, tangent = gelu_parts(value)
    half = 0.5 * value
    return half + half * tangent


def slope_of(value, square, tangent):
    inner_slope = gelu_coef + (3.0 * gelu_coef * cubic_coef) * square
    return 0.5 * (1.0 + tangent) + (0.5 * value) * (1.0 - tangent * tangent) * inner_slope


def inverse_rms(value):
    return lax.rsqrt(jnp.mean(value * value, axis=-1, keepdims=True) + eps_norm)


def column_of(row, count):
    return jnp.transpose(jnp.broadcast_to(row, (LANES, count)))


def pick_rows(column, depth):
    count = column.shape[0]
    lane = iota((count, LANES), 1)
    return jnp.concatenate(
        [marks(column == lane + base) for base in range(0, depth, LANES)], axis=1
    )


def mark_slots(row, start, count):
    return marks(iota((count, row.shape[1]), 0) + start == row)


def route_kernel(
    counts_ref, owner_in, lists_in, points_in, slots_ref, sent0, sent1, sent2, sent3,
    owner_ref, lists_ref, points_ref, sems, *, tiles, capacity
):
    fetches = [
        pltpu.make_async_copy(source, target, sems.at[at])
        for at, (source, target) in enumerate(
            ((owner_in, owner_ref), (lists_in, lists_ref), (points_in, points_ref))
        )
    ]
    for fetch in fetches:
        fetch.start()
    for fetch in fetches:
        fetch.wait()
    rows = owner_ref.shape[1]
    live = iota((1, rows), 1) < counts_ref[0]
    owned = jnp.where(live, owner_ref[...], tiles)
    members = owned == iota((tiles, rows), 0)
    earlier = marks(iota((rows, rows), 0) < iota((rows, rows), 1))
    before = dot(marks(members), earlier)
    rank = jnp.sum(jnp.where(members, before, 0.0), axis=0, keepdims=True)
    slots_ref[...] = jnp.where(live, owned * capacity + rank.astype(jnp.int32), -1)
    for direction, sent_ref in enumerate((sent0, sent1, sent2, sent3)):
        sent_ref[...] = dot(chosen_rows(lists_ref, direction, rows), points_ref[...], TN).astype(bf16)


def chosen_rows(lists_ref, direction, rows):
    listed = lists_ref[direction : direction + 1, :]
    return marks(iota((rows, listed.shape[1]), 0) == listed)


def pack_rows(slots_ref, rows_ref, packed_out, stage_ref, sems):
    slots = slots_ref[...]
    copies = []
    for at, start in enumerate(range(0, packed_out.shape[0], WIDE)):
        place = pl.ds(start, WIDE)
        stage_ref[place, :] = dot(mark_slots(slots, start, WIDE), rows_ref[...]).astype(bf16)
        copies.append(pltpu.make_async_copy(stage_ref.at[place], packed_out.at[place], sems.at[at]))
        copies[-1].start()
    for copy in copies:
        copy.wait()


def unpack_kernel(slots_ref, packed_ref, rows_ref):
    for start in range(0, rows_ref.shape[0], CHUNK):
        column = column_of(slots_ref[:, start : start + CHUNK], CHUNK)
        rows_ref[pl.ds(start, CHUNK), :] = dot(
            pick_rows(column, packed_ref.shape[0]), packed_ref[...]
        ).astype(bf16)


def count_kernel(near_ref, kept_ref, table_ref, sems):
    neighbours, rows = near_ref.shape
    step = 16
    zero = jnp.zeros((step, LANES), bf16)
    one = jnp.ones((step, LANES), bf16)
    row_blocks = table_ref.shape[0] // CHUNK

    def copy_out(row_block):
        place = pl.ds(pl.multiple_of(row_block * CHUNK, CHUNK), CHUNK)
        return pltpu.make_async_copy(table_ref.at[place], kept_ref.at[place], sems.at[row_block])

    def rows_of(row_block, _):
        row_at = pl.multiple_of(row_block * CHUNK, CHUNK)

        def block(lane_block, _):
            lane_at = pl.multiple_of(lane_block * LANES, LANES)
            local = (near_ref[:, pl.ds(lane_at, LANES)] - row_at).astype(f32)
            spread = [
                jnp.broadcast_to(local[k : k + 1, :], (step, LANES)).astype(bf16)
                for k in range(neighbours)
            ]
            base = iota((step, LANES), 0).astype(f32)
            for inner in range(0, CHUNK, step):
                here = (base + float(inner)).astype(bf16)
                total = zero
                for k in range(neighbours):
                    total = total + jnp.where(spread[k] == here, one, zero)
                table_ref[pl.ds(row_at + inner, step), pl.ds(lane_at, LANES)] = total
            return 0

        lax.fori_loop(0, rows // LANES, block, 0)
        copy_out(row_block).start()
        return 0

    lax.fori_loop(0, row_blocks, rows_of, 0)
    for row_block in range(row_blocks):
        copy_out(row_block).wait()


def lift_kernel(
    slots_ref, points_ref, grad_ref, halo0, halo1, halo2, halo3, table_ref, w_ref,
    average_out, pre_out, packed_out,
    average_ref, pre_ref, both_ref, stage_ref, sems, pack_sems, *, neighbours
):
    width = points_ref.shape[1]
    ext = jnp.concatenate([points_ref[...], halo0[...], halo1[...], halo2[...], halo3[...]], axis=0)
    average = (dot(ext, table_ref[...], TN) * (1.0 / neighbours)).astype(bf16)
    average_ref[...] = average
    keep_average = pltpu.make_async_copy(average_ref, average_out, sems.at[0])
    keep_average.start()
    pre_ref[...] = dot(average, w_ref[...], TN)
    keep_pre = pltpu.make_async_copy(pre_ref, pre_out, sems.at[1])
    keep_pre.start()
    for row in range(0, points_ref.shape[0], BLOCK):
        here = pl.ds(row, BLOCK)
        both_ref[here, 0:width] = (
            points_ref[here, :].astype(f32) + gelu_tanh(pre_ref[here, :])
        ).astype(bf16)
    both_ref[:, width:] = grad_ref[...]
    pack_rows(slots_ref, both_ref, packed_out, stage_ref, pack_sems)
    keep_average.wait()
    keep_pre.wait()


def tile_back_kernel(
    slots_ref, back_ref, w_ref, table_in, average_in, pre_in,
    row_out, near_ref, halo0, halo1, halo2, halo3,
    row_ref, table_ref, average_ref, pre_ref, act_ref, spread_ref, sems, *, neighbours
):
    rows = row_ref.shape[0]
    fetch_pre = pltpu.make_async_copy(pre_in, pre_ref, sems.at[0])
    fetch_average = pltpu.make_async_copy(average_in, average_ref, sems.at[1])
    fetch_table = pltpu.make_async_copy(table_in, table_ref, sems.at[2])

    def keep_row(start):
        place = pl.ds(start, WIDE)
        return pltpu.make_async_copy(row_ref.at[place], row_out.at[place], sems.at[3 + start // WIDE])

    fetch_pre.start()
    fetch_average.start()
    fetch_table.start()
    fetch_pre.wait()
    for start in range(0, rows, CHUNK):
        column = column_of(slots_ref[:, start : start + CHUNK], CHUNK)
        wide = dot(pick_rows(column, back_ref.shape[0]), back_ref[...])
        for row in range(0, CHUNK, BLOCK):
            here = pl.ds(start + row, BLOCK)
            lifted_grad = wide[row : row + BLOCK]
            row_ref[here, :] = lifted_grad
            value = pre_ref[here, :]
            square, tangent = gelu_parts(value)
            act_ref[here, :] = (lifted_grad * slope_of(value, square, tangent)).astype(bf16)
    fetch_average.wait()
    near_ref[...] = dot(average_ref[...], act_ref[...]).astype(near_ref.dtype)
    spread_ref[...] = (dot(act_ref[...], w_ref[...], NT) * (1.0 / neighbours)).astype(bf16)
    fetch_table.wait()
    halo = dot(table_ref[rows:, :], spread_ref[...]).astype(bf16)
    size = halo0.shape[0]
    for direction, halo_ref in enumerate((halo0, halo1, halo2, halo3)):
        halo_ref[...] = halo[direction * size : (direction + 1) * size]
    for start in range(0, rows, WIDE):
        here = pl.ds(start, WIDE)
        row_ref[here, :] = row_ref[here, :] + dot(table_ref[here, :], spread_ref[...])
        keep_row(start).start()
    for start in range(0, rows, WIDE):
        keep_row(start).wait()


def finish_kernel(lists_ref, back0, back1, back2, back3, row_in, out_ref, row_ref, sems):
    fetch = pltpu.make_async_copy(row_in, row_ref, sems.at[0])
    fetch.start()
    came = jnp.concatenate([back0[...], back1[...], back2[...], back3[...]], axis=0)
    total = dot(chosen_rows(lists_ref, 0, row_ref.shape[0]), came)
    fetch.wait()
    out_ref[...] = (row_ref[...] + total).astype(bf16)


def near_sum_kernel(parts_ref, share_ref, *, share):
    rows = parts_ref.shape[0]
    same = lax.rem(iota((rows, rows), 0), share) == lax.rem(iota((rows, rows), 1), share)
    share_ref[...] = dot(marks(same), parts_ref[...]).astype(bf16)


def full_taps(conv_ref, groups, inner):
    width = groups * inner
    rows = conv_ref.shape[0]
    repeat = marks(lax.rem(iota((inner, width), 1), inner) == iota((inner, width), 0))
    wide = dot(conv_ref[...], repeat)
    row_group = lax.div(lax.rem(iota((rows, width), 0), width), inner)
    same = row_group == lax.div(iota((rows, width), 1), inner)
    return jnp.where(same, wide, 0.0).astype(bf16)


def padded_zeros(ref):
    edge = jnp.zeros((PAD, ref.shape[1]), f32)
    ref[0:PAD, :] = edge
    ref[PAD + PATCH :, :] = edge


def forward_kernel(
    zorder_ref, conv_ref, gain_one_ref, gain_two_ref, up_ref, down_ref, came_in,
    serial_out, state_out, back_out,
    lifted_ref, serial_ref, state_ref, taps_ref, normed_ref, before_ref, here_ref, after_ref, second_ref, hidden_ref,
    result_ref, stage_ref, sems, pack_sems, *, groups, inner
):
    slots, width = lifted_ref.shape
    fetch = pltpu.make_async_copy(came_in.at[:, pl.ds(0, width)], lifted_ref, sems.at[2, 0])
    fetch.start()
    hidden_width = up_ref.shape[1]
    taps_ref[...] = full_taps(conv_ref, groups, inner)
    padded_zeros(before_ref)
    padded_zeros(after_ref)

    def keep(at):
        place = pl.ds(pl.multiple_of(at * PATCH, PATCH), PATCH)
        return (
            pltpu.make_async_copy(serial_ref.at[place], serial_out.at[place], sems.at[0, at]),
            pltpu.make_async_copy(state_ref.at[place], state_out.at[place], sems.at[1, at]),
        )

    def patch(at, _):
        origin = pl.multiple_of(at * PATCH, PATCH)
        for start in range(0, PATCH, WIDE):
            column = column_of(zorder_ref[:, pl.ds(origin + start, WIDE)], WIDE)
            wide = dot(pick_rows(column, slots), lifted_ref[...])
            for row in range(0, WIDE, BLOCK):
                serial = wide[row : row + BLOCK]
                serial_ref[pl.ds(origin + start + row, BLOCK), :] = serial.astype(bf16)
                normed = serial * inverse_rms(serial) * gain_one_ref[...]
                normed_ref[pl.ds(start + row, BLOCK), :] = normed.astype(bf16)
        before_ref[pl.ds(PAD, PATCH), :] = dot(normed_ref[...], taps_ref[0:width, :])
        here_ref[...] = dot(normed_ref[...], taps_ref[width : 2 * width, :])
        after_ref[pl.ds(PAD, PATCH), :] = dot(normed_ref[...], taps_ref[2 * width :, :])
        for row in range(0, PATCH, BLOCK):
            place = pl.ds(origin + row, BLOCK)
            state = serial_ref[place, :].astype(f32) + (
                before_ref[pl.ds(PAD + row - 1, BLOCK), :]
                + here_ref[pl.ds(row, BLOCK), :]
                + after_ref[pl.ds(PAD + row + 1, BLOCK), :]
            )
            state_ref[place, :] = state
            second = state * inverse_rms(state) * gain_two_ref[...]
            second_ref[pl.ds(row, BLOCK), :] = second.astype(bf16)
        for copy in keep(at):
            copy.start()
        for start in range(0, PATCH, CHUNK):
            value = dot(second_ref[pl.ds(start, CHUNK), :], up_ref[...])
            for row in range(0, CHUNK, 16):
                for col in range(0, hidden_width, 2 * LANES):
                    hidden_ref[pl.ds(start + row, 16), pl.ds(col, 2 * LANES)] = gelu_tanh(
                        value[row : row + 16, col : col + 2 * LANES]
                    ).astype(bf16)
        for start in range(0, PATCH, WIDE):
            place = pl.ds(origin + start, WIDE)
            result_ref[place, :] = (
                state_ref[place, :] + dot(hidden_ref[pl.ds(start, WIDE), :], down_ref[...])
            ).astype(bf16)
        return 0

    fetch.wait()
    lax.fori_loop(0, slots // PATCH, patch, 0)
    pack_rows(zorder_ref, result_ref, back_out, stage_ref, pack_sems)
    for at in range(slots // PATCH):
        for copy in keep(at):
            copy.wait()


def backward_kernel(
    bit_ref, zorder_ref, conv_ref, gain_one_ref, gain_two_ref, up_ref, down_ref, came_in, serial_in, state_in,
    back_out, keep_out, send_out,
    grad_ref, serial_ref, state_ref, out_grad_ref, serial_grad_ref, stage_ref, weights_ref, taps_ref,
    second_ref, hidden_ref, pre_grad_ref, state_grad_ref, mixed_ref, mixed_half_ref, before_ref, here_ref,
    after_ref, normed_ref, conv_sum_ref, gains_ref, sems, pack_sems, *, groups, inner
):
    slots, width = serial_ref.shape
    hidden_width = up_ref.shape[1]
    fetch_grad = pltpu.make_async_copy(came_in.at[:, pl.ds(width, width)], grad_ref, sems.at[0])
    fetch_state = pltpu.make_async_copy(state_in, state_ref, sems.at[1])
    fetch_serial = pltpu.make_async_copy(serial_in, serial_ref, sems.at[2])
    fetch_grad.start()
    fetch_state.start()
    fetch_serial.start()
    taps_ref[...] = full_taps(conv_ref, groups, inner)
    padded_zeros(before_ref)
    padded_zeros(after_ref)
    padded_zeros(mixed_ref)
    conv_sum_ref[...] = jnp.zeros_like(conv_sum_ref)
    gains_ref[...] = jnp.zeros_like(gains_ref)

    def patch(at, _):
        origin = pl.multiple_of(at * PATCH, PATCH)
        for start in range(0, PATCH, WIDE):
            column = column_of(zorder_ref[:, pl.ds(origin + start, WIDE)], WIDE)
            out_grad_ref[pl.ds(origin + start, WIDE), :] = dot(
                pick_rows(column, slots), grad_ref[...]
            ).astype(bf16)
        for start in range(0, PATCH, CHUNK):
            place = pl.ds(origin + start, CHUNK)
            for row in range(start, start + CHUNK, BLOCK):
                state = state_ref[pl.ds(origin + row, BLOCK), :]
                second = state * inverse_rms(state) * gain_two_ref[...]
                second_ref[pl.ds(origin + row, BLOCK), :] = second.astype(bf16)
            value_all = dot(second_ref[place, :], up_ref[...])
            hidden_grad_all = dot(out_grad_ref[place, :], down_ref[...], NT)
            for row in range(0, CHUNK, 16):
                for col in range(0, hidden_width, 2 * LANES):
                    value = value_all[row : row + 16, col : col + 2 * LANES]
                    hidden_grad = hidden_grad_all[row : row + 16, col : col + 2 * LANES]
                    square, tangent = gelu_parts(value)
                    half = 0.5 * value
                    piece = pl.ds(origin + start + row, 16), pl.ds(col, 2 * LANES)
                    hidden_ref[piece] = (half + half * tangent).astype(bf16)
                    pre_grad_ref[piece] = (
                        hidden_grad.astype(bf16).astype(f32) * slope_of(value, square, tangent)
                    ).astype(bf16)
            second_grad_all = dot(pre_grad_ref[place, :], up_ref[...], NT)
            for row in range(0, CHUNK, BLOCK):
                here = pl.ds(origin + start + row, BLOCK)
                state = state_ref[here, :]
                scale_two = inverse_rms(state)
                unit_two = state * scale_two
                second_grad = second_grad_all[row : row + BLOCK].astype(bf16).astype(f32)
                weighted = second_grad * gain_two_ref[...]
                product = second_grad * unit_two
                gains_ref[1:2, :] += jnp.sum(product, axis=0, keepdims=True)
                middle = jnp.mean(product * gain_two_ref[...], axis=-1, keepdims=True)
                state_grad = out_grad_ref[here, :].astype(f32) + scale_two * (weighted - unit_two * middle)
                state_grad_ref[pl.ds(start + row, BLOCK), :] = state_grad
                mixed_grad = state_grad.astype(bf16)
                mixed_half_ref[pl.ds(start + row, BLOCK), :] = mixed_grad
                mixed_ref[pl.ds(PAD + start + row, BLOCK), :] = mixed_grad.astype(f32)
        before_ref[pl.ds(PAD, PATCH), :] = dot(mixed_half_ref[...], taps_ref[0:width, :], NT)
        here_ref[...] = dot(mixed_half_ref[...], taps_ref[width : 2 * width, :], NT)
        after_ref[pl.ds(PAD, PATCH), :] = dot(mixed_half_ref[...], taps_ref[2 * width :, :], NT)
        for row in range(0, PATCH, BLOCK):
            place = pl.ds(origin + row, BLOCK)
            serial = serial_ref[place, :].astype(f32)
            scale_one = inverse_rms(serial)
            unit_one = serial * scale_one
            normed_ref[pl.ds(row, BLOCK), :] = (unit_one * gain_one_ref[...]).astype(bf16)
            normed_grad = (
                before_ref[pl.ds(PAD + row + 1, BLOCK), :]
                + here_ref[pl.ds(row, BLOCK), :]
                + after_ref[pl.ds(PAD + row - 1, BLOCK), :]
            ).astype(bf16).astype(f32)
            product = normed_grad * unit_one
            gains_ref[0:1, :] += jnp.sum(product, axis=0, keepdims=True)
            middle = jnp.mean(product * gain_one_ref[...], axis=-1, keepdims=True)
            weighted = normed_grad * gain_one_ref[...]
            serial_grad_ref[place, :] = (
                state_grad_ref[pl.ds(row, BLOCK), :] + scale_one * (weighted - unit_one * middle)
            ).astype(bf16)
        for tap in range(3):
            moved = mixed_ref[pl.ds(PAD + 1 - tap, PATCH), :].astype(bf16)
            conv_sum_ref[tap] += dot(normed_ref[...], moved, TN)
        return 0

    fetch_grad.wait()
    fetch_state.wait()
    fetch_serial.wait()
    lax.fori_loop(0, slots // PATCH, patch, 0)
    for start in range(0, hidden_width, width):
        block = slice(start, start + width)
        weights_ref[start : start + width, :] = jnp.transpose(
            dot(out_grad_ref[...], hidden_ref[:, block], TN)
        ).astype(bf16)
        weights_ref[hidden_width + start : hidden_width + start + width, :] = dot(
            second_ref[...], pre_grad_ref[:, block], TN
        ).astype(bf16)
    same = lax.div(iota((width, width), 0), inner) == lax.div(iota((width, width), 1), inner)
    for tap in range(3):
        kept = jnp.where(same, conv_sum_ref[tap], 0.0).reshape(groups, inner, width)
        at = 2 * hidden_width + tap * inner
        weights_ref[at : at + inner, :] = jnp.sum(kept, axis=0).astype(bf16)
    at = 2 * hidden_width + 3 * inner
    weights_ref[at : at + 16, :] = gains_ref[...].astype(bf16)
    at = at + 16
    weights_ref[at:, :] = jnp.zeros((weights_ref.shape[0] - at, width), bf16)
    half = keep_out.shape[0]
    bit = bit_ref[0]
    hand_out = [
        pltpu.make_async_copy(
            weights_ref.at[pl.ds(pl.multiple_of(at * half, 16), half)], out, sems.at[3 + which]
        )
        for which, (at, out) in enumerate(((bit, keep_out), (1 - bit, send_out)))
    ]
    for copy in hand_out:
        copy.start()
    pack_rows(zorder_ref, serial_grad_ref, back_out, stage_ref, pack_sems)
    for copy in hand_out:
        copy.wait()


def hold_kernel(rows_in, rows_out):
    pass


def split_rows(bit, rows, scratch_ref, keep_ref, send_ref):
    scratch_ref[...] = rows.astype(bf16)
    half = keep_ref.shape[0]
    keep_ref[...] = scratch_ref[pl.ds(pl.multiple_of(bit * half, 16), half), :]
    send_ref[...] = scratch_ref[pl.ds(pl.multiple_of((1 - bit) * half, 16), half), :]


def added(mine_ref, came_ref):
    return mine_ref[...].astype(f32) + came_ref[...].astype(f32)


def first_split_kernel(
    bit0_ref, bit1_ref, mine_ref, came_ref, keep0, send0, keep1, send1, scratch0, scratch1
):
    half = scratch0.shape[0]
    total = added(mine_ref, came_ref)
    split_rows(bit0_ref[0], total[:half], scratch0, keep0, send0)
    split_rows(bit1_ref[0], total[half:], scratch1, keep1, send1)


def next_split_kernel(
    bit0_ref, bit1_ref, mine0, came0, mine1, came1, keep0, send0, keep1, send1, scratch0, scratch1
):
    split_rows(bit0_ref[0], added(mine0, came0), scratch0, keep0, send0)
    split_rows(bit1_ref[0], added(mine1, came1), scratch1, keep1, send1)


def add_join_kernel(mine0, came0, mine1, came1, share_ref):
    half = mine0.shape[0]
    share_ref[0:half, :] = added(mine0, came0).astype(bf16)
    share_ref[half:, :] = added(mine1, came1).astype(bf16)


def add_kernel(mine_ref, came_ref, total_ref):
    total_ref[...] = added(mine_ref, came_ref).astype(bf16)


def join_kernel(bit_ref, mine_ref, came_ref, both_ref):
    half = mine_ref.shape[0]
    bit = bit_ref[0]
    both_ref[pl.ds(pl.multiple_of(bit * half, 16), half), :] = mine_ref[...]
    both_ref[pl.ds(pl.multiple_of((1 - bit) * half, 16), half), :] = came_ref[...]


def spread_kernel(
    bit_ref, mine_ref, came_ref, total_ref, up_ref, down_ref, conv_ref, gain_one_ref, gain_two_ref, near_ref,
    joined_ref, sums_ref, *, bits, scale
):
    join_kernel(bit_ref, mine_ref, came_ref, joined_ref)
    rows = sums_ref.shape[0]
    piece = (rows >> bits) // 2
    for at in range(1 << bits):
        digits = [(at >> (bits - 1 - bit)) & 1 for bit in range(bits)]
        for part, order in enumerate((digits[1:], digits[:0:-1])):
            place = 0
            for digit in order:
                place = 2 * place + digit
            start = digits[0] * (rows // 2) + part * (rows // 4) + place * piece
            source = (2 * at + part) * piece
            sums_ref[start : start + piece, :] = joined_ref[source : source + piece, :]
    width, hidden_width = up_ref.shape
    taps, groups, inner = conv_ref.shape[:3]
    down_ref[...] = sums_ref[0:hidden_width, :].astype(f32) * scale
    for start in range(0, hidden_width, width):
        up_ref[:, start : start + width] = (
            sums_ref[hidden_width + start : hidden_width + start + width, :].astype(f32) * scale
        )
    for tap in range(taps):
        at = 2 * hidden_width + tap * inner
        rows = sums_ref[at : at + inner, :].astype(f32) * scale
        for group in range(groups):
            conv_ref[tap, group] = rows[:, group * inner : (group + 1) * inner]
    at = 2 * hidden_width + taps * inner
    gains = sums_ref[at : at + 16, :].astype(f32) * scale
    gain_one_ref[...] = gains[0:1, :]
    gain_two_ref[...] = gains[1:2, :]
    near_ref[...] = total_ref[...].astype(f32) * scale


def call(kernel, outs, args, scratch=(), smem=0, flops=0, limit=16, held=0, stored=0, after=(), same=None, **static):
    moved = sum(math.prod(a.shape) * a.dtype.itemsize for a in (*args, *outs))
    specs = [pl.BlockSpec(memory_space=pltpu.SMEM)] * smem
    specs += [pl.BlockSpec(memory_space=pltpu.VMEM)] * (len(args) - smem - held)
    specs += [pl.BlockSpec(memory_space=pltpu.HBM)] * held
    specs += [pl.BlockSpec(memory_space=pltpu.HBM if a.shape[0] >= PATCH else pl.ANY) for a in after]
    after = [pltpu.with_memory_space_constraint(a, pltpu.HBM) if a.shape[0] >= PATCH else a for a in after]
    out_specs = [pl.BlockSpec(memory_space=pltpu.HBM)] * stored
    shapes = [pltpu.HBM(a.shape, a.dtype) for a in outs[:stored]] + list(outs[stored:])
    first_held = len(args) - held
    args = [*args[:first_held], *(pltpu.with_memory_space_constraint(a, pltpu.HBM) for a in args[first_held:])]
    out_specs += [pl.BlockSpec(memory_space=pltpu.VMEM)] * (len(outs) - stored)
    count = len(args)

    def run(*refs):
        kernel(*refs[:count], *refs[count + len(after) :], **static)

    return pl.pallas_call(
        run,
        out_shape=tuple(shapes),
        in_specs=specs,
        out_specs=tuple(out_specs),
        scratch_shapes=list(scratch),
        input_output_aliases=same or {},
        compiler_params=pltpu.CompilerParams(vmem_limit_bytes=limit * 1024 * 1024),
        cost_estimate=pl.CostEstimate(flops=int(flops), bytes_accessed=moved, transcendentals=0),
    )(*args, *after)


def shaped(*shape, dtype=bf16):
    return jax.ShapeDtypeStruct(shape, dtype)


def shifted(value, axis, steps):
    count = lax.axis_size(axis)
    initial, last = (max(0, -steps), min(count, count - steps))
    return lax.ppermute(value, axis, [(source, source + steps) for source in range(initial, last)])


def partner(value, axis, step):
    return lax.ppermute(value, axis, [(at, at ^ step) for at in range(lax.axis_size(axis))])


def bit_of(axis, step):
    return lax.rem(lax.div(lax.axis_index(axis), step), 2).astype(jnp.int32).reshape(1)


def steps_of(axis):
    return [1 << at for at in range(int(math.log2(lax.axis_size(axis))))]


def sum_over_mesh(keep, send, early, late):
    width = keep.shape[1]
    steps = steps_of("ty")
    orders = steps[1:], steps[:0:-1]

    def halves(kernel, rows, at, args, **options):
        return call(
            kernel,
            [shaped(rows // 2, width)] * 4,
            [bit_of("ty", order[at]) for order in orders] + list(args),
            scratch=[pltpu.VMEM((rows, width), bf16)] * 2,
            smem=2,
            flops=1e6,
            **options,
        )

    came = partner(send, "ty", steps[0])
    rows = keep.shape[0] // 2
    parts = halves(first_split_kernel, rows, 0, [keep, came], after=early)
    for at in range(len(orders[0])):
        rows = rows // 2
        pairs = []
        for which, order in enumerate(orders):
            pairs += [parts[2 * which], partner(parts[2 * which + 1], "ty", order[at])]
        if at + 1 < len(orders[0]):
            parts = halves(next_split_kernel, rows, at + 1, pairs)
    (share,) = call(add_join_kernel, [shaped(2 * rows, width)], pairs, flops=1e6)
    for step in steps_of("tx"):
        (share,) = call(
            add_kernel,
            [shaped(*share.shape)],
            [share, partner(share, "tx", step)],
            after=late.pop(0) if late else (),
            flops=1e6,
        )
    for step in steps[:0:-1]:
        (share,) = call(
            join_kernel,
            [shaped(2 * share.shape[0], width)],
            [bit_of("ty", step), share, partner(share, "ty", step)],
            after=late.pop(0) if late else (),
            smem=1,
            flops=1e6,
        )
    return share, partner(share, "ty", steps[0])


def exchange(rows, tiles):
    return lax.all_to_all(rows, ("tx", "ty"), split_axis=0, concat_axis=0, tiled=True)


def body(
    points,
    counts,
    owner,
    zorder,
    border,
    near,
    w_near,
    gain_one,
    conv_w,
    gain_two,
    w_up,
    w_down,
    grad_out,
):
    points_tile = points[0]
    tile_rows, width = points_tile.shape
    border_rows = border.shape[2]
    edge = 4 * border_rows
    ext = tile_rows + edge
    lists = border[0]
    near_tile = near[0]
    neighbours = near_tile.shape[0]
    tiles = lax.axis_size("tx") * lax.axis_size("ty")
    slots_count = zorder.shape[1]
    capacity = slots_count // tiles
    taps, groups, inner = conv_w.shape[:3]
    conv_rows = conv_w.reshape(taps * groups * inner, inner)
    gain_one_row = gain_one.reshape(1, width)
    gain_two_row = gain_two.reshape(1, width)
    hidden = w_up.shape[1]

    slots, *sent = call(
        route_kernel,
        [shaped(1, tile_rows, dtype=jnp.int32)] + [shaped(border_rows, width)] * 4,
        [counts, owner, lists, points_tile],
        scratch=[
            pltpu.VMEM((1, tile_rows), jnp.int32),
            pltpu.VMEM((4, border_rows), jnp.int32),
            pltpu.VMEM((tile_rows, width), bf16),
            pltpu.SemaphoreType.DMA((3,)),
        ],
        smem=1,
        held=3,
        flops=4e9,
        tiles=tiles,
        capacity=capacity,
    )
    halos = [
        shifted(sent[0], "tx", -1),
        shifted(sent[1], "tx", 1),
        shifted(sent[2], "ty", -1),
        shifted(sent[3], "ty", 1),
    ]
    kept_table, table = call(
        count_kernel,
        [shaped(ext, tile_rows), shaped(ext, tile_rows)],
        [near_tile],
        scratch=[pltpu.SemaphoreType.DMA((ext // CHUNK,))],
        flops=8e9,
        stored=1,
    )
    average, pre_act, packed = call(
        lift_kernel,
        [
            shaped(width, tile_rows),
            shaped(tile_rows, width, dtype=f32),
            shaped(slots_count, 2 * width),
        ],
        [slots, points_tile, grad_out[0], *halos, table, w_near],
        scratch=[
            pltpu.VMEM((width, tile_rows), bf16),
            pltpu.VMEM((tile_rows, width), f32),
            pltpu.VMEM((tile_rows, 2 * width), bf16),
            pltpu.VMEM((slots_count, 2 * width), bf16),
            pltpu.SemaphoreType.DMA((2,)),
            pltpu.SemaphoreType.DMA((slots_count // WIDE,)),
        ],
        flops=4e9,
        stored=3,
        neighbours=neighbours,
    )
    came = exchange(packed, tiles)
    patch_scratch = [
        pltpu.VMEM((PATCH + 2 * PAD, width), f32),
        pltpu.VMEM((PATCH, width), f32),
        pltpu.VMEM((PATCH + 2 * PAD, width), f32),
    ]
    serial, state, back_result = call(
        forward_kernel,
        [
            shaped(slots_count, width),
            shaped(slots_count, width, dtype=f32),
            shaped(slots_count, width),
        ],
        [zorder, conv_rows, gain_one_row, gain_two_row, w_up, w_down, came],
        held=1,
        scratch=[
            pltpu.VMEM((slots_count, width), bf16),
            pltpu.VMEM((slots_count, width), bf16),
            pltpu.VMEM((slots_count, width), f32),
            pltpu.VMEM((taps * width, width), bf16),
            pltpu.VMEM((PATCH, width), bf16),
            *patch_scratch,
            pltpu.VMEM((PATCH, width), bf16),
            pltpu.VMEM((PATCH, hidden), bf16),
            pltpu.VMEM((slots_count, width), bf16),
            pltpu.VMEM((slots_count, width), bf16),
            pltpu.SemaphoreType.DMA((3, slots_count // PATCH)),
            pltpu.SemaphoreType.DMA((slots_count // WIDE,)),
        ],
        flops=10e9,
        limit=32,
        stored=3,
        groups=groups,
        inner=inner,
    )
    came_result = exchange(back_result, tiles)
    lines = lax.axis_size("ty")
    sums_rows = 2 * hidden + taps * inner + 16
    sums_rows = -(-sums_rows // (32 * lines)) * (32 * lines)
    back_grad, keep, send = call(
        backward_kernel,
        [
            shaped(slots_count, width),
            shaped(sums_rows // 2, width),
            shaped(sums_rows // 2, width),
        ],
        [
            bit_of("ty", 1),
            zorder,
            conv_rows,
            gain_one_row,
            gain_two_row,
            w_up,
            w_down,
            came,
            serial,
            state,
        ],
        held=3,
        scratch=[
            pltpu.VMEM((slots_count, width), bf16),
            pltpu.VMEM((slots_count, width), bf16),
            pltpu.VMEM((slots_count, width), f32),
            pltpu.VMEM((slots_count, width), bf16),
            pltpu.VMEM((slots_count, width), bf16),
            pltpu.VMEM((slots_count, width), bf16),
            pltpu.VMEM((sums_rows, width), bf16),
            pltpu.VMEM((taps * width, width), bf16),
            pltpu.VMEM((slots_count, width), bf16),
            pltpu.VMEM((slots_count, hidden), bf16),
            pltpu.VMEM((slots_count, hidden), bf16),
            pltpu.VMEM((PATCH, width), f32),
            pltpu.VMEM((PATCH + 2 * PAD, width), f32),
            pltpu.VMEM((PATCH, width), bf16),
            *patch_scratch,
            pltpu.VMEM((PATCH, width), bf16),
            pltpu.VMEM((taps, width, width), f32),
            pltpu.VMEM((16, width), f32),
            pltpu.SemaphoreType.DMA((5,)),
            pltpu.SemaphoreType.DMA((slots_count // WIDE,)),
        ],
        stored=3,
        smem=1,
        flops=40e9,
        limit=44,
        groups=groups,
        inner=inner,
    )
    (back_grad,) = call(
        hold_kernel,
        [shaped(slots_count, width)],
        [back_grad],
        after=[came_result.reshape(tiles, capacity, width)],
        held=1,
        stored=1,
        same={0: 0},
    )
    came_back = exchange(back_grad, tiles)
    (out_rows,) = call(
        unpack_kernel, [shaped(tile_rows, width)], [slots, came_result], flops=4e9
    )
    row_grad, near_grad, *halo_grad = call(
        tile_back_kernel,
        [shaped(tile_rows, width, dtype=f32), shaped(width, width)]
        + [shaped(border_rows, width)] * 4,
        [slots, came_back, w_near, kept_table, average, pre_act],
        after=[out_rows],
        scratch=[
            pltpu.VMEM((tile_rows, width), f32),
            pltpu.VMEM((ext, tile_rows), bf16),
            pltpu.VMEM((width, tile_rows), bf16),
            pltpu.VMEM((tile_rows, width), f32),
            pltpu.VMEM((tile_rows, width), bf16),
            pltpu.VMEM((tile_rows, width), bf16),
            pltpu.SemaphoreType.DMA((3 + tile_rows // WIDE,)),
        ],
        flops=6e9,
        limit=24,
        held=3,
        stored=1,
        neighbours=neighbours,
    )
    returned = [
        shifted(halo_grad[0], "tx", 1),
        shifted(halo_grad[1], "tx", -1),
        shifted(halo_grad[2], "ty", 1),
        shifted(halo_grad[3], "ty", -1),
    ]
    (near_share,) = call(
        near_sum_kernel,
        [shaped(width, width)],
        [exchange(near_grad, tiles)],
        after=returned[:2],
        flops=1e6,
        share=width // tiles,
    )
    near_total = exchange(near_share, tiles)
    totals = sum_over_mesh(
        keep, send, [out_rows], [[near_grad], returned[:2], [near_share], [near_total, *returned[2:]]]
    )
    (grad_points,) = call(
        finish_kernel,
        [shaped(tile_rows, width)],
        [border.reshape(1, edge), *returned, row_grad],
        scratch=[pltpu.VMEM((tile_rows, width), f32), pltpu.SemaphoreType.DMA((1,))],
        held=1,
        flops=1e9,
    )
    scale = 1.0 / math.sqrt(tiles * tile_rows)
    up_sum, down_sum, conv_sum, gain_one_sum, gain_two_sum, near_sum = call(
        spread_kernel,
        [
            shaped(width, hidden, dtype=f32),
            shaped(hidden, width, dtype=f32),
            shaped(*conv_w.shape, dtype=f32),
            shaped(1, width, dtype=f32),
            shaped(1, width, dtype=f32),
            shaped(width, width, dtype=f32),
        ],
        [bit_of("ty", 1), *totals, near_total],
        scratch=[pltpu.VMEM((sums_rows, width), bf16)] * 2,
        smem=1,
        flops=1e6,
        bits=len(steps_of("ty")),
        scale=scale,
    )
    return (
        out_rows[None],
        grad_points[None],
        near_sum,
        gain_one_sum[0],
        conv_sum,
        gain_two_sum[0],
        up_sum,
        down_sum,
    )


def solution(mesh):
    placed = (
        P(("tx", "ty"), None, None),
        P(("tx", "ty")),
        P(("tx", "ty"), None),
        P(("tx", "ty"), None),
        P(("tx", "ty"), None, None),
        P(("tx", "ty"), None, None),
        P(),
        P(),
        P(),
        P(),
        P(),
        P(),
        P(("tx", "ty"), None, None),
    )
    return jax.shard_map(
        body,
        mesh=mesh,
        in_specs=placed,
        out_specs=(
            P(("tx", "ty"), None, None),
            P(("tx", "ty"), None, None),
            P(),
            P(),
            P(),
            P(),
            P(),
            P(),
        ),
        check_vma=False,
    )
```

```python
import math

import jax
import jax.numpy as jnp
from jax import lax
from jax.experimental import pallas as pl
from jax.experimental.pallas import tpu as pltpu
from jax.sharding import PartitionSpec as P

PATCH = 1024
CHUNK = 256
WIDE = 512
BLOCK = 64
LANES = 128
PAD = 8

eps_norm = 1e-06
gelu_coef = 0.7978845608028654
cubic_coef = 0.044715

bf16 = jnp.bfloat16
f32 = jnp.float32
NN = (((1,), (0,)), ((), ()))
NT = (((1,), (1,)), ((), ()))
TN = (((0,), (0,)), ((), ()))


def dot(left, right, dims=NN):
    return lax.dot_general(left, right, dims, preferred_element_type=f32)


def iota(shape, axis):
    return lax.broadcasted_iota(jnp.int32, shape, axis)


def marks(mask):
    return jnp.where(mask, 1.0, 0.0).astype(bf16)


def gelu_parts(value):
    square = value * value
    tangent = jnp.tanh(value * (gelu_coef + (gelu_coef * cubic_coef) * square))
    return square, tangent


def gelu_tanh(value):
    _, tangent = gelu_parts(value)
    half = 0.5 * value
    return half + half * tangent


def slope_of(value, square, tangent):
    inner_slope = gelu_coef + (3.0 * gelu_coef * cubic_coef) * square
    return 0.5 * (1.0 + tangent) + (0.5 * value) * (1.0 - tangent * tangent) * inner_slope


def inverse_rms(value):
    return lax.rsqrt(jnp.mean(value * value, axis=-1, keepdims=True) + eps_norm)


def column_of(row, count):
    return jnp.transpose(jnp.broadcast_to(row, (LANES, count)))


def pick_rows(column, depth):
    count = column.shape[0]
    lane = iota((count, LANES), 1)
    return jnp.concatenate(
        [marks(column == lane + base) for base in range(0, depth, LANES)], axis=1
    )


def mark_slots(row, start, count):
    return marks(iota((count, row.shape[1]), 0) + start == row)


def route_kernel(
    counts_ref, owner_in, lists_in, points_in, slots_ref, sent0, sent1, sent2, sent3,
    owner_ref, lists_ref, points_ref, sems, *, tiles, capacity
):
    fetches = [
        pltpu.make_async_copy(source, target, sems.at[at])
        for at, (source, target) in enumerate(
            ((owner_in, owner_ref), (lists_in, lists_ref), (points_in, points_ref))
        )
    ]
    for fetch in fetches:
        fetch.start()
    for fetch in fetches:
        fetch.wait()
    rows = owner_ref.shape[1]
    live = iota((1, rows), 1) < counts_ref[0]
    owned = jnp.where(live, owner_ref[...], tiles)
    members = owned == iota((tiles, rows), 0)
    earlier = marks(iota((rows, rows), 0) < iota((rows, rows), 1))
    before = dot(marks(members), earlier)
    rank = jnp.sum(jnp.where(members, before, 0.0), axis=0, keepdims=True)
    slots_ref[...] = jnp.where(live, owned * capacity + rank.astype(jnp.int32), -1)
    for direction, sent_ref in enumerate((sent0, sent1, sent2, sent3)):
        sent_ref[...] = dot(chosen_rows(lists_ref, direction, rows), points_ref[...], TN).astype(bf16)


def chosen_rows(lists_ref, direction, rows):
    listed = lists_ref[direction : direction + 1, :]
    return marks(iota((rows, listed.shape[1]), 0) == listed)


def pack_rows(slots_ref, rows_ref, packed_out, stage_ref, sems):
    slots = slots_ref[...]
    copies = []
    for at, start in enumerate(range(0, packed_out.shape[0], WIDE)):
        place = pl.ds(start, WIDE)
        stage_ref[place, :] = dot(mark_slots(slots, start, WIDE), rows_ref[...]).astype(bf16)
        copies.append(pltpu.make_async_copy(stage_ref.at[place], packed_out.at[place], sems.at[at]))
        copies[-1].start()
    for copy in copies:
        copy.wait()


def unpack_kernel(slots_ref, packed_ref, rows_ref):
    for start in range(0, rows_ref.shape[0], CHUNK):
        column = column_of(slots_ref[:, start : start + CHUNK], CHUNK)
        rows_ref[pl.ds(start, CHUNK), :] = dot(
            pick_rows(column, packed_ref.shape[0]), packed_ref[...]
        ).astype(bf16)


def count_kernel(near_ref, kept_ref, table_ref, sems):
    neighbours, rows = near_ref.shape
    step = 16
    zero = jnp.zeros((step, LANES), bf16)
    one = jnp.ones((step, LANES), bf16)
    row_blocks = table_ref.shape[0] // CHUNK

    def copy_out(row_block):
        place = pl.ds(pl.multiple_of(row_block * CHUNK, CHUNK), CHUNK)
        return pltpu.make_async_copy(table_ref.at[place], kept_ref.at[place], sems.at[row_block])

    def rows_of(row_block, _):
        row_at = pl.multiple_of(row_block * CHUNK, CHUNK)

        def block(lane_block, _):
            lane_at = pl.multiple_of(lane_block * LANES, LANES)
            local = (near_ref[:, pl.ds(lane_at, LANES)] - row_at).astype(f32)
            spread = [
                jnp.broadcast_to(local[k : k + 1, :], (step, LANES)).astype(bf16)
                for k in range(neighbours)
            ]
            base = iota((step, LANES), 0).astype(f32)
            for inner in range(0, CHUNK, step):
                here = (base + float(inner)).astype(bf16)
                total = zero
                for k in range(neighbours):
                    total = total + jnp.where(spread[k] == here, one, zero)
                table_ref[pl.ds(row_at + inner, step), pl.ds(lane_at, LANES)] = total
            return 0

        lax.fori_loop(0, rows // LANES, block, 0)
        copy_out(row_block).start()
        return 0

    lax.fori_loop(0, row_blocks, rows_of, 0)
    for row_block in range(row_blocks):
        copy_out(row_block).wait()


def lift_kernel(
    slots_ref, points_ref, grad_ref, halo0, halo1, halo2, halo3, table_ref, w_ref,
    average_out, pre_out, packed_out,
    average_ref, pre_ref, both_ref, stage_ref, sems, pack_sems, *, neighbours
):
    width = points_ref.shape[1]
    ext = jnp.concatenate([points_ref[...], halo0[...], halo1[...], halo2[...], halo3[...]], axis=0)
    average = (dot(ext, table_ref[...], TN) * (1.0 / neighbours)).astype(bf16)
    average_ref[...] = average
    keep_average = pltpu.make_async_copy(average_ref, average_out, sems.at[0])
    keep_average.start()
    pre_ref[...] = dot(average, w_ref[...], TN)
    keep_pre = pltpu.make_async_copy(pre_ref, pre_out, sems.at[1])
    keep_pre.start()
    for row in range(0, points_ref.shape[0], BLOCK):
        here = pl.ds(row, BLOCK)
        both_ref[here, 0:width] = (
            points_ref[here, :].astype(f32) + gelu_tanh(pre_ref[here, :])
        ).astype(bf16)
    both_ref[:, width:] = grad_ref[...]
    pack_rows(slots_ref, both_ref, packed_out, stage_ref, pack_sems)
    keep_average.wait()
    keep_pre.wait()


def tile_back_kernel(
    slots_ref, back_ref, w_ref, table_in, average_in, pre_in,
    lifted_out, spread_out, near_ref, halo0, halo1, halo2, halo3,
    table_ref, average_ref, pre_ref, lifted_ref, act_ref, spread_ref, sems, *, neighbours
):
    rows = lifted_ref.shape[0]
    halo_rows = table_ref.shape[0]
    fetch_pre = pltpu.make_async_copy(pre_in, pre_ref, sems.at[0])
    fetch_average = pltpu.make_async_copy(average_in, average_ref, sems.at[1])
    fetch_table = pltpu.make_async_copy(table_in.at[pl.ds(rows, halo_rows)], table_ref, sems.at[2])
    fetch_pre.start()
    fetch_average.start()
    fetch_table.start()
    keep_lifted = pltpu.make_async_copy(lifted_ref, lifted_out, sems.at[3])
    keep_spread = pltpu.make_async_copy(spread_ref, spread_out, sems.at[4])
    for start in range(0, rows, CHUNK):
        column = column_of(slots_ref[:, start : start + CHUNK], CHUNK)
        wide = dot(pick_rows(column, back_ref.shape[0]), back_ref[...])
        if start == 0:
            fetch_pre.wait()
        for row in range(0, CHUNK, BLOCK):
            here = pl.ds(start + row, BLOCK)
            lifted_grad = wide[row : row + BLOCK]
            lifted_ref[here, :] = lifted_grad.astype(bf16)
            value = pre_ref[here, :]
            square, tangent = gelu_parts(value)
            act_ref[here, :] = (lifted_grad * slope_of(value, square, tangent)).astype(bf16)
    keep_lifted.start()
    spread_ref[...] = (dot(act_ref[...], w_ref[...], NT) * (1.0 / neighbours)).astype(bf16)
    keep_spread.start()
    fetch_average.wait()
    near_ref[...] = dot(average_ref[...], act_ref[...]).astype(near_ref.dtype)
    fetch_table.wait()
    halo = dot(table_ref[...], spread_ref[...]).astype(bf16)
    size = halo0.shape[0]
    for direction, halo_ref in enumerate((halo0, halo1, halo2, halo3)):
        halo_ref[...] = halo[direction * size : (direction + 1) * size]
    keep_lifted.wait()
    keep_spread.wait()


def finish_kernel(
    lists_ref, back0, back1, back2, back3, table_in, spread_in, lifted_in,
    out_ref, table_ref, spread_ref, lifted_ref, sems
):
    rows = out_ref.shape[0]
    fetch_spread = pltpu.make_async_copy(spread_in, spread_ref, sems.at[0])
    fetch_table = pltpu.make_async_copy(table_in.at[pl.ds(0, rows)], table_ref, sems.at[1])
    fetch_lifted = pltpu.make_async_copy(lifted_in, lifted_ref, sems.at[2])
    fetch_spread.start()
    fetch_table.start()
    fetch_lifted.start()
    came = jnp.concatenate([back0[...], back1[...], back2[...], back3[...]], axis=0)
    returned = dot(chosen_rows(lists_ref, 0, rows), came)
    fetch_spread.wait()
    fetch_table.wait()
    fetch_lifted.wait()
    for start in range(0, rows, WIDE):
        here = pl.ds(start, WIDE)
        out_ref[here, :] = (
            lifted_ref[here, :].astype(f32)
            + dot(table_ref[here, :], spread_ref[...])
            + returned[start : start + WIDE]
        ).astype(bf16)


def near_sum_kernel(parts_ref, share_ref, *, share):
    rows = parts_ref.shape[0]
    same = lax.rem(iota((rows, rows), 0), share) == lax.rem(iota((rows, rows), 1), share)
    share_ref[...] = dot(marks(same), parts_ref[...]).astype(bf16)


def full_taps(conv_ref, groups, inner):
    width = groups * inner
    rows = conv_ref.shape[0]
    repeat = marks(lax.rem(iota((inner, width), 1), inner) == iota((inner, width), 0))
    wide = dot(conv_ref[...], repeat)
    row_group = lax.div(lax.rem(iota((rows, width), 0), width), inner)
    same = row_group == lax.div(iota((rows, width), 1), inner)
    return jnp.where(same, wide, 0.0).astype(bf16)


def padded_zeros(ref):
    edge = jnp.zeros((PAD, ref.shape[1]), f32)
    ref[0:PAD, :] = edge
    ref[PAD + PATCH :, :] = edge


def forward_kernel(
    zorder_ref, conv_ref, gain_one_ref, gain_two_ref, up_ref, down_ref, came_in,
    serial_out, state_out, back_out,
    lifted_ref, serial_ref, state_ref, taps_ref, normed_ref, before_ref, here_ref, after_ref, second_ref, hidden_ref,
    result_ref, stage_ref, sems, pack_sems, *, groups, inner
):
    slots, width = lifted_ref.shape
    fetch = pltpu.make_async_copy(came_in.at[:, pl.ds(0, width)], lifted_ref, sems.at[2, 0])
    fetch.start()
    hidden_width = up_ref.shape[1]
    taps_ref[...] = full_taps(conv_ref, groups, inner)

    def keep(at):
        place = pl.ds(at * PATCH, PATCH)
        return (
            pltpu.make_async_copy(serial_ref.at[place], serial_out.at[place], sems.at[0, at]),
            pltpu.make_async_copy(state_ref.at[place], state_out.at[place], sems.at[1, at]),
        )

    def patch(at):
        origin = at * PATCH
        normed_at, second_at, hidden_at = normed_ref.at[at], second_ref.at[at], hidden_ref.at[at]
        before_at, here_at, after_at = before_ref.at[at], here_ref.at[at], after_ref.at[at]
        padded_zeros(before_at)
        padded_zeros(after_at)
        for start in range(0, PATCH, WIDE):
            column = column_of(zorder_ref[:, origin + start : origin + start + WIDE], WIDE)
            wide = dot(pick_rows(column, slots), lifted_ref[...])
            for row in range(0, WIDE, BLOCK):
                serial = wide[row : row + BLOCK]
                serial_ref[pl.ds(origin + start + row, BLOCK), :] = serial.astype(bf16)
                normed = serial * inverse_rms(serial) * gain_one_ref[...]
                normed_at[pl.ds(start + row, BLOCK), :] = normed.astype(bf16)
            yield
        before_at[pl.ds(PAD, PATCH), :] = dot(normed_at[...], taps_ref[0:width, :])
        here_at[...] = dot(normed_at[...], taps_ref[width : 2 * width, :])
        after_at[pl.ds(PAD, PATCH), :] = dot(normed_at[...], taps_ref[2 * width :, :])
        yield
        for row in range(0, PATCH, BLOCK):
            place = pl.ds(origin + row, BLOCK)
            state = serial_ref[place, :].astype(f32) + (
                before_at[pl.ds(PAD + row - 1, BLOCK), :]
                + here_at[pl.ds(row, BLOCK), :]
                + after_at[pl.ds(PAD + row + 1, BLOCK), :]
            )
            state_ref[place, :] = state
            second = state * inverse_rms(state) * gain_two_ref[...]
            second_at[pl.ds(row, BLOCK), :] = second.astype(bf16)
        for copy in keep(at):
            copy.start()
        yield
        for start in range(0, PATCH, CHUNK):
            value = dot(second_at[pl.ds(start, CHUNK), :], up_ref[...])
            for row in range(0, CHUNK, 16):
                for col in range(0, hidden_width, 2 * LANES):
                    hidden_at[pl.ds(start + row, 16), pl.ds(col, 2 * LANES)] = gelu_tanh(
                        value[row : row + 16, col : col + 2 * LANES]
                    ).astype(bf16)
            if start + CHUNK == PATCH // 2:
                yield
        yield
        for start in range(0, PATCH, WIDE):
            place = pl.ds(origin + start, WIDE)
            result_ref[place, :] = (
                state_ref[place, :] + dot(hidden_at[pl.ds(start, WIDE), :], down_ref[...])
            ).astype(bf16)
        yield

    fetch.wait()
    waiting = [patch(at) for at in range(slots // PATCH)]
    running = []
    while waiting or running:
        if waiting:
            running.append(waiting.pop(0))
        running = [work for work in running if next(work, work) is not work]
    pack_rows(zorder_ref, result_ref, back_out, stage_ref, pack_sems)
    for at in range(slots // PATCH):
        for copy in keep(at):
            copy.wait()


def backward_kernel(
    bit_ref, zorder_ref, conv_ref, gain_one_ref, gain_two_ref, up_ref, down_ref, came_in, serial_in, state_in,
    back_out, keep_out, send_out,
    grad_ref, serial_ref, state_ref, out_grad_ref, serial_grad_ref, stage_ref, weights_ref, taps_ref,
    second_ref, hidden_ref, pre_grad_ref, state_grad_ref, mixed_ref, mixed_half_ref, before_ref, here_ref,
    after_ref, normed_ref, conv_sum_ref, gains_ref, sems, pack_sems, *, groups, inner
):
    slots, width = serial_ref.shape
    hidden_width = up_ref.shape[1]
    fetch_grad = pltpu.make_async_copy(came_in.at[:, pl.ds(width, width)], grad_ref, sems.at[0])
    fetch_state = pltpu.make_async_copy(state_in, state_ref, sems.at[1])
    fetch_serial = pltpu.make_async_copy(serial_in, serial_ref, sems.at[2])
    fetch_grad.start()
    fetch_state.start()
    fetch_serial.start()
    taps_ref[...] = full_taps(conv_ref, groups, inner)
    padded_zeros(before_ref)
    padded_zeros(after_ref)
    padded_zeros(mixed_ref)
    conv_sum_ref[...] = jnp.zeros_like(conv_sum_ref)
    gains_ref[...] = jnp.zeros_like(gains_ref)

    def patch(at, _):
        origin = pl.multiple_of(at * PATCH, PATCH)
        for start in range(0, PATCH, WIDE):
            column = column_of(zorder_ref[:, pl.ds(origin + start, WIDE)], WIDE)
            out_grad_ref[pl.ds(origin + start, WIDE), :] = dot(
                pick_rows(column, slots), grad_ref[...]
            ).astype(bf16)
        for start in range(0, PATCH, CHUNK):
            place = pl.ds(origin + start, CHUNK)
            for row in range(start, start + CHUNK, BLOCK):
                state = state_ref[pl.ds(origin + row, BLOCK), :]
                second = state * inverse_rms(state) * gain_two_ref[...]
                second_ref[pl.ds(origin + row, BLOCK), :] = second.astype(bf16)
            value_all = dot(second_ref[place, :], up_ref[...])
            hidden_grad_all = dot(out_grad_ref[place, :], down_ref[...], NT)
            for row in range(0, CHUNK, 16):
                for col in range(0, hidden_width, 2 * LANES):
                    value = value_all[row : row + 16, col : col + 2 * LANES]
                    hidden_grad = hidden_grad_all[row : row + 16, col : col + 2 * LANES]
                    square, tangent = gelu_parts(value)
                    half = 0.5 * value
                    piece = pl.ds(origin + start + row, 16), pl.ds(col, 2 * LANES)
                    hidden_ref[piece] = (half + half * tangent).astype(bf16)
                    pre_grad_ref[piece] = (
                        hidden_grad.astype(bf16).astype(f32) * slope_of(value, square, tangent)
                    ).astype(bf16)
            second_grad_all = dot(pre_grad_ref[place, :], up_ref[...], NT)
            for row in range(0, CHUNK, BLOCK):
                here = pl.ds(origin + start + row, BLOCK)
                state = state_ref[here, :]
                scale_two = inverse_rms(state)
                unit_two = state * scale_two
                second_grad = second_grad_all[row : row + BLOCK].astype(bf16).astype(f32)
                weighted = second_grad * gain_two_ref[...]
                product = second_grad * unit_two
                gains_ref[1:2, :] += jnp.sum(product, axis=0, keepdims=True)
                middle = jnp.mean(product * gain_two_ref[...], axis=-1, keepdims=True)
                state_grad = out_grad_ref[here, :].astype(f32) + scale_two * (weighted - unit_two * middle)
                state_grad_ref[pl.ds(start + row, BLOCK), :] = state_grad
                mixed_grad = state_grad.astype(bf16)
                mixed_half_ref[pl.ds(start + row, BLOCK), :] = mixed_grad
                mixed_ref[pl.ds(PAD + start + row, BLOCK), :] = mixed_grad.astype(f32)
        before_ref[pl.ds(PAD, PATCH), :] = dot(mixed_half_ref[...], taps_ref[0:width, :], NT)
        here_ref[...] = dot(mixed_half_ref[...], taps_ref[width : 2 * width, :], NT)
        after_ref[pl.ds(PAD, PATCH), :] = dot(mixed_half_ref[...], taps_ref[2 * width :, :], NT)
        for row in range(0, PATCH, BLOCK):
            place = pl.ds(origin + row, BLOCK)
            serial = serial_ref[place, :].astype(f32)
            scale_one = inverse_rms(serial)
            unit_one = serial * scale_one
            normed_ref[pl.ds(row, BLOCK), :] = (unit_one * gain_one_ref[...]).astype(bf16)
            normed_grad = (
                before_ref[pl.ds(PAD + row + 1, BLOCK), :]
                + here_ref[pl.ds(row, BLOCK), :]
                + after_ref[pl.ds(PAD + row - 1, BLOCK), :]
            ).astype(bf16).astype(f32)
            product = normed_grad * unit_one
            gains_ref[0:1, :] += jnp.sum(product, axis=0, keepdims=True)
            middle = jnp.mean(product * gain_one_ref[...], axis=-1, keepdims=True)
            weighted = normed_grad * gain_one_ref[...]
            serial_grad_ref[place, :] = (
                state_grad_ref[pl.ds(row, BLOCK), :] + scale_one * (weighted - unit_one * middle)
            ).astype(bf16)
        for tap in range(3):
            moved = mixed_ref[pl.ds(PAD + 1 - tap, PATCH), :].astype(bf16)
            conv_sum_ref[tap] += dot(normed_ref[...], moved, TN)
        return 0

    fetch_grad.wait()
    fetch_state.wait()
    fetch_serial.wait()
    lax.fori_loop(0, slots // PATCH, patch, 0)
    for start in range(0, hidden_width, width):
        block = slice(start, start + width)
        weights_ref[start : start + width, :] = jnp.transpose(
            dot(out_grad_ref[...], hidden_ref[:, block], TN)
        ).astype(bf16)
        weights_ref[hidden_width + start : hidden_width + start + width, :] = dot(
            second_ref[...], pre_grad_ref[:, block], TN
        ).astype(bf16)
    same = lax.div(iota((width, width), 0), inner) == lax.div(iota((width, width), 1), inner)
    for tap in range(3):
        kept = jnp.where(same, conv_sum_ref[tap], 0.0).reshape(groups, inner, width)
        at = 2 * hidden_width + tap * inner
        weights_ref[at : at + inner, :] = jnp.sum(kept, axis=0).astype(bf16)
    at = 2 * hidden_width + 3 * inner
    weights_ref[at : at + 16, :] = gains_ref[...].astype(bf16)
    at = at + 16
    weights_ref[at:, :] = jnp.zeros((weights_ref.shape[0] - at, width), bf16)
    half = keep_out.shape[0]
    bit = bit_ref[0]
    hand_out = [
        pltpu.make_async_copy(
            weights_ref.at[pl.ds(pl.multiple_of(at * half, 16), half)], out, sems.at[3 + which]
        )
        for which, (at, out) in enumerate(((bit, keep_out), (1 - bit, send_out)))
    ]
    for copy in hand_out:
        copy.start()
    pack_rows(zorder_ref, serial_grad_ref, back_out, stage_ref, pack_sems)
    for copy in hand_out:
        copy.wait()


def hold_kernel(rows_in, rows_out):
    pass


def split_rows(bit, rows, scratch_ref, keep_ref, send_ref):
    scratch_ref[...] = rows.astype(bf16)
    half = keep_ref.shape[0]
    keep_ref[...] = scratch_ref[pl.ds(pl.multiple_of(bit * half, 16), half), :]
    send_ref[...] = scratch_ref[pl.ds(pl.multiple_of((1 - bit) * half, 16), half), :]


def added(mine_ref, came_ref):
    return mine_ref[...].astype(f32) + came_ref[...].astype(f32)


def first_split_kernel(
    bit0_ref, bit1_ref, mine_ref, came_ref, keep0, send0, keep1, send1, scratch0, scratch1
):
    half = scratch0.shape[0]
    total = added(mine_ref, came_ref)
    split_rows(bit0_ref[0], total[:half], scratch0, keep0, send0)
    split_rows(bit1_ref[0], total[half:], scratch1, keep1, send1)


def next_split_kernel(
    bit0_ref, bit1_ref, mine0, came0, mine1, came1, keep0, send0, keep1, send1, scratch0, scratch1
):
    split_rows(bit0_ref[0], added(mine0, came0), scratch0, keep0, send0)
    split_rows(bit1_ref[0], added(mine1, came1), scratch1, keep1, send1)


def add_join_kernel(mine0, came0, mine1, came1, share_ref):
    half = mine0.shape[0]
    share_ref[0:half, :] = added(mine0, came0).astype(bf16)
    share_ref[half:, :] = added(mine1, came1).astype(bf16)


def add_kernel(mine_ref, came_ref, total_ref):
    total_ref[...] = added(mine_ref, came_ref).astype(bf16)


def join_kernel(bit_ref, mine_ref, came_ref, both_ref):
    half = mine_ref.shape[0]
    bit = bit_ref[0]
    both_ref[pl.ds(pl.multiple_of(bit * half, 16), half), :] = mine_ref[...]
    both_ref[pl.ds(pl.multiple_of((1 - bit) * half, 16), half), :] = came_ref[...]


def spread_kernel(
    bit_ref, mine_ref, came_ref, total_ref, up_ref, down_ref, conv_ref, gain_one_ref, gain_two_ref, near_ref,
    joined_ref, sums_ref, *, bits, scale
):
    join_kernel(bit_ref, mine_ref, came_ref, joined_ref)
    rows = sums_ref.shape[0]
    piece = (rows >> bits) // 2
    for at in range(1 << bits):
        digits = [(at >> (bits - 1 - bit)) & 1 for bit in range(bits)]
        for part, order in enumerate((digits[1:], digits[:0:-1])):
            place = 0
            for digit in order:
                place = 2 * place + digit
            start = digits[0] * (rows // 2) + part * (rows // 4) + place * piece
            source = (2 * at + part) * piece
            sums_ref[start : start + piece, :] = joined_ref[source : source + piece, :]
    width, hidden_width = up_ref.shape
    taps, groups, inner = conv_ref.shape[:3]
    down_ref[...] = sums_ref[0:hidden_width, :].astype(f32) * scale
    for start in range(0, hidden_width, width):
        up_ref[:, start : start + width] = (
            sums_ref[hidden_width + start : hidden_width + start + width, :].astype(f32) * scale
        )
    for tap in range(taps):
        at = 2 * hidden_width + tap * inner
        rows = sums_ref[at : at + inner, :].astype(f32) * scale
        for group in range(groups):
            conv_ref[tap, group] = rows[:, group * inner : (group + 1) * inner]
    at = 2 * hidden_width + taps * inner
    gains = sums_ref[at : at + 16, :].astype(f32) * scale
    gain_one_ref[...] = gains[0:1, :]
    gain_two_ref[...] = gains[1:2, :]
    near_ref[...] = total_ref[...].astype(f32) * scale


def call(kernel, outs, args, scratch=(), smem=0, flops=0, limit=16, held=0, stored=0, after=(), same=None, **static):
    moved = sum(math.prod(a.shape) * a.dtype.itemsize for a in (*args, *outs))
    specs = [pl.BlockSpec(memory_space=pltpu.SMEM)] * smem
    specs += [pl.BlockSpec(memory_space=pltpu.VMEM)] * (len(args) - smem - held)
    specs += [pl.BlockSpec(memory_space=pltpu.HBM)] * held
    specs += [pl.BlockSpec(memory_space=pltpu.HBM if a.shape[0] >= PATCH else pl.ANY) for a in after]
    after = [pltpu.with_memory_space_constraint(a, pltpu.HBM) if a.shape[0] >= PATCH else a for a in after]
    out_specs = [pl.BlockSpec(memory_space=pltpu.HBM)] * stored
    shapes = [pltpu.HBM(a.shape, a.dtype) for a in outs[:stored]] + list(outs[stored:])
    first_held = len(args) - held
    args = [*args[:first_held], *(pltpu.with_memory_space_constraint(a, pltpu.HBM) for a in args[first_held:])]
    out_specs += [pl.BlockSpec(memory_space=pltpu.VMEM)] * (len(outs) - stored)
    count = len(args)

    def run(*refs):
        kernel(*refs[:count], *refs[count + len(after) :], **static)

    return pl.pallas_call(
        run,
        out_shape=tuple(shapes),
        in_specs=specs,
        out_specs=tuple(out_specs),
        scratch_shapes=list(scratch),
        input_output_aliases=same or {},
        compiler_params=pltpu.CompilerParams(vmem_limit_bytes=limit * 1024 * 1024),
        cost_estimate=pl.CostEstimate(flops=int(flops), bytes_accessed=moved, transcendentals=0),
    )(*args, *after)


def shaped(*shape, dtype=bf16):
    return jax.ShapeDtypeStruct(shape, dtype)


def shifted(value, axis, steps):
    count = lax.axis_size(axis)
    initial, last = (max(0, -steps), min(count, count - steps))
    return lax.ppermute(value, axis, [(source, source + steps) for source in range(initial, last)])


def partner(value, axis, step):
    return lax.ppermute(value, axis, [(at, at ^ step) for at in range(lax.axis_size(axis))])


def bit_of(axis, step):
    return lax.rem(lax.div(lax.axis_index(axis), step), 2).astype(jnp.int32).reshape(1)


def steps_of(axis):
    return [1 << at for at in range(int(math.log2(lax.axis_size(axis))))]


def sum_over_mesh(keep, send, early, late):
    width = keep.shape[1]
    steps = steps_of("ty")
    orders = steps[1:], steps[:0:-1]

    def halves(kernel, rows, at, args, **options):
        return call(
            kernel,
            [shaped(rows // 2, width)] * 4,
            [bit_of("ty", order[at]) for order in orders] + list(args),
            scratch=[pltpu.VMEM((rows, width), bf16)] * 2,
            smem=2,
            flops=1e6,
            **options,
        )

    came = partner(send, "ty", steps[0])
    rows = keep.shape[0] // 2
    parts = halves(first_split_kernel, rows, 0, [keep, came], after=early)
    for at in range(len(orders[0])):
        rows = rows // 2
        pairs = []
        for which, order in enumerate(orders):
            pairs += [parts[2 * which], partner(parts[2 * which + 1], "ty", order[at])]
        if at + 1 < len(orders[0]):
            parts = halves(next_split_kernel, rows, at + 1, pairs)
    (share,) = call(add_join_kernel, [shaped(2 * rows, width)], pairs, flops=1e6)
    for step in steps_of("tx"):
        (share,) = call(
            add_kernel,
            [shaped(*share.shape)],
            [share, partner(share, "tx", step)],
            after=late.pop(0) if late else (),
            flops=1e6,
        )
    for step in steps[:0:-1]:
        (share,) = call(
            join_kernel,
            [shaped(2 * share.shape[0], width)],
            [bit_of("ty", step), share, partner(share, "ty", step)],
            after=late.pop(0) if late else (),
            smem=1,
            flops=1e6,
        )
    return share, partner(share, "ty", steps[0])


def exchange(rows, tiles):
    return lax.all_to_all(rows, ("tx", "ty"), split_axis=0, concat_axis=0, tiled=True)


def body(
    points,
    counts,
    owner,
    zorder,
    border,
    near,
    w_near,
    gain_one,
    conv_w,
    gain_two,
    w_up,
    w_down,
    grad_out,
):
    points_tile = points[0]
    tile_rows, width = points_tile.shape
    border_rows = border.shape[2]
    edge = 4 * border_rows
    ext = tile_rows + edge
    lists = border[0]
    near_tile = near[0]
    neighbours = near_tile.shape[0]
    tiles = lax.axis_size("tx") * lax.axis_size("ty")
    slots_count = zorder.shape[1]
    capacity = slots_count // tiles
    taps, groups, inner = conv_w.shape[:3]
    conv_rows = conv_w.reshape(taps * groups * inner, inner)
    gain_one_row = gain_one.reshape(1, width)
    gain_two_row = gain_two.reshape(1, width)
    hidden = w_up.shape[1]

    slots, *sent = call(
        route_kernel,
        [shaped(1, tile_rows, dtype=jnp.int32)] + [shaped(border_rows, width)] * 4,
        [counts, owner, lists, points_tile],
        scratch=[
            pltpu.VMEM((1, tile_rows), jnp.int32),
            pltpu.VMEM((4, border_rows), jnp.int32),
            pltpu.VMEM((tile_rows, width), bf16),
            pltpu.SemaphoreType.DMA((3,)),
        ],
        smem=1,
        held=3,
        flops=4e9,
        tiles=tiles,
        capacity=capacity,
    )
    halos = [
        shifted(sent[0], "tx", -1),
        shifted(sent[1], "tx", 1),
        shifted(sent[2], "ty", -1),
        shifted(sent[3], "ty", 1),
    ]
    kept_table, table = call(
        count_kernel,
        [shaped(ext, tile_rows), shaped(ext, tile_rows)],
        [near_tile],
        scratch=[pltpu.SemaphoreType.DMA((ext // CHUNK,))],
        flops=8e9,
        stored=1,
    )
    average, pre_act, packed = call(
        lift_kernel,
        [
            shaped(width, tile_rows),
            shaped(tile_rows, width, dtype=f32),
            shaped(slots_count, 2 * width),
        ],
        [slots, points_tile, grad_out[0], *halos, table, w_near],
        scratch=[
            pltpu.VMEM((width, tile_rows), bf16),
            pltpu.VMEM((tile_rows, width), f32),
            pltpu.VMEM((tile_rows, 2 * width), bf16),
            pltpu.VMEM((slots_count, 2 * width), bf16),
            pltpu.SemaphoreType.DMA((2,)),
            pltpu.SemaphoreType.DMA((slots_count // WIDE,)),
        ],
        flops=4e9,
        stored=3,
        neighbours=neighbours,
    )
    came = exchange(packed, tiles)
    patches = slots_count // PATCH
    patch_scratch = [
        pltpu.VMEM((PATCH + 2 * PAD, width), f32),
        pltpu.VMEM((PATCH, width), f32),
        pltpu.VMEM((PATCH + 2 * PAD, width), f32),
    ]
    serial, state, back_result = call(
        forward_kernel,
        [
            shaped(slots_count, width),
            shaped(slots_count, width, dtype=f32),
            shaped(slots_count, width),
        ],
        [zorder, conv_rows, gain_one_row, gain_two_row, w_up, w_down, came],
        held=1,
        scratch=[
            pltpu.VMEM((slots_count, width), bf16),
            pltpu.VMEM((slots_count, width), bf16),
            pltpu.VMEM((slots_count, width), f32),
            pltpu.VMEM((taps * width, width), bf16),
            pltpu.VMEM((patches, PATCH, width), bf16),
            pltpu.VMEM((patches, PATCH + 2 * PAD, width), f32),
            pltpu.VMEM((patches, PATCH, width), f32),
            pltpu.VMEM((patches, PATCH + 2 * PAD, width), f32),
            pltpu.VMEM((patches, PATCH, width), bf16),
            pltpu.VMEM((patches, PATCH, hidden), bf16),
            pltpu.VMEM((slots_count, width), bf16),
            pltpu.VMEM((slots_count, width), bf16),
            pltpu.SemaphoreType.DMA((3, slots_count // PATCH)),
            pltpu.SemaphoreType.DMA((slots_count // WIDE,)),
        ],
        flops=10e9,
        limit=44,
        stored=3,
        groups=groups,
        inner=inner,
    )
    came_result = exchange(back_result, tiles)
    lines = lax.axis_size("ty")
    sums_rows = 2 * hidden + taps * inner + 16
    sums_rows = -(-sums_rows // (32 * lines)) * (32 * lines)
    back_grad, keep, send = call(
        backward_kernel,
        [
            shaped(slots_count, width),
            shaped(sums_rows // 2, width),
            shaped(sums_rows // 2, width),
        ],
        [
            bit_of("ty", 1),
            zorder,
            conv_rows,
            gain_one_row,
            gain_two_row,
            w_up,
            w_down,
            came,
            serial,
            state,
        ],
        held=3,
        scratch=[
            pltpu.VMEM((slots_count, width), bf16),
            pltpu.VMEM((slots_count, width), bf16),
            pltpu.VMEM((slots_count, width), f32),
            pltpu.VMEM((slots_count, width), bf16),
            pltpu.VMEM((slots_count, width), bf16),
            pltpu.VMEM((slots_count, width), bf16),
            pltpu.VMEM((sums_rows, width), bf16),
            pltpu.VMEM((taps * width, width), bf16),
            pltpu.VMEM((slots_count, width), bf16),
            pltpu.VMEM((slots_count, hidden), bf16),
            pltpu.VMEM((slots_count, hidden), bf16),
            pltpu.VMEM((PATCH, width), f32),
            pltpu.VMEM((PATCH + 2 * PAD, width), f32),
            pltpu.VMEM((PATCH, width), bf16),
            *patch_scratch,
            pltpu.VMEM((PATCH, width), bf16),
            pltpu.VMEM((taps, width, width), f32),
            pltpu.VMEM((16, width), f32),
            pltpu.SemaphoreType.DMA((5,)),
            pltpu.SemaphoreType.DMA((slots_count // WIDE,)),
        ],
        stored=3,
        smem=1,
        flops=40e9,
        limit=44,
        groups=groups,
        inner=inner,
    )
    (back_grad,) = call(
        hold_kernel,
        [shaped(slots_count, width)],
        [back_grad],
        after=[came_result.reshape(tiles, capacity, width)],
        held=1,
        stored=1,
        same={0: 0},
    )
    came_back = exchange(back_grad, tiles)
    (out_rows,) = call(
        unpack_kernel, [shaped(tile_rows, width)], [slots, came_result], flops=4e9
    )
    lifted_grad, spread, near_grad, *halo_grad = call(
        tile_back_kernel,
        [shaped(tile_rows, width), shaped(tile_rows, width), shaped(width, width)]
        + [shaped(border_rows, width)] * 4,
        [slots, came_back, w_near, kept_table, average, pre_act],
        after=[out_rows],
        scratch=[
            pltpu.VMEM((edge, tile_rows), bf16),
            pltpu.VMEM((width, tile_rows), bf16),
            pltpu.VMEM((tile_rows, width), f32),
            pltpu.VMEM((tile_rows, width), bf16),
            pltpu.VMEM((tile_rows, width), bf16),
            pltpu.VMEM((tile_rows, width), bf16),
            pltpu.SemaphoreType.DMA((5,)),
        ],
        flops=6e9,
        limit=24,
        held=3,
        stored=2,
        neighbours=neighbours,
    )
    returned = [
        shifted(halo_grad[0], "tx", 1),
        shifted(halo_grad[1], "tx", -1),
        shifted(halo_grad[2], "ty", 1),
        shifted(halo_grad[3], "ty", -1),
    ]
    (near_share,) = call(
        near_sum_kernel,
        [shaped(width, width)],
        [exchange(near_grad, tiles)],
        after=returned[:2],
        flops=1e6,
        share=width // tiles,
    )
    near_total = exchange(near_share, tiles)
    totals = sum_over_mesh(
        keep, send, [out_rows], [[near_grad], returned[:2], [near_share], [near_total, *returned[2:]]]
    )
    (grad_points,) = call(
        finish_kernel,
        [shaped(tile_rows, width)],
        [border.reshape(1, edge), *returned, kept_table, spread, lifted_grad],
        scratch=[
            pltpu.VMEM((tile_rows, tile_rows), bf16),
            pltpu.VMEM((tile_rows, width), bf16),
            pltpu.VMEM((tile_rows, width), bf16),
            pltpu.SemaphoreType.DMA((3,)),
        ],
        held=3,
        flops=1e9,
    )
    scale = 1.0 / math.sqrt(tiles * tile_rows)
    up_sum, down_sum, conv_sum, gain_one_sum, gain_two_sum, near_sum = call(
        spread_kernel,
        [
            shaped(width, hidden, dtype=f32),
            shaped(hidden, width, dtype=f32),
            shaped(*conv_w.shape, dtype=f32),
            shaped(1, width, dtype=f32),
            shaped(1, width, dtype=f32),
            shaped(width, width, dtype=f32),
        ],
        [bit_of("ty", 1), *totals, near_total],
        scratch=[pltpu.VMEM((sums_rows, width), bf16)] * 2,
        smem=1,
        flops=1e6,
        bits=len(steps_of("ty")),
        scale=scale,
    )
    return (
        out_rows[None],
        grad_points[None],
        near_sum,
        gain_one_sum[0],
        conv_sum,
        gain_two_sum[0],
        up_sum,
        down_sum,
    )


def solution(mesh):
    placed = (
        P(("tx", "ty"), None, None),
        P(("tx", "ty")),
        P(("tx", "ty"), None),
        P(("tx", "ty"), None),
        P(("tx", "ty"), None, None),
        P(("tx", "ty"), None, None),
        P(),
        P(),
        P(),
        P(),
        P(),
        P(),
        P(("tx", "ty"), None, None),
    )
    return jax.shard_map(
        body,
        mesh=mesh,
        in_specs=placed,
        out_specs=(
            P(("tx", "ty"), None, None),
            P(("tx", "ty"), None, None),
            P(),
            P(),
            P(),
            P(),
            P(),
            P(),
        ),
        check_vma=False,
    )
```

```python
import math

import jax
import jax.numpy as jnp
from jax import lax
from jax.experimental import pallas as pl
from jax.experimental.pallas import tpu as pltpu
from jax.sharding import PartitionSpec as P

PATCH = 1024
CHUNK = 256
WIDE = 512
BLOCK = 64
LANES = 128
PAD = 8

eps_norm = 1e-06
gelu_coef = 0.7978845608028654
cubic_coef = 0.044715

bf16 = jnp.bfloat16
f32 = jnp.float32
NN = (((1,), (0,)), ((), ()))
NT = (((1,), (1,)), ((), ()))
TN = (((0,), (0,)), ((), ()))


def dot(left, right, dims=NN):
    return lax.dot_general(left, right, dims, preferred_element_type=f32)


def iota(shape, axis):
    return lax.broadcasted_iota(jnp.int32, shape, axis)


def marks(mask):
    return jnp.where(mask, 1.0, 0.0).astype(bf16)


def gelu_parts(value):
    square = value * value
    tangent = jnp.tanh(value * (gelu_coef + (gelu_coef * cubic_coef) * square))
    return square, tangent


def gelu_tanh(value):
    _, tangent = gelu_parts(value)
    half = 0.5 * value
    return half + half * tangent


def slope_of(value, square, tangent):
    inner_slope = gelu_coef + (3.0 * gelu_coef * cubic_coef) * square
    return 0.5 * (1.0 + tangent) + (0.5 * value) * (1.0 - tangent * tangent) * inner_slope


def inverse_rms(value):
    return lax.rsqrt(jnp.mean(value * value, axis=-1, keepdims=True) + eps_norm)


def column_of(row, count):
    return jnp.transpose(jnp.broadcast_to(row, (LANES, count)))


def pick_rows(column, depth):
    count = column.shape[0]
    lane = iota((count, LANES), 1)
    return jnp.concatenate(
        [marks(column == lane + base) for base in range(0, depth, LANES)], axis=1
    )


def mark_slots(row, start, count):
    return marks(iota((count, row.shape[1]), 0) + start == row)


def route_kernel(
    bits_ref, counts_ref, owner_in, lists_in, points_in, slots_ref, sent0, sent1, sent2, sent3,
    owner_ref, lists_ref, points_ref, sems, *, tiles, capacity
):
    fetches = [
        pltpu.make_async_copy(source, target, sems.at[at])
        for at, (source, target) in enumerate(
            ((owner_in, owner_ref), (lists_in, lists_ref), (points_in, points_ref))
        )
    ]
    for fetch in fetches:
        fetch.start()
    fetches[0].wait()
    rows = owner_ref.shape[1]
    live = iota((1, rows), 1) < counts_ref[0]
    owned = jnp.where(live, owner_ref[...], tiles)
    members = owned == iota((tiles, rows), 0)
    earlier = marks(iota((rows, rows), 0) < iota((rows, rows), 1))
    before = dot(marks(members), earlier)
    rank = jnp.sum(jnp.where(members, before, 0.0), axis=0, keepdims=True)
    slots_ref[...] = jnp.where(live, owned * capacity + rank.astype(jnp.int32), -1)
    fetches[1].wait()
    fetches[2].wait()
    for direction, sent_ref in zip(turns(bits_ref), (sent0, sent1, sent2, sent3)):
        sent_ref[...] = dot(chosen_rows(lists_ref, direction, rows), points_ref[...], TN).astype(bf16)


def turns(bits_ref):
    column, line = bits_ref[0], bits_ref[1]
    return 1 - column, column, 3 - line, 2 + line


def blocks(bits_ref):
    column, line = bits_ref[0], bits_ref[1]
    return column, 1 - column, 2 + line, 3 - line


def block_of(index, size, start=0):
    return pl.ds(pl.multiple_of(start + index * size, 16), size)


def chosen_rows(lists_ref, direction, rows):
    listed = lists_ref[pl.ds(direction, 1), :]
    return marks(iota((rows, listed.shape[1]), 0) == listed)


def pack_rows(slots_ref, rows_ref, packed_out, stage_ref, sems):
    slots = slots_ref[...]
    copies = []
    for at, start in enumerate(range(0, packed_out.shape[0], WIDE)):
        place = pl.ds(start, WIDE)
        stage_ref[place, :] = dot(mark_slots(slots, start, WIDE), rows_ref[...]).astype(bf16)
        copies.append(pltpu.make_async_copy(stage_ref.at[place], packed_out.at[place], sems.at[at]))
        copies[-1].start()
    for copy in copies:
        copy.wait()


def unpack_kernel(slots_ref, packed_ref, rows_ref):
    for start in range(0, rows_ref.shape[0], CHUNK):
        column = column_of(slots_ref[:, start : start + CHUNK], CHUNK)
        rows_ref[pl.ds(start, CHUNK), :] = dot(
            pick_rows(column, packed_ref.shape[0]), packed_ref[...]
        ).astype(bf16)


def count_kernel(near_ref, table_ref):
    neighbours, rows = near_ref.shape
    step = 16
    zero = jnp.zeros((step, LANES), bf16)
    one = jnp.ones((step, LANES), bf16)
    row_blocks = table_ref.shape[0] // CHUNK

    def rows_of(row_block, _):
        row_at = pl.multiple_of(row_block * CHUNK, CHUNK)

        def block(lane_block, _):
            lane_at = pl.multiple_of(lane_block * LANES, LANES)
            local = (near_ref[:, pl.ds(lane_at, LANES)] - row_at).astype(f32)
            spread = [
                jnp.broadcast_to(local[k : k + 1, :], (step, LANES)).astype(bf16)
                for k in range(neighbours)
            ]
            base = iota((step, LANES), 0).astype(f32)
            for inner in range(0, CHUNK, step):
                here = (base + float(inner)).astype(bf16)
                total = zero
                for k in range(neighbours):
                    total = total + jnp.where(spread[k] == here, one, zero)
                table_ref[pl.ds(row_at + inner, step), pl.ds(lane_at, LANES)] = total
            return 0

        lax.fori_loop(0, rows // LANES, block, 0)
        return 0

    lax.fori_loop(0, row_blocks, rows_of, 0)


def lift_kernel(
    bits_ref, slots_ref, points_ref, grad_ref, halo0, halo1, halo2, halo3, table_ref, w_ref,
    table_out, average_out, pre_out, packed_out,
    ext_ref, average_ref, pre_ref, both_ref, stage_ref, sems, pack_sems, *, neighbours
):
    width = points_ref.shape[1]
    keep_table = pltpu.make_async_copy(table_ref, table_out, sems.at[2])
    keep_table.start()
    rows = points_ref.shape[0]
    ext_ref[0:rows, :] = points_ref[...]
    for block, halo in zip(blocks(bits_ref), (halo0, halo1, halo2, halo3)):
        ext_ref[block_of(block, halo.shape[0], rows), :] = halo[...]
    average = (dot(ext_ref[...], table_ref[...], TN) * (1.0 / neighbours)).astype(bf16)
    average_ref[...] = average
    keep_average = pltpu.make_async_copy(average_ref, average_out, sems.at[0])
    keep_average.start()
    pre_ref[...] = dot(average, w_ref[...], TN)
    keep_pre = pltpu.make_async_copy(pre_ref, pre_out, sems.at[1])
    keep_pre.start()
    for row in range(0, points_ref.shape[0], BLOCK):
        here = pl.ds(row, BLOCK)
        both_ref[here, 0:width] = (
            points_ref[here, :].astype(f32) + gelu_tanh(pre_ref[here, :])
        ).astype(bf16)
    both_ref[:, width:] = grad_ref[...]
    pack_rows(slots_ref, both_ref, packed_out, stage_ref, pack_sems)
    keep_average.wait()
    keep_pre.wait()
    keep_table.wait()


def tile_back_kernel(
    bits_ref, slots_ref, back_ref, w_ref, table_in, average_in, pre_in,
    lifted_out, spread_out, near_ref, halo0, halo1, halo2, halo3,
    table_ref, average_ref, pre_ref, lifted_ref, act_ref, spread_ref, halo_ref, sems, *, neighbours
):
    rows = lifted_ref.shape[0]
    halo_rows = table_ref.shape[0]
    fetch_pre = pltpu.make_async_copy(pre_in, pre_ref, sems.at[0])
    fetch_average = pltpu.make_async_copy(average_in, average_ref, sems.at[1])
    fetch_table = pltpu.make_async_copy(table_in.at[pl.ds(rows, halo_rows)], table_ref, sems.at[2])
    fetch_pre.start()
    fetch_average.start()
    fetch_table.start()
    keep_lifted = pltpu.make_async_copy(lifted_ref, lifted_out, sems.at[3])
    keep_spread = pltpu.make_async_copy(spread_ref, spread_out, sems.at[4])
    for start in range(0, rows, CHUNK):
        column = column_of(slots_ref[:, start : start + CHUNK], CHUNK)
        wide = dot(pick_rows(column, back_ref.shape[0]), back_ref[...])
        if start == 0:
            fetch_pre.wait()
        for row in range(0, CHUNK, BLOCK):
            here = pl.ds(start + row, BLOCK)
            lifted_grad = wide[row : row + BLOCK]
            lifted_ref[here, :] = lifted_grad.astype(bf16)
            value = pre_ref[here, :]
            square, tangent = gelu_parts(value)
            act_ref[here, :] = (lifted_grad * slope_of(value, square, tangent)).astype(bf16)
    keep_lifted.start()
    spread_ref[...] = (dot(act_ref[...], w_ref[...], NT) * (1.0 / neighbours)).astype(bf16)
    keep_spread.start()
    fetch_average.wait()
    near_ref[...] = dot(average_ref[...], act_ref[...]).astype(near_ref.dtype)
    fetch_table.wait()
    halo_ref[...] = dot(table_ref[...], spread_ref[...]).astype(bf16)
    for block, back in zip(blocks(bits_ref), (halo0, halo1, halo2, halo3)):
        back[...] = halo_ref[block_of(block, back.shape[0]), :]
    keep_lifted.wait()
    keep_spread.wait()


def finish_kernel(
    bits_ref, lists_ref, back0, back1, back2, back3, table_in, spread_in, lifted_in,
    out_ref, came_ref, table_ref, spread_ref, lifted_ref, sems
):
    rows = out_ref.shape[0]
    fetch_spread = pltpu.make_async_copy(spread_in, spread_ref, sems.at[0])
    fetch_table = pltpu.make_async_copy(table_in.at[pl.ds(0, rows)], table_ref, sems.at[1])
    fetch_lifted = pltpu.make_async_copy(lifted_in, lifted_ref, sems.at[2])
    fetch_spread.start()
    fetch_table.start()
    fetch_lifted.start()
    for direction, back in zip(turns(bits_ref), (back0, back1, back2, back3)):
        came_ref[block_of(direction, back.shape[0]), :] = back[...]
    returned = dot(chosen_rows(lists_ref, 0, rows), came_ref[...])
    fetch_spread.wait()
    fetch_table.wait()
    fetch_lifted.wait()
    for start in range(0, rows, WIDE):
        here = pl.ds(start, WIDE)
        out_ref[here, :] = (
            lifted_ref[here, :].astype(f32)
            + dot(table_ref[here, :], spread_ref[...])
            + returned[start : start + WIDE]
        ).astype(bf16)


def near_sum_kernel(parts_ref, share_ref, *, share):
    rows = parts_ref.shape[0]
    same = lax.rem(iota((rows, rows), 0), share) == lax.rem(iota((rows, rows), 1), share)
    share_ref[...] = dot(marks(same), parts_ref[...]).astype(bf16)


def full_taps(conv_ref, groups, inner):
    width = groups * inner
    rows = conv_ref.shape[0]
    repeat = marks(lax.rem(iota((inner, width), 1), inner) == iota((inner, width), 0))
    wide = dot(conv_ref[...], repeat)
    row_group = lax.div(lax.rem(iota((rows, width), 0), width), inner)
    same = row_group == lax.div(iota((rows, width), 1), inner)
    return jnp.where(same, wide, 0.0).astype(bf16)


def padded_zeros(ref):
    edge = jnp.zeros((PAD, ref.shape[1]), f32)
    ref[0:PAD, :] = edge
    ref[PAD + PATCH :, :] = edge


def forward_kernel(
    zorder_ref, conv_ref, gain_one_ref, gain_two_ref, up_ref, down_ref, came_in,
    serial_out, state_out, back_out,
    lifted_ref, serial_ref, state_ref, taps_ref, normed_ref, before_ref, here_ref, after_ref, second_ref, hidden_ref,
    result_ref, stage_ref, sems, pack_sems, *, groups, inner
):
    slots, width = lifted_ref.shape
    fetch = pltpu.make_async_copy(came_in.at[:, pl.ds(0, width)], lifted_ref, sems.at[2, 0])
    fetch.start()
    hidden_width = up_ref.shape[1]
    taps_ref[...] = full_taps(conv_ref, groups, inner)

    def keep(at):
        place = pl.ds(at * PATCH, PATCH)
        return (
            pltpu.make_async_copy(serial_ref.at[place], serial_out.at[place], sems.at[0, at]),
            pltpu.make_async_copy(state_ref.at[place], state_out.at[place], sems.at[1, at]),
        )

    def patch(at):
        origin = at * PATCH
        normed_at, second_at, hidden_at = normed_ref.at[at], second_ref.at[at], hidden_ref.at[at]
        before_at, here_at, after_at = before_ref.at[at], here_ref.at[at], after_ref.at[at]
        padded_zeros(before_at)
        padded_zeros(after_at)
        for start in range(0, PATCH, WIDE):
            column = column_of(zorder_ref[:, origin + start : origin + start + WIDE], WIDE)
            wide = dot(pick_rows(column, slots), lifted_ref[...])
            for row in range(0, WIDE, BLOCK):
                serial = wide[row : row + BLOCK]
                serial_ref[pl.ds(origin + start + row, BLOCK), :] = serial.astype(bf16)
                normed = serial * inverse_rms(serial) * gain_one_ref[...]
                normed_at[pl.ds(start + row, BLOCK), :] = normed.astype(bf16)
            yield
        before_at[pl.ds(PAD, PATCH), :] = dot(normed_at[...], taps_ref[0:width, :])
        here_at[...] = dot(normed_at[...], taps_ref[width : 2 * width, :])
        after_at[pl.ds(PAD, PATCH), :] = dot(normed_at[...], taps_ref[2 * width :, :])
        yield
        for row in range(0, PATCH, BLOCK):
            place = pl.ds(origin + row, BLOCK)
            state = serial_ref[place, :].astype(f32) + (
                before_at[pl.ds(PAD + row - 1, BLOCK), :]
                + here_at[pl.ds(row, BLOCK), :]
                + after_at[pl.ds(PAD + row + 1, BLOCK), :]
            )
            state_ref[place, :] = state
            second = state * inverse_rms(state) * gain_two_ref[...]
            second_at[pl.ds(row, BLOCK), :] = second.astype(bf16)
        for copy in keep(at):
            copy.start()
        yield
        for start in range(0, PATCH, CHUNK):
            value = dot(second_at[pl.ds(start, CHUNK), :], up_ref[...])
            for row in range(0, CHUNK, 16):
                for col in range(0, hidden_width, 2 * LANES):
                    hidden_at[pl.ds(start + row, 16), pl.ds(col, 2 * LANES)] = gelu_tanh(
                        value[row : row + 16, col : col + 2 * LANES]
                    ).astype(bf16)
            if start + CHUNK == PATCH // 2:
                yield
        yield
        for start in range(0, PATCH, WIDE):
            place = pl.ds(origin + start, WIDE)
            result_ref[place, :] = (
                state_ref[place, :] + dot(hidden_at[pl.ds(start, WIDE), :], down_ref[...])
            ).astype(bf16)
        yield

    fetch.wait()
    waiting = [patch(at) for at in range(slots // PATCH)]
    running = []
    while waiting or running:
        if waiting:
            running.append(waiting.pop(0))
        running = [work for work in running if next(work, work) is not work]
    pack_rows(zorder_ref, result_ref, back_out, stage_ref, pack_sems)
    for at in range(slots // PATCH):
        for copy in keep(at):
            copy.wait()


def backward_kernel(
    bit_ref, zorder_ref, conv_ref, gain_one_ref, gain_two_ref, up_ref, down_ref, came_in, serial_in, state_in,
    back_out, keep_out, send_out,
    grad_ref, serial_ref, state_ref, out_grad_ref, serial_grad_ref, stage_ref, weights_ref, taps_ref,
    second_ref, hidden_ref, pre_grad_ref, state_grad_ref, mixed_ref, mixed_half_ref, before_ref, here_ref,
    after_ref, normed_ref, conv_sum_ref, gains_ref, sems, pack_sems, *, groups, inner
):
    slots, width = serial_ref.shape
    hidden_width = up_ref.shape[1]
    fetch_grad = pltpu.make_async_copy(came_in.at[:, pl.ds(width, width)], grad_ref, sems.at[0])
    fetch_state = pltpu.make_async_copy(state_in, state_ref, sems.at[1])
    fetch_serial = pltpu.make_async_copy(serial_in, serial_ref, sems.at[2])
    fetch_grad.start()
    fetch_state.start()
    fetch_serial.start()
    taps_ref[...] = full_taps(conv_ref, groups, inner)
    padded_zeros(before_ref)
    padded_zeros(after_ref)
    padded_zeros(mixed_ref)
    conv_sum_ref[...] = jnp.zeros_like(conv_sum_ref)
    gains_ref[...] = jnp.zeros_like(gains_ref)

    def patch(at, _):
        origin = pl.multiple_of(at * PATCH, PATCH)
        for start in range(0, PATCH, WIDE):
            column = column_of(zorder_ref[:, pl.ds(origin + start, WIDE)], WIDE)
            out_grad_ref[pl.ds(origin + start, WIDE), :] = dot(
                pick_rows(column, slots), grad_ref[...]
            ).astype(bf16)
        for start in range(0, PATCH, CHUNK):
            place = pl.ds(origin + start, CHUNK)
            for row in range(start, start + CHUNK, BLOCK):
                state = state_ref[pl.ds(origin + row, BLOCK), :]
                second = state * inverse_rms(state) * gain_two_ref[...]
                second_ref[pl.ds(origin + row, BLOCK), :] = second.astype(bf16)
            value_all = dot(second_ref[place, :], up_ref[...])
            hidden_grad_all = dot(out_grad_ref[place, :], down_ref[...], NT)
            for row in range(0, CHUNK, 16):
                for col in range(0, hidden_width, 2 * LANES):
                    value = value_all[row : row + 16, col : col + 2 * LANES]
                    hidden_grad = hidden_grad_all[row : row + 16, col : col + 2 * LANES]
                    square, tangent = gelu_parts(value)
                    half = 0.5 * value
                    piece = pl.ds(origin + start + row, 16), pl.ds(col, 2 * LANES)
                    hidden_ref[piece] = (half + half * tangent).astype(bf16)
                    pre_grad_ref[piece] = (
                        hidden_grad.astype(bf16).astype(f32) * slope_of(value, square, tangent)
                    ).astype(bf16)
            second_grad_all = dot(pre_grad_ref[place, :], up_ref[...], NT)
            for row in range(0, CHUNK, BLOCK):
                here = pl.ds(origin + start + row, BLOCK)
                state = state_ref[here, :]
                scale_two = inverse_rms(state)
                unit_two = state * scale_two
                second_grad = second_grad_all[row : row + BLOCK].astype(bf16).astype(f32)
                weighted = second_grad * gain_two_ref[...]
                product = second_grad * unit_two
                gains_ref[1:2, :] += jnp.sum(product, axis=0, keepdims=True)
                middle = jnp.mean(product * gain_two_ref[...], axis=-1, keepdims=True)
                state_grad = out_grad_ref[here, :].astype(f32) + scale_two * (weighted - unit_two * middle)
                state_grad_ref[pl.ds(start + row, BLOCK), :] = state_grad
                mixed_grad = state_grad.astype(bf16)
                mixed_half_ref[pl.ds(start + row, BLOCK), :] = mixed_grad
                mixed_ref[pl.ds(PAD + start + row, BLOCK), :] = mixed_grad.astype(f32)
        before_ref[pl.ds(PAD, PATCH), :] = dot(mixed_half_ref[...], taps_ref[0:width, :], NT)
        here_ref[...] = dot(mixed_half_ref[...], taps_ref[width : 2 * width, :], NT)
        after_ref[pl.ds(PAD, PATCH), :] = dot(mixed_half_ref[...], taps_ref[2 * width :, :], NT)
        for row in range(0, PATCH, BLOCK):
            place = pl.ds(origin + row, BLOCK)
            serial = serial_ref[place, :].astype(f32)
            scale_one = inverse_rms(serial)
            unit_one = serial * scale_one
            normed_ref[pl.ds(row, BLOCK), :] = (unit_one * gain_one_ref[...]).astype(bf16)
            normed_grad = (
                before_ref[pl.ds(PAD + row + 1, BLOCK), :]
                + here_ref[pl.ds(row, BLOCK), :]
                + after_ref[pl.ds(PAD + row - 1, BLOCK), :]
            ).astype(bf16).astype(f32)
            product = normed_grad * unit_one
            gains_ref[0:1, :] += jnp.sum(product, axis=0, keepdims=True)
            middle = jnp.mean(product * gain_one_ref[...], axis=-1, keepdims=True)
            weighted = normed_grad * gain_one_ref[...]
            serial_grad_ref[place, :] = (
                state_grad_ref[pl.ds(row, BLOCK), :] + scale_one * (weighted - unit_one * middle)
            ).astype(bf16)
        for tap in range(3):
            moved = mixed_ref[pl.ds(PAD + 1 - tap, PATCH), :].astype(bf16)
            conv_sum_ref[tap] += dot(normed_ref[...], moved, TN)
        return 0

    fetch_grad.wait()
    fetch_state.wait()
    fetch_serial.wait()
    lax.fori_loop(0, slots // PATCH, patch, 0)
    for start in range(0, hidden_width, width):
        block = slice(start, start + width)
        weights_ref[start : start + width, :] = jnp.transpose(
            dot(out_grad_ref[...], hidden_ref[:, block], TN)
        ).astype(bf16)
        weights_ref[hidden_width + start : hidden_width + start + width, :] = dot(
            second_ref[...], pre_grad_ref[:, block], TN
        ).astype(bf16)
    same = lax.div(iota((width, width), 0), inner) == lax.div(iota((width, width), 1), inner)
    for tap in range(3):
        kept = jnp.where(same, conv_sum_ref[tap], 0.0).reshape(groups, inner, width)
        at = 2 * hidden_width + tap * inner
        weights_ref[at : at + inner, :] = jnp.sum(kept, axis=0).astype(bf16)
    at = 2 * hidden_width + 3 * inner
    weights_ref[at : at + 16, :] = gains_ref[...].astype(bf16)
    at = at + 16
    weights_ref[at:, :] = jnp.zeros((weights_ref.shape[0] - at, width), bf16)
    half = keep_out.shape[0]
    bit = bit_ref[0]
    hand_out = [
        pltpu.make_async_copy(
            weights_ref.at[pl.ds(pl.multiple_of(at * half, 16), half)], out, sems.at[3 + which]
        )
        for which, (at, out) in enumerate(((bit, keep_out), (1 - bit, send_out)))
    ]
    for copy in hand_out:
        copy.start()
    pack_rows(zorder_ref, serial_grad_ref, back_out, stage_ref, pack_sems)
    for copy in hand_out:
        copy.wait()


def hold_kernel(rows_in, rows_out):
    pass


def split_rows(bit, rows, scratch_ref, keep_ref, send_ref):
    scratch_ref[...] = rows.astype(bf16)
    half = keep_ref.shape[0]
    keep_ref[...] = scratch_ref[pl.ds(pl.multiple_of(bit * half, 16), half), :]
    send_ref[...] = scratch_ref[pl.ds(pl.multiple_of((1 - bit) * half, 16), half), :]


def added(mine_ref, came_ref):
    return mine_ref[...].astype(f32) + came_ref[...].astype(f32)


def first_split_kernel(
    bit0_ref, bit1_ref, mine_ref, came_ref, keep0, send0, keep1, send1, scratch0, scratch1
):
    half = scratch0.shape[0]
    total = added(mine_ref, came_ref)
    split_rows(bit0_ref[0], total[:half], scratch0, keep0, send0)
    split_rows(bit1_ref[0], total[half:], scratch1, keep1, send1)


def next_split_kernel(
    bit0_ref, bit1_ref, mine0, came0, mine1, came1, keep0, send0, keep1, send1, scratch0, scratch1
):
    split_rows(bit0_ref[0], added(mine0, came0), scratch0, keep0, send0)
    split_rows(bit1_ref[0], added(mine1, came1), scratch1, keep1, send1)


def add_join_kernel(mine0, came0, mine1, came1, share_ref):
    half = mine0.shape[0]
    share_ref[0:half, :] = added(mine0, came0).astype(bf16)
    share_ref[half:, :] = added(mine1, came1).astype(bf16)


def add_kernel(mine_ref, came_ref, total_ref):
    total_ref[...] = added(mine_ref, came_ref).astype(bf16)


def join_kernel(bit_ref, mine_ref, came_ref, both_ref):
    half = mine_ref.shape[0]
    bit = bit_ref[0]
    both_ref[pl.ds(pl.multiple_of(bit * half, 16), half), :] = mine_ref[...]
    both_ref[pl.ds(pl.multiple_of((1 - bit) * half, 16), half), :] = came_ref[...]


def spread_kernel(
    bit_ref, mine_ref, came_ref, total_ref, up_ref, down_ref, conv_ref, gain_one_ref, gain_two_ref, near_ref,
    joined_ref, sums_ref, *, bits, scale
):
    join_kernel(bit_ref, mine_ref, came_ref, joined_ref)
    rows = sums_ref.shape[0]
    piece = (rows >> bits) // 2
    for at in range(1 << bits):
        digits = [(at >> (bits - 1 - bit)) & 1 for bit in range(bits)]
        for part, order in enumerate((digits[1:], digits[:0:-1])):
            place = 0
            for digit in order:
                place = 2 * place + digit
            start = digits[0] * (rows // 2) + part * (rows // 4) + place * piece
            source = (2 * at + part) * piece
            sums_ref[start : start + piece, :] = joined_ref[source : source + piece, :]
    width, hidden_width = up_ref.shape
    taps, groups, inner = conv_ref.shape[:3]
    down_ref[...] = sums_ref[0:hidden_width, :].astype(f32) * scale
    for start in range(0, hidden_width, width):
        up_ref[:, start : start + width] = (
            sums_ref[hidden_width + start : hidden_width + start + width, :].astype(f32) * scale
        )
    for tap in range(taps):
        at = 2 * hidden_width + tap * inner
        rows = sums_ref[at : at + inner, :].astype(f32) * scale
        for group in range(groups):
            conv_ref[tap, group] = rows[:, group * inner : (group + 1) * inner]
    at = 2 * hidden_width + taps * inner
    gains = sums_ref[at : at + 16, :].astype(f32) * scale
    gain_one_ref[...] = gains[0:1, :]
    gain_two_ref[...] = gains[1:2, :]
    near_ref[...] = total_ref[...].astype(f32) * scale


def call(kernel, outs, args, scratch=(), smem=0, flops=0, limit=16, held=0, stored=0, after=(), same=None, **static):
    moved = sum(math.prod(a.shape) * a.dtype.itemsize for a in (*args, *outs))
    specs = [pl.BlockSpec(memory_space=pltpu.SMEM)] * smem
    specs += [pl.BlockSpec(memory_space=pltpu.VMEM)] * (len(args) - smem - held)
    specs += [pl.BlockSpec(memory_space=pltpu.HBM)] * held
    specs += [pl.BlockSpec(memory_space=pltpu.HBM if a.shape[0] >= PATCH else pl.ANY) for a in after]
    after = [pltpu.with_memory_space_constraint(a, pltpu.HBM) if a.shape[0] >= PATCH else a for a in after]
    out_specs = [pl.BlockSpec(memory_space=pltpu.HBM)] * stored
    shapes = [pltpu.HBM(a.shape, a.dtype) for a in outs[:stored]] + list(outs[stored:])
    first_held = len(args) - held
    args = [*args[:first_held], *(pltpu.with_memory_space_constraint(a, pltpu.HBM) for a in args[first_held:])]
    out_specs += [pl.BlockSpec(memory_space=pltpu.VMEM)] * (len(outs) - stored)
    count = len(args)

    def run(*refs):
        kernel(*refs[:count], *refs[count + len(after) :], **static)

    return pl.pallas_call(
        run,
        out_shape=tuple(shapes),
        in_specs=specs,
        out_specs=tuple(out_specs),
        scratch_shapes=list(scratch),
        input_output_aliases=same or {},
        compiler_params=pltpu.CompilerParams(vmem_limit_bytes=limit * 1024 * 1024),
        cost_estimate=pl.CostEstimate(flops=int(flops), bytes_accessed=moved, transcendentals=0),
    )(*args, *after)


def shaped(*shape, dtype=bf16):
    return jax.ShapeDtypeStruct(shape, dtype)


def pairwise(first, second, axis):
    count = lax.axis_size(axis)
    pairs = [
        [pair for at in range(start, count - 1, 2) for pair in ((at, at + 1), (at + 1, at))] for start in (0, 1)
    ]
    return [lax.ppermute(rows, axis, pair) for rows, pair in zip((first, second), pairs)]


def partner(value, axis, step):
    return lax.ppermute(value, axis, [(at, at ^ step) for at in range(lax.axis_size(axis))])


def bit_of(axis, step):
    return lax.rem(lax.div(lax.axis_index(axis), step), 2).astype(jnp.int32).reshape(1)


def steps_of(axis):
    return [1 << at for at in range(int(math.log2(lax.axis_size(axis))))]


def sum_over_mesh(keep, send, early, late):
    width = keep.shape[1]
    steps = steps_of("ty")
    orders = steps[1:], steps[:0:-1]

    def halves(kernel, rows, at, args, **options):
        return call(
            kernel,
            [shaped(rows // 2, width)] * 4,
            [bit_of("ty", order[at]) for order in orders] + list(args),
            scratch=[pltpu.VMEM((rows, width), bf16)] * 2,
            smem=2,
            flops=1e6,
            **options,
        )

    came = partner(send, "ty", steps[0])
    rows = keep.shape[0] // 2
    parts = halves(first_split_kernel, rows, 0, [keep, came], after=early)
    for at in range(len(orders[0])):
        rows = rows // 2
        pairs = []
        for which, order in enumerate(orders):
            pairs += [parts[2 * which], partner(parts[2 * which + 1], "ty", order[at])]
        if at + 1 < len(orders[0]):
            parts = halves(next_split_kernel, rows, at + 1, pairs)
    (share,) = call(add_join_kernel, [shaped(2 * rows, width)], pairs, flops=1e6)
    for step in steps_of("tx"):
        (share,) = call(
            add_kernel,
            [shaped(*share.shape)],
            [share, partner(share, "tx", step)],
            after=late.pop(0) if late else (),
            flops=1e6,
        )
    for step in steps[:0:-1]:
        (share,) = call(
            join_kernel,
            [shaped(2 * share.shape[0], width)],
            [bit_of("ty", step), share, partner(share, "ty", step)],
            after=late.pop(0) if late else (),
            smem=1,
            flops=1e6,
        )
    return share, partner(share, "ty", steps[0])


def exchange(rows, tiles):
    return lax.all_to_all(rows, ("tx", "ty"), split_axis=0, concat_axis=0, tiled=True)


def body(
    points,
    counts,
    owner,
    zorder,
    border,
    near,
    w_near,
    gain_one,
    conv_w,
    gain_two,
    w_up,
    w_down,
    grad_out,
):
    points_tile = points[0]
    tile_rows, width = points_tile.shape
    border_rows = border.shape[2]
    edge = 4 * border_rows
    ext = tile_rows + edge
    lists = border[0]
    near_tile = near[0]
    neighbours = near_tile.shape[0]
    tiles = lax.axis_size("tx") * lax.axis_size("ty")
    slots_count = zorder.shape[1]
    capacity = slots_count // tiles
    taps, groups, inner = conv_w.shape[:3]
    conv_rows = conv_w.reshape(taps * groups * inner, inner)
    gain_one_row = gain_one.reshape(1, width)
    gain_two_row = gain_two.reshape(1, width)
    hidden = w_up.shape[1]

    bits = jnp.concatenate([bit_of("tx", 1), bit_of("ty", 1)])
    slots, *sent = call(
        route_kernel,
        [shaped(1, tile_rows, dtype=jnp.int32)] + [shaped(border_rows, width)] * 4,
        [bits, counts, owner, lists, points_tile],
        scratch=[
            pltpu.VMEM((1, tile_rows), jnp.int32),
            pltpu.VMEM((4, border_rows), jnp.int32),
            pltpu.VMEM((tile_rows, width), bf16),
            pltpu.SemaphoreType.DMA((3,)),
        ],
        smem=2,
        held=3,
        flops=4e9,
        tiles=tiles,
        capacity=capacity,
    )
    halos = pairwise(sent[0], sent[1], "tx") + pairwise(sent[2], sent[3], "ty")
    (table,) = call(count_kernel, [shaped(ext, tile_rows)], [near_tile], flops=8e9)
    kept_table, average, pre_act, packed = call(
        lift_kernel,
        [
            shaped(ext, tile_rows),
            shaped(width, tile_rows),
            shaped(tile_rows, width, dtype=f32),
            shaped(slots_count, 2 * width),
        ],
        [bits, slots, points_tile, grad_out[0], *halos, table, w_near],
        smem=1,
        scratch=[
            pltpu.VMEM((ext, width), bf16),
            pltpu.VMEM((width, tile_rows), bf16),
            pltpu.VMEM((tile_rows, width), f32),
            pltpu.VMEM((tile_rows, 2 * width), bf16),
            pltpu.VMEM((slots_count, 2 * width), bf16),
            pltpu.SemaphoreType.DMA((3,)),
            pltpu.SemaphoreType.DMA((slots_count // WIDE,)),
        ],
        flops=4e9,
        stored=4,
        neighbours=neighbours,
    )
    came = exchange(packed, tiles)
    patches = slots_count // PATCH
    patch_scratch = [
        pltpu.VMEM((PATCH + 2 * PAD, width), f32),
        pltpu.VMEM((PATCH, width), f32),
        pltpu.VMEM((PATCH + 2 * PAD, width), f32),
    ]
    serial, state, back_result = call(
        forward_kernel,
        [
            shaped(slots_count, width),
            shaped(slots_count, width, dtype=f32),
            shaped(slots_count, width),
        ],
        [zorder, conv_rows, gain_one_row, gain_two_row, w_up, w_down, came],
        held=1,
        scratch=[
            pltpu.VMEM((slots_count, width), bf16),
            pltpu.VMEM((slots_count, width), bf16),
            pltpu.VMEM((slots_count, width), f32),
            pltpu.VMEM((taps * width, width), bf16),
            pltpu.VMEM((patches, PATCH, width), bf16),
            pltpu.VMEM((patches, PATCH + 2 * PAD, width), f32),
            pltpu.VMEM((patches, PATCH, width), f32),
            pltpu.VMEM((patches, PATCH + 2 * PAD, width), f32),
            pltpu.VMEM((patches, PATCH, width), bf16),
            pltpu.VMEM((patches, PATCH, hidden), bf16),
            pltpu.VMEM((slots_count, width), bf16),
            pltpu.VMEM((slots_count, width), bf16),
            pltpu.SemaphoreType.DMA((3, slots_count // PATCH)),
            pltpu.SemaphoreType.DMA((slots_count // WIDE,)),
        ],
        flops=10e9,
        limit=44,
        stored=3,
        groups=groups,
        inner=inner,
    )
    came_result = exchange(back_result, tiles)
    lines = lax.axis_size("ty")
    sums_rows = 2 * hidden + taps * inner + 16
    sums_rows = -(-sums_rows // (32 * lines)) * (32 * lines)
    back_grad, keep, send = call(
        backward_kernel,
        [
            shaped(slots_count, width),
            shaped(sums_rows // 2, width),
            shaped(sums_rows // 2, width),
        ],
        [
            bit_of("ty", 1),
            zorder,
            conv_rows,
            gain_one_row,
            gain_two_row,
            w_up,
            w_down,
            came,
            serial,
            state,
        ],
        held=3,
        scratch=[
            pltpu.VMEM((slots_count, width), bf16),
            pltpu.VMEM((slots_count, width), bf16),
            pltpu.VMEM((slots_count, width), f32),
            pltpu.VMEM((slots_count, width), bf16),
            pltpu.VMEM((slots_count, width), bf16),
            pltpu.VMEM((slots_count, width), bf16),
            pltpu.VMEM((sums_rows, width), bf16),
            pltpu.VMEM((taps * width, width), bf16),
            pltpu.VMEM((slots_count, width), bf16),
            pltpu.VMEM((slots_count, hidden), bf16),
            pltpu.VMEM((slots_count, hidden), bf16),
            pltpu.VMEM((PATCH, width), f32),
            pltpu.VMEM((PATCH + 2 * PAD, width), f32),
            pltpu.VMEM((PATCH, width), bf16),
            *patch_scratch,
            pltpu.VMEM((PATCH, width), bf16),
            pltpu.VMEM((taps, width, width), f32),
            pltpu.VMEM((16, width), f32),
            pltpu.SemaphoreType.DMA((5,)),
            pltpu.SemaphoreType.DMA((slots_count // WIDE,)),
        ],
        stored=3,
        smem=1,
        flops=40e9,
        limit=44,
        groups=groups,
        inner=inner,
    )
    (back_grad,) = call(
        hold_kernel,
        [shaped(slots_count, width)],
        [back_grad],
        after=[came_result.reshape(tiles, capacity, width)],
        held=1,
        stored=1,
        same={0: 0},
    )
    came_back = exchange(back_grad, tiles)
    (out_rows,) = call(
        unpack_kernel, [shaped(tile_rows, width)], [slots, came_result], flops=4e9
    )
    lifted_grad, spread, near_grad, *halo_grad = call(
        tile_back_kernel,
        [shaped(tile_rows, width), shaped(tile_rows, width), shaped(width, width)]
        + [shaped(border_rows, width)] * 4,
        [bits, slots, came_back, w_near, kept_table, average, pre_act],
        smem=1,
        after=[out_rows],
        scratch=[
            pltpu.VMEM((edge, tile_rows), bf16),
            pltpu.VMEM((width, tile_rows), bf16),
            pltpu.VMEM((tile_rows, width), f32),
            pltpu.VMEM((tile_rows, width), bf16),
            pltpu.VMEM((tile_rows, width), bf16),
            pltpu.VMEM((tile_rows, width), bf16),
            pltpu.VMEM((edge, width), bf16),
            pltpu.SemaphoreType.DMA((5,)),
        ],
        flops=6e9,
        limit=24,
        held=3,
        stored=2,
        neighbours=neighbours,
    )
    returned = pairwise(halo_grad[0], halo_grad[1], "tx") + pairwise(halo_grad[2], halo_grad[3], "ty")
    (near_share,) = call(
        near_sum_kernel,
        [shaped(width, width)],
        [exchange(near_grad, tiles)],
        after=returned[:2],
        flops=1e6,
        share=width // tiles,
    )
    near_total = exchange(near_share, tiles)
    totals = sum_over_mesh(
        keep, send, [out_rows], [[near_grad], returned[:2], [near_share], [near_total, *returned[2:]]]
    )
    (grad_points,) = call(
        finish_kernel,
        [shaped(tile_rows, width)],
        [bits, border.reshape(1, edge), *returned, kept_table, spread, lifted_grad],
        smem=1,
        scratch=[
            pltpu.VMEM((edge, width), bf16),
            pltpu.VMEM((tile_rows, tile_rows), bf16),
            pltpu.VMEM((tile_rows, width), bf16),
            pltpu.VMEM((tile_rows, width), bf16),
            pltpu.SemaphoreType.DMA((3,)),
        ],
        held=3,
        flops=1e9,
    )
    scale = 1.0 / math.sqrt(tiles * tile_rows)
    up_sum, down_sum, conv_sum, gain_one_sum, gain_two_sum, near_sum = call(
        spread_kernel,
        [
            shaped(width, hidden, dtype=f32),
            shaped(hidden, width, dtype=f32),
            shaped(*conv_w.shape, dtype=f32),
            shaped(1, width, dtype=f32),
            shaped(1, width, dtype=f32),
            shaped(width, width, dtype=f32),
        ],
        [bit_of("ty", 1), *totals, near_total],
        scratch=[pltpu.VMEM((sums_rows, width), bf16)] * 2,
        smem=1,
        flops=1e6,
        bits=len(steps_of("ty")),
        scale=scale,
    )
    return (
        out_rows[None],
        grad_points[None],
        near_sum,
        gain_one_sum[0],
        conv_sum,
        gain_two_sum[0],
        up_sum,
        down_sum,
    )


def solution(mesh):
    placed = (
        P(("tx", "ty"), None, None),
        P(("tx", "ty")),
        P(("tx", "ty"), None),
        P(("tx", "ty"), None),
        P(("tx", "ty"), None, None),
        P(("tx", "ty"), None, None),
        P(),
        P(),
        P(),
        P(),
        P(),
        P(),
        P(("tx", "ty"), None, None),
    )
    return jax.shard_map(
        body,
        mesh=mesh,
        in_specs=placed,
        out_specs=(
            P(("tx", "ty"), None, None),
            P(("tx", "ty"), None, None),
            P(),
            P(),
            P(),
            P(),
            P(),
            P(),
        ),
        check_vma=False,
    )
```

```python
import math

import jax
import jax.numpy as jnp
from jax import lax
from jax.experimental import pallas as pl
from jax.experimental.pallas import tpu as pltpu
from jax.sharding import PartitionSpec as P

PATCH = 1024
CHUNK = 256
WIDE = 512
BLOCK = 64
LANES = 128
PAD = 8

eps_norm = 1e-06
gelu_coef = 0.7978845608028654
cubic_coef = 0.044715

bf16 = jnp.bfloat16
f32 = jnp.float32
NN = (((1,), (0,)), ((), ()))
NT = (((1,), (1,)), ((), ()))
TN = (((0,), (0,)), ((), ()))


def dot(left, right, dims=NN):
    return lax.dot_general(left, right, dims, preferred_element_type=f32)


def iota(shape, axis):
    return lax.broadcasted_iota(jnp.int32, shape, axis)


def marks(mask):
    return jnp.where(mask, 1.0, 0.0).astype(bf16)


def gelu_parts(value):
    square = value * value
    tangent = jnp.tanh(value * (gelu_coef + (gelu_coef * cubic_coef) * square))
    return square, tangent


def gelu_tanh(value):
    _, tangent = gelu_parts(value)
    half = 0.5 * value
    return half + half * tangent


def slope_of(value, square, tangent):
    inner_slope = gelu_coef + (3.0 * gelu_coef * cubic_coef) * square
    return 0.5 * (1.0 + tangent) + (0.5 * value) * (1.0 - tangent * tangent) * inner_slope


def inverse_rms(value):
    return lax.rsqrt(jnp.mean(value * value, axis=-1, keepdims=True) + eps_norm)


def column_of(row, count):
    return jnp.transpose(jnp.broadcast_to(row, (LANES, count)))


def pick_rows(column, depth):
    count = column.shape[0]
    lane = iota((count, LANES), 1)
    return jnp.concatenate(
        [marks(column == lane + base) for base in range(0, depth, LANES)], axis=1
    )


def mark_slots(row, start, count):
    return marks(iota((count, row.shape[1]), 0) + start == row)


def route_kernel(
    bits_ref, counts_ref, owner_in, lists_in, points_in, slots_ref, sent0, sent1, sent2, sent3,
    owner_ref, lists_ref, points_ref, sems, *, tiles, capacity
):
    fetches = [
        pltpu.make_async_copy(source, target, sems.at[at])
        for at, (source, target) in enumerate(
            ((owner_in, owner_ref), (lists_in, lists_ref), (points_in, points_ref))
        )
    ]
    for fetch in fetches:
        fetch.start()
    fetches[0].wait()
    rows = owner_ref.shape[1]
    live = iota((1, rows), 1) < counts_ref[0]
    owned = jnp.where(live, owner_ref[...], tiles)
    members = owned == iota((tiles, rows), 0)
    earlier = marks(iota((rows, rows), 0) < iota((rows, rows), 1))
    before = dot(marks(members), earlier)
    rank = jnp.sum(jnp.where(members, before, 0.0), axis=0, keepdims=True)
    slots_ref[...] = jnp.where(live, owned * capacity + rank.astype(jnp.int32), -1)
    fetches[1].wait()
    fetches[2].wait()
    for direction, sent_ref in zip(turns(bits_ref), (sent0, sent1, sent2, sent3)):
        sent_ref[...] = dot(chosen_rows(lists_ref, direction, rows), points_ref[...], TN).astype(bf16)


def turns(bits_ref):
    column, line = bits_ref[0], bits_ref[1]
    return 1 - column, column, 3 - line, 2 + line


def swapped(bits_ref, rows):
    column, line = bits_ref[0] == 0, bits_ref[1] == 0
    first, second, third, fourth = rows
    return [
        jnp.where(column, first, second),
        jnp.where(column, second, first),
        jnp.where(line, third, fourth),
        jnp.where(line, fourth, third),
    ]


def chosen_rows(lists_ref, direction, rows):
    listed = lists_ref[pl.ds(direction, 1), :]
    return marks(iota((rows, listed.shape[1]), 0) == listed)


def pack_rows(slots_ref, rows_ref, packed_out, stage_ref, sems):
    slots = slots_ref[...]
    copies = []
    for at, start in enumerate(range(0, packed_out.shape[0], WIDE)):
        place = pl.ds(start, WIDE)
        stage_ref[place, :] = dot(mark_slots(slots, start, WIDE), rows_ref[...]).astype(bf16)
        copies.append(pltpu.make_async_copy(stage_ref.at[place], packed_out.at[place], sems.at[at]))
        copies[-1].start()
    for copy in copies:
        copy.wait()


def unpack_kernel(slots_ref, packed_ref, rows_ref):
    for start in range(0, rows_ref.shape[0], CHUNK):
        column = column_of(slots_ref[:, start : start + CHUNK], CHUNK)
        rows_ref[pl.ds(start, CHUNK), :] = dot(
            pick_rows(column, packed_ref.shape[0]), packed_ref[...]
        ).astype(bf16)


def count_kernel(near_ref, kept_ref, table_ref, sems):
    neighbours, rows = near_ref.shape
    step = 16
    zero = jnp.zeros((step, LANES), bf16)
    one = jnp.ones((step, LANES), bf16)
    row_blocks = table_ref.shape[0] // CHUNK

    def copy_out(row_block):
        place = pl.ds(pl.multiple_of(row_block * CHUNK, CHUNK), CHUNK)
        return pltpu.make_async_copy(table_ref.at[place], kept_ref.at[place], sems.at[row_block])

    def rows_of(row_block, _):
        row_at = pl.multiple_of(row_block * CHUNK, CHUNK)

        def block(lane_block, _):
            lane_at = pl.multiple_of(lane_block * LANES, LANES)
            local = (near_ref[:, pl.ds(lane_at, LANES)] - row_at).astype(f32)
            spread = [
                jnp.broadcast_to(local[k : k + 1, :], (step, LANES)).astype(bf16)
                for k in range(neighbours)
            ]
            base = iota((step, LANES), 0).astype(f32)
            for inner in range(0, CHUNK, step):
                here = (base + float(inner)).astype(bf16)
                total = zero
                for k in range(neighbours):
                    total = total + jnp.where(spread[k] == here, one, zero)
                table_ref[pl.ds(row_at + inner, step), pl.ds(lane_at, LANES)] = total
            return 0

        lax.fori_loop(0, rows // LANES, block, 0)
        copy_out(row_block).start()
        return 0

    lax.fori_loop(0, row_blocks, rows_of, 0)
    for row_block in range(row_blocks):
        copy_out(row_block).wait()


def lift_kernel(
    bits_ref, slots_ref, points_ref, grad_ref, halo0, halo1, halo2, halo3, table_ref, w_ref,
    average_out, pre_out, packed_out,
    average_ref, pre_ref, both_ref, stage_ref, sems, pack_sems, *, neighbours
):
    width = points_ref.shape[1]
    halo = swapped(bits_ref, [halo0[...], halo1[...], halo2[...], halo3[...]])
    ext = jnp.concatenate([points_ref[...], *halo], axis=0)
    average = (dot(ext, table_ref[...], TN) * (1.0 / neighbours)).astype(bf16)
    average_ref[...] = average
    keep_average = pltpu.make_async_copy(average_ref, average_out, sems.at[0])
    keep_average.start()
    pre_ref[...] = dot(average, w_ref[...], TN)
    keep_pre = pltpu.make_async_copy(pre_ref, pre_out, sems.at[1])
    keep_pre.start()
    for row in range(0, points_ref.shape[0], BLOCK):
        here = pl.ds(row, BLOCK)
        both_ref[here, 0:width] = (
            points_ref[here, :].astype(f32) + gelu_tanh(pre_ref[here, :])
        ).astype(bf16)
    both_ref[:, width:] = grad_ref[...]
    pack_rows(slots_ref, both_ref, packed_out, stage_ref, pack_sems)
    keep_average.wait()
    keep_pre.wait()


def tile_back_kernel(
    bits_ref, slots_ref, back_ref, w_ref, table_in, average_in, pre_in,
    lifted_out, spread_out, near_ref, halo0, halo1, halo2, halo3,
    table_ref, average_ref, pre_ref, lifted_ref, act_ref, spread_ref, sems, *, neighbours
):
    rows = lifted_ref.shape[0]
    halo_rows = table_ref.shape[0]
    fetch_pre = pltpu.make_async_copy(pre_in, pre_ref, sems.at[0])
    fetch_average = pltpu.make_async_copy(average_in, average_ref, sems.at[1])
    fetch_table = pltpu.make_async_copy(table_in.at[pl.ds(rows, halo_rows)], table_ref, sems.at[2])
    fetch_pre.start()
    fetch_average.start()
    fetch_table.start()
    keep_lifted = pltpu.make_async_copy(lifted_ref, lifted_out, sems.at[3])
    keep_spread = pltpu.make_async_copy(spread_ref, spread_out, sems.at[4])
    for start in range(0, rows, CHUNK):
        column = column_of(slots_ref[:, start : start + CHUNK], CHUNK)
        wide = dot(pick_rows(column, back_ref.shape[0]), back_ref[...])
        if start == 0:
            fetch_pre.wait()
        for row in range(0, CHUNK, BLOCK):
            here = pl.ds(start + row, BLOCK)
            lifted_grad = wide[row : row + BLOCK]
            lifted_ref[here, :] = lifted_grad.astype(bf16)
            value = pre_ref[here, :]
            square, tangent = gelu_parts(value)
            act_ref[here, :] = (lifted_grad * slope_of(value, square, tangent)).astype(bf16)
    keep_lifted.start()
    spread_ref[...] = (dot(act_ref[...], w_ref[...], NT) * (1.0 / neighbours)).astype(bf16)
    keep_spread.start()
    fetch_average.wait()
    near_ref[...] = dot(average_ref[...], act_ref[...]).astype(near_ref.dtype)
    fetch_table.wait()
    halo = dot(table_ref[...], spread_ref[...])
    size = halo0.shape[0]
    parts = swapped(bits_ref, [halo[at * size : (at + 1) * size] for at in range(4)])
    for part, back in zip(parts, (halo0, halo1, halo2, halo3)):
        back[...] = part.astype(bf16)
    keep_lifted.wait()
    keep_spread.wait()


def finish_kernel(
    bits_ref, lists_ref, back0, back1, back2, back3, table_in, spread_in, lifted_in,
    out_ref, table_ref, spread_ref, lifted_ref, sems
):
    rows = out_ref.shape[0]
    fetch_spread = pltpu.make_async_copy(spread_in, spread_ref, sems.at[0])
    fetch_table = pltpu.make_async_copy(table_in.at[pl.ds(0, rows)], table_ref, sems.at[1])
    fetch_lifted = pltpu.make_async_copy(lifted_in, lifted_ref, sems.at[2])
    fetch_spread.start()
    fetch_table.start()
    fetch_lifted.start()
    came = swapped(bits_ref, [back1[...], back0[...], back3[...], back2[...]])
    returned = dot(chosen_rows(lists_ref, 0, rows), jnp.concatenate(came, axis=0))
    fetch_spread.wait()
    fetch_table.wait()
    fetch_lifted.wait()
    for start in range(0, rows, WIDE):
        here = pl.ds(start, WIDE)
        out_ref[here, :] = (
            lifted_ref[here, :].astype(f32)
            + dot(table_ref[here, :], spread_ref[...])
            + returned[start : start + WIDE]
        ).astype(bf16)


def near_sum_kernel(parts_ref, share_ref, *, share):
    rows = parts_ref.shape[0]
    same = lax.rem(iota((rows, rows), 0), share) == lax.rem(iota((rows, rows), 1), share)
    share_ref[...] = dot(marks(same), parts_ref[...]).astype(bf16)


def full_taps(conv_ref, groups, inner):
    width = groups * inner
    rows = conv_ref.shape[0]
    repeat = marks(lax.rem(iota((inner, width), 1), inner) == iota((inner, width), 0))
    wide = dot(conv_ref[...], repeat)
    row_group = lax.div(lax.rem(iota((rows, width), 0), width), inner)
    same = row_group == lax.div(iota((rows, width), 1), inner)
    return jnp.where(same, wide, 0.0).astype(bf16)


def padded_zeros(ref):
    edge = jnp.zeros((PAD, ref.shape[1]), f32)
    ref[0:PAD, :] = edge
    ref[PAD + PATCH :, :] = edge


def forward_kernel(
    zorder_ref, conv_ref, gain_one_ref, gain_two_ref, up_ref, down_ref, came_in,
    serial_out, state_out, back_out,
    lifted_ref, serial_ref, state_ref, taps_ref, normed_ref, before_ref, here_ref, after_ref, second_ref, hidden_ref,
    result_ref, stage_ref, sems, pack_sems, *, groups, inner
):
    slots, width = lifted_ref.shape
    fetch = pltpu.make_async_copy(came_in.at[:, pl.ds(0, width)], lifted_ref, sems.at[2, 0])
    fetch.start()
    hidden_width = up_ref.shape[1]
    taps_ref[...] = full_taps(conv_ref, groups, inner)

    def keep(at):
        place = pl.ds(at * PATCH, PATCH)
        return (
            pltpu.make_async_copy(serial_ref.at[place], serial_out.at[place], sems.at[0, at]),
            pltpu.make_async_copy(state_ref.at[place], state_out.at[place], sems.at[1, at]),
        )

    def patch(at):
        origin = at * PATCH
        normed_at, second_at, hidden_at = normed_ref.at[at], second_ref.at[at], hidden_ref.at[at]
        before_at, here_at, after_at = before_ref.at[at], here_ref.at[at], after_ref.at[at]
        padded_zeros(before_at)
        padded_zeros(after_at)
        for start in range(0, PATCH, WIDE):
            column = column_of(zorder_ref[:, origin + start : origin + start + WIDE], WIDE)
            wide = dot(pick_rows(column, slots), lifted_ref[...])
            for row in range(0, WIDE, BLOCK):
                serial = wide[row : row + BLOCK]
                serial_ref[pl.ds(origin + start + row, BLOCK), :] = serial.astype(bf16)
                normed = serial * inverse_rms(serial) * gain_one_ref[...]
                normed_at[pl.ds(start + row, BLOCK), :] = normed.astype(bf16)
            yield
        before_at[pl.ds(PAD, PATCH), :] = dot(normed_at[...], taps_ref[0:width, :])
        here_at[...] = dot(normed_at[...], taps_ref[width : 2 * width, :])
        after_at[pl.ds(PAD, PATCH), :] = dot(normed_at[...], taps_ref[2 * width :, :])
        yield
        for row in range(0, PATCH, BLOCK):
            place = pl.ds(origin + row, BLOCK)
            state = serial_ref[place, :].astype(f32) + (
                before_at[pl.ds(PAD + row - 1, BLOCK), :]
                + here_at[pl.ds(row, BLOCK), :]
                + after_at[pl.ds(PAD + row + 1, BLOCK), :]
            )
            state_ref[place, :] = state
            second = state * inverse_rms(state) * gain_two_ref[...]
            second_at[pl.ds(row, BLOCK), :] = second.astype(bf16)
        for copy in keep(at):
            copy.start()
        yield
        for start in range(0, PATCH, CHUNK):
            value = dot(second_at[pl.ds(start, CHUNK), :], up_ref[...])
            for row in range(0, CHUNK, 16):
                for col in range(0, hidden_width, 2 * LANES):
                    hidden_at[pl.ds(start + row, 16), pl.ds(col, 2 * LANES)] = gelu_tanh(
                        value[row : row + 16, col : col + 2 * LANES]
                    ).astype(bf16)
            if start + CHUNK == PATCH // 2:
                yield
        yield
        for start in range(0, PATCH, WIDE):
            place = pl.ds(origin + start, WIDE)
            result_ref[place, :] = (
                state_ref[place, :] + dot(hidden_at[pl.ds(start, WIDE), :], down_ref[...])
            ).astype(bf16)
        yield

    fetch.wait()
    waiting = [patch(at) for at in range(slots // PATCH)]
    running = []
    while waiting or running:
        if waiting:
            running.append(waiting.pop(0))
        running = [work for work in running if next(work, work) is not work]
    pack_rows(zorder_ref, result_ref, back_out, stage_ref, pack_sems)
    for at in range(slots // PATCH):
        for copy in keep(at):
            copy.wait()


def backward_kernel(
    bit_ref, zorder_ref, conv_ref, gain_one_ref, gain_two_ref, up_ref, down_ref, came_in, serial_in, state_in,
    back_out, keep_out, send_out,
    grad_ref, serial_ref, state_ref, out_grad_ref, serial_grad_ref, stage_ref, weights_ref, taps_ref,
    second_ref, hidden_ref, pre_grad_ref, state_grad_ref, mixed_ref, mixed_half_ref, before_ref, here_ref,
    after_ref, normed_ref, conv_sum_ref, gains_ref, sems, pack_sems, *, groups, inner
):
    slots, width = serial_ref.shape
    hidden_width = up_ref.shape[1]
    fetch_grad = pltpu.make_async_copy(came_in.at[:, pl.ds(width, width)], grad_ref, sems.at[0])
    fetch_state = pltpu.make_async_copy(state_in, state_ref, sems.at[1])
    fetch_serial = pltpu.make_async_copy(serial_in, serial_ref, sems.at[2])
    fetch_grad.start()
    fetch_state.start()
    fetch_serial.start()
    taps_ref[...] = full_taps(conv_ref, groups, inner)
    padded_zeros(before_ref)
    padded_zeros(after_ref)
    padded_zeros(mixed_ref)
    conv_sum_ref[...] = jnp.zeros_like(conv_sum_ref)
    gains_ref[...] = jnp.zeros_like(gains_ref)

    def patch(at, _):
        origin = pl.multiple_of(at * PATCH, PATCH)
        for start in range(0, PATCH, WIDE):
            column = column_of(zorder_ref[:, pl.ds(origin + start, WIDE)], WIDE)
            out_grad_ref[pl.ds(origin + start, WIDE), :] = dot(
                pick_rows(column, slots), grad_ref[...]
            ).astype(bf16)
        for start in range(0, PATCH, CHUNK):
            place = pl.ds(origin + start, CHUNK)
            for row in range(start, start + CHUNK, BLOCK):
                state = state_ref[pl.ds(origin + row, BLOCK), :]
                second = state * inverse_rms(state) * gain_two_ref[...]
                second_ref[pl.ds(origin + row, BLOCK), :] = second.astype(bf16)
            value_all = dot(second_ref[place, :], up_ref[...])
            hidden_grad_all = dot(out_grad_ref[place, :], down_ref[...], NT)
            for row in range(0, CHUNK, 16):
                for col in range(0, hidden_width, 2 * LANES):
                    value = value_all[row : row + 16, col : col + 2 * LANES]
                    hidden_grad = hidden_grad_all[row : row + 16, col : col + 2 * LANES]
                    square, tangent = gelu_parts(value)
                    half = 0.5 * value
                    piece = pl.ds(origin + start + row, 16), pl.ds(col, 2 * LANES)
                    hidden_ref[piece] = (half + half * tangent).astype(bf16)
                    pre_grad_ref[piece] = (
                        hidden_grad.astype(bf16).astype(f32) * slope_of(value, square, tangent)
                    ).astype(bf16)
            second_grad_all = dot(pre_grad_ref[place, :], up_ref[...], NT)
            for row in range(0, CHUNK, BLOCK):
                here = pl.ds(origin + start + row, BLOCK)
                state = state_ref[here, :]
                scale_two = inverse_rms(state)
                unit_two = state * scale_two
                second_grad = second_grad_all[row : row + BLOCK].astype(bf16).astype(f32)
                weighted = second_grad * gain_two_ref[...]
                product = second_grad * unit_two
                gains_ref[1:2, :] += jnp.sum(product, axis=0, keepdims=True)
                middle = jnp.mean(product * gain_two_ref[...], axis=-1, keepdims=True)
                state_grad = out_grad_ref[here, :].astype(f32) + scale_two * (weighted - unit_two * middle)
                state_grad_ref[pl.ds(start + row, BLOCK), :] = state_grad
                mixed_grad = state_grad.astype(bf16)
                mixed_half_ref[pl.ds(start + row, BLOCK), :] = mixed_grad
                mixed_ref[pl.ds(PAD + start + row, BLOCK), :] = mixed_grad.astype(f32)
        before_ref[pl.ds(PAD, PATCH), :] = dot(mixed_half_ref[...], taps_ref[0:width, :], NT)
        here_ref[...] = dot(mixed_half_ref[...], taps_ref[width : 2 * width, :], NT)
        after_ref[pl.ds(PAD, PATCH), :] = dot(mixed_half_ref[...], taps_ref[2 * width :, :], NT)
        for row in range(0, PATCH, BLOCK):
            place = pl.ds(origin + row, BLOCK)
            serial = serial_ref[place, :].astype(f32)
            scale_one = inverse_rms(serial)
            unit_one = serial * scale_one
            normed_ref[pl.ds(row, BLOCK), :] = (unit_one * gain_one_ref[...]).astype(bf16)
            normed_grad = (
                before_ref[pl.ds(PAD + row + 1, BLOCK), :]
                + here_ref[pl.ds(row, BLOCK), :]
                + after_ref[pl.ds(PAD + row - 1, BLOCK), :]
            ).astype(bf16).astype(f32)
            product = normed_grad * unit_one
            gains_ref[0:1, :] += jnp.sum(product, axis=0, keepdims=True)
            middle = jnp.mean(product * gain_one_ref[...], axis=-1, keepdims=True)
            weighted = normed_grad * gain_one_ref[...]
            serial_grad_ref[place, :] = (
                state_grad_ref[pl.ds(row, BLOCK), :] + scale_one * (weighted - unit_one * middle)
            ).astype(bf16)
        for tap in range(3):
            moved = mixed_ref[pl.ds(PAD + 1 - tap, PATCH), :].astype(bf16)
            conv_sum_ref[tap] += dot(normed_ref[...], moved, TN)
        return 0

    fetch_grad.wait()
    fetch_state.wait()
    fetch_serial.wait()
    lax.fori_loop(0, slots // PATCH, patch, 0)
    for start in range(0, hidden_width, width):
        block = slice(start, start + width)
        weights_ref[start : start + width, :] = jnp.transpose(
            dot(out_grad_ref[...], hidden_ref[:, block], TN)
        ).astype(bf16)
        weights_ref[hidden_width + start : hidden_width + start + width, :] = dot(
            second_ref[...], pre_grad_ref[:, block], TN
        ).astype(bf16)
    same = lax.div(iota((width, width), 0), inner) == lax.div(iota((width, width), 1), inner)
    for tap in range(3):
        kept = jnp.where(same, conv_sum_ref[tap], 0.0).reshape(groups, inner, width)
        at = 2 * hidden_width + tap * inner
        weights_ref[at : at + inner, :] = jnp.sum(kept, axis=0).astype(bf16)
    at = 2 * hidden_width + 3 * inner
    weights_ref[at : at + 16, :] = gains_ref[...].astype(bf16)
    at = at + 16
    weights_ref[at:, :] = jnp.zeros((weights_ref.shape[0] - at, width), bf16)
    half = keep_out.shape[0]
    bit = bit_ref[0]
    hand_out = [
        pltpu.make_async_copy(
            weights_ref.at[pl.ds(pl.multiple_of(at * half, 16), half)], out, sems.at[3 + which]
        )
        for which, (at, out) in enumerate(((bit, keep_out), (1 - bit, send_out)))
    ]
    for copy in hand_out:
        copy.start()
    pack_rows(zorder_ref, serial_grad_ref, back_out, stage_ref, pack_sems)
    for copy in hand_out:
        copy.wait()


def hold_kernel(rows_in, rows_out):
    pass


def split_rows(bit, rows, scratch_ref, keep_ref, send_ref):
    scratch_ref[...] = rows.astype(bf16)
    half = keep_ref.shape[0]
    keep_ref[...] = scratch_ref[pl.ds(pl.multiple_of(bit * half, 16), half), :]
    send_ref[...] = scratch_ref[pl.ds(pl.multiple_of((1 - bit) * half, 16), half), :]


def added(mine_ref, came_ref):
    return mine_ref[...].astype(f32) + came_ref[...].astype(f32)


def first_split_kernel(
    bit0_ref, bit1_ref, mine_ref, came_ref, keep0, send0, keep1, send1, scratch0, scratch1
):
    half = scratch0.shape[0]
    total = added(mine_ref, came_ref)
    split_rows(bit0_ref[0], total[:half], scratch0, keep0, send0)
    split_rows(bit1_ref[0], total[half:], scratch1, keep1, send1)


def next_split_kernel(
    bit0_ref, bit1_ref, mine0, came0, mine1, came1, keep0, send0, keep1, send1, scratch0, scratch1
):
    split_rows(bit0_ref[0], added(mine0, came0), scratch0, keep0, send0)
    split_rows(bit1_ref[0], added(mine1, came1), scratch1, keep1, send1)


def add_join_kernel(mine0, came0, mine1, came1, share_ref):
    half = mine0.shape[0]
    share_ref[0:half, :] = added(mine0, came0).astype(bf16)
    share_ref[half:, :] = added(mine1, came1).astype(bf16)


def add_kernel(mine_ref, came_ref, total_ref):
    total_ref[...] = added(mine_ref, came_ref).astype(bf16)


def join_kernel(bit_ref, mine_ref, came_ref, both_ref):
    half = mine_ref.shape[0]
    bit = bit_ref[0]
    both_ref[pl.ds(pl.multiple_of(bit * half, 16), half), :] = mine_ref[...]
    both_ref[pl.ds(pl.multiple_of((1 - bit) * half, 16), half), :] = came_ref[...]


def spread_kernel(
    bit_ref, mine_ref, came_ref, total_ref, up_ref, down_ref, conv_ref, gain_one_ref, gain_two_ref, near_ref,
    joined_ref, sums_ref, *, bits, scale
):
    join_kernel(bit_ref, mine_ref, came_ref, joined_ref)
    rows = sums_ref.shape[0]
    piece = (rows >> bits) // 2
    for at in range(1 << bits):
        digits = [(at >> (bits - 1 - bit)) & 1 for bit in range(bits)]
        for part, order in enumerate((digits[1:], digits[:0:-1])):
            place = 0
            for digit in order:
                place = 2 * place + digit
            start = digits[0] * (rows // 2) + part * (rows // 4) + place * piece
            source = (2 * at + part) * piece
            sums_ref[start : start + piece, :] = joined_ref[source : source + piece, :]
    width, hidden_width = up_ref.shape
    taps, groups, inner = conv_ref.shape[:3]
    down_ref[...] = sums_ref[0:hidden_width, :].astype(f32) * scale
    for start in range(0, hidden_width, width):
        up_ref[:, start : start + width] = (
            sums_ref[hidden_width + start : hidden_width + start + width, :].astype(f32) * scale
        )
    for tap in range(taps):
        at = 2 * hidden_width + tap * inner
        rows = sums_ref[at : at + inner, :].astype(f32) * scale
        for group in range(groups):
            conv_ref[tap, group] = rows[:, group * inner : (group + 1) * inner]
    at = 2 * hidden_width + taps * inner
    gains = sums_ref[at : at + 16, :].astype(f32) * scale
    gain_one_ref[...] = gains[0:1, :]
    gain_two_ref[...] = gains[1:2, :]
    near_ref[...] = total_ref[...].astype(f32) * scale


def call(kernel, outs, args, scratch=(), smem=0, flops=0, limit=16, held=0, stored=0, after=(), same=None, **static):
    moved = sum(math.prod(a.shape) * a.dtype.itemsize for a in (*args, *outs))
    specs = [pl.BlockSpec(memory_space=pltpu.SMEM)] * smem
    specs += [pl.BlockSpec(memory_space=pltpu.VMEM)] * (len(args) - smem - held)
    specs += [pl.BlockSpec(memory_space=pltpu.HBM)] * held
    specs += [pl.BlockSpec(memory_space=pltpu.HBM if a.shape[0] >= PATCH else pl.ANY) for a in after]
    after = [pltpu.with_memory_space_constraint(a, pltpu.HBM) if a.shape[0] >= PATCH else a for a in after]
    out_specs = [pl.BlockSpec(memory_space=pltpu.HBM)] * stored
    shapes = [pltpu.HBM(a.shape, a.dtype) for a in outs[:stored]] + list(outs[stored:])
    first_held = len(args) - held
    args = [*args[:first_held], *(pltpu.with_memory_space_constraint(a, pltpu.HBM) for a in args[first_held:])]
    out_specs += [pl.BlockSpec(memory_space=pltpu.VMEM)] * (len(outs) - stored)
    count = len(args)

    def run(*refs):
        kernel(*refs[:count], *refs[count + len(after) :], **static)

    return pl.pallas_call(
        run,
        out_shape=tuple(shapes),
        in_specs=specs,
        out_specs=tuple(out_specs),
        scratch_shapes=list(scratch),
        input_output_aliases=same or {},
        compiler_params=pltpu.CompilerParams(vmem_limit_bytes=limit * 1024 * 1024),
        cost_estimate=pl.CostEstimate(flops=int(flops), bytes_accessed=moved, transcendentals=0),
    )(*args, *after)


def shaped(*shape, dtype=bf16):
    return jax.ShapeDtypeStruct(shape, dtype)


def pairwise(first, second, axis):
    count = lax.axis_size(axis)
    pairs = [
        [pair for at in range(start, count - 1, 2) for pair in ((at, at + 1), (at + 1, at))] for start in (0, 1)
    ]
    return [lax.ppermute(rows, axis, pair) for rows, pair in zip((first, second), pairs)]


def partner(value, axis, step):
    return lax.ppermute(value, axis, [(at, at ^ step) for at in range(lax.axis_size(axis))])


def bit_of(axis, step):
    return lax.rem(lax.div(lax.axis_index(axis), step), 2).astype(jnp.int32).reshape(1)


def steps_of(axis):
    return [1 << at for at in range(int(math.log2(lax.axis_size(axis))))]


def sum_over_mesh(keep, send, early, late):
    width = keep.shape[1]
    steps = steps_of("ty")
    orders = steps[1:], steps[:0:-1]

    def halves(kernel, rows, at, args, **options):
        return call(
            kernel,
            [shaped(rows // 2, width)] * 4,
            [bit_of("ty", order[at]) for order in orders] + list(args),
            scratch=[pltpu.VMEM((rows, width), bf16)] * 2,
            smem=2,
            flops=1e6,
            **options,
        )

    came = partner(send, "ty", steps[0])
    rows = keep.shape[0] // 2
    parts = halves(first_split_kernel, rows, 0, [keep, came], after=early)
    for at in range(len(orders[0])):
        rows = rows // 2
        pairs = []
        for which, order in enumerate(orders):
            pairs += [parts[2 * which], partner(parts[2 * which + 1], "ty", order[at])]
        if at + 1 < len(orders[0]):
            parts = halves(next_split_kernel, rows, at + 1, pairs)
    (share,) = call(add_join_kernel, [shaped(2 * rows, width)], pairs, flops=1e6)
    for step in steps_of("tx"):
        (share,) = call(
            add_kernel,
            [shaped(*share.shape)],
            [share, partner(share, "tx", step)],
            after=late.pop(0) if late else (),
            flops=1e6,
        )
    for step in steps[:0:-1]:
        (share,) = call(
            join_kernel,
            [shaped(2 * share.shape[0], width)],
            [bit_of("ty", step), share, partner(share, "ty", step)],
            after=late.pop(0) if late else (),
            smem=1,
            flops=1e6,
        )
    return share, partner(share, "ty", steps[0])


def exchange(rows, tiles):
    return lax.all_to_all(rows, ("tx", "ty"), split_axis=0, concat_axis=0, tiled=True)


def body(
    points,
    counts,
    owner,
    zorder,
    border,
    near,
    w_near,
    gain_one,
    conv_w,
    gain_two,
    w_up,
    w_down,
    grad_out,
):
    points_tile = points[0]
    tile_rows, width = points_tile.shape
    border_rows = border.shape[2]
    edge = 4 * border_rows
    ext = tile_rows + edge
    lists = border[0]
    near_tile = near[0]
    neighbours = near_tile.shape[0]
    tiles = lax.axis_size("tx") * lax.axis_size("ty")
    slots_count = zorder.shape[1]
    capacity = slots_count // tiles
    taps, groups, inner = conv_w.shape[:3]
    conv_rows = conv_w.reshape(taps * groups * inner, inner)
    gain_one_row = gain_one.reshape(1, width)
    gain_two_row = gain_two.reshape(1, width)
    hidden = w_up.shape[1]

    bits = jnp.concatenate([bit_of("tx", 1), bit_of("ty", 1)])
    slots, *sent = call(
        route_kernel,
        [shaped(1, tile_rows, dtype=jnp.int32)] + [shaped(border_rows, width)] * 4,
        [bits, counts, owner, lists, points_tile],
        scratch=[
            pltpu.VMEM((1, tile_rows), jnp.int32),
            pltpu.VMEM((4, border_rows), jnp.int32),
            pltpu.VMEM((tile_rows, width), bf16),
            pltpu.SemaphoreType.DMA((3,)),
        ],
        smem=2,
        held=3,
        flops=4e9,
        tiles=tiles,
        capacity=capacity,
    )
    halos = pairwise(sent[0], sent[1], "tx") + pairwise(sent[2], sent[3], "ty")
    kept_table, table = call(
        count_kernel,
        [shaped(ext, tile_rows), shaped(ext, tile_rows)],
        [near_tile],
        scratch=[pltpu.SemaphoreType.DMA((ext // CHUNK,))],
        flops=8e9,
        stored=1,
    )
    average, pre_act, packed = call(
        lift_kernel,
        [
            shaped(width, tile_rows),
            shaped(tile_rows, width, dtype=f32),
            shaped(slots_count, 2 * width),
        ],
        [bits, slots, points_tile, grad_out[0], *halos, table, w_near],
        smem=1,
        scratch=[
            pltpu.VMEM((width, tile_rows), bf16),
            pltpu.VMEM((tile_rows, width), f32),
            pltpu.VMEM((tile_rows, 2 * width), bf16),
            pltpu.VMEM((slots_count, 2 * width), bf16),
            pltpu.SemaphoreType.DMA((2,)),
            pltpu.SemaphoreType.DMA((slots_count // WIDE,)),
        ],
        flops=4e9,
        stored=3,
        neighbours=neighbours,
    )
    came = exchange(packed, tiles)
    patches = slots_count // PATCH
    patch_scratch = [
        pltpu.VMEM((PATCH + 2 * PAD, width), f32),
        pltpu.VMEM((PATCH, width), f32),
        pltpu.VMEM((PATCH + 2 * PAD, width), f32),
    ]
    serial, state, back_result = call(
        forward_kernel,
        [
            shaped(slots_count, width),
            shaped(slots_count, width, dtype=f32),
            shaped(slots_count, width),
        ],
        [zorder, conv_rows, gain_one_row, gain_two_row, w_up, w_down, came],
        held=1,
        scratch=[
            pltpu.VMEM((slots_count, width), bf16),
            pltpu.VMEM((slots_count, width), bf16),
            pltpu.VMEM((slots_count, width), f32),
            pltpu.VMEM((taps * width, width), bf16),
            pltpu.VMEM((patches, PATCH, width), bf16),
            pltpu.VMEM((patches, PATCH + 2 * PAD, width), f32),
            pltpu.VMEM((patches, PATCH, width), f32),
            pltpu.VMEM((patches, PATCH + 2 * PAD, width), f32),
            pltpu.VMEM((patches, PATCH, width), bf16),
            pltpu.VMEM((patches, PATCH, hidden), bf16),
            pltpu.VMEM((slots_count, width), bf16),
            pltpu.VMEM((slots_count, width), bf16),
            pltpu.SemaphoreType.DMA((3, slots_count // PATCH)),
            pltpu.SemaphoreType.DMA((slots_count // WIDE,)),
        ],
        flops=10e9,
        limit=44,
        stored=3,
        groups=groups,
        inner=inner,
    )
    came_result = exchange(back_result, tiles)
    lines = lax.axis_size("ty")
    sums_rows = 2 * hidden + taps * inner + 16
    sums_rows = -(-sums_rows // (32 * lines)) * (32 * lines)
    back_grad, keep, send = call(
        backward_kernel,
        [
            shaped(slots_count, width),
            shaped(sums_rows // 2, width),
            shaped(sums_rows // 2, width),
        ],
        [
            bit_of("ty", 1),
            zorder,
            conv_rows,
            gain_one_row,
            gain_two_row,
            w_up,
            w_down,
            came,
            serial,
            state,
        ],
        held=3,
        scratch=[
            pltpu.VMEM((slots_count, width), bf16),
            pltpu.VMEM((slots_count, width), bf16),
            pltpu.VMEM((slots_count, width), f32),
            pltpu.VMEM((slots_count, width), bf16),
            pltpu.VMEM((slots_count, width), bf16),
            pltpu.VMEM((slots_count, width), bf16),
            pltpu.VMEM((sums_rows, width), bf16),
            pltpu.VMEM((taps * width, width), bf16),
            pltpu.VMEM((slots_count, width), bf16),
            pltpu.VMEM((slots_count, hidden), bf16),
            pltpu.VMEM((slots_count, hidden), bf16),
            pltpu.VMEM((PATCH, width), f32),
            pltpu.VMEM((PATCH + 2 * PAD, width), f32),
            pltpu.VMEM((PATCH, width), bf16),
            *patch_scratch,
            pltpu.VMEM((PATCH, width), bf16),
            pltpu.VMEM((taps, width, width), f32),
            pltpu.VMEM((16, width), f32),
            pltpu.SemaphoreType.DMA((5,)),
            pltpu.SemaphoreType.DMA((slots_count // WIDE,)),
        ],
        stored=3,
        smem=1,
        flops=40e9,
        limit=44,
        groups=groups,
        inner=inner,
    )
    (back_grad,) = call(
        hold_kernel,
        [shaped(slots_count, width)],
        [back_grad],
        after=[came_result.reshape(tiles, capacity, width)],
        held=1,
        stored=1,
        same={0: 0},
    )
    came_back = exchange(back_grad, tiles)
    (out_rows,) = call(
        unpack_kernel, [shaped(tile_rows, width)], [slots, came_result], flops=4e9
    )
    lifted_grad, spread, near_grad, *halo_grad = call(
        tile_back_kernel,
        [shaped(tile_rows, width), shaped(tile_rows, width), shaped(width, width)]
        + [shaped(border_rows, width)] * 4,
        [bits, slots, came_back, w_near, kept_table, average, pre_act],
        smem=1,
        after=[out_rows],
        scratch=[
            pltpu.VMEM((edge, tile_rows), bf16),
            pltpu.VMEM((width, tile_rows), bf16),
            pltpu.VMEM((tile_rows, width), f32),
            pltpu.VMEM((tile_rows, width), bf16),
            pltpu.VMEM((tile_rows, width), bf16),
            pltpu.VMEM((tile_rows, width), bf16),
            pltpu.SemaphoreType.DMA((5,)),
        ],
        flops=6e9,
        limit=24,
        held=3,
        stored=2,
        neighbours=neighbours,
    )
    returned = pairwise(halo_grad[0], halo_grad[1], "tx") + pairwise(halo_grad[2], halo_grad[3], "ty")
    (near_share,) = call(
        near_sum_kernel,
        [shaped(width, width)],
        [exchange(near_grad, tiles)],
        after=returned[:2],
        flops=1e6,
        share=width // tiles,
    )
    near_total = exchange(near_share, tiles)
    (grad_points,) = call(
        finish_kernel,
        [shaped(tile_rows, width)],
        [bits, border.reshape(1, edge), *returned, kept_table, spread, lifted_grad],
        after=[near_total],
        smem=1,
        scratch=[
            pltpu.VMEM((tile_rows, tile_rows), bf16),
            pltpu.VMEM((tile_rows, width), bf16),
            pltpu.VMEM((tile_rows, width), bf16),
            pltpu.SemaphoreType.DMA((3,)),
        ],
        held=3,
        flops=1e9,
    )
    totals = sum_over_mesh(
        keep, send, [out_rows], [[near_grad], returned[:2], [near_share, *returned[2:]], [grad_points]]
    )
    scale = 1.0 / math.sqrt(tiles * tile_rows)
    up_sum, down_sum, conv_sum, gain_one_sum, gain_two_sum, near_sum = call(
        spread_kernel,
        [
            shaped(width, hidden, dtype=f32),
            shaped(hidden, width, dtype=f32),
            shaped(*conv_w.shape, dtype=f32),
            shaped(1, width, dtype=f32),
            shaped(1, width, dtype=f32),
            shaped(width, width, dtype=f32),
        ],
        [bit_of("ty", 1), *totals, near_total],
        scratch=[pltpu.VMEM((sums_rows, width), bf16)] * 2,
        smem=1,
        flops=1e6,
        bits=len(steps_of("ty")),
        scale=scale,
    )
    return (
        out_rows[None],
        grad_points[None],
        near_sum,
        gain_one_sum[0],
        conv_sum,
        gain_two_sum[0],
        up_sum,
        down_sum,
    )


def solution(mesh):
    placed = (
        P(("tx", "ty"), None, None),
        P(("tx", "ty")),
        P(("tx", "ty"), None),
        P(("tx", "ty"), None),
        P(("tx", "ty"), None, None),
        P(("tx", "ty"), None, None),
        P(),
        P(),
        P(),
        P(),
        P(),
        P(),
        P(("tx", "ty"), None, None),
    )
    return jax.shard_map(
        body,
        mesh=mesh,
        in_specs=placed,
        out_specs=(
            P(("tx", "ty"), None, None),
            P(("tx", "ty"), None, None),
            P(),
            P(),
            P(),
            P(),
            P(),
            P(),
        ),
        check_vma=False,
    )
```

```python
import math

import jax
import jax.numpy as jnp
from jax import lax
from jax.experimental import pallas as pl
from jax.experimental.pallas import tpu as pltpu
from jax.sharding import PartitionSpec as P

PATCH = 1024
CHUNK = 256
WIDE = 512
BLOCK = 64
LANES = 128
PAD = 8

eps_norm = 1e-06
gelu_coef = 0.7978845608028654
cubic_coef = 0.044715

bf16 = jnp.bfloat16
f32 = jnp.float32
NN = (((1,), (0,)), ((), ()))
NT = (((1,), (1,)), ((), ()))
TN = (((0,), (0,)), ((), ()))


def dot(left, right, dims=NN):
    return lax.dot_general(left, right, dims, preferred_element_type=f32)


def iota(shape, axis):
    return lax.broadcasted_iota(jnp.int32, shape, axis)


def marks(mask):
    return jnp.where(mask, 1.0, 0.0).astype(bf16)


def gelu_parts(value):
    square = value * value
    tangent = jnp.tanh(value * (gelu_coef + (gelu_coef * cubic_coef) * square))
    return square, tangent


def gelu_tanh(value):
    _, tangent = gelu_parts(value)
    half = 0.5 * value
    return half + half * tangent


def slope_of(value, square, tangent):
    inner_slope = gelu_coef + (3.0 * gelu_coef * cubic_coef) * square
    return 0.5 * (1.0 + tangent) + (0.5 * value) * (1.0 - tangent * tangent) * inner_slope


def inverse_rms(value):
    return lax.rsqrt(jnp.mean(value * value, axis=-1, keepdims=True) + eps_norm)


def column_of(row, count):
    return jnp.transpose(jnp.broadcast_to(row, (LANES, count)))


def pick_rows(column, depth):
    count = column.shape[0]
    lane = iota((count, LANES), 1)
    return jnp.concatenate(
        [marks(column == lane + base) for base in range(0, depth, LANES)], axis=1
    )


def mark_slots(row, start, count):
    return marks(iota((count, row.shape[1]), 0) + start == row)


def route_kernel(
    bits_ref, counts_ref, owner_in, lists_in, points_in, slots_ref, sent0, sent1, sent2, sent3,
    owner_ref, lists_ref, points_ref, sems, *, tiles, capacity
):
    fetches = [
        pltpu.make_async_copy(source, target, sems.at[at])
        for at, (source, target) in enumerate(
            ((owner_in, owner_ref), (lists_in, lists_ref), (points_in, points_ref))
        )
    ]
    for fetch in fetches:
        fetch.start()
    fetches[0].wait()
    rows = owner_ref.shape[1]
    live = iota((1, rows), 1) < counts_ref[0]
    owned = jnp.where(live, owner_ref[...], tiles)
    members = owned == iota((tiles, rows), 0)
    earlier = marks(iota((rows, rows), 0) < iota((rows, rows), 1))
    before = dot(marks(members), earlier)
    rank = jnp.sum(jnp.where(members, before, 0.0), axis=0, keepdims=True)
    slots_ref[...] = jnp.where(live, owned * capacity + rank.astype(jnp.int32), -1)
    fetches[1].wait()
    fetches[2].wait()
    for direction, sent_ref in zip(turns(bits_ref), (sent0, sent1, sent2, sent3)):
        sent_ref[...] = dot(chosen_rows(lists_ref, direction, rows), points_ref[...], TN).astype(bf16)


def turns(bits_ref):
    column, line = bits_ref[0], bits_ref[1]
    return 1 - column, column, 3 - line, 2 + line


def blocks(bits_ref):
    column, line = bits_ref[0], bits_ref[1]
    return column, 1 - column, 2 + line, 3 - line


def block_of(index, size, start=0):
    return pl.ds(pl.multiple_of(start + index * size, 16), size)


def chosen_rows(lists_ref, direction, rows):
    listed = lists_ref[pl.ds(direction, 1), :]
    return marks(iota((rows, listed.shape[1]), 0) == listed)


def pack_rows(slots_ref, rows_ref, packed_out, stage_ref, sems):
    slots = slots_ref[...]
    copies = []
    for at, start in enumerate(range(0, packed_out.shape[0], WIDE)):
        place = pl.ds(start, WIDE)
        stage_ref[place, :] = dot(mark_slots(slots, start, WIDE), rows_ref[...]).astype(bf16)
        copies.append(pltpu.make_async_copy(stage_ref.at[place], packed_out.at[place], sems.at[at]))
        copies[-1].start()
    for copy in copies:
        copy.wait()


def unpack_kernel(slots_ref, packed_ref, rows_ref):
    for start in range(0, rows_ref.shape[0], CHUNK):
        column = column_of(slots_ref[:, start : start + CHUNK], CHUNK)
        rows_ref[pl.ds(start, CHUNK), :] = dot(
            pick_rows(column, packed_ref.shape[0]), packed_ref[...]
        ).astype(bf16)


def count_kernel(near_ref, table_ref):
    neighbours, rows = near_ref.shape
    step = 16
    zero = jnp.zeros((step, LANES), bf16)
    one = jnp.ones((step, LANES), bf16)
    row_blocks = table_ref.shape[0] // CHUNK

    def rows_of(row_block, _):
        row_at = pl.multiple_of(row_block * CHUNK, CHUNK)

        def block(lane_block, _):
            lane_at = pl.multiple_of(lane_block * LANES, LANES)
            local = (near_ref[:, pl.ds(lane_at, LANES)] - row_at).astype(f32)
            spread = [
                jnp.broadcast_to(local[k : k + 1, :], (step, LANES)).astype(bf16)
                for k in range(neighbours)
            ]
            base = iota((step, LANES), 0).astype(f32)
            for inner in range(0, CHUNK, step):
                here = (base + float(inner)).astype(bf16)
                total = zero
                for k in range(neighbours):
                    total = total + jnp.where(spread[k] == here, one, zero)
                table_ref[pl.ds(row_at + inner, step), pl.ds(lane_at, LANES)] = total
            return 0

        lax.fori_loop(0, rows // LANES, block, 0)
        return 0

    lax.fori_loop(0, row_blocks, rows_of, 0)


def lift_kernel(
    bits_ref, slots_ref, points_ref, grad_ref, halo0, halo1, halo2, halo3, table_ref, w_ref,
    table_out, average_out, pre_out, packed_out,
    ext_ref, average_ref, pre_ref, both_ref, stage_ref, sems, pack_sems, *, neighbours
):
    width = points_ref.shape[1]
    keep_table = pltpu.make_async_copy(table_ref, table_out, sems.at[2])
    keep_table.start()
    rows = points_ref.shape[0]
    ext_ref[0:rows, :] = points_ref[...]
    for block, halo in zip(blocks(bits_ref), (halo0, halo1, halo2, halo3)):
        ext_ref[block_of(block, halo.shape[0], rows), :] = halo[...]
    average = (dot(ext_ref[...], table_ref[...], TN) * (1.0 / neighbours)).astype(bf16)
    average_ref[...] = average
    keep_average = pltpu.make_async_copy(average_ref, average_out, sems.at[0])
    keep_average.start()
    pre_ref[...] = dot(average, w_ref[...], TN)
    keep_pre = pltpu.make_async_copy(pre_ref, pre_out, sems.at[1])
    keep_pre.start()
    for row in range(0, points_ref.shape[0], BLOCK):
        here = pl.ds(row, BLOCK)
        both_ref[here, 0:width] = (
            points_ref[here, :].astype(f32) + gelu_tanh(pre_ref[here, :])
        ).astype(bf16)
    both_ref[:, width:] = grad_ref[...]
    pack_rows(slots_ref, both_ref, packed_out, stage_ref, pack_sems)
    keep_average.wait()
    keep_pre.wait()
    keep_table.wait()


def tile_back_kernel(
    bits_ref, slots_ref, back_ref, w_ref, table_in, average_in, pre_in,
    lifted_out, spread_out, near_ref, halo0, halo1, halo2, halo3,
    table_ref, average_ref, pre_ref, lifted_ref, act_ref, spread_ref, halo_ref, sems, *, neighbours
):
    rows = lifted_ref.shape[0]
    halo_rows = table_ref.shape[0]
    fetch_pre = pltpu.make_async_copy(pre_in, pre_ref, sems.at[0])
    fetch_average = pltpu.make_async_copy(average_in, average_ref, sems.at[1])
    fetch_table = pltpu.make_async_copy(table_in.at[pl.ds(rows, halo_rows)], table_ref, sems.at[2])
    fetch_pre.start()
    fetch_average.start()
    fetch_table.start()
    keep_lifted = pltpu.make_async_copy(lifted_ref, lifted_out, sems.at[3])
    keep_spread = pltpu.make_async_copy(spread_ref, spread_out, sems.at[4])
    for start in range(0, rows, WIDE):
        column = column_of(slots_ref[:, start : start + WIDE], WIDE)
        wide = dot(pick_rows(column, back_ref.shape[0]), back_ref[...])
        if start == 0:
            fetch_pre.wait()
        for row in range(0, WIDE, BLOCK):
            here = pl.ds(start + row, BLOCK)
            lifted_grad = wide[row : row + BLOCK]
            lifted_ref[here, :] = lifted_grad.astype(bf16)
            value = pre_ref[here, :]
            square, tangent = gelu_parts(value)
            act_ref[here, :] = (lifted_grad * slope_of(value, square, tangent)).astype(bf16)
    keep_lifted.start()
    spread_ref[...] = (dot(act_ref[...], w_ref[...], NT) * (1.0 / neighbours)).astype(bf16)
    keep_spread.start()
    fetch_average.wait()
    near_ref[...] = dot(average_ref[...], act_ref[...]).astype(near_ref.dtype)
    fetch_table.wait()
    halo_ref[...] = dot(table_ref[...], spread_ref[...]).astype(bf16)
    for block, back in zip(blocks(bits_ref), (halo0, halo1, halo2, halo3)):
        back[...] = halo_ref[block_of(block, back.shape[0]), :]
    keep_lifted.wait()
    keep_spread.wait()


def finish_kernel(
    bits_ref, lists_ref, back0, back1, back2, back3, table_in, spread_in, lifted_in,
    out_ref, came_ref, table_ref, spread_ref, lifted_ref, sems
):
    rows = out_ref.shape[0]
    fetch_spread = pltpu.make_async_copy(spread_in, spread_ref, sems.at[0])
    fetch_table = pltpu.make_async_copy(table_in.at[pl.ds(0, rows)], table_ref, sems.at[1])
    fetch_lifted = pltpu.make_async_copy(lifted_in, lifted_ref, sems.at[2])
    fetch_spread.start()
    fetch_table.start()
    fetch_lifted.start()
    for direction, back in zip(turns(bits_ref), (back0, back1, back2, back3)):
        came_ref[block_of(direction, back.shape[0]), :] = back[...]
    returned = dot(chosen_rows(lists_ref, 0, rows), came_ref[...])
    fetch_spread.wait()
    fetch_table.wait()
    fetch_lifted.wait()
    for start in range(0, rows, WIDE):
        here = pl.ds(start, WIDE)
        out_ref[here, :] = (
            lifted_ref[here, :].astype(f32)
            + dot(table_ref[here, :], spread_ref[...])
            + returned[start : start + WIDE]
        ).astype(bf16)


def near_sum_kernel(parts_ref, share_ref, *, share):
    rows = parts_ref.shape[0]
    same = lax.rem(iota((rows, rows), 0), share) == lax.rem(iota((rows, rows), 1), share)
    share_ref[...] = dot(marks(same), parts_ref[...]).astype(bf16)


def full_taps(conv_ref, groups, inner):
    width = groups * inner
    rows = conv_ref.shape[0]
    repeat = marks(lax.rem(iota((inner, width), 1), inner) == iota((inner, width), 0))
    wide = dot(conv_ref[...], repeat)
    row_group = lax.div(lax.rem(iota((rows, width), 0), width), inner)
    same = row_group == lax.div(iota((rows, width), 1), inner)
    return jnp.where(same, wide, 0.0).astype(bf16)


def padded_zeros(ref):
    edge = jnp.zeros((PAD, ref.shape[1]), f32)
    ref[0:PAD, :] = edge
    ref[PAD + PATCH :, :] = edge


def forward_kernel(
    zorder_ref, conv_ref, gain_one_ref, gain_two_ref, up_ref, down_ref, came_in,
    serial_out, state_out, back_out,
    lifted_ref, serial_ref, state_ref, taps_ref, normed_ref, before_ref, here_ref, after_ref, second_ref, hidden_ref,
    result_ref, stage_ref, sems, pack_sems, *, groups, inner
):
    slots, width = lifted_ref.shape
    fetch = pltpu.make_async_copy(came_in.at[:, pl.ds(0, width)], lifted_ref, sems.at[2, 0])
    fetch.start()
    hidden_width = up_ref.shape[1]
    taps_ref[...] = full_taps(conv_ref, groups, inner)

    def keep(at):
        place = pl.ds(at * PATCH, PATCH)
        return (
            pltpu.make_async_copy(serial_ref.at[place], serial_out.at[place], sems.at[0, at]),
            pltpu.make_async_copy(state_ref.at[place], state_out.at[place], sems.at[1, at]),
        )

    def patch(at):
        origin = at * PATCH
        normed_at, second_at, hidden_at = normed_ref.at[at], second_ref.at[at], hidden_ref.at[at]
        before_at, here_at, after_at = before_ref.at[at], here_ref.at[at], after_ref.at[at]
        padded_zeros(before_at)
        padded_zeros(after_at)
        for start in range(0, PATCH, WIDE):
            column = column_of(zorder_ref[:, origin + start : origin + start + WIDE], WIDE)
            wide = dot(pick_rows(column, slots), lifted_ref[...])
            for row in range(0, WIDE, BLOCK):
                serial = wide[row : row + BLOCK]
                serial_ref[pl.ds(origin + start + row, BLOCK), :] = serial.astype(bf16)
                normed = serial * inverse_rms(serial) * gain_one_ref[...]
                normed_at[pl.ds(start + row, BLOCK), :] = normed.astype(bf16)
            yield
        before_at[pl.ds(PAD, PATCH), :] = dot(normed_at[...], taps_ref[0:width, :])
        here_at[...] = dot(normed_at[...], taps_ref[width : 2 * width, :])
        after_at[pl.ds(PAD, PATCH), :] = dot(normed_at[...], taps_ref[2 * width :, :])
        yield
        for row in range(0, PATCH, BLOCK):
            place = pl.ds(origin + row, BLOCK)
            state = serial_ref[place, :].astype(f32) + (
                before_at[pl.ds(PAD + row - 1, BLOCK), :]
                + here_at[pl.ds(row, BLOCK), :]
                + after_at[pl.ds(PAD + row + 1, BLOCK), :]
            )
            state_ref[place, :] = state
            second = state * inverse_rms(state) * gain_two_ref[...]
            second_at[pl.ds(row, BLOCK), :] = second.astype(bf16)
        for copy in keep(at):
            copy.start()
        yield
        for start in range(0, PATCH, WIDE):
            value = dot(second_at[pl.ds(start, WIDE), :], up_ref[...])
            for row in range(0, WIDE, 16):
                for col in range(0, hidden_width, 2 * LANES):
                    hidden_at[pl.ds(start + row, 16), pl.ds(col, 2 * LANES)] = gelu_tanh(
                        value[row : row + 16, col : col + 2 * LANES]
                    ).astype(bf16)
            if start + WIDE == PATCH // 2:
                yield
        yield
        for start in range(0, PATCH, WIDE):
            place = pl.ds(origin + start, WIDE)
            result_ref[place, :] = (
                state_ref[place, :] + dot(hidden_at[pl.ds(start, WIDE), :], down_ref[...])
            ).astype(bf16)
        yield

    fetch.wait()
    waiting = [patch(at) for at in range(slots // PATCH)]
    running = []
    while waiting or running:
        if waiting:
            running.append(waiting.pop(0))
        running = [work for work in running if next(work, work) is not work]
    pack_rows(zorder_ref, result_ref, back_out, stage_ref, pack_sems)
    for at in range(slots // PATCH):
        for copy in keep(at):
            copy.wait()


def backward_kernel(
    bit_ref, zorder_ref, conv_ref, gain_one_ref, gain_two_ref, up_ref, down_ref, came_in, serial_in, state_in,
    back_out, keep_out, send_out,
    grad_ref, serial_ref, state_ref, out_grad_ref, serial_grad_ref, stage_ref, weights_ref, taps_ref,
    second_ref, hidden_ref, pre_grad_ref, state_grad_ref, mixed_ref, mixed_half_ref, before_ref, here_ref,
    after_ref, normed_ref, conv_sum_ref, gains_ref, sems, pack_sems, *, groups, inner
):
    slots, width = serial_ref.shape
    hidden_width = up_ref.shape[1]
    fetch_grad = pltpu.make_async_copy(came_in.at[:, pl.ds(width, width)], grad_ref, sems.at[0])
    fetch_state = pltpu.make_async_copy(state_in, state_ref, sems.at[1])
    fetch_serial = pltpu.make_async_copy(serial_in, serial_ref, sems.at[2])
    fetch_grad.start()
    fetch_state.start()
    fetch_serial.start()
    taps_ref[...] = full_taps(conv_ref, groups, inner)
    padded_zeros(before_ref)
    padded_zeros(after_ref)
    padded_zeros(mixed_ref)
    conv_sum_ref[...] = jnp.zeros_like(conv_sum_ref)
    gains_ref[...] = jnp.zeros_like(gains_ref)

    def patch(at, _):
        origin = pl.multiple_of(at * PATCH, PATCH)
        for start in range(0, PATCH, WIDE):
            column = column_of(zorder_ref[:, pl.ds(origin + start, WIDE)], WIDE)
            out_grad_ref[pl.ds(origin + start, WIDE), :] = dot(
                pick_rows(column, slots), grad_ref[...]
            ).astype(bf16)
        for start in range(0, PATCH, CHUNK):
            place = pl.ds(origin + start, CHUNK)
            for row in range(start, start + CHUNK, BLOCK):
                state = state_ref[pl.ds(origin + row, BLOCK), :]
                second = state * inverse_rms(state) * gain_two_ref[...]
                second_ref[pl.ds(origin + row, BLOCK), :] = second.astype(bf16)
            value_all = dot(second_ref[place, :], up_ref[...])
            hidden_grad_all = dot(out_grad_ref[place, :], down_ref[...], NT)
            for row in range(0, CHUNK, 16):
                for col in range(0, hidden_width, 2 * LANES):
                    value = value_all[row : row + 16, col : col + 2 * LANES]
                    hidden_grad = hidden_grad_all[row : row + 16, col : col + 2 * LANES]
                    square, tangent = gelu_parts(value)
                    half = 0.5 * value
                    piece = pl.ds(origin + start + row, 16), pl.ds(col, 2 * LANES)
                    hidden_ref[piece] = (half + half * tangent).astype(bf16)
                    pre_grad_ref[piece] = (
                        hidden_grad.astype(bf16).astype(f32) * slope_of(value, square, tangent)
                    ).astype(bf16)
            second_grad_all = dot(pre_grad_ref[place, :], up_ref[...], NT)
            for row in range(0, CHUNK, BLOCK):
                here = pl.ds(origin + start + row, BLOCK)
                state = state_ref[here, :]
                scale_two = inverse_rms(state)
                unit_two = state * scale_two
                second_grad = second_grad_all[row : row + BLOCK].astype(bf16).astype(f32)
                weighted = second_grad * gain_two_ref[...]
                product = second_grad * unit_two
                gains_ref[1:2, :] += jnp.sum(product, axis=0, keepdims=True)
                middle = jnp.mean(product * gain_two_ref[...], axis=-1, keepdims=True)
                state_grad = out_grad_ref[here, :].astype(f32) + scale_two * (weighted - unit_two * middle)
                state_grad_ref[pl.ds(start + row, BLOCK), :] = state_grad
                mixed_grad = state_grad.astype(bf16)
                mixed_half_ref[pl.ds(start + row, BLOCK), :] = mixed_grad
                mixed_ref[pl.ds(PAD + start + row, BLOCK), :] = mixed_grad.astype(f32)
        before_ref[pl.ds(PAD, PATCH), :] = dot(mixed_half_ref[...], taps_ref[0:width, :], NT)
        here_ref[...] = dot(mixed_half_ref[...], taps_ref[width : 2 * width, :], NT)
        after_ref[pl.ds(PAD, PATCH), :] = dot(mixed_half_ref[...], taps_ref[2 * width :, :], NT)
        for row in range(0, PATCH, BLOCK):
            place = pl.ds(origin + row, BLOCK)
            serial = serial_ref[place, :].astype(f32)
            scale_one = inverse_rms(serial)
            unit_one = serial * scale_one
            normed_ref[pl.ds(row, BLOCK), :] = (unit_one * gain_one_ref[...]).astype(bf16)
            normed_grad = (
                before_ref[pl.ds(PAD + row + 1, BLOCK), :]
                + here_ref[pl.ds(row, BLOCK), :]
                + after_ref[pl.ds(PAD + row - 1, BLOCK), :]
            ).astype(bf16).astype(f32)
            product = normed_grad * unit_one
            gains_ref[0:1, :] += jnp.sum(product, axis=0, keepdims=True)
            middle = jnp.mean(product * gain_one_ref[...], axis=-1, keepdims=True)
            weighted = normed_grad * gain_one_ref[...]
            serial_grad_ref[place, :] = (
                state_grad_ref[pl.ds(row, BLOCK), :] + scale_one * (weighted - unit_one * middle)
            ).astype(bf16)
        for tap in range(3):
            moved = mixed_ref[pl.ds(PAD + 1 - tap, PATCH), :].astype(bf16)
            conv_sum_ref[tap] += dot(normed_ref[...], moved, TN)
        return 0

    fetch_grad.wait()
    fetch_state.wait()
    fetch_serial.wait()
    lax.fori_loop(0, slots // PATCH, patch, 0)
    for start in range(0, hidden_width, width):
        block = slice(start, start + width)
        weights_ref[start : start + width, :] = jnp.transpose(
            dot(out_grad_ref[...], hidden_ref[:, block], TN)
        ).astype(bf16)
        weights_ref[hidden_width + start : hidden_width + start + width, :] = dot(
            second_ref[...], pre_grad_ref[:, block], TN
        ).astype(bf16)
    same = lax.div(iota((width, width), 0), inner) == lax.div(iota((width, width), 1), inner)
    for tap in range(3):
        kept = jnp.where(same, conv_sum_ref[tap], 0.0).reshape(groups, inner, width)
        at = 2 * hidden_width + tap * inner
        weights_ref[at : at + inner, :] = jnp.sum(kept, axis=0).astype(bf16)
    at = 2 * hidden_width + 3 * inner
    weights_ref[at : at + 16, :] = gains_ref[...].astype(bf16)
    at = at + 16
    weights_ref[at:, :] = jnp.zeros((weights_ref.shape[0] - at, width), bf16)
    half = keep_out.shape[0]
    bit = bit_ref[0]
    hand_out = [
        pltpu.make_async_copy(
            weights_ref.at[pl.ds(pl.multiple_of(at * half, 16), half)], out, sems.at[3 + which]
        )
        for which, (at, out) in enumerate(((bit, keep_out), (1 - bit, send_out)))
    ]
    for copy in hand_out:
        copy.start()
    pack_rows(zorder_ref, serial_grad_ref, back_out, stage_ref, pack_sems)
    for copy in hand_out:
        copy.wait()


def hold_kernel(rows_in, rows_out):
    pass


def split_rows(bit, rows, scratch_ref, keep_ref, send_ref):
    scratch_ref[...] = rows.astype(bf16)
    half = keep_ref.shape[0]
    keep_ref[...] = scratch_ref[pl.ds(pl.multiple_of(bit * half, 16), half), :]
    send_ref[...] = scratch_ref[pl.ds(pl.multiple_of((1 - bit) * half, 16), half), :]


def added(mine_ref, came_ref):
    return mine_ref[...].astype(f32) + came_ref[...].astype(f32)


def first_split_kernel(
    bit0_ref, bit1_ref, mine_ref, came_ref, keep0, send0, keep1, send1, scratch0, scratch1
):
    half = scratch0.shape[0]
    total = added(mine_ref, came_ref)
    split_rows(bit0_ref[0], total[:half], scratch0, keep0, send0)
    split_rows(bit1_ref[0], total[half:], scratch1, keep1, send1)


def next_split_kernel(
    bit0_ref, bit1_ref, mine0, came0, mine1, came1, keep0, send0, keep1, send1, scratch0, scratch1
):
    split_rows(bit0_ref[0], added(mine0, came0), scratch0, keep0, send0)
    split_rows(bit1_ref[0], added(mine1, came1), scratch1, keep1, send1)


def add_join_kernel(mine0, came0, mine1, came1, share_ref):
    half = mine0.shape[0]
    share_ref[0:half, :] = added(mine0, came0).astype(bf16)
    share_ref[half:, :] = added(mine1, came1).astype(bf16)


def add_kernel(mine_ref, came_ref, total_ref):
    total_ref[...] = added(mine_ref, came_ref).astype(bf16)


def join_kernel(bit_ref, mine_ref, came_ref, both_ref):
    half = mine_ref.shape[0]
    bit = bit_ref[0]
    both_ref[pl.ds(pl.multiple_of(bit * half, 16), half), :] = mine_ref[...]
    both_ref[pl.ds(pl.multiple_of((1 - bit) * half, 16), half), :] = came_ref[...]


def spread_kernel(
    bit_ref, mine_ref, came_ref, total_ref, up_ref, down_ref, conv_ref, gain_one_ref, gain_two_ref, near_ref,
    joined_ref, sums_ref, *, bits, scale
):
    join_kernel(bit_ref, mine_ref, came_ref, joined_ref)
    rows = sums_ref.shape[0]
    piece = (rows >> bits) // 2
    for at in range(1 << bits):
        digits = [(at >> (bits - 1 - bit)) & 1 for bit in range(bits)]
        for part, order in enumerate((digits[1:], digits[:0:-1])):
            place = 0
            for digit in order:
                place = 2 * place + digit
            start = digits[0] * (rows // 2) + part * (rows // 4) + place * piece
            source = (2 * at + part) * piece
            sums_ref[start : start + piece, :] = joined_ref[source : source + piece, :]
    width, hidden_width = up_ref.shape
    taps, groups, inner = conv_ref.shape[:3]
    down_ref[...] = sums_ref[0:hidden_width, :].astype(f32) * scale
    for start in range(0, hidden_width, width):
        up_ref[:, start : start + width] = (
            sums_ref[hidden_width + start : hidden_width + start + width, :].astype(f32) * scale
        )
    for tap in range(taps):
        at = 2 * hidden_width + tap * inner
        rows = sums_ref[at : at + inner, :].astype(f32) * scale
        for group in range(groups):
            conv_ref[tap, group] = rows[:, group * inner : (group + 1) * inner]
    at = 2 * hidden_width + taps * inner
    gains = sums_ref[at : at + 16, :].astype(f32) * scale
    gain_one_ref[...] = gains[0:1, :]
    gain_two_ref[...] = gains[1:2, :]
    near_ref[...] = total_ref[...].astype(f32) * scale


def call(kernel, outs, args, scratch=(), smem=0, flops=0, limit=16, held=0, stored=0, after=(), same=None, **static):
    moved = sum(math.prod(a.shape) * a.dtype.itemsize for a in (*args, *outs))
    specs = [pl.BlockSpec(memory_space=pltpu.SMEM)] * smem
    specs += [pl.BlockSpec(memory_space=pltpu.VMEM)] * (len(args) - smem - held)
    specs += [pl.BlockSpec(memory_space=pltpu.HBM)] * held
    specs += [pl.BlockSpec(memory_space=pltpu.HBM if a.shape[0] >= PATCH else pl.ANY) for a in after]
    after = [pltpu.with_memory_space_constraint(a, pltpu.HBM) if a.shape[0] >= PATCH else a for a in after]
    out_specs = [pl.BlockSpec(memory_space=pltpu.HBM)] * stored
    shapes = [pltpu.HBM(a.shape, a.dtype) for a in outs[:stored]] + list(outs[stored:])
    first_held = len(args) - held
    args = [*args[:first_held], *(pltpu.with_memory_space_constraint(a, pltpu.HBM) for a in args[first_held:])]
    out_specs += [pl.BlockSpec(memory_space=pltpu.VMEM)] * (len(outs) - stored)
    count = len(args)

    def run(*refs):
        kernel(*refs[:count], *refs[count + len(after) :], **static)

    return pl.pallas_call(
        run,
        out_shape=tuple(shapes),
        in_specs=specs,
        out_specs=tuple(out_specs),
        scratch_shapes=list(scratch),
        input_output_aliases=same or {},
        compiler_params=pltpu.CompilerParams(vmem_limit_bytes=limit * 1024 * 1024),
        cost_estimate=pl.CostEstimate(flops=int(flops), bytes_accessed=moved, transcendentals=0),
    )(*args, *after)


def shaped(*shape, dtype=bf16):
    return jax.ShapeDtypeStruct(shape, dtype)


def pairwise(first, second, axis):
    count = lax.axis_size(axis)
    pairs = [
        [pair for at in range(start, count - 1, 2) for pair in ((at, at + 1), (at + 1, at))] for start in (0, 1)
    ]
    return [lax.ppermute(rows, axis, pair) for rows, pair in zip((first, second), pairs)]


def partner(value, axis, step):
    return lax.ppermute(value, axis, [(at, at ^ step) for at in range(lax.axis_size(axis))])


def bit_of(axis, step):
    return lax.rem(lax.div(lax.axis_index(axis), step), 2).astype(jnp.int32).reshape(1)


def steps_of(axis):
    return [1 << at for at in range(int(math.log2(lax.axis_size(axis))))]


def sum_over_mesh(keep, send, early, late):
    width = keep.shape[1]
    steps = steps_of("ty")
    orders = steps[1:], steps[:0:-1]

    def halves(kernel, rows, at, args, **options):
        return call(
            kernel,
            [shaped(rows // 2, width)] * 4,
            [bit_of("ty", order[at]) for order in orders] + list(args),
            scratch=[pltpu.VMEM((rows, width), bf16)] * 2,
            smem=2,
            flops=1e6,
            **options,
        )

    came = partner(send, "ty", steps[0])
    rows = keep.shape[0] // 2
    parts = halves(first_split_kernel, rows, 0, [keep, came], after=early)
    for at in range(len(orders[0])):
        rows = rows // 2
        pairs = []
        for which, order in enumerate(orders):
            pairs += [parts[2 * which], partner(parts[2 * which + 1], "ty", order[at])]
        if at + 1 < len(orders[0]):
            parts = halves(next_split_kernel, rows, at + 1, pairs)
    (share,) = call(add_join_kernel, [shaped(2 * rows, width)], pairs, flops=1e6)
    for step in steps_of("tx"):
        (share,) = call(
            add_kernel,
            [shaped(*share.shape)],
            [share, partner(share, "tx", step)],
            after=late.pop(0) if late else (),
            flops=1e6,
        )
    for step in steps[:0:-1]:
        (share,) = call(
            join_kernel,
            [shaped(2 * share.shape[0], width)],
            [bit_of("ty", step), share, partner(share, "ty", step)],
            after=late.pop(0) if late else (),
            smem=1,
            flops=1e6,
        )
    return share, partner(share, "ty", steps[0])


def exchange(rows, tiles):
    return lax.all_to_all(rows, ("tx", "ty"), split_axis=0, concat_axis=0, tiled=True)


def body(
    points,
    counts,
    owner,
    zorder,
    border,
    near,
    w_near,
    gain_one,
    conv_w,
    gain_two,
    w_up,
    w_down,
    grad_out,
):
    points_tile = points[0]
    tile_rows, width = points_tile.shape
    border_rows = border.shape[2]
    edge = 4 * border_rows
    ext = tile_rows + edge
    lists = border[0]
    near_tile = near[0]
    neighbours = near_tile.shape[0]
    tiles = lax.axis_size("tx") * lax.axis_size("ty")
    slots_count = zorder.shape[1]
    capacity = slots_count // tiles
    taps, groups, inner = conv_w.shape[:3]
    conv_rows = conv_w.reshape(taps * groups * inner, inner)
    gain_one_row = gain_one.reshape(1, width)
    gain_two_row = gain_two.reshape(1, width)
    hidden = w_up.shape[1]

    bits = jnp.concatenate([bit_of("tx", 1), bit_of("ty", 1)])
    slots, *sent = call(
        route_kernel,
        [shaped(1, tile_rows, dtype=jnp.int32)] + [shaped(border_rows, width)] * 4,
        [bits, counts, owner, lists, points_tile],
        scratch=[
            pltpu.VMEM((1, tile_rows), jnp.int32),
            pltpu.VMEM((4, border_rows), jnp.int32),
            pltpu.VMEM((tile_rows, width), bf16),
            pltpu.SemaphoreType.DMA((3,)),
        ],
        smem=2,
        held=3,
        flops=4e9,
        tiles=tiles,
        capacity=capacity,
    )
    halos = pairwise(sent[0], sent[1], "tx") + pairwise(sent[2], sent[3], "ty")
    (table,) = call(count_kernel, [shaped(ext, tile_rows)], [near_tile], flops=8e9)
    kept_table, average, pre_act, packed = call(
        lift_kernel,
        [
            shaped(ext, tile_rows),
            shaped(width, tile_rows),
            shaped(tile_rows, width, dtype=f32),
            shaped(slots_count, 2 * width),
        ],
        [bits, slots, points_tile, grad_out[0], *halos, table, w_near],
        smem=1,
        scratch=[
            pltpu.VMEM((ext, width), bf16),
            pltpu.VMEM((width, tile_rows), bf16),
            pltpu.VMEM((tile_rows, width), f32),
            pltpu.VMEM((tile_rows, 2 * width), bf16),
            pltpu.VMEM((slots_count, 2 * width), bf16),
            pltpu.SemaphoreType.DMA((3,)),
            pltpu.SemaphoreType.DMA((slots_count // WIDE,)),
        ],
        flops=4e9,
        stored=4,
        neighbours=neighbours,
    )
    came = exchange(packed, tiles)
    patches = slots_count // PATCH
    patch_scratch = [
        pltpu.VMEM((PATCH + 2 * PAD, width), f32),
        pltpu.VMEM((PATCH, width), f32),
        pltpu.VMEM((PATCH + 2 * PAD, width), f32),
    ]
    serial, state, back_result = call(
        forward_kernel,
        [
            shaped(slots_count, width),
            shaped(slots_count, width, dtype=f32),
            shaped(slots_count, width),
        ],
        [zorder, conv_rows, gain_one_row, gain_two_row, w_up, w_down, came],
        held=1,
        scratch=[
            pltpu.VMEM((slots_count, width), bf16),
            pltpu.VMEM((slots_count, width), bf16),
            pltpu.VMEM((slots_count, width), f32),
            pltpu.VMEM((taps * width, width), bf16),
            pltpu.VMEM((patches, PATCH, width), bf16),
            pltpu.VMEM((patches, PATCH + 2 * PAD, width), f32),
            pltpu.VMEM((patches, PATCH, width), f32),
            pltpu.VMEM((patches, PATCH + 2 * PAD, width), f32),
            pltpu.VMEM((patches, PATCH, width), bf16),
            pltpu.VMEM((patches, PATCH, hidden), bf16),
            pltpu.VMEM((slots_count, width), bf16),
            pltpu.VMEM((slots_count, width), bf16),
            pltpu.SemaphoreType.DMA((3, slots_count // PATCH)),
            pltpu.SemaphoreType.DMA((slots_count // WIDE,)),
        ],
        flops=10e9,
        limit=44,
        stored=3,
        groups=groups,
        inner=inner,
    )
    came_result = exchange(back_result, tiles)
    lines = lax.axis_size("ty")
    sums_rows = 2 * hidden + taps * inner + 16
    sums_rows = -(-sums_rows // (32 * lines)) * (32 * lines)
    back_grad, keep, send = call(
        backward_kernel,
        [
            shaped(slots_count, width),
            shaped(sums_rows // 2, width),
            shaped(sums_rows // 2, width),
        ],
        [
            bit_of("ty", 1),
            zorder,
            conv_rows,
            gain_one_row,
            gain_two_row,
            w_up,
            w_down,
            came,
            serial,
            state,
        ],
        held=3,
        scratch=[
            pltpu.VMEM((slots_count, width), bf16),
            pltpu.VMEM((slots_count, width), bf16),
            pltpu.VMEM((slots_count, width), f32),
            pltpu.VMEM((slots_count, width), bf16),
            pltpu.VMEM((slots_count, width), bf16),
            pltpu.VMEM((slots_count, width), bf16),
            pltpu.VMEM((sums_rows, width), bf16),
            pltpu.VMEM((taps * width, width), bf16),
            pltpu.VMEM((slots_count, width), bf16),
            pltpu.VMEM((slots_count, hidden), bf16),
            pltpu.VMEM((slots_count, hidden), bf16),
            pltpu.VMEM((PATCH, width), f32),
            pltpu.VMEM((PATCH + 2 * PAD, width), f32),
            pltpu.VMEM((PATCH, width), bf16),
            *patch_scratch,
            pltpu.VMEM((PATCH, width), bf16),
            pltpu.VMEM((taps, width, width), f32),
            pltpu.VMEM((16, width), f32),
            pltpu.SemaphoreType.DMA((5,)),
            pltpu.SemaphoreType.DMA((slots_count // WIDE,)),
        ],
        stored=3,
        smem=1,
        flops=40e9,
        limit=44,
        groups=groups,
        inner=inner,
    )
    (back_grad,) = call(
        hold_kernel,
        [shaped(slots_count, width)],
        [back_grad],
        after=[came_result.reshape(tiles, capacity, width)],
        held=1,
        stored=1,
        same={0: 0},
    )
    came_back = exchange(back_grad, tiles)
    (out_rows,) = call(
        unpack_kernel, [shaped(tile_rows, width)], [slots, came_result], flops=4e9
    )
    lifted_grad, spread, near_grad, *halo_grad = call(
        tile_back_kernel,
        [shaped(tile_rows, width), shaped(tile_rows, width), shaped(width, width)]
        + [shaped(border_rows, width)] * 4,
        [bits, slots, came_back, w_near, kept_table, average, pre_act],
        smem=1,
        after=[out_rows],
        scratch=[
            pltpu.VMEM((edge, tile_rows), bf16),
            pltpu.VMEM((width, tile_rows), bf16),
            pltpu.VMEM((tile_rows, width), f32),
            pltpu.VMEM((tile_rows, width), bf16),
            pltpu.VMEM((tile_rows, width), bf16),
            pltpu.VMEM((tile_rows, width), bf16),
            pltpu.VMEM((edge, width), bf16),
            pltpu.SemaphoreType.DMA((5,)),
        ],
        flops=6e9,
        limit=24,
        held=3,
        stored=2,
        neighbours=neighbours,
    )
    returned = pairwise(halo_grad[0], halo_grad[1], "tx") + pairwise(halo_grad[2], halo_grad[3], "ty")
    (near_share,) = call(
        near_sum_kernel,
        [shaped(width, width)],
        [exchange(near_grad, tiles)],
        after=returned[:2],
        flops=1e6,
        share=width // tiles,
    )
    near_total = exchange(near_share, tiles)
    totals = sum_over_mesh(
        keep, send, [out_rows], [[near_grad], returned[:2], [near_share], [near_total, *returned[2:]]]
    )
    (grad_points,) = call(
        finish_kernel,
        [shaped(tile_rows, width)],
        [bits, border.reshape(1, edge), *returned, kept_table, spread, lifted_grad],
        smem=1,
        scratch=[
            pltpu.VMEM((edge, width), bf16),
            pltpu.VMEM((tile_rows, tile_rows), bf16),
            pltpu.VMEM((tile_rows, width), bf16),
            pltpu.VMEM((tile_rows, width), bf16),
            pltpu.SemaphoreType.DMA((3,)),
        ],
        held=3,
        flops=1e9,
    )
    scale = 1.0 / math.sqrt(tiles * tile_rows)
    up_sum, down_sum, conv_sum, gain_one_sum, gain_two_sum, near_sum = call(
        spread_kernel,
        [
            shaped(width, hidden, dtype=f32),
            shaped(hidden, width, dtype=f32),
            shaped(*conv_w.shape, dtype=f32),
            shaped(1, width, dtype=f32),
            shaped(1, width, dtype=f32),
            shaped(width, width, dtype=f32),
        ],
        [bit_of("ty", 1), *totals, near_total],
        scratch=[pltpu.VMEM((sums_rows, width), bf16)] * 2,
        smem=1,
        flops=1e6,
        bits=len(steps_of("ty")),
        scale=scale,
    )
    return (
        out_rows[None],
        grad_points[None],
        near_sum,
        gain_one_sum[0],
        conv_sum,
        gain_two_sum[0],
        up_sum,
        down_sum,
    )


def solution(mesh):
    placed = (
        P(("tx", "ty"), None, None),
        P(("tx", "ty")),
        P(("tx", "ty"), None),
        P(("tx", "ty"), None),
        P(("tx", "ty"), None, None),
        P(("tx", "ty"), None, None),
        P(),
        P(),
        P(),
        P(),
        P(),
        P(),
        P(("tx", "ty"), None, None),
    )
    return jax.shard_map(
        body,
        mesh=mesh,
        in_specs=placed,
        out_specs=(
            P(("tx", "ty"), None, None),
            P(("tx", "ty"), None, None),
            P(),
            P(),
            P(),
            P(),
            P(),
            P(),
        ),
        check_vma=False,
    )
```
